128 devices in a mesh: tm: 16 (over x, z_hi, core), row: 8 (over y, z_lo).
Axes of the slice: x: 4, y: 4, z: 4 (z_hi: 2, z_lo: 2; z = z_hi * 2 + z_lo), core: 2. Of those that a mesh axis runs over, the one named last changes fastest.
Arguments:
- stream: float32 [64, 512, 3072], P('tm', 'row'), may hold values from -6 to 6
- clip_ids: int32 [64], replicated, may hold values from 0 to 7, never falling along the last dimension, each value on 1 to 16 neighbouring positions
- modulation: float32 [8, 3, 3072], replicated, may hold values from -2 to 3, as said below
- qkv_weight: bfloat16 [3072, 3, 2048], P(None, None, 'row'), may hold values from -3 to 3
- out_weight: bfloat16 [2048, 3072], replicated, may hold values from -0.125 to 0.125
Outputs:
- update: float32 [64, 512, 3072], P('tm', 'row')
The draws below stay inside these ranges and needn't reach their ends.
Inputs may be any that keep to these rules, and one draw needn't show every extreme that they name: clip_ids never falls along the frames; each clip holds 1 to 16 consecutive frames. `modulation`: 1 + scale and the gate are positive.
All inputs are finite; a program needn't handle non-finite values.
Results may differ from the reference program's by a relative error of at most 0.0095.
Values may be sent and summed in bfloat16 or wider, within the bound.
A program may use at most 192 MiB of HBM per device.

```python
import math
import jax
import jax.numpy as jnp
import numpy as np
from jax import lax

D = 3072
HEADS = 16
HD = 128
CLIP_MOST = 16
HW = 2048
F = 64
S = 512
CLIPS = 8


def draw_modulation(key, part):
    key = jax.random.fold_in(key, 7)
    key_shift, key_scale, key_gate = jax.random.split(key, 3)
    shift = 0.5 * jax.random.truncated_normal(key_shift, -4.0, 4.0, (CLIPS, 1, D), jnp.float32)
    scale_term = jax.random.uniform(key_scale, (CLIPS, 1, D), jnp.float32, 0.0, 1.0)
    gate_term = jnp.exp(jax.random.uniform(key_gate, (CLIPS, 1, D), jnp.float32, jnp.log(0.3), jnp.log(3.0)))
    return jnp.concatenate([shift, scale_term, gate_term], axis=1)


def draw_qkv_weight(key, part):
    key = jax.random.fold_in(key, 11)
    key_base = jax.random.fold_in(key, 0)
    base = jax.random.truncated_normal(key_base, -6.0, 6.0, (D, 3, HW), jnp.float32) * D ** (-0.5)
    return base.astype(jnp.bfloat16)


def level_of(rng, dims, cuts, least, high):
    level, own = 1.0, jax.random.fold_in(rng, 6)
    for dim, blocks in cuts:
        heights = jnp.exp(jax.random.uniform(jax.random.fold_in(own, dim), (blocks,), jnp.float32, least / len(cuts), high / len(cuts)))
        level = level * jnp.repeat(heights, dims[dim] // blocks).reshape([-1 if axis == dim else 1 for axis in range(len(dims))])
    return level


def length_profile(count, total, bound, skew):
    weights = [(1 << 20) // math.isqrt(rank ** skew) + 1 for rank in range(2, count + 1)]
    surplus, given = total - bound - (count - 1), [1] * (count - 1)
    while surplus > 0:
        candidates = [i for i in range(count - 1) if given[i] < bound]
        whole, budget = sum([weights[i] for i in candidates]), surplus
        for i in candidates:
            more = min(bound - given[i], max(1, budget * weights[i] // whole), surplus)
            given[i] = given[i] + more
            surplus = surplus - more
    return np.array([bound] + given)


def ragged_sizes(key, number_of, total, most, lean):
    if number_of == 2:
        one = jax.random.randint(key, (), max(1, total - most), min(most, total - 1) + 1)
        return jnp.stack([one, total - one])
    sizes = jnp.asarray(length_profile(number_of, total, most, lean), jnp.int32)
    twos = (number_of - 1) // 2
    donor, taker = sizes[1:1 + 2 * twos:2], sizes[2:2 + 2 * twos:2]
    room = jnp.minimum(donor - 1, most - taker)
    passed = jax.random.randint(jax.random.fold_in(key, 1), (twos,), 0, 1 << 20) % (room + 1)
    sizes = sizes.at[1:1 + 2 * twos:2].set(donor - passed).at[2:2 + 2 * twos:2].set(taker + passed)
    return sizes[jax.random.permutation(jax.random.fold_in(key, 2), number_of)]


def scatter_about(stream_key, dims, spread, most, cuts=(), held_as=jnp.bfloat16):
    entries = spread * jax.random.normal(stream_key, dims, jnp.float32)
    if cuts:
        entries = entries * level_of(stream_key, dims, cuts, -0.22, 0.18)
    return jnp.clip(entries, -most, most).astype(held_as)


def setup_inputs(seed: int = 0) -> dict:
    keys = jax.random.split(jax.random.key(seed), 6)
    stream = scatter_about(keys[0], (F, S, D), 1.0, 6.0, ((0, 16), (1, 8)), jnp.float32)
    clip_ids = jnp.searchsorted(jnp.cumsum(ragged_sizes(keys[1], CLIPS, F, CLIP_MOST, 1)), jnp.arange(F), side="right").astype(jnp.int32)
    modulation = draw_modulation(jax.random.fold_in(keys[5], 71), 0)
    qkv_weight = draw_qkv_weight(jax.random.fold_in(keys[5], 71), 0)
    out_weight = scatter_about(keys[4], (HW, D), HW ** -0.5, 0.125)
    return dict(stream=stream, clip_ids=clip_ids, modulation=modulation, qkv_weight=qkv_weight, out_weight=out_weight)


def layer_norm(activation):
    average = lax.optimization_barrier(jnp.mean(activation, axis=-1, keepdims=True))
    centred = activation - average
    variance = lax.optimization_barrier(jnp.mean(centred * centred, axis=-1, keepdims=True))
    return centred * lax.rsqrt(variance + 1e-06)

def reference(stream, clip_ids, modulation, qkv_weight, out_weight):
    onehot = (clip_ids[:, None] == jnp.arange(CLIPS, dtype=jnp.int32)[None, :]).astype(jnp.float32)
    per_frame = jnp.dot(onehot, modulation.reshape(CLIPS, 3 * D), precision=lax.Precision.HIGHEST).reshape(F, 3, D)
    normed = layer_norm(stream) * (1.0 + per_frame[:, 1][:, None, :]) + per_frame[:, 0][:, None, :]
    normed = normed.astype(jnp.bfloat16)
    projected = jnp.dot(normed.reshape(F * S, D), qkv_weight.reshape(D, 3 * HW), preferred_element_type=jnp.float32)
    projected = projected.astype(jnp.bfloat16).reshape(F, S, 3, HEADS, HD)
    by_head = jnp.transpose(projected, (3, 2, 0, 1, 4))
    same_clip = clip_ids[:, None] == clip_ids[None, :]

    def one_head(head_block):
        queries = head_block[0].astype(jnp.float32)
        key_rows = head_block[1].astype(jnp.float32)
        values = head_block[2].astype(jnp.float32)
        scores = jnp.einsum('fsd,ftd->fst', queries, key_rows) / math.sqrt(HD)
        row_max = lax.optimization_barrier(jnp.max(scores, axis=-1, keepdims=True))
        weights = jnp.exp(scores - row_max)
        rounded = lax.optimization_barrier(weights.astype(jnp.bfloat16)).astype(jnp.float32)
        spatial_out = jnp.einsum('fst,ftd->fsd', rounded, values) / lax.optimization_barrier(jnp.sum(weights, axis=-1, keepdims=True))
        scores = jnp.einsum('fsd,gsd->sfg', queries, key_rows) / math.sqrt(HD)
        scores = jnp.where(same_clip[None], scores, -1e+30)
        row_max = lax.optimization_barrier(jnp.max(scores, axis=-1, keepdims=True))
        weights = jnp.where(same_clip[None], jnp.exp(scores - row_max), 0.0)
        rounded = lax.optimization_barrier(weights.astype(jnp.bfloat16)).astype(jnp.float32)
        denom_sum = jnp.transpose(lax.optimization_barrier(jnp.sum(weights, axis=-1)))
        temporal_out = jnp.einsum('sfg,gsd->fsd', rounded, values) / denom_sum[:, :, None]
        return (spatial_out + temporal_out).astype(jnp.bfloat16)
    combined = lax.map(one_head, by_head)
    combined = jnp.transpose(combined, (1, 2, 0, 3)).reshape(F * S, HW)
    update = jnp.dot(combined, out_weight, preferred_element_type=jnp.float32).reshape(F, S, D)
    return update * per_frame[:, 2][:, None, :]
```

```python
import functools
import math

import jax
import jax.numpy as jnp
from jax import lax
from jax.experimental import pallas as pl
from jax.experimental.pallas import tpu as pltpu
from jax.sharding import PartitionSpec as P

HD = 128
MESH = pl.DeviceIdType.MESH
BF = jnp.bfloat16
F32 = jnp.float32
LOG2E = 1.4426950408889634


def dot(a, b):
    return jnp.dot(a, b, preferred_element_type=F32)


def dot_nt(a, b):
    return lax.dot_general(a, b, (((1,), (1,)), ((), ())), preferred_element_type=F32)


def attention_kernel(
    clip_ref, stream_hbm, mod_ref, w_hbm, comb_ref,
    stream_v, xg, wbuf, qkv, tsend, trecv, osend, orecv, csend, sp, perm, perm_t, mask,
    load_sem, y_send, y_recv, w_send, w_recv, z_send, z_recv, t_send, t_recv,
    o_send, o_recv, c_send, c_recv,
):
    tm = lax.axis_index("tm")
    row = lax.axis_index("row")
    zh = (tm // 2) % 2
    core = tm % 2
    y = row // 2
    zl = row % 2
    hz = (zl + zh) % 2
    partner_row = y * 2 + (1 - zl)
    outer_tm = tm + 2 - 4 * zh
    other_core = tm + 1 - 2 * core
    up_row = ((y + 1) % 4) * 2 + zl
    down_row = ((y + 3) % 4) * 2 + zl

    def rcopy(src, dst, send, recv, dev):
        return pltpu.make_async_remote_copy(
            src_ref=src, dst_ref=dst, send_sem=send, recv_sem=recv,
            device_id=dev, device_id_type=MESH,
        )

    def time_peer(t):
        return (t, y * 2 + (hz + (t // 2) % 2) % 2)

    load_stream = pltpu.make_async_copy(stream_hbm, stream_v, load_sem.at[0])
    load_stream.start()
    load_w = pltpu.make_async_copy(w_hbm, wbuf.at[zl], load_sem.at[1])
    load_w.start()

    barrier = pltpu.get_barrier_semaphore()

    @pl.loop(1, 16)
    def _(k):
        pl.semaphore_signal(barrier, inc=1, device_id=time_peer((tm + k) % 16), device_id_type=MESH)

    @pl.loop(1, 8)
    def _(k):
        pl.semaphore_signal(barrier, inc=1, device_id=(tm, (row + k) % 8), device_id_type=MESH)

    pl.semaphore_wait(barrier, 22)

    qa = core * 2
    w_out = [
        rcopy(w_hbm.at[:, qa], wbuf.at[zl, :, qa], w_send.at[0], w_recv.at[0], (tm, partner_row)),
        rcopy(w_hbm.at[:, qa + 1], wbuf.at[zl, :, qa + 1], w_send.at[1], w_recv.at[1],
              (outer_tm, partner_row)),
    ]
    for c in w_out:
        c.start()

    load_stream.wait()

    def norm_frame(f):
        clip = clip_ref[tm * 4 + f]
        shift = mod_ref[0, pl.ds(clip, 1), :]
        scale = 1.0 + mod_ref[1, pl.ds(clip, 1), :]
        for part in range(2):
            v = stream_v[f, pl.ds(part * 32, 32), :]
            centred = v - jnp.mean(v, axis=-1, keepdims=True)
            var = jnp.mean(centred * centred, axis=-1, keepdims=True)
            n = centred * lax.rsqrt(var + 1e-06) * scale + shift
            xg[y, pl.ds(f * 64 + part * 32, 32), :] = n.astype(BF)

    lo, hi = pl.ds(0, 128), pl.ds(128, 128)
    ym, yp, yq = (y + 3) % 4, (y + 1) % 4, (y + 2) % 4
    up, down = (tm, up_row), (tm, down_row)

    def ycopy(block, half, i, dev):
        return rcopy(xg.at[block, half], xg.at[block, half], y_send.at[i], y_recv.at[i], dev)

    @pl.loop(0, 2)
    def _(f):
        norm_frame(f)

    ycopy(y, lo, 0, up).start()

    @pl.loop(2, 4)
    def _(f):
        norm_frame(f)

    ycopy(y, hi, 2, down).start()
    ycopy(y, hi, 1, up).start()
    ycopy(y, lo, 3, down).start()

    def frame_row(j):
        return ((j // 4) % 4) * 64 + (j // 16) * 4 + j % 4

    r_i = lax.broadcasted_iota(jnp.int32, (256, 256), 0)
    c_i = lax.broadcasted_iota(jnp.int32, (256, 256), 1)
    perm[...] = (frame_row(r_i) == c_i).astype(BF)
    perm_t[...] = (frame_row(c_i) == r_i).astype(BF)
    fr = r_i // 4
    fc = c_i // 4

    def clip_of(f, carry):
        a, b = carry
        c = clip_ref[f]
        return jnp.where(fr == f, c, a), jnp.where(fc == f, c, b)

    zero = jnp.zeros((256, 256), jnp.int32)
    clip_r, clip_c = lax.fori_loop(0, 64, clip_of, (zero, zero))
    same = (clip_r == clip_c) & (r_i % 4 == c_i % 4)
    mask[...] = jnp.where(same, 0.0, -1e30).astype(F32)

    def project(yb, pz):
        kk = (pz + hz) % 2
        slot = kk * 2 + (1 - kk) * zl

        @pl.loop(0, 3)
        def _(part):
            acc = dot(xg[yb, :, 0:768], wbuf[pz, part, 0])
            for q in range(1, 4):
                acc = acc + dot(xg[yb, :, q * 768:(q + 1) * 768], wbuf[pz, part, q])
            qkv[yb, slot, part] = acc.astype(BF)

    def zcopy(yb, d):
        return rcopy(qkv.at[yb, 2], qkv.at[yb, zl], z_send.at[d], z_recv.at[d], (tm, partner_row))

    def tcopy(yb, d, t):
        return rcopy(tsend.at[yb, :, :, t], trecv.at[yb, :, :, tm], t_send.at[d, t], t_recv.at[d, tm],
                     time_peer(t))

    def stage_time(yb, d):
        rcopy(qkv.at[yb, 2], qkv.at[yb, 1 - zl], z_send.at[d], z_recv.at[d], (tm, partner_row)).wait_recv()

        @pl.loop(0, 6)
        def _(i):
            zz, part = i // 3, i % 3
            moved = dot(perm[...], qkv[yb, zz, part]).astype(BF)
            tsend[yb, zz, part] = moved.reshape(16, 16, 256)
            trecv[yb, zz, part, tm] = tsend[yb, zz, part, tm]

        @pl.loop(1, 16)
        def _(k):
            tcopy(yb, d, (tm + k) % 16).start()

    load_w.wait()
    project(y, zl)

    oz = 1 - zl
    for i in range(2):
        rcopy(w_hbm.at[:, qa + i], wbuf.at[oz, :, qa + i], w_send.at[i], w_recv.at[i],
              (tm, partner_row)).wait_recv()
        rcopy(wbuf.at[oz, :, qa + i], wbuf.at[oz, :, qa + i], w_send.at[2 + i], w_recv.at[2 + i],
              (other_core, row)).start()
    ycopy(ym, lo, 0, up).wait_recv()
    ycopy(ym, lo, 4, up).start()
    ycopy(yp, hi, 2, down).wait_recv()
    ycopy(yp, hi, 5, down).start()
    qb = (1 - core) * 2
    for i in range(2):
        rcopy(wbuf.at[oz, :, qb + i], wbuf.at[oz, :, qb + i], w_send.at[2 + i], w_recv.at[2 + i],
              (other_core, row)).wait_recv()

    project(y, oz)
    zcopy(y, 0).start()

    ycopy(ym, hi, 1, up).wait_recv()
    project(ym, 1 - hz)
    zcopy(ym, 1).start()
    project(ym, hz)
    stage_time(y, 0)

    ycopy(yp, lo, 3, down).wait_recv()
    project(yp, 1 - hz)
    zcopy(yp, 2).start()
    project(yp, hz)
    stage_time(ym, 1)

    ycopy(yq, lo, 4, up).wait_recv()
    ycopy(yq, hi, 5, down).wait_recv()
    project(yq, 1 - hz)
    zcopy(yq, 3).start()
    project(yq, hz)
    stage_time(yp, 2)
    stage_time(yq, 3)

    factor = LOG2E / math.sqrt(HD)

    def soften(s):
        p = jnp.exp2((s - jnp.max(s, axis=-1, keepdims=True)) * factor)
        return p, jnp.sum(p, axis=-1, keepdims=True)

    @pl.loop(0, 4)
    def _(f):
        rows = pl.ds(pl.multiple_of(f * 64, 64), 64)
        for h in range(2):
            cols = pl.ds(h * HD, HD)
            q, k, v = (qkv[:, 0:2, part, rows, cols].reshape(512, HD) for part in range(3))
            for half in range(2):
                p, total = soften(dot_nt(q[half * 256:(half + 1) * 256], k))
                o = dot(p.astype(BF), v) / total
                sp[pl.ds(half * 2, 2), :, rows, cols] = o.reshape(2, 2, 64, HD)

    for d, yb in enumerate((y, ym, yp, yq)):
        @pl.loop(1, 16)
        def _(k, d=d, yb=yb):
            t = (tm + k) % 16
            rcopy(tsend.at[yb, :, :, t], trecv.at[yb, :, :, t], t_send.at[d, t], t_recv.at[d, t],
                  time_peer(t)).wait_recv()

        @pl.loop(0, 2)
        def _(zz, yb=yb):
            for h in range(2):
                cols = pl.ds(h * HD, HD)
                q, k, v = (trecv[yb, zz, part, :, :, cols].reshape(256, HD) for part in range(3))
                p, total = soften(dot_nt(q, k) + mask[...])
                o = dot(p.astype(BF), v) / total
                osend[yb, zz, :, :, cols] = o.astype(BF).reshape(16, 16, HD)

    def ocopy(t, at):
        return rcopy(osend.at[:, :, t], orecv.at[:, :, at], o_send.at[t], o_recv.at[at], time_peer(t))

    @pl.loop(1, 16)
    def _(k):
        ocopy((tm + k) % 16, tm).start()

    orecv[:, :, tm] = osend[:, :, tm]

    @pl.loop(1, 16)
    def _(k):
        t = (tm + k) % 16
        ocopy(t, t).wait_recv()

    def cols_of(r):
        return pl.ds(pl.multiple_of((2 * (r // 2) + (r % 2 + zh) % 2) * 256, 256), 256)

    def ccopy(r, owner):
        return rcopy(csend.at[r], comb_ref.at[:, cols_of(owner)], c_send.at[r], c_recv.at[owner], (tm, r))

    def combine(r):
        back = dot(perm_t[...], orecv[r // 2, r % 2].reshape(256, 256))
        csend[r] = (sp[r // 2, r % 2] + back).astype(BF)

    @pl.loop(1, 8)
    def _(k):
        r = (row + k) % 8
        combine(r)
        ccopy(r, row).start()

    combine(row)
    comb_ref[:, cols_of(row)] = csend[row]

    @pl.loop(1, 8)
    def _(k):
        r = (row + k) % 8
        ccopy(r, r).wait_recv()

    for c in w_out:
        c.wait_send()
    for i in range(2):
        rcopy(wbuf.at[oz, :, qa + i], wbuf.at[oz, :, qa + i], w_send.at[2 + i], w_recv.at[2 + i],
              (other_core, row)).wait_send()
    for i, (block, half) in enumerate(((y, lo), (y, hi), (y, hi), (y, lo), (ym, lo), (yp, hi))):
        ycopy(block, half, i, up).wait_send()
    for d, yb in enumerate((y, ym, yp, yq)):
        zcopy(yb, d).wait_send()

        @pl.loop(1, 16)
        def _(k, d=d, yb=yb):
            tcopy(yb, d, (tm + k) % 16).wait_send()

    @pl.loop(1, 16)
    def _(k):
        ocopy((tm + k) % 16, tm).wait_send()

    @pl.loop(1, 8)
    def _(k):
        ccopy((row + k) % 8, row).wait_send()


def attention(clip_ids, stream, mod, weight):
    vmem = pl.BlockSpec(memory_space=pltpu.VMEM)
    hbm = pl.BlockSpec(memory_space=pl.ANY)
    dma = pltpu.SemaphoreType.DMA
    return pl.pallas_call(
        attention_kernel,
        out_shape=jax.ShapeDtypeStruct((256, 2048), BF),
        in_specs=[pl.BlockSpec(memory_space=pltpu.SMEM), hbm, vmem, hbm],
        out_specs=vmem,
        scratch_shapes=[
            pltpu.VMEM((4, 64, 3072), F32),
            pltpu.VMEM((4, 256, 3072), BF),
            pltpu.VMEM((2, 3, 4, 768, 256), BF),
            pltpu.VMEM((4, 3, 3, 256, 256), BF),
            pltpu.VMEM((4, 2, 3, 16, 16, 256), BF),
            pltpu.VMEM((4, 2, 3, 16, 16, 256), BF),
            pltpu.VMEM((4, 2, 16, 16, 256), BF),
            pltpu.VMEM((4, 2, 16, 16, 256), BF),
            pltpu.VMEM((8, 256, 256), BF),
            pltpu.VMEM((4, 2, 256, 256), F32),
            pltpu.VMEM((256, 256), BF),
            pltpu.VMEM((256, 256), BF),
            pltpu.VMEM((256, 256), F32),
            dma((2,)),
            dma((6,)), dma((6,)),
            dma((4,)), dma((4,)),
            dma((4,)), dma((4,)),
            dma((4, 16)), dma((4, 16)),
            dma((16,)), dma((16,)),
            dma((8,)), dma((8,)),
        ],
        compiler_params=pltpu.CompilerParams(
            collective_id=0, has_side_effects=True, vmem_limit_bytes=58 * 1024 * 1024
        ),
        name="attention",
    )(clip_ids, stream, mod, weight)


def out_kernel(clip_ref, comb_ref, weight_ref, gate_ref, out_ref):
    tm = lax.axis_index("tm")
    acc = dot(comb_ref[...], weight_ref[...])
    for f in range(4):
        clip = clip_ref[tm * 4 + f]
        out_ref[f] = acc[f * 64:(f + 1) * 64] * gate_ref[0, pl.ds(clip, 1), :]


def out_projection(clip_ids, comb, out_weight, mod):
    tile = 512
    return pl.pallas_call(
        out_kernel,
        grid=(3072 // tile,),
        out_shape=jax.ShapeDtypeStruct((4, 64, 3072), F32),
        in_specs=[
            pl.BlockSpec(memory_space=pltpu.SMEM),
            pl.BlockSpec((256, 2048), lambda i: (0, 0)),
            pl.BlockSpec((2048, tile), lambda i: (0, i)),
            pl.BlockSpec((1, 8, tile), lambda i: (2, 0, i)),
        ],
        out_specs=pl.BlockSpec((4, 64, tile), lambda i: (0, 0, i)),
        compiler_params=pltpu.CompilerParams(vmem_limit_bytes=32 * 1024 * 1024),
        name="out_projection",
    )(clip_ids, comb, out_weight, mod)


def per_device(stream, clip_ids, modulation, qkv_weight, out_weight):
    mod = jnp.transpose(modulation, (1, 0, 2))
    weight = jnp.transpose(qkv_weight, (1, 0, 2)).reshape(3, 4, 768, 256)
    comb = attention(clip_ids, stream, mod, weight)
    return out_projection(clip_ids, comb, out_weight, mod)


def solution(mesh):
    placed = (P("tm", "row", None), P(), P(), P(None, None, "row"), P())
    return jax.shard_map(
        per_device, mesh=mesh, in_specs=placed, out_specs=P("tm", "row", None), check_vma=False
    )
```

```python
import functools
import math

import jax
import jax.numpy as jnp
from jax import lax
from jax.experimental import pallas as pl
from jax.experimental.pallas import tpu as pltpu
from jax.sharding import PartitionSpec as P

HD = 128
MESH = pl.DeviceIdType.MESH
BF = jnp.bfloat16
F32 = jnp.float32
LOG2E = 1.4426950408889634


def dot(a, b):
    return jnp.dot(a, b, preferred_element_type=F32)


def dot_nt(a, b):
    return lax.dot_general(a, b, (((1,), (1,)), ((), ())), preferred_element_type=F32)


def attention_kernel(
    clip_ref, stream_hbm, mod_ref, w_hbm, wo_hbm, out_ref,
    stream_v, xg, wbuf, wo, qkv, tsend, trecv, osend, orecv, csend, comb, sp, perm, perm_t, mask,
    load_sem, y_send, y_recv, w_send, w_recv, z_send, z_recv, t_send, t_recv,
    o_send, o_recv, c_send, c_recv,
):
    tm = lax.axis_index("tm")
    row = lax.axis_index("row")
    zh = (tm // 2) % 2
    core = tm % 2
    y = row // 2
    zl = row % 2
    hz = (zl + zh) % 2
    partner_row = y * 2 + (1 - zl)
    outer_tm = tm + 2 - 4 * zh
    other_core = tm + 1 - 2 * core
    up_row = ((y + 1) % 4) * 2 + zl
    down_row = ((y + 3) % 4) * 2 + zl

    def rcopy(src, dst, send, recv, dev):
        return pltpu.make_async_remote_copy(
            src_ref=src, dst_ref=dst, send_sem=send, recv_sem=recv,
            device_id=dev, device_id_type=MESH,
        )

    def time_peer(t):
        return (t, y * 2 + (hz + (t // 2) % 2) % 2)

    load_stream = pltpu.make_async_copy(stream_hbm, stream_v, load_sem.at[0])
    load_stream.start()
    load_w = pltpu.make_async_copy(w_hbm, wbuf.at[zl], load_sem.at[1])
    load_w.start()
    load_wo = pltpu.make_async_copy(wo_hbm, wo, load_sem.at[2])
    load_wo.start()

    barrier = pltpu.get_barrier_semaphore()

    @pl.loop(1, 16)
    def _(k):
        pl.semaphore_signal(barrier, inc=1, device_id=time_peer((tm + k) % 16), device_id_type=MESH)

    @pl.loop(1, 8)
    def _(k):
        pl.semaphore_signal(barrier, inc=1, device_id=(tm, (row + k) % 8), device_id_type=MESH)

    pl.semaphore_wait(barrier, 22)

    qa = core * 2
    w_out = [
        rcopy(w_hbm.at[:, qa], wbuf.at[zl, :, qa], w_send.at[0], w_recv.at[0], (tm, partner_row)),
        rcopy(w_hbm.at[:, qa + 1], wbuf.at[zl, :, qa + 1], w_send.at[1], w_recv.at[1],
              (outer_tm, partner_row)),
    ]
    for c in w_out:
        c.start()

    load_stream.wait()

    def norm_frame(f):
        clip = clip_ref[tm * 4 + f]
        shift = mod_ref[0, pl.ds(clip, 1), :]
        scale = 1.0 + mod_ref[1, pl.ds(clip, 1), :]
        for part in range(2):
            v = stream_v[f, pl.ds(part * 32, 32), :]
            centred = v - jnp.mean(v, axis=-1, keepdims=True)
            var = jnp.mean(centred * centred, axis=-1, keepdims=True)
            n = centred * lax.rsqrt(var + 1e-06) * scale + shift
            xg[y, pl.ds(f * 64 + part * 32, 32), :] = n.astype(BF)

    lo, hi = pl.ds(0, 128), pl.ds(128, 128)
    ym, yp, yq = (y + 3) % 4, (y + 1) % 4, (y + 2) % 4
    up, down = (tm, up_row), (tm, down_row)

    def ycopy(block, half, i, dev):
        return rcopy(xg.at[block, half], xg.at[block, half], y_send.at[i], y_recv.at[i], dev)

    @pl.loop(0, 2)
    def _(f):
        norm_frame(f)

    ycopy(y, lo, 0, up).start()

    @pl.loop(2, 4)
    def _(f):
        norm_frame(f)

    ycopy(y, hi, 2, down).start()
    ycopy(y, hi, 1, up).start()
    ycopy(y, lo, 3, down).start()

    def frame_row(j):
        return ((j // 4) % 4) * 64 + (j // 16) * 4 + j % 4

    r_i = lax.broadcasted_iota(jnp.int32, (256, 256), 0)
    c_i = lax.broadcasted_iota(jnp.int32, (256, 256), 1)
    perm[...] = (frame_row(r_i) == c_i).astype(BF)
    perm_t[...] = (frame_row(c_i) == r_i).astype(BF)
    fr = r_i // 4
    fc = c_i // 4

    def clip_of(f, carry):
        a, b = carry
        c = clip_ref[f]
        return jnp.where(fr == f, c, a), jnp.where(fc == f, c, b)

    zero = jnp.zeros((256, 256), jnp.int32)
    clip_r, clip_c = lax.fori_loop(0, 64, clip_of, (zero, zero))
    same = (clip_r == clip_c) & (r_i % 4 == c_i % 4)
    mask[...] = jnp.where(same, 0.0, -1e30).astype(F32)

    def project(yb, pz):
        kk = (pz + hz) % 2
        slot = kk * 2 + (1 - kk) * zl

        @pl.loop(0, 3)
        def _(part):
            acc = dot(xg[yb, :, 0:768], wbuf[pz, part, 0])
            for q in range(1, 4):
                acc = acc + dot(xg[yb, :, q * 768:(q + 1) * 768], wbuf[pz, part, q])
            qkv[yb, slot, part] = acc.astype(BF)

    def zcopy(yb, d):
        return rcopy(qkv.at[yb, 2], qkv.at[yb, zl], z_send.at[d], z_recv.at[d], (tm, partner_row))

    def tcopy(yb, d, zz, t, at):
        return rcopy(tsend.at[yb, zz, :, t], trecv.at[yb, zz, :, at], t_send.at[d, zz, t],
                     t_recv.at[d, zz, at], time_peer(t))

    def stage_time(yb, d, zz):
        @pl.loop(0, 3)
        def _(part):
            moved = dot(perm[...], qkv[yb, zz, part]).astype(BF)
            tsend[yb, zz, part] = moved.reshape(16, 16, 256)
            trecv[yb, zz, part, tm] = tsend[yb, zz, part, tm]

        @pl.loop(1, 16)
        def _(k):
            tcopy(yb, d, zz, (tm + k) % 16, tm).start()

    def stage_partner(yb, d):
        rcopy(qkv.at[yb, 2], qkv.at[yb, 1 - zl], z_send.at[d], z_recv.at[d], (tm, partner_row)).wait_recv()
        stage_time(yb, d, 1 - zl)

    factor = LOG2E / math.sqrt(HD)

    def soften(s):
        p = jnp.exp2((s - jnp.max(s, axis=-1, keepdims=True)) * factor)
        return p, jnp.sum(p, axis=-1, keepdims=True)

    def ocopy(yb, d, t, at):
        return rcopy(osend.at[yb, :, t], orecv.at[yb, :, at], o_send.at[d, t], o_recv.at[d, at],
                     time_peer(t))

    def temporal(yb, d):
        @pl.loop(0, 30)
        def _(i):
            t = (tm + 1 + i % 15) % 16
            tcopy(yb, d, i // 15, t, t).wait_recv()

        @pl.loop(0, 2)
        def _(zz):
            for h in range(2):
                cols = pl.ds(h * HD, HD)
                q, k, v = (trecv[yb, zz, part, :, :, cols].reshape(256, HD) for part in range(3))
                p, total = soften(dot_nt(q, k) + mask[...])
                o = dot(p.astype(BF), v) / total
                osend[yb, zz, :, :, cols] = o.astype(BF).reshape(16, 16, HD)

        orecv[yb, :, tm] = osend[yb, :, tm]

        @pl.loop(1, 16)
        def _(k):
            ocopy(yb, d, (tm + k) % 16, tm).start()

    def spatial():
        @pl.loop(0, 4)
        def _(f):
            rows = pl.ds(pl.multiple_of(f * 64, 64), 64)
            for h in range(2):
                cols = pl.ds(h * HD, HD)
                q, k, v = (qkv[:, 0:2, part, rows, cols].reshape(512, HD) for part in range(3))
                for half in range(2):
                    p, total = soften(dot_nt(q[half * 256:(half + 1) * 256], k))
                    o = dot(p.astype(BF), v) / total
                    sp[pl.ds(half * 2, 2), :, rows, cols] = o.reshape(2, 2, 64, HD)

    def ccopy(r, at, kept):
        return rcopy(csend.at[r], comb.at[kept], c_send.at[r], c_recv.at[at], (tm, r))

    def combine(yb, zz):
        back = dot(perm_t[...], orecv[yb, zz].reshape(256, 256))
        return (sp[yb, zz] + back).astype(BF)

    def combine_send(yb, zz):
        r = yb * 2 + zz
        csend[r] = combine(yb, zz)
        ccopy(r, row, y * 2 + hz).start()

    def wait_back(yb, d):
        @pl.loop(1, 16)
        def _(k):
            t = (tm + k) % 16
            ocopy(yb, d, t, t).wait_recv()

    def combine_block(yb, d):
        wait_back(yb, d)
        for zz in range(2):
            combine_send(yb, zz)

    def project_out(ys, first=False, last=False):
        for i in range(2):
            r = ys * 2 + i
            if first:
                @pl.when(i != zl)
                def _(r=r):
                    ccopy(r, r, y * 2 + (r + zh) % 2).wait_recv()
            else:
                ccopy(r, r, ys * 2 + (r + zh) % 2).wait_recv()

        @pl.loop(0, 6)
        def _(n):
            cols = pl.ds(pl.multiple_of(n * 512, 512), 512)
            acc = dot(comb[2 * ys], wo[2 * ys, :, cols]) + dot(comb[2 * ys + 1], wo[2 * ys + 1, :, cols])
            acc = acc.reshape(4, 64, 512)
            if not first:
                acc = acc + out_ref[:, :, cols]
            if not last:
                out_ref[:, :, cols] = acc
            else:
                for f in range(4):
                    clip = clip_ref[tm * 4 + f]
                    out_ref[f, :, cols] = acc[f] * mod_ref[2, pl.ds(clip, 1), cols]

    load_w.wait()
    project(y, zl)

    oz = 1 - zl
    for i in range(2):
        rcopy(w_hbm.at[:, qa + i], wbuf.at[oz, :, qa + i], w_send.at[i], w_recv.at[i],
              (tm, partner_row)).wait_recv()
        rcopy(wbuf.at[oz, :, qa + i], wbuf.at[oz, :, qa + i], w_send.at[2 + i], w_recv.at[2 + i],
              (other_core, row)).start()
    ycopy(ym, lo, 0, up).wait_recv()
    ycopy(ym, lo, 4, up).start()
    ycopy(yp, hi, 2, down).wait_recv()
    ycopy(yp, hi, 5, down).start()
    qb = (1 - core) * 2
    for i in range(2):
        rcopy(wbuf.at[oz, :, qb + i], wbuf.at[oz, :, qb + i], w_send.at[2 + i], w_recv.at[2 + i],
              (other_core, row)).wait_recv()

    project(y, oz)
    zcopy(y, 0).start()
    stage_time(y, 0, zl)

    ycopy(ym, hi, 1, up).wait_recv()
    project(ym, 1 - hz)
    zcopy(ym, 1).start()
    project(ym, hz)
    stage_time(ym, 1, zl)
    stage_partner(y, 0)

    ycopy(yp, lo, 3, down).wait_recv()
    project(yp, 1 - hz)
    zcopy(yp, 2).start()
    project(yp, hz)
    stage_time(yp, 2, zl)
    stage_partner(ym, 1)
    temporal(y, 0)
    stage_partner(yp, 2)

    ycopy(yq, lo, 4, up).wait_recv()
    ycopy(yq, hi, 5, down).wait_recv()
    project(yq, 1 - hz)
    zcopy(yq, 3).start()
    project(yq, hz)
    stage_time(yq, 3, zl)
    temporal(ym, 1)
    stage_partner(yq, 3)
    temporal(yp, 2)
    spatial()

    wait_back(y, 0)
    combine_send(y, 1 - zl)
    comb[y * 2 + hz] = combine(y, zl)
    combine_block(ym, 1)
    temporal(yq, 3)
    combine_block(yp, 2)
    load_wo.wait()
    project_out(y, first=True)
    combine_block(yq, 3)
    project_out(yp)
    project_out(ym)
    project_out(yq, last=True)

    for c in w_out:
        c.wait_send()
    for i in range(2):
        rcopy(wbuf.at[oz, :, qa + i], wbuf.at[oz, :, qa + i], w_send.at[2 + i], w_recv.at[2 + i],
              (other_core, row)).wait_send()
    for i, (block, half) in enumerate(((y, lo), (y, hi), (y, hi), (y, lo), (ym, lo), (yp, hi))):
        ycopy(block, half, i, up).wait_send()
    for d, yb in enumerate((y, ym, yp, yq)):
        zcopy(yb, d).wait_send()

        @pl.loop(0, 30)
        def _(i, d=d, yb=yb):
            tcopy(yb, d, i // 15, (tm + 1 + i % 15) % 16, tm).wait_send()

        @pl.loop(1, 16)
        def _(k, d=d, yb=yb):
            ocopy(yb, d, (tm + k) % 16, tm).wait_send()

    @pl.loop(1, 8)
    def _(k):
        ccopy((row + k) % 8, row, y * 2 + hz).wait_send()


def attention(clip_ids, stream, mod, weight, out_weight):
    vmem = pl.BlockSpec(memory_space=pltpu.VMEM)
    hbm = pl.BlockSpec(memory_space=pl.ANY)
    dma = pltpu.SemaphoreType.DMA
    return pl.pallas_call(
        attention_kernel,
        out_shape=jax.ShapeDtypeStruct((4, 64, 3072), F32),
        in_specs=[pl.BlockSpec(memory_space=pltpu.SMEM), hbm, vmem, hbm, hbm],
        out_specs=vmem,
        scratch_shapes=[
            pltpu.VMEM((4, 64, 3072), F32),
            pltpu.VMEM((4, 256, 3072), BF),
            pltpu.VMEM((2, 3, 4, 768, 256), BF),
            pltpu.VMEM((8, 256, 3072), BF),
            pltpu.VMEM((4, 3, 3, 256, 256), BF),
            pltpu.VMEM((4, 2, 3, 16, 16, 256), BF),
            pltpu.VMEM((4, 2, 3, 16, 16, 256), BF),
            pltpu.VMEM((4, 2, 16, 16, 256), BF),
            pltpu.VMEM((4, 2, 16, 16, 256), BF),
            pltpu.VMEM((8, 256, 256), BF),
            pltpu.VMEM((8, 256, 256), BF),
            pltpu.VMEM((4, 2, 256, 256), F32),
            pltpu.VMEM((256, 256), BF),
            pltpu.VMEM((256, 256), BF),
            pltpu.VMEM((256, 256), F32),
            dma((3,)),
            dma((6,)), dma((6,)),
            dma((4,)), dma((4,)),
            dma((4,)), dma((4,)),
            dma((4, 2, 16)), dma((4, 2, 16)),
            dma((4, 16)), dma((4, 16)),
            dma((8,)), dma((8,)),
        ],
        compiler_params=pltpu.CompilerParams(
            collective_id=0, has_side_effects=True, vmem_limit_bytes=60 * 1024 * 1024
        ),
        name="attention",
    )(clip_ids, stream, mod, weight, out_weight)


def per_device(stream, clip_ids, modulation, qkv_weight, out_weight):
    mod = jnp.transpose(modulation, (1, 0, 2))
    weight = jnp.transpose(qkv_weight, (1, 0, 2)).reshape(3, 4, 768, 256)
    return attention(clip_ids, stream, mod, weight, out_weight.reshape(8, 256, 3072))


def solution(mesh):
    placed = (P("tm", "row", None), P(), P(), P(None, None, "row"), P())
    return jax.shard_map(
        per_device, mesh=mesh, in_specs=placed, out_specs=P("tm", "row", None), check_vma=False
    )
```

```python
import functools
import math

import jax
import jax.numpy as jnp
from jax import lax
from jax.experimental import pallas as pl
from jax.experimental.pallas import tpu as pltpu
from jax.sharding import PartitionSpec as P

HD = 128
MESH = pl.DeviceIdType.MESH
BF = jnp.bfloat16
F32 = jnp.float32
LOG2E = 1.4426950408889634


def dot(a, b):
    return jnp.dot(a, b, preferred_element_type=F32)


def dot_nt(a, b):
    return lax.dot_general(a, b, (((1,), (1,)), ((), ())), preferred_element_type=F32)


def attention_kernel(
    clip_ref, stream_hbm, mod_ref, w_hbm, wo_hbm, out_ref,
    stream_v, xg, wbuf, wo, qkv, tsend, trecv, osend, orecv, csend, comb, sp, perm, perm_t, mask,
    load_sem, y_send, y_recv, wz_send, wz_recv, wx_send, wx_recv, wc_send, wc_recv, z_send, z_recv, t_send, t_recv,
    o_send, o_recv, c_send, c_recv,
):
    tm = lax.axis_index("tm")
    row = lax.axis_index("row")
    zh = (tm // 2) % 2
    core = tm % 2
    y = row // 2
    zl = row % 2
    hz = (zl + zh) % 2
    partner_row = y * 2 + (1 - zl)
    outer_tm = tm + 2 - 4 * zh
    other_core = tm + 1 - 2 * core
    up_row = ((y + 1) % 4) * 2 + zl
    down_row = ((y + 3) % 4) * 2 + zl

    def rcopy(src, dst, send, recv, dev):
        return pltpu.make_async_remote_copy(
            src_ref=src, dst_ref=dst, send_sem=send, recv_sem=recv,
            device_id=dev, device_id_type=MESH,
        )

    def time_peer(t):
        return (t, y * 2 + (hz + (t // 2) % 2) % 2)

    load_stream = pltpu.make_async_copy(stream_hbm, stream_v, load_sem.at[0])
    load_stream.start()
    load_w = pltpu.make_async_copy(w_hbm, wbuf.at[zl], load_sem.at[1])
    load_w.start()
    load_wo = pltpu.make_async_copy(wo_hbm, wo, load_sem.at[2])
    load_wo.start()

    barrier = pltpu.get_barrier_semaphore()

    @pl.loop(1, 16)
    def _(k):
        pl.semaphore_signal(barrier, inc=1, device_id=time_peer((tm + k) % 16), device_id_type=MESH)

    @pl.loop(1, 8)
    def _(k):
        pl.semaphore_signal(barrier, inc=1, device_id=(tm, (row + k) % 8), device_id_type=MESH)

    pl.semaphore_wait(barrier, 22)

    x_par = (tm // 4) % 2
    x_up, x_down = (tm + 4) % 16, (tm + 12) % 16
    oz = 1 - zl
    e_own = core * 4 + x_par * 2
    e_x = core * 4 + (1 - x_par) * 2
    e_cores = ((1 - core) * 4 + x_par * 2, (1 - core) * 4 + (1 - x_par) * 2)

    def wz_copy(p, i, side):
        dev = ((tm, partner_row), (outer_tm, partner_row))[i]
        return rcopy(w_hbm.at[p, e_own + i], wbuf.at[side, p, e_own + i],
                     wz_send.at[p, i], wz_recv.at[p, i], dev)

    def wx_copy(p, i, e):
        dev = ((x_up, row), (x_down, row))[i]
        return rcopy(wbuf.at[oz, p, e + i], wbuf.at[oz, p, e + i],
                     wx_send.at[p, i], wx_recv.at[p, i], dev)

    def wc_copy(p, j, e):
        pair = wbuf.at[oz, p, pl.ds(e, 2)]
        return rcopy(pair, pair, wc_send.at[p, j], wc_recv.at[p, j], (other_core, row))

    for p in range(3):
        for i in range(2):
            wz_copy(p, i, zl).start()

    load_stream.wait()

    def norm_frame(f):
        clip = clip_ref[tm * 4 + f]
        shift = mod_ref[0, pl.ds(clip, 1), :]
        scale = 1.0 + mod_ref[1, pl.ds(clip, 1), :]
        for part in range(2):
            v = stream_v[f, pl.ds(part * 32, 32), :]
            centred = v - jnp.mean(v, axis=-1, keepdims=True)
            var = jnp.mean(centred * centred, axis=-1, keepdims=True)
            n = centred * lax.rsqrt(var + 1e-06) * scale + shift
            xg[y, pl.ds(f * 64 + part * 32, 32), :] = n.astype(BF)

    lo, hi = pl.ds(0, 128), pl.ds(128, 128)
    ym, yp, yq = (y + 3) % 4, (y + 1) % 4, (y + 2) % 4
    up, down = (tm, up_row), (tm, down_row)

    def ycopy(block, half, i, dev):
        return rcopy(xg.at[block, half], xg.at[block, half], y_send.at[i], y_recv.at[i], dev)

    @pl.loop(0, 2)
    def _(f):
        norm_frame(f)

    ycopy(y, lo, 0, up).start()

    @pl.loop(2, 4)
    def _(f):
        norm_frame(f)

    ycopy(y, hi, 2, down).start()
    ycopy(y, hi, 1, up).start()
    ycopy(y, lo, 3, down).start()

    def frame_row(j):
        return ((j // 4) % 4) * 64 + (j // 16) * 4 + j % 4

    r_i = lax.broadcasted_iota(jnp.int32, (256, 256), 0)
    c_i = lax.broadcasted_iota(jnp.int32, (256, 256), 1)
    perm[...] = (frame_row(r_i) == c_i).astype(BF)
    perm_t[...] = (frame_row(c_i) == r_i).astype(BF)
    fr = r_i // 4
    fc = c_i // 4

    def clip_of(f, carry):
        a, b = carry
        c = clip_ref[f]
        return jnp.where(fr == f, c, a), jnp.where(fc == f, c, b)

    zero = jnp.zeros((256, 256), jnp.int32)
    clip_r, clip_c = lax.fori_loop(0, 64, clip_of, (zero, zero))
    same = (clip_r == clip_c) & (r_i % 4 == c_i % 4)
    mask[...] = jnp.where(same, 0.0, -1e30).astype(F32)

    def project_part(yb, pz, part):
        kk = (pz + hz) % 2
        slot = kk * 2 + (1 - kk) * zl
        qkv[yb, slot, part] = dot(xg[yb], wbuf[pz, part].reshape(3072, 256)).astype(BF)

    def zcopy(yb, d, part, slot):
        return rcopy(qkv.at[yb, 2, part], qkv.at[yb, slot, part], z_send.at[d, part],
                     z_recv.at[d, part], (tm, partner_row))

    def project(yb, d):
        @pl.loop(0, 3)
        def _(part):
            project_part(yb, 1 - hz, part)
            zcopy(yb, d, part, zl).start()

        @pl.loop(0, 3)
        def _(part):
            project_part(yb, hz, part)

    def tcopy(yb, d, zz, t, at):
        return rcopy(tsend.at[yb, zz, :, t], trecv.at[yb, zz, :, at], t_send.at[d, zz, t],
                     t_recv.at[d, zz, at], time_peer(t))

    def stage_part(yb, zz, part):
        moved = dot(perm[...], qkv[yb, zz, part]).astype(BF)
        tsend[yb, zz, part] = moved.reshape(16, 16, 256)
        trecv[yb, zz, part, tm] = tsend[yb, zz, part, tm]

    def send_time(yb, d, zz):
        @pl.loop(1, 16)
        def _(k):
            tcopy(yb, d, zz, (tm + k) % 16, tm).start()

    def stage_own(yb, d):
        @pl.loop(0, 3)
        def _(part):
            stage_part(yb, zl, part)

        send_time(yb, d, zl)

    def stage_partner(yb, d):
        @pl.loop(0, 3)
        def _(part):
            zcopy(yb, d, part, 1 - zl).wait_recv()
            stage_part(yb, 1 - zl, part)

        send_time(yb, d, 1 - zl)

    factor = LOG2E / math.sqrt(HD)

    def soften(s):
        p = jnp.exp2((s - jnp.max(s, axis=-1, keepdims=True)) * factor)
        return p, jnp.sum(p, axis=-1, keepdims=True)

    def ocopy(yb, d, t, at):
        return rcopy(osend.at[yb, :, t], orecv.at[yb, :, at], o_send.at[d, t], o_recv.at[d, at],
                     time_peer(t))

    def temporal(yb, d):
        @pl.loop(0, 30)
        def _(i):
            t = (tm + 1 + i % 15) % 16
            tcopy(yb, d, i // 15, t, t).wait_recv()

        @pl.loop(0, 2)
        def _(zz):
            for h in range(2):
                cols = pl.ds(h * HD, HD)
                q, k, v = (trecv[yb, zz, part, :, :, cols].reshape(256, HD) for part in range(3))
                p, total = soften(dot_nt(q, k) + mask[...])
                o = dot(p.astype(BF), v) / total
                osend[yb, zz, :, :, cols] = o.astype(BF).reshape(16, 16, HD)

        orecv[yb, :, tm] = osend[yb, :, tm]

        @pl.loop(1, 16)
        def _(k):
            ocopy(yb, d, (tm + k) % 16, tm).start()

    def spatial():
        @pl.loop(0, 4)
        def _(f):
            rows = pl.ds(pl.multiple_of(f * 64, 64), 64)
            for h in range(2):
                cols = pl.ds(h * HD, HD)
                q, k, v = (qkv[:, 0:2, part, rows, cols].reshape(512, HD) for part in range(3))
                for half in range(2):
                    p, total = soften(dot_nt(q[half * 256:(half + 1) * 256], k))
                    o = dot(p.astype(BF), v) / total
                    sp[pl.ds(half * 2, 2), :, rows, cols] = o.reshape(2, 2, 64, HD)

    def ccopy(r, at, kept):
        return rcopy(csend.at[r], comb.at[kept], c_send.at[r], c_recv.at[at], (tm, r))

    def combine(yb, zz):
        back = dot(perm_t[...], orecv[yb, zz].reshape(256, 256))
        return (sp[yb, zz] + back).astype(BF)

    def combine_send(yb, zz):
        r = yb * 2 + zz
        csend[r] = combine(yb, zz)
        ccopy(r, row, y * 2 + hz).start()

    def wait_back(yb, d):
        @pl.loop(1, 16)
        def _(k):
            t = (tm + k) % 16
            ocopy(yb, d, t, t).wait_recv()

    def combine_block(yb, d):
        wait_back(yb, d)
        for zz in range(2):
            combine_send(yb, zz)

    def project_out(ys, first=False, last=False):
        for i in range(2):
            r = ys * 2 + i
            if first:
                @pl.when(i != zl)
                def _(r=r):
                    ccopy(r, r, y * 2 + (r + zh) % 2).wait_recv()
            else:
                ccopy(r, r, ys * 2 + (r + zh) % 2).wait_recv()

        @pl.loop(0, 6)
        def _(n):
            cols = pl.ds(pl.multiple_of(n * 512, 512), 512)
            acc = dot(comb[2 * ys], wo[2 * ys, :, cols]) + dot(comb[2 * ys + 1], wo[2 * ys + 1, :, cols])
            acc = acc.reshape(4, 64, 512)
            if not first:
                acc = acc + out_ref[:, :, cols]
            if not last:
                out_ref[:, :, cols] = acc
            else:
                for f in range(4):
                    clip = clip_ref[tm * 4 + f]
                    out_ref[f, :, cols] = acc[f] * mod_ref[2, pl.ds(clip, 1), cols]

    load_w.wait()
    for p in range(3):
        for i in range(2):
            wz_copy(p, i, oz).wait_recv()
            wx_copy(p, i, e_own).start()
        wc_copy(p, 0, e_own).start()
        project_part(y, zl, p)
    for p in range(3):
        for i in range(2):
            wx_copy(p, i, e_x).wait_recv()
        wc_copy(p, 1, e_x).start()
    ycopy(ym, lo, 0, up).wait_recv()
    ycopy(ym, lo, 4, up).start()
    ycopy(yp, hi, 2, down).wait_recv()
    ycopy(yp, hi, 5, down).start()
    for p in range(3):
        for j in range(2):
            wc_copy(p, j, e_cores[j]).wait_recv()
        project_part(y, oz, p)
        zcopy(y, 0, p, zl).start()
    stage_own(y, 0)

    ycopy(ym, hi, 1, up).wait_recv()
    project(ym, 1)
    stage_own(ym, 1)
    stage_partner(y, 0)

    ycopy(yp, lo, 3, down).wait_recv()
    project(yp, 2)
    stage_own(yp, 2)
    stage_partner(ym, 1)
    temporal(y, 0)
    stage_partner(yp, 2)

    ycopy(yq, lo, 4, up).wait_recv()
    ycopy(yq, hi, 5, down).wait_recv()
    project(yq, 3)
    stage_own(yq, 3)
    temporal(ym, 1)
    stage_partner(yq, 3)
    temporal(yp, 2)
    spatial()

    wait_back(y, 0)
    combine_send(y, 1 - zl)
    comb[y * 2 + hz] = combine(y, zl)
    combine_block(ym, 1)
    temporal(yq, 3)
    combine_block(yp, 2)
    load_wo.wait()
    project_out(y, first=True)
    combine_block(yq, 3)
    project_out(yp)
    project_out(ym)
    project_out(yq, last=True)

    for p in range(3):
        for i in range(2):
            wz_copy(p, i, zl).wait_send()
            wx_copy(p, i, e_own).wait_send()
            wc_copy(p, i, e_own).wait_send()
    for i, (block, half) in enumerate(((y, lo), (y, hi), (y, hi), (y, lo), (ym, lo), (yp, hi))):
        ycopy(block, half, i, up).wait_send()
    for d, yb in enumerate((y, ym, yp, yq)):
        for part in range(3):
            zcopy(yb, d, part, zl).wait_send()

        @pl.loop(0, 30)
        def _(i, d=d, yb=yb):
            tcopy(yb, d, i // 15, (tm + 1 + i % 15) % 16, tm).wait_send()

        @pl.loop(1, 16)
        def _(k, d=d, yb=yb):
            ocopy(yb, d, (tm + k) % 16, tm).wait_send()

    @pl.loop(1, 8)
    def _(k):
        ccopy((row + k) % 8, row, y * 2 + hz).wait_send()


def attention(clip_ids, stream, mod, weight, out_weight):
    vmem = pl.BlockSpec(memory_space=pltpu.VMEM)
    hbm = pl.BlockSpec(memory_space=pl.ANY)
    dma = pltpu.SemaphoreType.DMA
    return pl.pallas_call(
        attention_kernel,
        out_shape=pltpu.VMEM((4, 64, 3072), F32),
        in_specs=[pl.BlockSpec(memory_space=pltpu.SMEM), hbm, vmem, hbm, hbm],
        out_specs=vmem,
        scratch_shapes=[
            pltpu.VMEM((4, 64, 3072), F32),
            pltpu.VMEM((4, 256, 3072), BF),
            pltpu.VMEM((2, 3, 8, 384, 256), BF),
            pltpu.VMEM((8, 256, 3072), BF),
            pltpu.VMEM((4, 3, 3, 256, 256), BF),
            pltpu.VMEM((4, 2, 3, 16, 16, 256), BF),
            pltpu.VMEM((4, 2, 3, 16, 16, 256), BF),
            pltpu.VMEM((4, 2, 16, 16, 256), BF),
            pltpu.VMEM((4, 2, 16, 16, 256), BF),
            pltpu.VMEM((8, 256, 256), BF),
            pltpu.VMEM((8, 256, 256), BF),
            pltpu.VMEM((4, 2, 256, 256), F32),
            pltpu.VMEM((256, 256), BF),
            pltpu.VMEM((256, 256), BF),
            pltpu.VMEM((256, 256), F32),
            dma((3,)),
            dma((6,)), dma((6,)),
            dma((3, 2)), dma((3, 2)),
            dma((3, 2)), dma((3, 2)),
            dma((3, 2)), dma((3, 2)),
            dma((4, 3)), dma((4, 3)),
            dma((4, 2, 16)), dma((4, 2, 16)),
            dma((4, 16)), dma((4, 16)),
            dma((8,)), dma((8,)),
        ],
        compiler_params=pltpu.CompilerParams(
            collective_id=0, has_side_effects=True, vmem_limit_bytes=60 * 1024 * 1024
        ),
        name="attention",
    )(clip_ids, stream, mod, weight, out_weight)


def per_device(stream, clip_ids, modulation, qkv_weight, out_weight):
    mod = jnp.transpose(modulation, (1, 0, 2))
    weight = jnp.transpose(qkv_weight, (1, 0, 2)).reshape(3, 8, 384, 256)
    return attention(clip_ids, stream, mod, weight, out_weight.reshape(8, 256, 3072))


def solution(mesh):
    placed = (P("tm", "row", None), P(), P(), P(None, None, "row"), P())
    return jax.shard_map(
        per_device, mesh=mesh, in_specs=placed, out_specs=P("tm", "row", None), check_vma=False
    )
```

```python
import functools
import math

import jax
import jax.numpy as jnp
from jax import lax
from jax.experimental import pallas as pl
from jax.experimental.pallas import tpu as pltpu
from jax.sharding import PartitionSpec as P

HD = 128
MESH = pl.DeviceIdType.MESH
BF = jnp.bfloat16
F32 = jnp.float32
LOG2E = 1.4426950408889634


def dot(a, b):
    return jnp.dot(a, b, preferred_element_type=F32)


def dot_nt(a, b):
    return lax.dot_general(a, b, (((1,), (1,)), ((), ())), preferred_element_type=F32)


def attention_kernel(
    clip_ref, stream_hbm, mod_ref, w_hbm, wo_hbm, out_ref,
    stream_v, xg, wbuf, wo, qkv, tsend, trecv, osend, orecv, csend, comb, relay, sp, perm, perm_t, mask,
    load_sem, y_send, y_recv, wz_send, wz_recv, wx_send, wx_recv, wc_send, wc_recv, z_send, z_recv, t_send, t_recv, b_send, b_recv, f_send,
    o_send, o_recv, c_send, c_recv,
):
    tm = lax.axis_index("tm")
    row = lax.axis_index("row")
    zh = (tm // 2) % 2
    core = tm % 2
    y = row // 2
    zl = row % 2
    hz = (zl + zh) % 2
    partner_row = y * 2 + (1 - zl)
    outer_tm = tm + 2 - 4 * zh
    other_core = tm + 1 - 2 * core
    up_row = ((y + 1) % 4) * 2 + zl
    down_row = ((y + 3) % 4) * 2 + zl

    def rcopy(src, dst, send, recv, dev):
        return pltpu.make_async_remote_copy(
            src_ref=src, dst_ref=dst, send_sem=send, recv_sem=recv,
            device_id=dev, device_id_type=MESH,
        )

    def time_peer(t):
        return (t, y * 2 + (hz + (t // 2) % 2) % 2)

    load_stream = pltpu.make_async_copy(stream_hbm, stream_v, load_sem.at[0])
    load_stream.start()
    load_w = pltpu.make_async_copy(w_hbm, wbuf.at[zl], load_sem.at[1])
    load_w.start()
    load_wo = pltpu.make_async_copy(wo_hbm, wo, load_sem.at[2])
    load_wo.start()

    barrier = pltpu.get_barrier_semaphore()

    @pl.loop(1, 16)
    def _(k):
        pl.semaphore_signal(barrier, inc=1, device_id=time_peer((tm + k) % 16), device_id_type=MESH)

    @pl.loop(1, 8)
    def _(k):
        pl.semaphore_signal(barrier, inc=1, device_id=(tm, (row + k) % 8), device_id_type=MESH)

    pl.semaphore_wait(barrier, 22)

    x_par = (tm // 4) % 2
    x_up, x_down = (tm + 4) % 16, (tm + 12) % 16
    x_far = ((tm // 4 + 2) % 4) * 4
    oz = 1 - zl
    e_own = core * 4 + x_par * 2
    e_x = core * 4 + (1 - x_par) * 2
    e_cores = ((1 - core) * 4 + x_par * 2, (1 - core) * 4 + (1 - x_par) * 2)

    def wz_copy(p, i, side):
        dev = ((tm, partner_row), (outer_tm, partner_row))[i]
        return rcopy(w_hbm.at[p, e_own + i], wbuf.at[side, p, e_own + i],
                     wz_send.at[p, i], wz_recv.at[p, i], dev)

    def wx_copy(p, i, e):
        dev = ((x_up, row), (x_down, row))[i]
        return rcopy(wbuf.at[oz, p, e + i], wbuf.at[oz, p, e + i],
                     wx_send.at[p, i], wx_recv.at[p, i], dev)

    def wc_copy(p, j, e):
        pair = wbuf.at[oz, p, pl.ds(e, 2)]
        return rcopy(pair, pair, wc_send.at[p, j], wc_recv.at[p, j], (other_core, row))

    for p in range(3):
        for i in range(2):
            wz_copy(p, i, zl).start()

    load_stream.wait()

    def norm_frame(f):
        clip = clip_ref[tm * 4 + f]
        shift = mod_ref[0, pl.ds(clip, 1), :]
        scale = 1.0 + mod_ref[1, pl.ds(clip, 1), :]
        for part in range(2):
            v = stream_v[f, pl.ds(part * 32, 32), :]
            centred = v - jnp.mean(v, axis=-1, keepdims=True)
            var = jnp.mean(centred * centred, axis=-1, keepdims=True)
            n = centred * lax.rsqrt(var + 1e-06) * scale + shift
            xg[y, pl.ds(f * 64 + part * 32, 32), :] = n.astype(BF)

    lo, hi = pl.ds(0, 128), pl.ds(128, 128)
    ym, yp, yq = (y + 3) % 4, (y + 1) % 4, (y + 2) % 4
    up, down = (tm, up_row), (tm, down_row)

    def ycopy(block, half, i, dev):
        return rcopy(xg.at[block, half], xg.at[block, half], y_send.at[i], y_recv.at[i], dev)

    @pl.loop(0, 2)
    def _(f):
        norm_frame(f)

    ycopy(y, lo, 0, up).start()

    @pl.loop(2, 4)
    def _(f):
        norm_frame(f)

    ycopy(y, hi, 2, down).start()
    ycopy(y, hi, 1, up).start()
    ycopy(y, lo, 3, down).start()

    def frame_row(j):
        return ((j // 4) % 4) * 64 + (j // 16) * 4 + j % 4

    r_i = lax.broadcasted_iota(jnp.int32, (256, 256), 0)
    c_i = lax.broadcasted_iota(jnp.int32, (256, 256), 1)
    perm[...] = (frame_row(r_i) == c_i).astype(BF)
    perm_t[...] = (frame_row(c_i) == r_i).astype(BF)
    fr = r_i // 4
    fc = c_i // 4

    def clip_of(f, carry):
        a, b = carry
        c = clip_ref[f]
        return jnp.where(fr == f, c, a), jnp.where(fc == f, c, b)

    zero = jnp.zeros((256, 256), jnp.int32)
    clip_r, clip_c = lax.fori_loop(0, 64, clip_of, (zero, zero))
    same = (clip_r == clip_c) & (r_i % 4 == c_i % 4)
    mask[...] = jnp.where(same, 0.0, -1e30).astype(F32)

    def project_part(yb, pz, part):
        kk = (pz + hz) % 2
        slot = kk * 2 + (1 - kk) * zl
        qkv[yb, slot, part] = dot(xg[yb], wbuf[pz, part].reshape(3072, 256)).astype(BF)

    def zcopy(yb, d, part, slot):
        return rcopy(qkv.at[yb, 2, part], qkv.at[yb, slot, part], z_send.at[d, part],
                     z_recv.at[d, part], (tm, partner_row))

    def project(yb, d):
        @pl.loop(0, 3)
        def _(part):
            project_part(yb, 1 - hz, part)
            zcopy(yb, d, part, zl).start()

        @pl.loop(0, 3)
        def _(part):
            project_part(yb, hz, part)

    def tcopy(yb, d, zz, t, at):
        return rcopy(tsend.at[yb, zz, :, t], trecv.at[yb, zz, :, at], t_send.at[d, zz, t],
                     t_recv.at[d, zz, at], time_peer(t))

    def stage_part(yb, zz, part):
        moved = dot(perm[...], qkv[yb, zz, part]).astype(BF)
        tsend[yb, zz, part] = moved.reshape(16, 16, 256)
        trecv[yb, zz, part, tm] = tsend[yb, zz, part, tm]

    def send_time(yb, d, zz):
        @pl.loop(1, 16)
        def _(k):
            tcopy(yb, d, zz, (tm + k) % 16, tm).start()

    def stage_own(yb, d):
        @pl.loop(0, 3)
        def _(part):
            stage_part(yb, zl, part)

        @pl.loop(0, 11)
        def _(k):
            m = (5 + tm % 4 + k) % 12
            tcopy(yb, d, zl, (x_far + 4 + m) % 16, tm).start()

        bundle(yb, d).start()

    def bundle(yb, d):
        return rcopy(tsend.at[yb, zl, :, pl.ds(x_far, 4)], relay.at[d], b_send.at[d], b_recv.at[d],
                     (x_down, row))

    def fcopy(yb, d, j):
        return rcopy(relay.at[d, :, j], trecv.at[yb, zl, :, x_up], f_send.at[d, j],
                     t_recv.at[d, zl, x_up], time_peer((x_down // 4) * 4 + j))

    def pass_on(yb, d):
        bundle(yb, d).wait_recv()
        for j in range(4):
            fcopy(yb, d, j).start()

    def stage_partner(yb, d):
        @pl.loop(0, 3)
        def _(part):
            zcopy(yb, d, part, 1 - zl).wait_recv()
            stage_part(yb, 1 - zl, part)

        send_time(yb, d, 1 - zl)

    factor = LOG2E / math.sqrt(HD)

    def soften(s):
        p = jnp.exp2((s - jnp.max(s, axis=-1, keepdims=True)) * factor)
        return p, jnp.sum(p, axis=-1, keepdims=True)

    def ocopy(yb, d, t, at):
        return rcopy(osend.at[yb, :, t], orecv.at[yb, :, at], o_send.at[d, t], o_recv.at[d, at],
                     time_peer(t))

    def temporal(yb, d):
        @pl.loop(0, 30)
        def _(i):
            t = (tm + 1 + i % 15) % 16
            tcopy(yb, d, i // 15, t, t).wait_recv()

        @pl.loop(0, 2)
        def _(zz):
            for h in range(2):
                cols = pl.ds(h * HD, HD)
                q, k, v = (trecv[yb, zz, part, :, :, cols].reshape(256, HD) for part in range(3))
                p, total = soften(dot_nt(q, k) + mask[...])
                o = dot(p.astype(BF), v) / total
                osend[yb, zz, :, :, cols] = o.astype(BF).reshape(16, 16, HD)

        orecv[yb, :, tm] = osend[yb, :, tm]

        @pl.loop(1, 16)
        def _(k):
            ocopy(yb, d, (tm + k) % 16, tm).start()

    def spatial():
        @pl.loop(0, 4)
        def _(f):
            rows = pl.ds(pl.multiple_of(f * 64, 64), 64)
            for h in range(2):
                cols = pl.ds(h * HD, HD)
                q, k, v = (qkv[:, 0:2, part, rows, cols].reshape(512, HD) for part in range(3))
                for half in range(2):
                    p, total = soften(dot_nt(q[half * 256:(half + 1) * 256], k))
                    o = dot(p.astype(BF), v) / total
                    sp[pl.ds(half * 2, 2), :, rows, cols] = o.reshape(2, 2, 64, HD)

    def ccopy(r, at, kept):
        return rcopy(csend.at[r], comb.at[kept], c_send.at[r], c_recv.at[at], (tm, r))

    def combine(yb, zz):
        back = dot(perm_t[...], orecv[yb, zz].reshape(256, 256))
        return (sp[yb, zz] + back).astype(BF)

    def combine_send(yb, zz):
        r = yb * 2 + zz
        csend[r] = combine(yb, zz)
        ccopy(r, row, y * 2 + hz).start()

    def wait_back(yb, d):
        @pl.loop(1, 16)
        def _(k):
            t = (tm + k) % 16
            ocopy(yb, d, t, t).wait_recv()

    def combine_block(yb, d):
        wait_back(yb, d)
        for zz in range(2):
            combine_send(yb, zz)

    def project_out(ys, first=False, last=False):
        for i in range(2):
            r = ys * 2 + i
            if first:
                @pl.when(i != zl)
                def _(r=r):
                    ccopy(r, r, y * 2 + (r + zh) % 2).wait_recv()
            else:
                ccopy(r, r, ys * 2 + (r + zh) % 2).wait_recv()

        @pl.loop(0, 6)
        def _(n):
            cols = pl.ds(pl.multiple_of(n * 512, 512), 512)
            acc = dot(comb[2 * ys], wo[2 * ys, :, cols]) + dot(comb[2 * ys + 1], wo[2 * ys + 1, :, cols])
            acc = acc.reshape(4, 64, 512)
            if not first:
                acc = acc + out_ref[:, :, cols]
            if not last:
                out_ref[:, :, cols] = acc
            else:
                for f in range(4):
                    clip = clip_ref[tm * 4 + f]
                    out_ref[f, :, cols] = acc[f] * mod_ref[2, pl.ds(clip, 1), cols]

    load_w.wait()
    for p in range(3):
        for i in range(2):
            wz_copy(p, i, oz).wait_recv()
            wx_copy(p, i, e_own).start()
        wc_copy(p, 0, e_own).start()
        project_part(y, zl, p)
    for p in range(3):
        for i in range(2):
            wx_copy(p, i, e_x).wait_recv()
        wc_copy(p, 1, e_x).start()
    ycopy(ym, lo, 0, up).wait_recv()
    ycopy(ym, lo, 4, up).start()
    ycopy(yp, hi, 2, down).wait_recv()
    ycopy(yp, hi, 5, down).start()
    for p in range(3):
        for j in range(2):
            wc_copy(p, j, e_cores[j]).wait_recv()
        project_part(y, oz, p)
        zcopy(y, 0, p, zl).start()
    stage_own(y, 0)

    ycopy(ym, hi, 1, up).wait_recv()
    project(ym, 1)
    stage_own(ym, 1)
    pass_on(y, 0)
    stage_partner(y, 0)

    ycopy(yp, lo, 3, down).wait_recv()
    project(yp, 2)
    stage_own(yp, 2)
    pass_on(ym, 1)
    stage_partner(ym, 1)
    temporal(y, 0)
    pass_on(yp, 2)
    stage_partner(yp, 2)

    ycopy(yq, lo, 4, up).wait_recv()
    ycopy(yq, hi, 5, down).wait_recv()
    project(yq, 3)
    stage_own(yq, 3)
    temporal(ym, 1)
    pass_on(yq, 3)
    stage_partner(yq, 3)
    temporal(yp, 2)
    spatial()

    wait_back(y, 0)
    combine_send(y, 1 - zl)
    comb[y * 2 + hz] = combine(y, zl)
    combine_block(ym, 1)
    temporal(yq, 3)
    combine_block(yp, 2)
    load_wo.wait()
    project_out(y, first=True)
    combine_block(yq, 3)
    project_out(yp)
    project_out(ym)
    project_out(yq, last=True)

    for p in range(3):
        for i in range(2):
            wz_copy(p, i, zl).wait_send()
            wx_copy(p, i, e_own).wait_send()
            wc_copy(p, i, e_own).wait_send()
    for i, (block, half) in enumerate(((y, lo), (y, hi), (y, hi), (y, lo), (ym, lo), (yp, hi))):
        ycopy(block, half, i, up).wait_send()
    for d, yb in enumerate((y, ym, yp, yq)):
        for part in range(3):
            zcopy(yb, d, part, zl).wait_send()

        @pl.loop(0, 11)
        def _(k, d=d, yb=yb):
            m = (5 + tm % 4 + k) % 12
            tcopy(yb, d, zl, (x_far + 4 + m) % 16, tm).wait_send()

        bundle(yb, d).wait_send()
        for j in range(4):
            fcopy(yb, d, j).wait_send()

        @pl.loop(1, 16)
        def _(k, d=d, yb=yb):
            tcopy(yb, d, 1 - zl, (tm + k) % 16, tm).wait_send()

        @pl.loop(1, 16)
        def _(k, d=d, yb=yb):
            ocopy(yb, d, (tm + k) % 16, tm).wait_send()

    @pl.loop(1, 8)
    def _(k):
        ccopy((row + k) % 8, row, y * 2 + hz).wait_send()


def attention(clip_ids, stream, mod, weight, out_weight):
    vmem = pl.BlockSpec(memory_space=pltpu.VMEM)
    hbm = pl.BlockSpec(memory_space=pl.ANY)
    dma = pltpu.SemaphoreType.DMA
    return pl.pallas_call(
        attention_kernel,
        out_shape=pltpu.VMEM((4, 64, 3072), F32),
        in_specs=[pl.BlockSpec(memory_space=pltpu.SMEM), hbm, vmem, hbm, hbm],
        out_specs=vmem,
        scratch_shapes=[
            pltpu.VMEM((4, 64, 3072), F32),
            pltpu.VMEM((4, 256, 3072), BF),
            pltpu.VMEM((2, 3, 8, 384, 256), BF),
            pltpu.VMEM((8, 256, 3072), BF),
            pltpu.VMEM((4, 3, 3, 256, 256), BF),
            pltpu.VMEM((4, 2, 3, 16, 16, 256), BF),
            pltpu.VMEM((4, 2, 3, 16, 16, 256), BF),
            pltpu.VMEM((4, 2, 16, 16, 256), BF),
            pltpu.VMEM((4, 2, 16, 16, 256), BF),
            pltpu.VMEM((8, 256, 256), BF),
            pltpu.VMEM((8, 256, 256), BF),
            pltpu.VMEM((4, 3, 4, 16, 256), BF),
            pltpu.VMEM((4, 2, 256, 256), F32),
            pltpu.VMEM((256, 256), BF),
            pltpu.VMEM((256, 256), BF),
            pltpu.VMEM((256, 256), F32),
            dma((3,)),
            dma((6,)), dma((6,)),
            dma((3, 2)), dma((3, 2)),
            dma((3, 2)), dma((3, 2)),
            dma((3, 2)), dma((3, 2)),
            dma((4, 3)), dma((4, 3)),
            dma((4, 2, 16)), dma((4, 2, 16)),
            dma((4,)), dma((4,)), dma((4, 4)),
            dma((4, 16)), dma((4, 16)),
            dma((8,)), dma((8,)),
        ],
        compiler_params=pltpu.CompilerParams(
            collective_id=0, has_side_effects=True, vmem_limit_bytes=60 * 1024 * 1024
        ),
        name="attention",
    )(clip_ids, stream, mod, weight, out_weight)


def per_device(stream, clip_ids, modulation, qkv_weight, out_weight):
    mod = jnp.transpose(modulation, (1, 0, 2))
    weight = jnp.transpose(qkv_weight, (1, 0, 2)).reshape(3, 8, 384, 256)
    return attention(clip_ids, stream, mod, weight, out_weight.reshape(8, 256, 3072))


def solution(mesh):
    placed = (P("tm", "row", None), P(), P(), P(None, None, "row"), P())
    return jax.shard_map(
        per_device, mesh=mesh, in_specs=placed, out_specs=P("tm", "row", None), check_vma=False
    )
```

```python
import math

import jax
import jax.numpy as jnp
from jax import lax
from jax.experimental import pallas as pl
from jax.experimental.pallas import tpu as pltpu
from jax.sharding import PartitionSpec as P

HD = 128
MESH = pl.DeviceIdType.MESH
BF = jnp.bfloat16
F32 = jnp.float32
LOG2E = 1.4426950408889634


def dot(a, b):
    return jnp.dot(a, b, preferred_element_type=F32)


def dot_nt(a, b):
    return lax.dot_general(a, b, (((1,), (1,)), ((), ())), preferred_element_type=F32)


def attention_kernel(
    clip_ref, stream_hbm, mod_ref, w_hbm, wo_hbm, out_ref,
    stream_v, xg, wbuf, wo, qkv, tsend, trecv, osend, orecv, csend, comb, sp, perm, perm_t, mask,
    load_sem, y_send, y_recv, wz_send, wz_recv, wx_send, wx_recv, wc_send, wc_recv, z_send, z_recv,
    t_send, t_recv, o_send, o_recv, c_send, c_recv,
):
    batches = ((0, 2), (2, 2), (4, 2), (6, 1), (7, 1))
    tm = lax.axis_index("tm")
    row = lax.axis_index("row")
    zh = (tm // 2) % 2
    core = tm % 2
    y = row // 2
    zl = row % 2
    hz = (zl + zh) % 2
    oz = 1 - zl
    partner_row = y * 2 + oz
    outer_tm = tm + 2 - 4 * zh
    other_core = tm + 1 - 2 * core
    ym, yp, yq = (y + 3) % 4, (y + 1) % 4, (y + 2) % 4
    up, down = (tm, yp * 2 + zl), (tm, ym * 2 + zl)
    y_of = (y, y, ym, yp, ym, yp, yq, yq)
    half_of = (0, 1, 0, 0, 1, 1, 0, 1)

    def rcopy(src, dst, send, recv, dev):
        return pltpu.make_async_remote_copy(
            src_ref=src, dst_ref=dst, send_sem=send, recv_sem=recv,
            device_id=dev, device_id_type=MESH,
        )

    def await_bytes(ref, sem):
        pltpu.make_async_copy(ref, ref, sem).wait()

    def time_peer(t):
        return (t, y * 2 + (hz + (t // 2) % 2) % 2)

    load_stream = pltpu.make_async_copy(stream_hbm, stream_v, load_sem.at[0])
    load_stream.start()
    load_w = pltpu.make_async_copy(w_hbm, wbuf.at[zl], load_sem.at[1])
    load_w.start()
    load_wo = pltpu.make_async_copy(wo_hbm, wo, load_sem.at[2])
    load_wo.start()

    barrier = pltpu.get_barrier_semaphore()

    @pl.loop(1, 16)
    def _(k):
        pl.semaphore_signal(barrier, inc=1, device_id=time_peer((tm + k) % 16), device_id_type=MESH)

    @pl.loop(1, 8)
    def _(k):
        pl.semaphore_signal(barrier, inc=1, device_id=(tm, (row + k) % 8), device_id_type=MESH)

    pl.semaphore_wait(barrier, 22)

    x_par = (tm // 4) % 2
    x_up, x_down = (tm + 4) % 16, (tm + 12) % 16
    e_own = core * 4 + x_par * 2
    e_x = core * 4 + (1 - x_par) * 2
    e_cores = ((1 - core) * 4 + x_par * 2, (1 - core) * 4 + (1 - x_par) * 2)

    def wz_copy(p, i, side):
        dev = ((tm, partner_row), (outer_tm, partner_row))[i]
        return rcopy(w_hbm.at[p, e_own + i], wbuf.at[side, p, e_own + i],
                     wz_send.at[p, i], wz_recv.at[p, i], dev)

    def wx_copy(p, i, e):
        dev = ((x_up, row), (x_down, row))[i]
        return rcopy(wbuf.at[oz, p, e + i], wbuf.at[oz, p, e + i],
                     wx_send.at[p, i], wx_recv.at[p, i], dev)

    def wc_copy(p, j, e):
        pair = wbuf.at[oz, p, pl.ds(e, 2)]
        return rcopy(pair, pair, wc_send.at[p, j], wc_recv.at[p, j], (other_core, row))

    for p in range(3):
        for i in range(2):
            wz_copy(p, i, zl).start()

    load_stream.wait()

    def norm(unit):
        @pl.loop(0, 4)
        def _(f):
            clip = clip_ref[tm * 4 + f]
            shift = mod_ref[0, pl.ds(clip, 1), :]
            scale = 1.0 + mod_ref[1, pl.ds(clip, 1), :]
            v = stream_v[f, pl.ds(unit * 32, 32), :]
            centred = v - jnp.mean(v, axis=-1, keepdims=True)
            var = jnp.mean(centred * centred, axis=-1, keepdims=True)
            n = centred * lax.rsqrt(var + 1e-06) * scale + shift
            xg[unit, pl.ds(f * 32, 32), :] = n.astype(BF)

    def ycopy(i, src, dst, half, dev):
        if half is None:
            return rcopy(xg.at[src], xg.at[dst], y_send.at[i], y_recv.at[i], dev)
        rows = pl.ds(half * 64, 64)
        return rcopy(xg.at[src, rows], xg.at[dst, rows], y_send.at[i], y_recv.at[i], dev)

    y_copies = [
        ycopy(0, 0, 2, None, up), ycopy(1, 0, 3, None, down),
        ycopy(2, 1, 4, None, up), ycopy(3, 1, 5, None, down),
        ycopy(4, 2, 6, 0, up), ycopy(5, 3, 6, 1, down),
        ycopy(6, 4, 7, 0, up), ycopy(7, 5, 7, 1, down),
    ]
    for unit in range(2):
        norm(unit)
        y_copies[2 * unit].start()
        y_copies[2 * unit + 1].start()

    def unit_row(j):
        return (j // 128) * 128 + ((j // 4) % 4) * 32 + ((j // 16) % 8) * 4 + j % 4

    r_i = lax.broadcasted_iota(jnp.int32, (256, 256), 0)
    c_i = lax.broadcasted_iota(jnp.int32, (256, 256), 1)
    perm[...] = (unit_row(r_i) == c_i).astype(BF)
    perm_t[...] = (unit_row(c_i) == r_i).astype(BF)
    fr = r_i // 4
    fc = c_i // 4

    def clip_of(f, carry):
        a, b = carry
        c = clip_ref[f]
        return jnp.where(fr == f, c, a), jnp.where(fc == f, c, b)

    zero = jnp.zeros((256, 256), jnp.int32)
    clip_r, clip_c = lax.fori_loop(0, 64, clip_of, (zero, zero))
    same = (clip_r == clip_c) & (r_i % 4 == c_i % 4)
    mask[...] = jnp.where(same, 0.0, -1e30).astype(F32)

    def project_part(b, pz, part):
        k, n = batches[b]
        kk = (pz + hz) % 2
        slot = kk * 2 + (1 - kk) * zl
        x = xg[k:k + n].reshape(n * 128, 3072)
        out = dot(x, wbuf[pz, part].reshape(3072, 256)).astype(BF)
        qkv[slot, part, k:k + n] = out.reshape(n, 128, 256)

    def zcopy(b, part, slot):
        k, n = batches[b]
        units = pl.ds(k, n)
        return rcopy(qkv.at[2, part, units], qkv.at[slot, part, units], z_send.at[b, part],
                     z_recv.at[b, part], (tm, partner_row))

    def project(b):
        @pl.loop(0, 3)
        def _(part):
            project_part(b, 1 - hz, part)
            zcopy(b, part, zl).start()

        @pl.loop(0, 3)
        def _(part):
            project_part(b, hz, part)

    def stage_part(b, zz, part):
        k, n = batches[b]
        rows = qkv[zz, part, k:k + n].reshape(n * 128, 256)
        moved = dot(perm[:n * 128, :n * 128], rows).astype(BF).reshape(n, 8, 16, 256)
        tsend[k:k + n, part, pl.ds(zz * 8, 8)] = moved

    def send_time(b, zz):
        k, n = batches[b]
        units = pl.ds(k, n)

        @pl.loop(0, 8)
        def _(i):
            t = zz * 8 + (tm + i) % 8

            @pl.when(t != tm)
            def _():
                rcopy(tsend.at[units, :, t], trecv.at[units, :, tm], t_send.at[b], t_recv.at[b],
                      time_peer(t)).start()

            @pl.when(t == tm)
            def _():
                trecv[k:k + n, :, tm] = tsend[k:k + n, :, tm]

    def stage_own(b):
        @pl.loop(0, 3)
        def _(part):
            stage_part(b, zl, part)

        send_time(b, zl)

    def stage_partner(b):
        @pl.loop(0, 3)
        def _(part):
            zcopy(b, part, oz).wait_recv()
            stage_part(b, oz, part)

        send_time(b, oz)

    factor = LOG2E / math.sqrt(HD)

    def soften(s):
        p = jnp.exp2((s - jnp.max(s, axis=-1, keepdims=True)) * factor)
        return p, jnp.sum(p, axis=-1, keepdims=True)

    def temporal(b):
        k, n = batches[b]
        units = pl.ds(k, n)
        await_bytes(trecv.at[units, :, pl.ds(0, 15)], t_recv.at[b])
        for u in range(k, k + n):
            for h in range(2):
                cols = slice(h * HD, (h + 1) * HD)
                q, kk, v = (trecv[u, part, :, :, cols].reshape(256, HD) for part in range(3))
                p, total = soften(dot_nt(q, kk) + mask[...])
                o = dot(p.astype(BF), v) / total
                osend[u, :, :, cols] = o.astype(BF).reshape(16, 16, HD)
        orecv[k:k + n, tm] = osend[k:k + n, tm]

        @pl.loop(1, 16)
        def _(i):
            t = (tm + i) % 16
            rcopy(osend.at[units, t], orecv.at[units, tm], o_send.at[b], o_recv.at[b],
                  time_peer(t)).start()

    def wait_back(b):
        k, n = batches[b]
        await_bytes(orecv.at[pl.ds(k, n), pl.ds(0, 15)], o_recv.at[b])

    def spatial(k):
        @pl.loop(0, 4)
        def _(f):
            rows = pl.ds(pl.multiple_of(f * 32, 32), 32)
            for h in range(2):
                cols = slice(h * HD, (h + 1) * HD)
                q = qkv[0:2, 0, k:k + 2, rows, cols].reshape(128, HD)
                kk, v = (qkv[0:2, part, :, rows, cols].reshape(512, HD) for part in (1, 2))
                p, total = soften(dot_nt(q, kk))
                o = dot(p.astype(BF), v) / total
                sp[:, k:k + 2, rows, cols] = o.reshape(2, 2, 32, HD)

    def ccopy(u, r, at, kept):
        half = half_of[u]
        return rcopy(csend.at[u, r % 2], comb.at[kept, half], c_send.at[u, r % 2], c_recv.at[at, half],
                     (tm, r))

    def combine(u):
        for zz in range(2):
            back = dot(perm_t[:128, :128], orecv[u, zz * 8:(zz + 1) * 8].reshape(128, 256))
            csend[u, zz] = (sp[zz, u] + back).astype(BF)
        if u < 2:
            ccopy(u, partner_row, row, y * 2 + hz).start()
            comb[y * 2 + hz, u] = csend[u, zl]
        else:
            for zz in range(2):
                ccopy(u, y_of[u] * 2 + zz, row, y * 2 + hz).start()

    def project_out(ys, first=False, last=False):
        for i in range(2):
            r = ys * 2 + i
            for half in range(2):
                def wait(r=r, half=half):
                    dst = comb.at[ys * 2 + (r + zh) % 2, half]
                    rcopy(csend.at[0, 0], dst, c_send.at[0, 0], c_recv.at[r, half], (tm, r)).wait_recv()
                if first:
                    pl.when(i != zl)(wait)
                else:
                    wait()

        @pl.loop(0, 6)
        def _(n):
            cols = pl.ds(pl.multiple_of(n * 512, 512), 512)
            acc = dot(comb[2 * ys].reshape(256, 256), wo[2 * ys, :, cols])
            acc = acc + dot(comb[2 * ys + 1].reshape(256, 256), wo[2 * ys + 1, :, cols])
            for half in range(2):
                for f in range(4):
                    at = (half * 4 + f) * 32
                    rows = slice(half * 32, (half + 1) * 32)
                    piece = acc[at:at + 32]
                    if not first:
                        piece = piece + out_ref[f, rows, cols]
                    if last:
                        clip = clip_ref[tm * 4 + f]
                        piece = piece * mod_ref[2, pl.ds(clip, 1), cols]
                    out_ref[f, rows, cols] = piece

    load_w.wait()
    for p in range(3):
        for i in range(2):
            wz_copy(p, i, oz).wait_recv()
            wx_copy(p, i, e_own).start()
        wc_copy(p, 0, e_own).start()
        project_part(0, zl, p)
    for p in range(3):
        for i in range(2):
            wx_copy(p, i, e_x).wait_recv()
        wc_copy(p, 1, e_x).start()
    for p in range(3):
        for j in range(2):
            wc_copy(p, j, e_cores[j]).wait_recv()
        project_part(0, oz, p)
        zcopy(0, p, zl).start()
    for i in range(2):
        y_copies[i].wait_recv()
        y_copies[4 + i].start()
    stage_own(0)
    project(1)
    stage_own(1)
    stage_partner(0)

    for i in range(2):
        y_copies[2 + i].wait_recv()
        y_copies[6 + i].start()
    project(2)
    stage_own(2)
    stage_partner(1)
    temporal(0)

    y_copies[4].wait_recv()
    y_copies[5].wait_recv()
    project(3)
    stage_own(3)
    stage_partner(2)
    temporal(1)

    y_copies[6].wait_recv()
    y_copies[7].wait_recv()
    project(4)
    stage_own(4)
    stage_partner(3)
    temporal(2)
    stage_partner(4)
    temporal(3)

    spatial(2)
    wait_back(1)
    combine(2)
    combine(3)
    spatial(4)
    wait_back(2)
    combine(4)
    combine(5)
    temporal(4)
    spatial(6)
    wait_back(3)
    combine(6)
    spatial(0)
    wait_back(0)
    combine(0)
    combine(1)
    wait_back(4)
    combine(7)
    load_wo.wait()
    project_out(y, first=True)
    project_out(yp)
    project_out(ym)
    project_out(yq, last=True)

    for p in range(3):
        for i in range(2):
            wz_copy(p, i, zl).wait_send()
            wx_copy(p, i, e_own).wait_send()
            wc_copy(p, i, e_own).wait_send()
    for c in y_copies:
        c.wait_send()
    for b, (k, n) in enumerate(batches):
        for part in range(3):
            zcopy(b, part, zl).wait_send()
        await_bytes(tsend.at[pl.ds(k, n), :, pl.ds(0, 15)], t_send.at[b])
        await_bytes(osend.at[pl.ds(k, n), pl.ds(0, 15)], o_send.at[b])
    for u in range(8):
        if u < 2:
            ccopy(u, partner_row, row, y * 2 + hz).wait_send()
        else:
            for zz in range(2):
                ccopy(u, y_of[u] * 2 + zz, row, y * 2 + hz).wait_send()


def attention(clip_ids, stream, mod, weight, out_weight):
    vmem = pl.BlockSpec(memory_space=pltpu.VMEM)
    hbm = pl.BlockSpec(memory_space=pl.ANY)
    dma = pltpu.SemaphoreType.DMA
    return pl.pallas_call(
        attention_kernel,
        out_shape=pltpu.VMEM((4, 64, 3072), F32),
        in_specs=[pl.BlockSpec(memory_space=pltpu.SMEM), hbm, vmem, hbm, hbm],
        out_specs=vmem,
        scratch_shapes=[
            pltpu.VMEM((4, 64, 3072), F32),
            pltpu.VMEM((8, 128, 3072), BF),
            pltpu.VMEM((2, 3, 8, 384, 256), BF),
            pltpu.VMEM((8, 256, 3072), BF),
            pltpu.VMEM((3, 3, 8, 128, 256), BF),
            pltpu.VMEM((8, 3, 16, 16, 256), BF),
            pltpu.VMEM((8, 3, 16, 16, 256), BF),
            pltpu.VMEM((8, 16, 16, 256), BF),
            pltpu.VMEM((8, 16, 16, 256), BF),
            pltpu.VMEM((8, 2, 128, 256), BF),
            pltpu.VMEM((8, 2, 128, 256), BF),
            pltpu.VMEM((2, 8, 128, 256), F32),
            pltpu.VMEM((256, 256), BF),
            pltpu.VMEM((256, 256), BF),
            pltpu.VMEM((256, 256), F32),
            dma((3,)),
            dma((8,)), dma((8,)),
            dma((3, 2)), dma((3, 2)),
            dma((3, 2)), dma((3, 2)),
            dma((3, 2)), dma((3, 2)),
            dma((5, 3)), dma((5, 3)),
            dma((5,)), dma((5,)),
            dma((5,)), dma((5,)),
            dma((8, 2)), dma((8, 2)),
        ],
        compiler_params=pltpu.CompilerParams(
            collective_id=0, has_side_effects=True, vmem_limit_bytes=60 * 1024 * 1024
        ),
        name="attention",
    )(clip_ids, stream, mod, weight, out_weight)


def per_device(stream, clip_ids, modulation, qkv_weight, out_weight):
    mod = jnp.transpose(modulation, (1, 0, 2))
    weight = jnp.transpose(qkv_weight, (1, 0, 2)).reshape(3, 8, 384, 256)
    return attention(clip_ids, stream, mod, weight, out_weight.reshape(8, 256, 3072))


def solution(mesh):
    placed = (P("tm", "row", None), P(), P(), P(None, None, "row"), P())
    return jax.shard_map(
        per_device, mesh=mesh, in_specs=placed, out_specs=P("tm", "row", None), check_vma=False
    )
```

```python
import math

import jax
import jax.numpy as jnp
from jax import lax
from jax.experimental import pallas as pl
from jax.experimental.pallas import tpu as pltpu
from jax.sharding import PartitionSpec as P

HD = 128
MESH = pl.DeviceIdType.MESH
BF = jnp.bfloat16
F32 = jnp.float32
LOG2E = 1.4426950408889634


def dot(a, b):
    return jnp.dot(a, b, preferred_element_type=F32)


def dot_nt(a, b):
    return lax.dot_general(a, b, (((1,), (1,)), ((), ())), preferred_element_type=F32)


def attention_kernel(
    clip_ref, stream_hbm, mod_ref, w_hbm, wo_hbm, out_ref,
    stream_v, xg, wbuf, wo, qkv, tsend, trecv, osend, orecv, csend, comb, sp, perm, perm_t, mask,
    load_sem, y_send, y_recv, wz_send, wz_recv, wx_send, wx_recv, wc_send, wc_recv, z_send, z_recv,
    t_send, t_recv, o_send, o_recv, c_send, c_recv,
):
    batches = ((0, 2), (2, 2), (4, 2), (6, 1), (7, 1))
    tm = lax.axis_index("tm")
    row = lax.axis_index("row")
    zh = (tm // 2) % 2
    core = tm % 2
    y = row // 2
    zl = row % 2
    hz = (zl + zh) % 2
    oz = 1 - zl
    partner_row = y * 2 + oz
    outer_tm = tm + 2 - 4 * zh
    other_core = tm + 1 - 2 * core
    ym, yp, yq = (y + 3) % 4, (y + 1) % 4, (y + 2) % 4
    up, down = (tm, yp * 2 + zl), (tm, ym * 2 + zl)
    y_of = (y, y, ym, yp, ym, yp, yq, yq)
    half_of = (0, 1, 0, 0, 1, 1, 0, 1)

    def rcopy(src, dst, send, recv, dev):
        return pltpu.make_async_remote_copy(
            src_ref=src, dst_ref=dst, send_sem=send, recv_sem=recv,
            device_id=dev, device_id_type=MESH,
        )

    def await_bytes(ref, sem):
        pltpu.make_async_copy(ref, ref, sem).wait()

    x = tm // 4
    xs = [((x + d) % 4) for d in range(4)]
    zs = [zh, 1 - zh]
    cs = [core, 1 - core]
    rows_of = [y * 2 + (hz + zh) % 2, y * 2 + (hz + 1 - zh) % 2]
    offsets = [(dx, dz, dc) for dx in (1, 3, 2, 0) for dz in range(2) for dc in range(2)][:-4]
    offsets = offsets + [(0, 1, 0), (0, 1, 1), (0, 0, 1)]
    me_at = core * 8 + x * 2 + zh

    def peer(dx, dz, dc):
        t = xs[dx] * 4 + zs[dz] * 2 + cs[dc]
        return (t, rows_of[dz]), cs[dc] * 8 + xs[dx] * 2 + zs[dz]

    load_stream = [
        pltpu.make_async_copy(stream_hbm.at[:, pl.ds(32 * u, 32)], stream_v.at[:, pl.ds(32 * u, 32)],
                              load_sem.at[u])
        for u in range(2)
    ]
    load_w = pltpu.make_async_copy(w_hbm, wbuf.at[zl], load_sem.at[2])
    load_wo = pltpu.make_async_copy(wo_hbm, wo, load_sem.at[3])
    for c in load_stream:
        c.start()

    barrier = pltpu.get_barrier_semaphore()
    for o in offsets:
        pl.semaphore_signal(barrier, inc=1, device_id=peer(*o)[0], device_id_type=MESH)
    row_peers = [(tm, r * 2 + (zl if i == 0 else oz)) for r in (y, ym, yp, yq) for i in range(2)][1:]
    for dev in row_peers:
        pl.semaphore_signal(barrier, inc=1, device_id=dev, device_id_type=MESH)
    pl.semaphore_wait(barrier, 22)

    x_par = x % 2
    x_up, x_down = (tm + 4) % 16, (tm + 12) % 16
    e_own = core * 4 + x_par * 2
    e_x = core * 4 + (1 - x_par) * 2
    e_cores = ((1 - core) * 4 + x_par * 2, (1 - core) * 4 + (1 - x_par) * 2)

    def wz_copy(p, i, side):
        dev = ((tm, partner_row), (outer_tm, partner_row))[i]
        return rcopy(w_hbm.at[p, e_own + i], wbuf.at[side, p, e_own + i],
                     wz_send.at[p, i], wz_recv.at[p, i], dev)

    def wx_copy(p, i, e):
        dev = ((x_up, row), (x_down, row))[i]
        return rcopy(wbuf.at[oz, p, e + i], wbuf.at[oz, p, e + i],
                     wx_send.at[p, i], wx_recv.at[p, i], dev)

    def wc_copy(p, j, e):
        pair = wbuf.at[oz, p, pl.ds(e, 2)]
        return rcopy(pair, pair, wc_send.at[p, j], wc_recv.at[p, j], (other_core, row))

    for p in range(3):
        for i in range(2):
            wz_copy(p, i, zl).start()


    def norm(unit):
        @pl.loop(0, 4)
        def _(f):
            clip = clip_ref[tm * 4 + f]
            shift = mod_ref[0, pl.ds(clip, 1), :]
            scale = 1.0 + mod_ref[1, pl.ds(clip, 1), :]
            v = stream_v[f, pl.ds(unit * 32, 32), :]
            centred = v - jnp.mean(v, axis=-1, keepdims=True)
            var = jnp.mean(centred * centred, axis=-1, keepdims=True)
            n = centred * lax.rsqrt(var + 1e-06) * scale + shift
            xg[unit, pl.ds(f * 32, 32), :] = n.astype(BF)

    def ycopy(i, src, dst, half, dev):
        if half is None:
            return rcopy(xg.at[src], xg.at[dst], y_send.at[i], y_recv.at[i], dev)
        rows = pl.ds(half * 64, 64)
        return rcopy(xg.at[src, rows], xg.at[dst, rows], y_send.at[i], y_recv.at[i], dev)

    y_copies = [
        ycopy(0, 0, 2, None, up), ycopy(1, 0, 3, None, down),
        ycopy(2, 1, 4, None, up), ycopy(3, 1, 5, None, down),
        ycopy(4, 2, 6, 0, up), ycopy(5, 3, 6, 1, down),
        ycopy(6, 4, 7, 0, up), ycopy(7, 5, 7, 1, down),
    ]
    for unit in range(2):
        load_stream[unit].wait()
        if unit == 0:
            load_w.start()
        norm(unit)
        y_copies[2 * unit].start()
        y_copies[2 * unit + 1].start()

    def unit_row(j):
        return (j & 128) + ((j >> 2) & 3) * 32 + ((j >> 4) & 7) * 4 + (j & 3)

    r_i = lax.broadcasted_iota(jnp.int32, (256, 256), 0)
    c_i = lax.broadcasted_iota(jnp.int32, (256, 256), 1)
    perm[...] = (unit_row(r_i) == c_i).astype(BF)
    perm_t[...] = (unit_row(c_i) == r_i).astype(BF)
    lane = lax.broadcasted_iota(jnp.int32, (1, 256), 1)

    def clip_of(f, found):
        return jnp.where((lane >> 2) == f, clip_ref[f], found)

    key = lax.fori_loop(0, 64, clip_of, jnp.zeros((1, 256), jnp.int32)) * 4 + (lane & 3)
    key = jnp.broadcast_to(key.astype(F32), (256, 256))
    mask[...] = jnp.where(key == key.T, 0.0, -1e30).astype(F32)

    def project_part(b, pz, part):
        k, n = batches[b]
        kk = (pz + hz) % 2
        slot = kk * 2 + (1 - kk) * zl
        x = xg[k:k + n].reshape(n * 128, 3072)
        out = dot(x, wbuf[pz, part].reshape(3072, 256)).astype(BF)
        qkv[slot, part, k:k + n] = out.reshape(n, 128, 256)

    def zcopy(b, part, slot):
        k, n = batches[b]
        units = pl.ds(k, n)
        return rcopy(qkv.at[2, part, units], qkv.at[slot, part, units], z_send.at[b, part],
                     z_recv.at[b, part], (tm, partner_row))

    def project(b):
        @pl.loop(0, 3)
        def _(part):
            project_part(b, 1 - hz, part)
            zcopy(b, part, zl).start()

        @pl.loop(0, 3)
        def _(part):
            project_part(b, hz, part)

    def stage_part(b, zz, part):
        k, n = batches[b]
        rows = qkv[zz, part, k:k + n].reshape(n * 128, 256)
        moved = dot(perm[:n * 128, :n * 128], rows).astype(BF).reshape(n, 8, 16, 256)
        tsend[k:k + n, part, pl.ds(zz * 8, 8)] = moved

    def send_time(b, zz):
        k, n = batches[b]
        units = pl.ds(k, n)
        for dx in (1, 3, 2, 0):
            for dz in (1, 0):
                t = xs[dx] * 4 + zs[dz] * 2 + zz
                at = zz * 8 + xs[dx] * 2 + zs[dz]

                def send(t=t, at=at, dz=dz):
                    rcopy(tsend.at[units, :, at], trecv.at[units, :, tm], t_send.at[b], t_recv.at[b],
                          (t, rows_of[dz])).start()

                def keep(at=at):
                    trecv[k:k + n, :, tm] = tsend[k:k + n, :, at]

                if (dx, dz) == (0, 0):
                    pl.when(zz != core)(send)
                    pl.when(zz == core)(keep)
                else:
                    send()

    def stage_own(b):
        @pl.loop(0, 3)
        def _(part):
            stage_part(b, zl, part)

        send_time(b, zl)

    def stage_partner(b):
        @pl.loop(0, 3)
        def _(part):
            zcopy(b, part, oz).wait_recv()
            stage_part(b, oz, part)

        send_time(b, oz)

    factor = LOG2E / math.sqrt(HD)

    def soften(s):
        p = jnp.exp2((s - jnp.max(s, axis=-1, keepdims=True)) * factor)
        return p, jnp.sum(p, axis=-1, keepdims=True)

    def temporal(b):
        k, n = batches[b]
        units = pl.ds(k, n)
        await_bytes(trecv.at[units, :, pl.ds(0, 15)], t_recv.at[b])
        for u in range(k, k + n):
            for h in range(2):
                cols = slice(h * HD, (h + 1) * HD)
                q, kk, v = (trecv[u, part, :, :, cols].reshape(256, HD) for part in range(3))
                p, total = soften(dot_nt(q, kk) + mask[...])
                o = dot(p.astype(BF), v) / total
                osend[u, :, :, cols] = o.astype(BF).reshape(16, 16, HD)
        orecv[k:k + n, me_at] = osend[k:k + n, tm]
        for o in offsets:
            dev, _ = peer(*o)
            rcopy(osend.at[units, dev[0]], orecv.at[units, me_at], o_send.at[b], o_recv.at[b], dev).start()

    def wait_back(b):
        k, n = batches[b]
        await_bytes(orecv.at[pl.ds(k, n), pl.ds(0, 15)], o_recv.at[b])

    def spatial(k):
        @pl.loop(0, 4)
        def _(f):
            rows = pl.ds(pl.multiple_of(f * 32, 32), 32)
            for h in range(2):
                cols = slice(h * HD, (h + 1) * HD)
                q = qkv[0:2, 0, k:k + 2, rows, cols].reshape(128, HD)
                kk, v = (qkv[0:2, part, :, rows, cols].reshape(512, HD) for part in (1, 2))
                p, total = soften(dot_nt(q, kk))
                o = dot(p.astype(BF), v) / total
                sp[:, k:k + 2, rows, cols] = o.reshape(2, 2, 32, HD)

    def ccopy(u, r, at, kept):
        half = half_of[u]
        return rcopy(csend.at[u, r % 2], comb.at[kept, half], c_send.at[u, r % 2], c_recv.at[at, half],
                     (tm, r))

    def combine(u):
        for zz in range(2):
            back = dot(perm_t[:128, :128], orecv[u, zz * 8:(zz + 1) * 8].reshape(128, 256))
            csend[u, zz] = (sp[zz, u] + back).astype(BF)
        if u < 2:
            ccopy(u, partner_row, row, y * 2 + hz).start()
            comb[y * 2 + hz, u] = csend[u, zl]
        else:
            for zz in range(2):
                ccopy(u, y_of[u] * 2 + zz, row, y * 2 + hz).start()

    def project_out(pair, first):
        for ys in pair:
            for i in range(2):
                r = ys * 2 + i
                for half in range(2):
                    def wait(r=r, half=half, ys=ys):
                        dst = comb.at[ys * 2 + (r + zh) % 2, half]
                        rcopy(csend.at[0, 0], dst, c_send.at[0, 0], c_recv.at[r, half], (tm, r)).wait_recv()
                    if ys is y:
                        pl.when(i != zl)(wait)
                    else:
                        wait()

        @pl.loop(0, 6)
        def _(n):
            cols = pl.ds(pl.multiple_of(n * 512, 512), 512)
            heads = [2 * ys + i for ys in pair for i in range(2)]
            left = jnp.concatenate([comb[h].reshape(256, 256) for h in heads], axis=1)
            right = jnp.concatenate([wo[h, :, cols] for h in heads], axis=0)
            acc = dot(left, right)
            for half in range(2):
                for f in range(4):
                    at = (half * 4 + f) * 32
                    rows = slice(half * 32, (half + 1) * 32)
                    piece = acc[at:at + 32]
                    if not first:
                        clip = clip_ref[tm * 4 + f]
                        piece = (piece + out_ref[f, rows, cols]) * mod_ref[2, pl.ds(clip, 1), cols]
                    out_ref[f, rows, cols] = piece

    load_w.wait()
    for p in range(3):
        for i in range(2):
            wz_copy(p, i, oz).wait_recv()
            wx_copy(p, i, e_own).start()
        wc_copy(p, 0, e_own).start()
        project_part(0, zl, p)
    for p in range(3):
        for i in range(2):
            wx_copy(p, i, e_x).wait_recv()
        wc_copy(p, 1, e_x).start()
    for p in range(3):
        for j in range(2):
            wc_copy(p, j, e_cores[j]).wait_recv()
        project_part(0, oz, p)
        zcopy(0, p, zl).start()
    load_wo.start()
    for i in range(2):
        y_copies[i].wait_recv()
        y_copies[4 + i].start()
    stage_own(0)
    project(1)
    stage_own(1)
    stage_partner(0)

    for i in range(2):
        y_copies[2 + i].wait_recv()
        y_copies[6 + i].start()
    project(2)
    stage_own(2)
    stage_partner(1)
    temporal(0)

    y_copies[4].wait_recv()
    y_copies[5].wait_recv()
    project(3)
    stage_own(3)
    stage_partner(2)
    temporal(1)
    stage_partner(3)

    y_copies[6].wait_recv()
    y_copies[7].wait_recv()
    project(4)
    stage_own(4)
    temporal(2)
    stage_partner(4)
    temporal(3)

    spatial(2)
    wait_back(1)
    combine(2)
    combine(3)
    spatial(4)
    wait_back(2)
    combine(4)
    combine(5)
    temporal(4)
    spatial(6)
    wait_back(3)
    combine(6)
    spatial(0)
    wait_back(0)
    combine(0)
    combine(1)
    load_wo.wait()
    project_out((yp, ym), first=True)
    wait_back(4)
    combine(7)
    project_out((y, yq), first=False)

    for p in range(3):
        for i in range(2):
            wz_copy(p, i, zl).wait_send()
            wx_copy(p, i, e_own).wait_send()
            wc_copy(p, i, e_own).wait_send()
    for c in y_copies:
        c.wait_send()
    for b, (k, n) in enumerate(batches):
        for part in range(3):
            zcopy(b, part, zl).wait_send()
        await_bytes(tsend.at[pl.ds(k, n), :, pl.ds(0, 15)], t_send.at[b])
        await_bytes(osend.at[pl.ds(k, n), pl.ds(0, 15)], o_send.at[b])
    for u in range(8):
        if u < 2:
            ccopy(u, partner_row, row, y * 2 + hz).wait_send()
        else:
            for zz in range(2):
                ccopy(u, y_of[u] * 2 + zz, row, y * 2 + hz).wait_send()


def attention(clip_ids, stream, mod, weight, out_weight):
    vmem = pl.BlockSpec(memory_space=pltpu.VMEM)
    hbm = pl.BlockSpec(memory_space=pl.ANY)
    dma = pltpu.SemaphoreType.DMA
    return pl.pallas_call(
        attention_kernel,
        out_shape=pltpu.VMEM((4, 64, 3072), F32),
        in_specs=[pl.BlockSpec(memory_space=pltpu.SMEM), hbm, vmem, hbm, hbm],
        out_specs=vmem,
        scratch_shapes=[
            pltpu.VMEM((4, 64, 3072), F32),
            pltpu.VMEM((8, 128, 3072), BF),
            pltpu.VMEM((2, 3, 8, 384, 256), BF),
            pltpu.VMEM((8, 256, 3072), BF),
            pltpu.VMEM((3, 3, 8, 128, 256), BF),
            pltpu.VMEM((8, 3, 16, 16, 256), BF),
            pltpu.VMEM((8, 3, 16, 16, 256), BF),
            pltpu.VMEM((8, 16, 16, 256), BF),
            pltpu.VMEM((8, 16, 16, 256), BF),
            pltpu.VMEM((8, 2, 128, 256), BF),
            pltpu.VMEM((8, 2, 128, 256), BF),
            pltpu.VMEM((2, 8, 128, 256), F32),
            pltpu.VMEM((256, 256), BF),
            pltpu.VMEM((256, 256), BF),
            pltpu.VMEM((256, 256), F32),
            dma((4,)),
            dma((8,)), dma((8,)),
            dma((3, 2)), dma((3, 2)),
            dma((3, 2)), dma((3, 2)),
            dma((3, 2)), dma((3, 2)),
            dma((5, 3)), dma((5, 3)),
            dma((5,)), dma((5,)),
            dma((5,)), dma((5,)),
            dma((8, 2)), dma((8, 2)),
        ],
        compiler_params=pltpu.CompilerParams(
            collective_id=0, has_side_effects=True, vmem_limit_bytes=60 * 1024 * 1024
        ),
        name="attention",
    )(clip_ids, stream, mod, weight, out_weight)


def per_device(stream, clip_ids, modulation, qkv_weight, out_weight):
    mod = jnp.transpose(modulation, (1, 0, 2))
    weight = jnp.transpose(qkv_weight, (1, 0, 2)).reshape(3, 8, 384, 256)
    return attention(clip_ids, stream, mod, weight, out_weight.reshape(8, 256, 3072))


def solution(mesh):
    placed = (P("tm", "row", None), P(), P(), P(None, None, "row"), P())
    return jax.shard_map(
        per_device, mesh=mesh, in_specs=placed, out_specs=P("tm", "row", None), check_vma=False
    )
```

```python
import math

import jax
import jax.numpy as jnp
from jax import lax
from jax.experimental import pallas as pl
from jax.experimental.pallas import tpu as pltpu
from jax.sharding import PartitionSpec as P

HD = 128
MESH = pl.DeviceIdType.MESH
BF = jnp.bfloat16
F32 = jnp.float32
LOG2E = 1.4426950408889634


def dot(a, b):
    return jnp.dot(a, b, preferred_element_type=F32)


def dot_nt(a, b):
    return lax.dot_general(a, b, (((1,), (1,)), ((), ())), preferred_element_type=F32)


def attention_kernel(
    clip_ref, stream_hbm, mod_ref, w_hbm, wo_hbm, out_ref,
    stream_v, xg, wbuf, wo, qkv, tsend, trecv, osend, orecv, csend, comb, sp, perm, perm_t, mask,
    load_sem, y_send, y_recv, wz_send, wz_recv, wx_send, wx_recv, wc_send, wc_recv, z_send, z_recv,
    t_send, t_recv, o_send, o_recv, c_send, c_recv,
):
    batches = ((0, 2), (2, 2), (4, 2), (6, 1), (7, 1))
    tm = lax.axis_index("tm")
    row = lax.axis_index("row")
    zh = (tm // 2) % 2
    core = tm % 2
    y = row // 2
    zl = row % 2
    hz = (zl + zh) % 2
    oz = 1 - zl
    partner_row = y * 2 + oz
    outer_tm = tm + 2 - 4 * zh
    other_core = tm + 1 - 2 * core
    ym, yp, yq = (y + 3) % 4, (y + 1) % 4, (y + 2) % 4
    up, down = (tm, yp * 2 + zl), (tm, ym * 2 + zl)
    y_of = (y, y, ym, yp, ym, yp, yq, yq)
    half_of = (0, 1, 0, 0, 1, 1, 0, 1)

    def rcopy(src, dst, send, recv, dev):
        return pltpu.make_async_remote_copy(
            src_ref=src, dst_ref=dst, send_sem=send, recv_sem=recv,
            device_id=dev, device_id_type=MESH,
        )

    def await_bytes(ref, sem):
        pltpu.make_async_copy(ref, ref, sem).wait()

    x = tm // 4
    xs = [((x + d) % 4) for d in range(4)]
    zs = [zh, 1 - zh]
    cs = [core, 1 - core]
    rows_of = [y * 2 + (hz + zh) % 2, y * 2 + (hz + 1 - zh) % 2]
    offsets = [(dx, dz, dc) for dx in (1, 3, 2, 0) for dz in range(2) for dc in range(2)][:-4]
    offsets = offsets + [(0, 1, 0), (0, 1, 1), (0, 0, 1)]
    me_at = core * 8 + x * 2 + zh

    def peer(dx, dz, dc):
        t = xs[dx] * 4 + zs[dz] * 2 + cs[dc]
        return (t, rows_of[dz]), cs[dc] * 8 + xs[dx] * 2 + zs[dz]

    load_stream = [
        pltpu.make_async_copy(stream_hbm.at[:, pl.ds(32 * u, 32)], stream_v.at[:, pl.ds(32 * u, 32)],
                              load_sem.at[u])
        for u in range(2)
    ]
    load_w = pltpu.make_async_copy(w_hbm, wbuf.at[zl], load_sem.at[2])
    load_wo = pltpu.make_async_copy(wo_hbm, wo, load_sem.at[3])
    for c in load_stream:
        c.start()

    barrier = pltpu.get_barrier_semaphore()
    for o in offsets:
        pl.semaphore_signal(barrier, inc=1, device_id=peer(*o)[0], device_id_type=MESH)
    row_peers = [(tm, r * 2 + (zl if i == 0 else oz)) for r in (y, ym, yp, yq) for i in range(2)][1:]
    for dev in row_peers:
        pl.semaphore_signal(barrier, inc=1, device_id=dev, device_id_type=MESH)

    x_par = x % 2
    x_up, x_down = (tm + 4) % 16, (tm + 12) % 16
    e_own = core * 4 + x_par * 2
    e_x = core * 4 + (1 - x_par) * 2
    e_cores = ((1 - core) * 4 + x_par * 2, (1 - core) * 4 + (1 - x_par) * 2)

    def wz_copy(p, i, side):
        dev = ((tm, partner_row), (outer_tm, partner_row))[i]
        return rcopy(w_hbm.at[p, e_own + i], wbuf.at[side, p, e_own + i],
                     wz_send.at[p, i], wz_recv.at[p, i], dev)

    def wx_copy(p, i, e):
        dev = ((x_up, row), (x_down, row))[i]
        return rcopy(wbuf.at[oz, p, e + i], wbuf.at[oz, p, e + i],
                     wx_send.at[p, i], wx_recv.at[p, i], dev)

    def wc_copy(p, j, e):
        pair = wbuf.at[oz, p, pl.ds(e, 2)]
        return rcopy(pair, pair, wc_send.at[p, j], wc_recv.at[p, j], (other_core, row))


    def norm(unit):
        @pl.loop(0, 4)
        def _(f):
            clip = clip_ref[tm * 4 + f]
            shift = mod_ref[0, pl.ds(clip, 1), :]
            scale = 1.0 + mod_ref[1, pl.ds(clip, 1), :]
            v = stream_v[f, pl.ds(unit * 32, 32), :]
            centred = v - jnp.mean(v, axis=-1, keepdims=True)
            var = jnp.mean(centred * centred, axis=-1, keepdims=True)
            n = centred * lax.rsqrt(var + 1e-06) * scale + shift
            xg[unit, pl.ds(f * 32, 32), :] = n.astype(BF)

    def ycopy(i, src, dst, half, dev):
        if half is None:
            return rcopy(xg.at[src], xg.at[dst], y_send.at[i], y_recv.at[i], dev)
        rows = pl.ds(half * 64, 64)
        return rcopy(xg.at[src, rows], xg.at[dst, rows], y_send.at[i], y_recv.at[i], dev)

    y_copies = [
        ycopy(0, 0, 2, None, up), ycopy(1, 0, 3, None, down),
        ycopy(2, 1, 4, None, up), ycopy(3, 1, 5, None, down),
        ycopy(4, 2, 6, 0, up), ycopy(5, 3, 6, 1, down),
        ycopy(6, 4, 7, 0, up), ycopy(7, 5, 7, 1, down),
    ]
    for unit in range(2):
        load_stream[unit].wait()
        norm(unit)
        if unit == 0:
            pl.semaphore_wait(barrier, 22)
            load_w.start()
            for p in range(3):
                for i in range(2):
                    wz_copy(p, i, zl).start()
        y_copies[2 * unit].start()
        y_copies[2 * unit + 1].start()

    def unit_row(j):
        return (j & 128) + ((j >> 2) & 3) * 32 + ((j >> 4) & 7) * 4 + (j & 3)

    r_i = lax.broadcasted_iota(jnp.int32, (256, 256), 0)
    c_i = lax.broadcasted_iota(jnp.int32, (256, 256), 1)
    perm[...] = (unit_row(r_i) == c_i).astype(BF)
    perm_t[...] = (unit_row(c_i) == r_i).astype(BF)
    lane = lax.broadcasted_iota(jnp.int32, (1, 256), 1)

    def clip_of(f, found):
        return jnp.where((lane >> 2) == f, clip_ref[f], found)

    key = lax.fori_loop(0, 64, clip_of, jnp.zeros((1, 256), jnp.int32)) * 4 + (lane & 3)
    key = jnp.broadcast_to(key.astype(F32), (256, 256))
    mask[...] = jnp.where(key == key.T, 0.0, -1e30).astype(F32)

    def project_part(b, pz, part):
        k, n = batches[b]
        kk = (pz + hz) % 2
        slot = kk * 2 + (1 - kk) * zl
        x = xg[k:k + n].reshape(n * 128, 3072)
        out = dot(x, wbuf[pz, part].reshape(3072, 256)).astype(BF)
        qkv[slot, part, k:k + n] = out.reshape(n, 128, 256)

    def zcopy(b, part, slot):
        k, n = batches[b]
        units = pl.ds(k, n)
        return rcopy(qkv.at[2, part, units], qkv.at[slot, part, units], z_send.at[b, part],
                     z_recv.at[b, part], (tm, partner_row))

    def project(b):
        @pl.loop(0, 3)
        def _(part):
            project_part(b, 1 - hz, part)
            zcopy(b, part, zl).start()

        @pl.loop(0, 3)
        def _(part):
            project_part(b, hz, part)

    def stage_part(b, zz, part):
        k, n = batches[b]
        rows = qkv[zz, part, k:k + n].reshape(n * 128, 256)
        moved = dot(perm[:n * 128, :n * 128], rows).astype(BF).reshape(n, 8, 16, 256)
        tsend[k:k + n, part, pl.ds(zz * 8, 8)] = moved

    def send_time(b, zz):
        k, n = batches[b]
        units = pl.ds(k, n)
        for dx in (1, 3, 2, 0):
            for dz in (1, 0):
                t = xs[dx] * 4 + zs[dz] * 2 + zz
                at = zz * 8 + xs[dx] * 2 + zs[dz]

                def send(t=t, at=at, dz=dz):
                    rcopy(tsend.at[units, :, at], trecv.at[units, :, tm], t_send.at[b], t_recv.at[b],
                          (t, rows_of[dz])).start()

                def keep(at=at):
                    trecv[k:k + n, :, tm] = tsend[k:k + n, :, at]

                if (dx, dz) == (0, 0):
                    pl.when(zz != core)(send)
                    pl.when(zz == core)(keep)
                else:
                    send()

    def stage_own(b):
        @pl.loop(0, 3)
        def _(part):
            stage_part(b, zl, part)

        send_time(b, zl)

    def stage_partner(b):
        @pl.loop(0, 3)
        def _(part):
            zcopy(b, part, oz).wait_recv()
            stage_part(b, oz, part)

        send_time(b, oz)

    factor = LOG2E / math.sqrt(HD)

    def soften(s):
        p = jnp.exp2((s - jnp.max(s, axis=-1, keepdims=True)) * factor)
        return p, jnp.sum(p, axis=-1, keepdims=True)

    def temporal(b):
        k, n = batches[b]
        units = pl.ds(k, n)
        await_bytes(trecv.at[units, :, pl.ds(0, 15)], t_recv.at[b])
        for u in range(k, k + n):
            for h in range(2):
                cols = slice(h * HD, (h + 1) * HD)
                q, kk, v = (trecv[u, part, :, :, cols].reshape(256, HD) for part in range(3))
                p, total = soften(dot_nt(q, kk) + mask[...])
                o = dot(p.astype(BF), v) / total
                osend[u, :, :, cols] = o.astype(BF).reshape(16, 16, HD)
        orecv[k:k + n, me_at] = osend[k:k + n, tm]
        for o in offsets:
            dev, _ = peer(*o)
            rcopy(osend.at[units, dev[0]], orecv.at[units, me_at], o_send.at[b], o_recv.at[b], dev).start()

    def wait_back(b):
        k, n = batches[b]
        await_bytes(orecv.at[pl.ds(k, n), pl.ds(0, 15)], o_recv.at[b])

    def spatial(ka, kb):
        @pl.loop(0, 2)
        def _(pair):
            for f in range(2):
                rows = pl.ds(pl.multiple_of(pair * 64 + f * 32, 32), 32)
                for h in range(2):
                    cols = slice(h * HD, (h + 1) * HD)
                    q = jnp.concatenate(
                        [qkv[0:2, 0, k:k + 2, rows, cols].reshape(128, HD) for k in (ka, kb)], axis=0)
                    kk, v = (qkv[0:2, part, :, rows, cols].reshape(512, HD) for part in (1, 2))
                    p, total = soften(dot_nt(q, kk))
                    o = (dot(p.astype(BF), v) / total).reshape(2, 2, 2, 32, HD)
                    sp[:, ka:ka + 2, rows, cols] = o[0]
                    sp[:, kb:kb + 2, rows, cols] = o[1]

    def ccopy(u, r, at, kept):
        half = half_of[u]
        return rcopy(csend.at[u, r % 2], comb.at[kept, half], c_send.at[u, r % 2], c_recv.at[at, half],
                     (tm, r))

    def combine(u):
        for zz in range(2):
            back = dot(perm_t[:128, :128], orecv[u, zz * 8:(zz + 1) * 8].reshape(128, 256))
            csend[u, zz] = (sp[zz, u] + back).astype(BF)
        if u < 2:
            ccopy(u, partner_row, row, y * 2 + hz).start()
            comb[y * 2 + hz, u] = csend[u, zl]
        else:
            for zz in range(2):
                ccopy(u, y_of[u] * 2 + zz, row, y * 2 + hz).start()

    def project_out(pair, first, last=True):
        for ys in pair:
            for i in range(2):
                r = ys * 2 + i
                for half in range(2):
                    def wait(r=r, half=half, ys=ys):
                        dst = comb.at[ys * 2 + (r + zh) % 2, half]
                        rcopy(csend.at[0, 0], dst, c_send.at[0, 0], c_recv.at[r, half], (tm, r)).wait_recv()
                    if ys is y:
                        pl.when(i != zl)(wait)
                    else:
                        wait()

        @pl.loop(0, 6)
        def _(n):
            cols = pl.ds(pl.multiple_of(n * 512, 512), 512)
            heads = [2 * ys + i for ys in pair for i in range(2)]
            left = jnp.concatenate([comb[h].reshape(256, 256) for h in heads], axis=1)
            right = jnp.concatenate([wo[h, :, cols] for h in heads], axis=0)
            acc = dot(left, right)
            for half in range(2):
                for f in range(4):
                    at = (half * 4 + f) * 32
                    rows = slice(half * 32, (half + 1) * 32)
                    piece = acc[at:at + 32]
                    if not first:
                        piece = piece + out_ref[f, rows, cols]
                    if not first and last:
                        clip = clip_ref[tm * 4 + f]
                        piece = piece * mod_ref[2, pl.ds(clip, 1), cols]
                    out_ref[f, rows, cols] = piece

    load_w.wait()
    for p in range(3):
        for i in range(2):
            wz_copy(p, i, oz).wait_recv()
            wx_copy(p, i, e_own).start()
        wc_copy(p, 0, e_own).start()
        project_part(0, zl, p)
    def pass_x(p):
        for i in range(2):
            wx_copy(p, i, e_x).wait_recv()
        wc_copy(p, 1, e_x).start()

    pass_x(0)
    pass_x(1)
    for p in range(3):
        for j in range(2):
            wc_copy(p, j, e_cores[j]).wait_recv()
        project_part(0, oz, p)
        zcopy(0, p, zl).start()
        if p == 0:
            pass_x(2)
    load_wo.start()
    for i in range(2):
        y_copies[i].wait_recv()
        y_copies[4 + i].start()
    stage_own(0)
    project(1)
    stage_own(1)
    stage_partner(0)

    for i in range(2):
        y_copies[2 + i].wait_recv()
        y_copies[6 + i].start()
    project(2)
    stage_own(2)
    stage_partner(1)
    temporal(0)

    y_copies[4].wait_recv()
    y_copies[5].wait_recv()
    project(3)
    stage_own(3)
    stage_partner(2)
    temporal(1)
    stage_partner(3)

    y_copies[6].wait_recv()
    y_copies[7].wait_recv()
    project(4)
    stage_own(4)
    temporal(2)
    stage_partner(4)
    temporal(3)

    spatial(2, 4)
    wait_back(1)
    combine(2)
    combine(3)
    wait_back(2)
    combine(4)
    combine(5)
    temporal(4)
    spatial(6, 0)
    wait_back(3)
    combine(6)
    wait_back(0)
    combine(0)
    combine(1)
    wait_back(4)
    combine(7)
    load_wo.wait()
    project_out((yp, ym), first=True)
    project_out((y,), first=False, last=False)
    project_out((yq,), first=False)

    for p in range(3):
        for i in range(2):
            wz_copy(p, i, zl).wait_send()
            wx_copy(p, i, e_own).wait_send()
            wc_copy(p, i, e_own).wait_send()
    for c in y_copies:
        c.wait_send()
    for b, (k, n) in enumerate(batches):
        for part in range(3):
            zcopy(b, part, zl).wait_send()
        await_bytes(tsend.at[pl.ds(k, n), :, pl.ds(0, 15)], t_send.at[b])
        await_bytes(osend.at[pl.ds(k, n), pl.ds(0, 15)], o_send.at[b])
    for u in range(8):
        if u < 2:
            ccopy(u, partner_row, row, y * 2 + hz).wait_send()
        else:
            for zz in range(2):
                ccopy(u, y_of[u] * 2 + zz, row, y * 2 + hz).wait_send()


def attention(clip_ids, stream, mod, weight, out_weight):
    vmem = pl.BlockSpec(memory_space=pltpu.VMEM)
    hbm = pl.BlockSpec(memory_space=pl.ANY)
    dma = pltpu.SemaphoreType.DMA
    return pl.pallas_call(
        attention_kernel,
        out_shape=pltpu.VMEM((4, 64, 3072), F32),
        in_specs=[pl.BlockSpec(memory_space=pltpu.SMEM), hbm, vmem, hbm, hbm],
        out_specs=vmem,
        scratch_shapes=[
            pltpu.VMEM((4, 64, 3072), F32),
            pltpu.VMEM((8, 128, 3072), BF),
            pltpu.VMEM((2, 3, 8, 384, 256), BF),
            pltpu.VMEM((8, 256, 3072), BF),
            pltpu.VMEM((3, 3, 8, 128, 256), BF),
            pltpu.VMEM((8, 3, 16, 16, 256), BF),
            pltpu.VMEM((8, 3, 16, 16, 256), BF),
            pltpu.VMEM((8, 16, 16, 256), BF),
            pltpu.VMEM((8, 16, 16, 256), BF),
            pltpu.VMEM((8, 2, 128, 256), BF),
            pltpu.VMEM((8, 2, 128, 256), BF),
            pltpu.VMEM((2, 8, 128, 256), F32),
            pltpu.VMEM((256, 256), BF),
            pltpu.VMEM((256, 256), BF),
            pltpu.VMEM((256, 256), F32),
            dma((4,)),
            dma((8,)), dma((8,)),
            dma((3, 2)), dma((3, 2)),
            dma((3, 2)), dma((3, 2)),
            dma((3, 2)), dma((3, 2)),
            dma((5, 3)), dma((5, 3)),
            dma((5,)), dma((5,)),
            dma((5,)), dma((5,)),
            dma((8, 2)), dma((8, 2)),
        ],
        compiler_params=pltpu.CompilerParams(
            collective_id=0, has_side_effects=True, vmem_limit_bytes=60 * 1024 * 1024
        ),
        name="attention",
    )(clip_ids, stream, mod, weight, out_weight)


def per_device(stream, clip_ids, modulation, qkv_weight, out_weight):
    mod = jnp.transpose(modulation, (1, 0, 2))
    weight = jnp.transpose(qkv_weight, (1, 0, 2)).reshape(3, 8, 384, 256)
    return attention(clip_ids, stream, mod, weight, out_weight.reshape(8, 256, 3072))


def solution(mesh):
    placed = (P("tm", "row", None), P(), P(), P(None, None, "row"), P())
    return jax.shard_map(
        per_device, mesh=mesh, in_specs=placed, out_specs=P("tm", "row", None), check_vma=False
    )
```

```python
import math

import jax
import jax.numpy as jnp
from jax import lax
from jax.experimental import pallas as pl
from jax.experimental.pallas import tpu as pltpu
from jax.sharding import PartitionSpec as P

HD = 128
MESH = pl.DeviceIdType.MESH
BF = jnp.bfloat16
F32 = jnp.float32
LOG2E = 1.4426950408889634


def dot(a, b):
    return jnp.dot(a, b, preferred_element_type=F32)


def dot_nt(a, b):
    return lax.dot_general(a, b, (((1,), (1,)), ((), ())), preferred_element_type=F32)


def attention_kernel(
    clip_ref, stream_hbm, mod_ref, w_hbm, wo_hbm, out_ref,
    stream_v, xg, wbuf, wo, qkv, qf, trecv, osend, orecv, csend, comb, sp, perm_t, mask,
    load_sem, y_send, y_recv, wz_send, wz_recv, wx_send, wx_recv, wc_send, wc_recv, z_send, z_recv,
    t_send, t_recv, o_send, o_recv, c_send, c_recv,
):
    batches = ((0, 2), (2, 2), (4, 2), (6, 1), (7, 1))
    sets = ((0, 4), (4, 3), (7, 1))
    tm = lax.axis_index("tm")
    row = lax.axis_index("row")
    zh = (tm // 2) % 2
    core = tm % 2
    y = row // 2
    zl = row % 2
    hz = (zl + zh) % 2
    oz = 1 - zl
    partner_row = y * 2 + oz
    outer_tm = tm + 2 - 4 * zh
    other_core = tm + 1 - 2 * core
    ym, yp, yq = (y + 3) % 4, (y + 1) % 4, (y + 2) % 4
    up, down = (tm, yp * 2 + zl), (tm, ym * 2 + zl)
    y_of = (y, y, ym, yp, ym, yp, yq, yq)
    half_of = (0, 1, 0, 0, 1, 1, 0, 1)

    def rcopy(src, dst, send, recv, dev):
        return pltpu.make_async_remote_copy(
            src_ref=src, dst_ref=dst, send_sem=send, recv_sem=recv,
            device_id=dev, device_id_type=MESH,
        )

    def await_bytes(ref, sem):
        pltpu.make_async_copy(ref, ref, sem).wait()

    x = tm // 4
    xs = [((x + d) % 4) for d in range(4)]
    zs = [zh, 1 - zh]
    cs = [core, 1 - core]
    rows_of = [y * 2 + (hz + zh) % 2, y * 2 + (hz + 1 - zh) % 2]
    offsets = [(dx, dz, dc) for dx in (1, 3, 2, 0) for dz in range(2) for dc in range(2)][:-4]
    offsets = offsets + [(0, 1, 0), (0, 1, 1), (0, 0, 1)]
    me_at = core * 8 + x * 2 + zh

    def peer(dx, dz, dc):
        t = xs[dx] * 4 + zs[dz] * 2 + cs[dc]
        return (t, rows_of[dz]), cs[dc] * 8 + xs[dx] * 2 + zs[dz]

    load_stream = [
        pltpu.make_async_copy(stream_hbm.at[:, pl.ds(32 * u, 32)], stream_v.at[:, pl.ds(32 * u, 32)],
                              load_sem.at[u])
        for u in range(2)
    ]
    load_w = pltpu.make_async_copy(w_hbm, wbuf.at[zl], load_sem.at[2])
    load_wo = pltpu.make_async_copy(wo_hbm, wo, load_sem.at[3])
    for c in load_stream:
        c.start()

    barrier = pltpu.get_barrier_semaphore()
    for o in offsets:
        pl.semaphore_signal(barrier, inc=1, device_id=peer(*o)[0], device_id_type=MESH)
    row_peers = [(tm, r * 2 + (zl if i == 0 else oz)) for r in (y, ym, yp, yq) for i in range(2)][1:]
    for dev in row_peers:
        pl.semaphore_signal(barrier, inc=1, device_id=dev, device_id_type=MESH)

    x_par = x % 2
    x_up, x_down = (tm + 4) % 16, (tm + 12) % 16
    e_own = core * 4 + x_par * 2
    e_x = core * 4 + (1 - x_par) * 2
    e_cores = ((1 - core) * 4 + x_par * 2, (1 - core) * 4 + (1 - x_par) * 2)

    def wz_copy(p, i, side):
        dev = ((tm, partner_row), (outer_tm, partner_row))[i]
        return rcopy(w_hbm.at[p, e_own + i], wbuf.at[side, p, e_own + i],
                     wz_send.at[p, i], wz_recv.at[p, i], dev)

    def wx_copy(p, i, e):
        dev = ((x_up, row), (x_down, row))[i]
        return rcopy(wbuf.at[oz, p, e + i], wbuf.at[oz, p, e + i],
                     wx_send.at[p, i], wx_recv.at[p, i], dev)

    def wc_copy(p, j, e):
        pair = wbuf.at[oz, p, pl.ds(e, 2)]
        return rcopy(pair, pair, wc_send.at[p, j], wc_recv.at[p, j], (other_core, row))


    def norm(unit):
        low = lax.broadcasted_iota(jnp.int32, (8, 3072), 0) < 4

        @pl.loop(0, 4)
        def _(j):
            here, moved = [], []
            for f in range(4):
                clip = clip_ref[tm * 4 + f]
                shift = mod_ref[0, pl.ds(clip, 1), :]
                scale = 1.0 + mod_ref[1, pl.ds(clip, 1), :]
                v = stream_v[f, pl.ds(pl.multiple_of(unit * 32 + j * 8, 8), 8), :]
                centred = v - jnp.mean(v, axis=-1, keepdims=True)
                var = jnp.mean(centred * centred, axis=-1, keepdims=True)
                here.append(centred * lax.rsqrt(var + 1e-06) * scale + shift)
                moved.append(pltpu.roll(here[f], 4, 0))
            rows = [jnp.where(low, here[f], moved[f + 1]) for f in (0, 2)]
            rows += [jnp.where(low, moved[f], here[f + 1]) for f in (0, 2)]
            xg[unit, pl.ds(pl.multiple_of(j * 32, 32), 32), :] = jnp.concatenate(rows, axis=0).astype(BF)

    def ycopy(i, src, dst, half, dev):
        if half is None:
            return rcopy(xg.at[src], xg.at[dst], y_send.at[i], y_recv.at[i], dev)
        rows = pl.ds(half * 64, 64)
        return rcopy(xg.at[src, rows], xg.at[dst, rows], y_send.at[i], y_recv.at[i], dev)

    y_copies = [
        ycopy(0, 0, 2, None, up), ycopy(1, 0, 3, None, down),
        ycopy(2, 1, 4, None, up), ycopy(3, 1, 5, None, down),
        ycopy(4, 2, 6, 0, up), ycopy(5, 3, 6, 1, down),
        ycopy(6, 4, 7, 0, up), ycopy(7, 5, 7, 1, down),
    ]
    for unit in range(2):
        load_stream[unit].wait()
        norm(unit)
        if unit == 0:
            pl.semaphore_wait(barrier, 22)
            load_w.start()
            for p in range(3):
                for i in range(2):
                    wz_copy(p, i, zl).start()
        y_copies[2 * unit].start()
        y_copies[2 * unit + 1].start()

    def unit_row(j):
        return (j & 128) + ((j >> 2) & 3) * 32 + ((j >> 4) & 7) * 4 + (j & 3)

    r_i = lax.broadcasted_iota(jnp.int32, (256, 256), 0)
    c_i = lax.broadcasted_iota(jnp.int32, (256, 256), 1)
    perm_t[...] = (unit_row(c_i) == r_i).astype(BF)
    lane = lax.broadcasted_iota(jnp.int32, (1, 256), 1)

    def clip_of(f, found):
        return jnp.where((lane >> 2) == f, clip_ref[f], found)

    key = lax.fori_loop(0, 64, clip_of, jnp.zeros((1, 256), jnp.int32)) * 4 + (lane & 3)
    key = jnp.broadcast_to(key.astype(F32), (256, 256))
    mask[...] = jnp.where(key == key.T, 0.0, -1e30).astype(F32)

    def project_part(b, pz, part):
        k, n = batches[b]
        kk = (pz + hz) % 2
        slot = kk * 2 + (1 - kk) * zl
        x = xg[k:k + n].reshape(n * 128, 3072)
        out = dot(x, wbuf[pz, part].reshape(3072, 256)).astype(BF)
        qkv[slot, part, k:k + n] = out.reshape(n, 128, 256)

    def zcopy(b, part, slot):
        k, n = batches[b]
        units = pl.ds(k, n)
        return rcopy(qkv.at[2, part, units], qkv.at[slot, part, units], z_send.at[b, part],
                     z_recv.at[b, part], (tm, partner_row))

    def project(b):
        @pl.loop(0, 3)
        def _(part):
            project_part(b, 1 - hz, part)
            zcopy(b, part, zl).start()

        @pl.loop(0, 3)
        def _(part):
            project_part(b, hz, part)

    def send_time(s, zz):
        k, n = sets[s]
        units = pl.ds(k, n)
        for dx in (1, 3, 2, 0):
            for dz in (1, 0):
                t = xs[dx] * 4 + zs[dz] * 2 + zz
                rows = pl.ds(pl.multiple_of((xs[dx] * 2 + zs[dz]) * 16, 16), 16)

                def send(t=t, rows=rows, dz=dz):
                    rcopy(qkv.at[zz, :, units, rows], trecv.at[:, units, tm], t_send.at[s], t_recv.at[s],
                          (t, rows_of[dz])).start()

                def keep(rows=rows):
                    trecv[:, k:k + n, tm] = qkv[zz, :, k:k + n, rows]

                if (dx, dz) == (0, 0):
                    pl.when(zz != core)(send)
                    pl.when(zz == core)(keep)
                else:
                    send()

    def wait_partner(b):
        for part in range(3):
            zcopy(b, part, oz).wait_recv()

    def by_frame(b):
        k, n = batches[b]

        @pl.loop(0, 6)
        def _(i):
            zz, part = i // 3, i % 3
            rows = qkv[zz, part, k:k + n].reshape(n * 128, 256)
            moved = dot(perm_t[:n * 128, :n * 128], rows).astype(BF)
            qf[zz, part, k:k + n] = moved.reshape(n, 128, 256)

    factor = LOG2E / math.sqrt(HD)

    def soften(s):
        p = jnp.exp2((s - jnp.max(s, axis=-1, keepdims=True)) * factor)
        return p, jnp.sum(p, axis=-1, keepdims=True)

    def temporal(s):
        k, n = sets[s]
        units = pl.ds(k, n)
        await_bytes(trecv.at[:, units, pl.ds(0, 15)], t_recv.at[s])
        for u in range(k, k + n):
            for h in range(2):
                cols = slice(h * HD, (h + 1) * HD)
                q, kk, v = (trecv[part, u, :, :, cols].reshape(256, HD) for part in range(3))
                p, total = soften(dot_nt(q, kk) + mask[...])
                o = dot(p.astype(BF), v) / total
                osend[u, :, :, cols] = o.astype(BF).reshape(16, 16, HD)
        orecv[k:k + n, me_at] = osend[k:k + n, tm]
        for o in offsets:
            dev, _ = peer(*o)
            rcopy(osend.at[units, dev[0]], orecv.at[units, me_at], o_send.at[s], o_recv.at[s], dev).start()

    def wait_back(s):
        k, n = sets[s]
        await_bytes(orecv.at[pl.ds(k, n), pl.ds(0, 15)], o_recv.at[s])

    def spatial(ka, kb):
        @pl.loop(0, 2)
        def _(pair):
            for f in range(2):
                rows = pl.ds(pl.multiple_of(pair * 64 + f * 32, 32), 32)
                for h in range(2):
                    cols = slice(h * HD, (h + 1) * HD)
                    q = jnp.concatenate(
                        [qf[:, 0, k:k + 2, rows, cols].reshape(128, HD) for k in (ka, kb)], axis=0)
                    kk, v = (qf[:, part, :, rows, cols].reshape(512, HD) for part in (1, 2))
                    p, total = soften(dot_nt(q, kk))
                    o = (dot(p.astype(BF), v) / total).reshape(2, 2, 2, 32, HD)
                    sp[:, ka:ka + 2, rows, cols] = o[0]
                    sp[:, kb:kb + 2, rows, cols] = o[1]

    def ccopy(u, r, at, kept):
        half = half_of[u]
        return rcopy(csend.at[u, r % 2], comb.at[kept, half], c_send.at[u, r % 2], c_recv.at[at, half],
                     (tm, r))

    def combine(u):
        for zz in range(2):
            back = dot(perm_t[:128, :128], orecv[u, zz * 8:(zz + 1) * 8].reshape(128, 256))
            csend[u, zz] = (sp[zz, u] + back).astype(BF)
        if u < 2:
            ccopy(u, partner_row, row, y * 2 + hz).start()
            comb[y * 2 + hz, u] = csend[u, zl]
        else:
            for zz in range(2):
                ccopy(u, y_of[u] * 2 + zz, row, y * 2 + hz).start()

    def project_out(pair, first, last=True):
        for ys in pair:
            for i in range(2):
                r = ys * 2 + i
                for half in range(2):
                    def wait(r=r, half=half, ys=ys):
                        dst = comb.at[ys * 2 + (r + zh) % 2, half]
                        rcopy(csend.at[0, 0], dst, c_send.at[0, 0], c_recv.at[r, half], (tm, r)).wait_recv()
                    if ys is y:
                        pl.when(i != zl)(wait)
                    else:
                        wait()

        @pl.loop(0, 6)
        def _(n):
            cols = pl.ds(pl.multiple_of(n * 512, 512), 512)
            heads = [2 * ys + i for ys in pair for i in range(2)]
            left = jnp.concatenate([comb[h].reshape(256, 256) for h in heads], axis=1)
            right = jnp.concatenate([wo[h, :, cols] for h in heads], axis=0)
            acc = dot(left, right)
            for half in range(2):
                for f in range(4):
                    at = (half * 4 + f) * 32
                    rows = slice(half * 32, (half + 1) * 32)
                    piece = acc[at:at + 32]
                    if not first:
                        piece = piece + out_ref[f, rows, cols]
                    if not first and last:
                        clip = clip_ref[tm * 4 + f]
                        piece = piece * mod_ref[2, pl.ds(clip, 1), cols]
                    out_ref[f, rows, cols] = piece

    load_w.wait()
    for p in range(3):
        for i in range(2):
            wz_copy(p, i, oz).wait_recv()
            wx_copy(p, i, e_own).start()
        wc_copy(p, 0, e_own).start()
        project_part(0, zl, p)
    def pass_x(p):
        for i in range(2):
            wx_copy(p, i, e_x).wait_recv()
        wc_copy(p, 1, e_x).start()

    pass_x(0)
    pass_x(1)
    for p in range(3):
        for j in range(2):
            wc_copy(p, j, e_cores[j]).wait_recv()
        project_part(0, oz, p)
        zcopy(0, p, zl).start()
        if p == 0:
            pass_x(2)
    load_wo.start()
    for i in range(2):
        y_copies[i].wait_recv()
        y_copies[4 + i].start()
    project(1)
    send_time(0, zl)
    wait_partner(0)
    wait_partner(1)
    send_time(0, oz)

    for i in range(2):
        y_copies[2 + i].wait_recv()
        y_copies[6 + i].start()
    project(2)
    by_frame(0)
    by_frame(1)
    temporal(0)

    y_copies[4].wait_recv()
    y_copies[5].wait_recv()
    project(3)
    send_time(1, zl)
    wait_partner(2)
    by_frame(2)
    wait_partner(3)
    send_time(1, oz)
    by_frame(3)

    y_copies[6].wait_recv()
    y_copies[7].wait_recv()
    project(4)
    send_time(2, zl)
    temporal(1)
    wait_partner(4)
    send_time(2, oz)
    by_frame(4)

    spatial(2, 4)
    wait_back(0)
    combine(2)
    combine(3)
    wait_back(1)
    combine(4)
    combine(5)
    temporal(2)
    spatial(6, 0)
    combine(6)
    combine(0)
    combine(1)
    wait_back(2)
    combine(7)
    load_wo.wait()
    project_out((yp, ym), first=True)
    project_out((y,), first=False, last=False)
    project_out((yq,), first=False)

    for p in range(3):
        for i in range(2):
            wz_copy(p, i, zl).wait_send()
            wx_copy(p, i, e_own).wait_send()
            wc_copy(p, i, e_own).wait_send()
    for c in y_copies:
        c.wait_send()
    for b, (k, n) in enumerate(batches):
        for part in range(3):
            zcopy(b, part, zl).wait_send()
    for s, (k, n) in enumerate(sets):
        await_bytes(trecv.at[:, pl.ds(k, n), pl.ds(0, 15)], t_send.at[s])
        await_bytes(osend.at[pl.ds(k, n), pl.ds(0, 15)], o_send.at[s])
    for u in range(8):
        if u < 2:
            ccopy(u, partner_row, row, y * 2 + hz).wait_send()
        else:
            for zz in range(2):
                ccopy(u, y_of[u] * 2 + zz, row, y * 2 + hz).wait_send()


def attention(clip_ids, stream, mod, weight, out_weight):
    vmem = pl.BlockSpec(memory_space=pltpu.VMEM)
    hbm = pl.BlockSpec(memory_space=pl.ANY)
    dma = pltpu.SemaphoreType.DMA
    return pl.pallas_call(
        attention_kernel,
        out_shape=pltpu.VMEM((4, 64, 3072), F32),
        in_specs=[pl.BlockSpec(memory_space=pltpu.SMEM), hbm, vmem, hbm, hbm],
        out_specs=vmem,
        scratch_shapes=[
            pltpu.VMEM((4, 64, 3072), F32),
            pltpu.VMEM((8, 128, 3072), BF),
            pltpu.VMEM((2, 3, 8, 384, 256), BF),
            pltpu.VMEM((8, 256, 3072), BF),
            pltpu.VMEM((3, 3, 8, 128, 256), BF),
            pltpu.VMEM((2, 3, 8, 128, 256), BF),
            pltpu.VMEM((3, 8, 16, 16, 256), BF),
            pltpu.VMEM((8, 16, 16, 256), BF),
            pltpu.VMEM((8, 16, 16, 256), BF),
            pltpu.VMEM((8, 2, 128, 256), BF),
            pltpu.VMEM((8, 2, 128, 256), BF),
            pltpu.VMEM((2, 8, 128, 256), F32),
            pltpu.VMEM((256, 256), BF),
            pltpu.VMEM((256, 256), F32),
            dma((4,)),
            dma((8,)), dma((8,)),
            dma((3, 2)), dma((3, 2)),
            dma((3, 2)), dma((3, 2)),
            dma((3, 2)), dma((3, 2)),
            dma((5, 3)), dma((5, 3)),
            dma((3,)), dma((3,)),
            dma((3,)), dma((3,)),
            dma((8, 2)), dma((8, 2)),
        ],
        compiler_params=pltpu.CompilerParams(
            collective_id=0, has_side_effects=True, vmem_limit_bytes=60 * 1024 * 1024
        ),
        name="attention",
    )(clip_ids, stream, mod, weight, out_weight)


def per_device(stream, clip_ids, modulation, qkv_weight, out_weight):
    mod = jnp.transpose(modulation, (1, 0, 2))
    weight = jnp.transpose(qkv_weight, (1, 0, 2)).reshape(3, 8, 384, 256)
    return attention(clip_ids, stream, mod, weight, out_weight.reshape(8, 256, 3072))


def solution(mesh):
    placed = (P("tm", "row", None), P(), P(), P(None, None, "row"), P())
    return jax.shard_map(
        per_device, mesh=mesh, in_specs=placed, out_specs=P("tm", "row", None), check_vma=False
    )
```

```python
import math

import jax
import jax.numpy as jnp
from jax import lax
from jax.experimental import pallas as pl
from jax.experimental.pallas import tpu as pltpu
from jax.sharding import PartitionSpec as P

HD = 128
MESH = pl.DeviceIdType.MESH
BF = jnp.bfloat16
F32 = jnp.float32
LOG2E = 1.4426950408889634


def dot(a, b):
    return jnp.dot(a, b, preferred_element_type=F32)


def dot_nt(a, b):
    return lax.dot_general(a, b, (((1,), (1,)), ((), ())), preferred_element_type=F32)


def attention_kernel(
    clip_ref, stream_hbm, mod_ref, w_hbm, wo_hbm, out_ref,
    stream_v, xg, wbuf, wo, qkv, tsend, trecv, osend, orecv, csend, comb, relay, sp, perm, perm_t, mask,
    load_sem, y_send, y_recv, wz_send, wz_recv, wx_send, wx_recv, wc_send, wc_recv, z_send, z_recv,
    t_send, t_recv, b_send, b_recv, f_send, o_send, o_recv, c_send, c_recv,
):
    batches = ((0, 2), (2, 2), (4, 2), (6, 1), (7, 1))
    tm = lax.axis_index("tm")
    row = lax.axis_index("row")
    zh = (tm // 2) % 2
    core = tm % 2
    y = row // 2
    zl = row % 2
    hz = (zl + zh) % 2
    oz = 1 - zl
    partner_row = y * 2 + oz
    outer_tm = tm + 2 - 4 * zh
    other_core = tm + 1 - 2 * core
    ym, yp, yq = (y + 3) % 4, (y + 1) % 4, (y + 2) % 4
    up, down = (tm, yp * 2 + zl), (tm, ym * 2 + zl)
    y_of = (y, y, ym, yp, ym, yp, yq, yq)
    half_of = (0, 1, 0, 0, 1, 1, 0, 1)

    def rcopy(src, dst, send, recv, dev):
        return pltpu.make_async_remote_copy(
            src_ref=src, dst_ref=dst, send_sem=send, recv_sem=recv,
            device_id=dev, device_id_type=MESH,
        )

    def await_bytes(ref, sem):
        pltpu.make_async_copy(ref, ref, sem).wait()

    x = tm // 4
    xs = [((x + d) % 4) for d in range(4)]
    zs = [zh, 1 - zh]
    cs = [core, 1 - core]
    rows_of = [y * 2 + (hz + zh) % 2, y * 2 + (hz + 1 - zh) % 2]
    offsets = [(dx, dz, dc) for dx in (1, 3, 2, 0) for dz in range(2) for dc in range(2)][:-4]
    offsets = offsets + [(0, 1, 0), (0, 1, 1), (0, 0, 1)]
    me_at = core * 8 + x * 2 + zh

    def peer(dx, dz, dc):
        t = xs[dx] * 4 + zs[dz] * 2 + cs[dc]
        return (t, rows_of[dz]), cs[dc] * 8 + xs[dx] * 2 + zs[dz]

    load_stream = [
        pltpu.make_async_copy(stream_hbm.at[:, pl.ds(32 * u, 32)], stream_v.at[:, pl.ds(32 * u, 32)],
                              load_sem.at[u])
        for u in range(2)
    ]
    load_w = pltpu.make_async_copy(w_hbm, wbuf.at[zl], load_sem.at[2])
    load_wo = pltpu.make_async_copy(wo_hbm, wo, load_sem.at[3])
    for c in load_stream:
        c.start()

    barrier = pltpu.get_barrier_semaphore()
    for o in offsets:
        pl.semaphore_signal(barrier, inc=1, device_id=peer(*o)[0], device_id_type=MESH)
    row_peers = [(tm, r * 2 + (zl if i == 0 else oz)) for r in (y, ym, yp, yq) for i in range(2)][1:]
    for dev in row_peers:
        pl.semaphore_signal(barrier, inc=1, device_id=dev, device_id_type=MESH)

    x_par = x % 2
    x_up, x_down = (tm + 4) % 16, (tm + 12) % 16
    e_own = core * 4 + x_par * 2
    e_x = core * 4 + (1 - x_par) * 2
    e_cores = ((1 - core) * 4 + x_par * 2, (1 - core) * 4 + (1 - x_par) * 2)

    def wz_copy(p, i, side):
        dev = ((tm, partner_row), (outer_tm, partner_row))[i]
        return rcopy(w_hbm.at[p, e_own + i], wbuf.at[side, p, e_own + i],
                     wz_send.at[p, i], wz_recv.at[p, i], dev)

    def wx_copy(p, i, e):
        dev = ((x_up, row), (x_down, row))[i]
        return rcopy(wbuf.at[oz, p, e + i], wbuf.at[oz, p, e + i],
                     wx_send.at[p, i], wx_recv.at[p, i], dev)

    def wc_copy(p, j, e):
        pair = wbuf.at[oz, p, pl.ds(e, 2)]
        return rcopy(pair, pair, wc_send.at[p, j], wc_recv.at[p, j], (other_core, row))


    def norm(unit):
        @pl.loop(0, 4)
        def _(f):
            clip = clip_ref[tm * 4 + f]
            shift = mod_ref[0, pl.ds(clip, 1), :]
            scale = 1.0 + mod_ref[1, pl.ds(clip, 1), :]
            v = stream_v[f, pl.ds(unit * 32, 32), :]
            centred = v - jnp.mean(v, axis=-1, keepdims=True)
            var = jnp.mean(centred * centred, axis=-1, keepdims=True)
            n = centred * lax.rsqrt(var + 1e-06) * scale + shift
            xg[unit, pl.ds(f * 32, 32), :] = n.astype(BF)

    def ycopy(i, src, dst, half, dev):
        if half is None:
            return rcopy(xg.at[src], xg.at[dst], y_send.at[i], y_recv.at[i], dev)
        rows = pl.ds(half * 64, 64)
        return rcopy(xg.at[src, rows], xg.at[dst, rows], y_send.at[i], y_recv.at[i], dev)

    y_copies = [
        ycopy(0, 0, 2, None, up), ycopy(1, 0, 3, None, down),
        ycopy(2, 1, 4, None, up), ycopy(3, 1, 5, None, down),
        ycopy(4, 2, 6, 0, up), ycopy(5, 3, 6, 1, down),
        ycopy(6, 4, 7, 0, up), ycopy(7, 5, 7, 1, down),
    ]
    for unit in range(2):
        load_stream[unit].wait()
        norm(unit)
        if unit == 0:
            pl.semaphore_wait(barrier, 22)
            load_w.start()
            for p in range(3):
                for i in range(2):
                    wz_copy(p, i, zl).start()
        y_copies[2 * unit].start()
        y_copies[2 * unit + 1].start()

    def unit_row(j):
        return (j & 128) + ((j >> 2) & 3) * 32 + ((j >> 4) & 7) * 4 + (j & 3)

    r_i = lax.broadcasted_iota(jnp.int32, (256, 256), 0)
    c_i = lax.broadcasted_iota(jnp.int32, (256, 256), 1)
    perm[...] = (unit_row(r_i) == c_i).astype(BF)
    perm_t[...] = (unit_row(c_i) == r_i).astype(BF)
    lane = lax.broadcasted_iota(jnp.int32, (1, 256), 1)

    def clip_of(f, found):
        return jnp.where((lane >> 2) == f, clip_ref[f], found)

    key = lax.fori_loop(0, 64, clip_of, jnp.zeros((1, 256), jnp.int32)) * 4 + (lane & 3)
    key = jnp.broadcast_to(key.astype(F32), (256, 256))
    mask[...] = jnp.where(key == key.T, 0.0, -1e30).astype(F32)

    def project_part(b, pz, part):
        k, n = batches[b]
        kk = (pz + hz) % 2
        slot = kk * 2 + (1 - kk) * zl
        x = xg[k:k + n].reshape(n * 128, 3072)
        out = dot(x, wbuf[pz, part].reshape(3072, 256)).astype(BF)
        qkv[slot, part, k:k + n] = out.reshape(n, 128, 256)

    def zcopy(b, part, slot):
        k, n = batches[b]
        units = pl.ds(k, n)
        return rcopy(qkv.at[2, part, units], qkv.at[slot, part, units], z_send.at[b, part],
                     z_recv.at[b, part], (tm, partner_row))

    def project(b):
        @pl.loop(0, 3)
        def _(part):
            project_part(b, 1 - hz, part)
            zcopy(b, part, zl).start()

        @pl.loop(0, 3)
        def _(part):
            project_part(b, hz, part)

    def stage_part(b, zz, part):
        k, n = batches[b]
        rows = qkv[zz, part, k:k + n].reshape(n * 128, 256)
        moved = dot(perm[:n * 128, :n * 128], rows).astype(BF).reshape(n, 8, 16, 256)
        tsend[k:k + n, part, pl.ds(zz * 8, 8)] = moved

    def send_time(b, zz):
        k, n = batches[b]
        units = pl.ds(k, n)
        if b < 3:
            bundle(b, zz).start()
        for dx in (1, 3, 0) if b < 3 else (1, 3, 2, 0):
            for dz in (1, 0):
                t = xs[dx] * 4 + zs[dz] * 2 + zz
                at = zz * 8 + xs[dx] * 2 + zs[dz]

                def send(t=t, at=at, dz=dz):
                    rcopy(tsend.at[units, :, at], trecv.at[units, :, tm], t_send.at[b], t_recv.at[b],
                          (t, rows_of[dz])).start()

                def keep(at=at):
                    trecv[k:k + n, :, tm] = tsend[k:k + n, :, at]

                if (dx, dz) == (0, 0):
                    pl.when(zz != core)(send)
                    pl.when(zz == core)(keep)
                else:
                    send()

    def bundle(b, zz):
        k, n = batches[b]
        units = pl.ds(k, n)
        return rcopy(tsend.at[units, :, pl.ds(zz * 8 + xs[2] * 2, 2)], relay.at[units, :, zz],
                     b_send.at[b, zz], b_recv.at[b, zz], (x_up, row))

    def fcopy(b, zz, z):
        k, n = batches[b]
        units = pl.ds(k, n)
        dev = (xs[1] * 4 + z * 2 + zz, y * 2 + (hz + z) % 2)
        return rcopy(relay.at[units, :, zz, z], trecv.at[units, :, x_down], f_send.at[b, zz, z],
                     t_recv.at[b], dev)

    def pass_on(b):
        for zz in range(2):
            bundle(b, zz).wait_recv()
            for z in range(2):
                fcopy(b, zz, z).start()

    def stage_own(b):
        @pl.loop(0, 3)
        def _(part):
            stage_part(b, zl, part)

        send_time(b, zl)

    def stage_partner(b):
        @pl.loop(0, 3)
        def _(part):
            zcopy(b, part, oz).wait_recv()
            stage_part(b, oz, part)

        send_time(b, oz)

    factor = LOG2E / math.sqrt(HD)

    def soften(s):
        p = jnp.exp2((s - jnp.max(s, axis=-1, keepdims=True)) * factor)
        return p, jnp.sum(p, axis=-1, keepdims=True)

    def temporal(b):
        k, n = batches[b]
        units = pl.ds(k, n)
        await_bytes(trecv.at[units, :, pl.ds(0, 15)], t_recv.at[b])
        for u in range(k, k + n):
            for h in range(2):
                cols = slice(h * HD, (h + 1) * HD)
                q, kk, v = (trecv[u, part, :, :, cols].reshape(256, HD) for part in range(3))
                p, total = soften(dot_nt(q, kk) + mask[...])
                o = dot(p.astype(BF), v) / total
                osend[u, :, :, cols] = o.astype(BF).reshape(16, 16, HD)
        orecv[k:k + n, me_at] = osend[k:k + n, tm]
        for o in offsets:
            dev, _ = peer(*o)
            rcopy(osend.at[units, dev[0]], orecv.at[units, me_at], o_send.at[b], o_recv.at[b], dev).start()

    def wait_back(b):
        k, n = batches[b]
        await_bytes(orecv.at[pl.ds(k, n), pl.ds(0, 15)], o_recv.at[b])

    def spatial(ka, kb):
        @pl.loop(0, 2)
        def _(pair):
            for f in range(2):
                rows = pl.ds(pl.multiple_of(pair * 64 + f * 32, 32), 32)
                for h in range(2):
                    cols = slice(h * HD, (h + 1) * HD)
                    q = jnp.concatenate(
                        [qkv[0:2, 0, k:k + 2, rows, cols].reshape(128, HD) for k in (ka, kb)], axis=0)
                    kk, v = (qkv[0:2, part, :, rows, cols].reshape(512, HD) for part in (1, 2))
                    p, total = soften(dot_nt(q, kk))
                    o = (dot(p.astype(BF), v) / total).reshape(2, 2, 2, 32, HD)
                    sp[:, ka:ka + 2, rows, cols] = o[0]
                    sp[:, kb:kb + 2, rows, cols] = o[1]

    def ccopy(u, r, at, kept):
        half = half_of[u]
        return rcopy(csend.at[u, r % 2], comb.at[kept, half], c_send.at[u, r % 2], c_recv.at[at, half],
                     (tm, r))

    def combine(u):
        for zz in range(2):
            back = dot(perm_t[:128, :128], orecv[u, zz * 8:(zz + 1) * 8].reshape(128, 256))
            csend[u, zz] = (sp[zz, u] + back).astype(BF)
        if u < 2:
            ccopy(u, partner_row, row, y * 2 + hz).start()
            comb[y * 2 + hz, u] = csend[u, zl]
        else:
            for zz in range(2):
                ccopy(u, y_of[u] * 2 + zz, row, y * 2 + hz).start()

    def project_out(pair, first, last=True):
        for ys in pair:
            for i in range(2):
                r = ys * 2 + i
                for half in range(2):
                    def wait(r=r, half=half, ys=ys):
                        dst = comb.at[ys * 2 + (r + zh) % 2, half]
                        rcopy(csend.at[0, 0], dst, c_send.at[0, 0], c_recv.at[r, half], (tm, r)).wait_recv()
                    if ys is y:
                        pl.when(i != zl)(wait)
                    else:
                        wait()

        @pl.loop(0, 6)
        def _(n):
            cols = pl.ds(pl.multiple_of(n * 512, 512), 512)
            heads = [2 * ys + i for ys in pair for i in range(2)]
            left = jnp.concatenate([comb[h].reshape(256, 256) for h in heads], axis=1)
            right = jnp.concatenate([wo[h, :, cols] for h in heads], axis=0)
            acc = dot(left, right)
            for half in range(2):
                for f in range(4):
                    at = (half * 4 + f) * 32
                    rows = slice(half * 32, (half + 1) * 32)
                    piece = acc[at:at + 32]
                    if not first:
                        piece = piece + out_ref[f, rows, cols]
                    if not first and last:
                        clip = clip_ref[tm * 4 + f]
                        piece = piece * mod_ref[2, pl.ds(clip, 1), cols]
                    out_ref[f, rows, cols] = piece

    load_w.wait()
    for p in range(3):
        for i in range(2):
            wz_copy(p, i, oz).wait_recv()
            wx_copy(p, i, e_own).start()
        wc_copy(p, 0, e_own).start()
        project_part(0, zl, p)
    def pass_x(p):
        for i in range(2):
            wx_copy(p, i, e_x).wait_recv()
        wc_copy(p, 1, e_x).start()

    pass_x(0)
    pass_x(1)
    for p in range(3):
        for j in range(2):
            wc_copy(p, j, e_cores[j]).wait_recv()
        project_part(0, oz, p)
        zcopy(0, p, zl).start()
        if p == 0:
            pass_x(2)
    load_wo.start()
    for i in range(2):
        y_copies[i].wait_recv()
        y_copies[4 + i].start()
    stage_own(0)
    project(1)
    stage_own(1)
    stage_partner(0)

    for i in range(2):
        y_copies[2 + i].wait_recv()
        y_copies[6 + i].start()
    project(2)
    pass_on(0)
    stage_own(2)
    stage_partner(1)
    temporal(0)

    y_copies[4].wait_recv()
    y_copies[5].wait_recv()
    project(3)
    pass_on(1)
    stage_own(3)
    stage_partner(2)
    temporal(1)
    stage_partner(3)

    y_copies[6].wait_recv()
    y_copies[7].wait_recv()
    project(4)
    stage_own(4)
    pass_on(2)
    stage_partner(4)
    temporal(3)
    temporal(2)

    spatial(2, 4)
    wait_back(1)
    combine(2)
    combine(3)
    wait_back(2)
    combine(4)
    combine(5)
    temporal(4)
    spatial(6, 0)
    wait_back(3)
    combine(6)
    wait_back(0)
    combine(0)
    combine(1)
    wait_back(4)
    combine(7)
    load_wo.wait()
    project_out((yp, ym), first=True)
    project_out((y,), first=False, last=False)
    project_out((yq,), first=False)

    for p in range(3):
        for i in range(2):
            wz_copy(p, i, zl).wait_send()
            wx_copy(p, i, e_own).wait_send()
            wc_copy(p, i, e_own).wait_send()
    for c in y_copies:
        c.wait_send()
    for b, (k, n) in enumerate(batches):
        for part in range(3):
            zcopy(b, part, zl).wait_send()
        await_bytes(tsend.at[pl.ds(k, n), :, pl.ds(0, 11 if b < 3 else 15)], t_send.at[b])
        if b < 3:
            for zz in range(2):
                bundle(b, zz).wait_send()
                for z in range(2):
                    fcopy(b, zz, z).wait_send()
        await_bytes(osend.at[pl.ds(k, n), pl.ds(0, 15)], o_send.at[b])
    for u in range(8):
        if u < 2:
            ccopy(u, partner_row, row, y * 2 + hz).wait_send()
        else:
            for zz in range(2):
                ccopy(u, y_of[u] * 2 + zz, row, y * 2 + hz).wait_send()


def attention(clip_ids, stream, mod, weight, out_weight):
    vmem = pl.BlockSpec(memory_space=pltpu.VMEM)
    hbm = pl.BlockSpec(memory_space=pl.ANY)
    dma = pltpu.SemaphoreType.DMA
    return pl.pallas_call(
        attention_kernel,
        out_shape=pltpu.VMEM((4, 64, 3072), F32),
        in_specs=[pl.BlockSpec(memory_space=pltpu.SMEM), hbm, vmem, hbm, hbm],
        out_specs=vmem,
        scratch_shapes=[
            pltpu.VMEM((4, 64, 3072), F32),
            pltpu.VMEM((8, 128, 3072), BF),
            pltpu.VMEM((2, 3, 8, 384, 256), BF),
            pltpu.VMEM((8, 256, 3072), BF),
            pltpu.VMEM((3, 3, 8, 128, 256), BF),
            pltpu.VMEM((8, 3, 16, 16, 256), BF),
            pltpu.VMEM((8, 3, 16, 16, 256), BF),
            pltpu.VMEM((8, 16, 16, 256), BF),
            pltpu.VMEM((8, 16, 16, 256), BF),
            pltpu.VMEM((8, 2, 128, 256), BF),
            pltpu.VMEM((8, 2, 128, 256), BF),
            pltpu.VMEM((6, 3, 2, 2, 16, 256), BF),
            pltpu.VMEM((2, 8, 128, 256), F32),
            pltpu.VMEM((256, 256), BF),
            pltpu.VMEM((256, 256), BF),
            pltpu.VMEM((256, 256), F32),
            dma((4,)),
            dma((8,)), dma((8,)),
            dma((3, 2)), dma((3, 2)),
            dma((3, 2)), dma((3, 2)),
            dma((3, 2)), dma((3, 2)),
            dma((5, 3)), dma((5, 3)),
            dma((5,)), dma((5,)),
            dma((3, 2)), dma((3, 2)), dma((3, 2, 2)),
            dma((5,)), dma((5,)),
            dma((8, 2)), dma((8, 2)),
        ],
        compiler_params=pltpu.CompilerParams(
            collective_id=0, has_side_effects=True, vmem_limit_bytes=60 * 1024 * 1024
        ),
        name="attention",
    )(clip_ids, stream, mod, weight, out_weight)


def per_device(stream, clip_ids, modulation, qkv_weight, out_weight):
    mod = jnp.transpose(modulation, (1, 0, 2))
    weight = jnp.transpose(qkv_weight, (1, 0, 2)).reshape(3, 8, 384, 256)
    return attention(clip_ids, stream, mod, weight, out_weight.reshape(8, 256, 3072))


def solution(mesh):
    placed = (P("tm", "row", None), P(), P(), P(None, None, "row"), P())
    return jax.shard_map(
        per_device, mesh=mesh, in_specs=placed, out_specs=P("tm", "row", None), check_vma=False
    )
```

```python
import math

import jax
import jax.numpy as jnp
from jax import lax
from jax.experimental import pallas as pl
from jax.experimental.pallas import tpu as pltpu
from jax.sharding import PartitionSpec as P

HD = 128
MESH = pl.DeviceIdType.MESH
BF = jnp.bfloat16
F32 = jnp.float32
LOG2E = 1.4426950408889634


def dot(a, b):
    return jnp.dot(a, b, preferred_element_type=F32)


def dot_nt(a, b):
    return lax.dot_general(a, b, (((1,), (1,)), ((), ())), preferred_element_type=F32)


def attention_kernel(
    clip_ref, stream_hbm, mod_ref, w_hbm, wo_hbm, out_ref,
    stream_v, xg, wbuf, wo, qkv, tsend, trecv, osend, orecv, csend, comb, sp, perm, perm_t, mask,
    load_sem, y_send, y_recv, wz_send, wz_recv, wx_send, wx_recv, wc_send, wc_recv, z_send, z_recv,
    t_send, t_recv, o_send, o_recv, c_send, c_recv,
):
    batches = ((0, 2), (2, 2), (4, 2), (6, 1), (7, 1))
    tm = lax.axis_index("tm")
    row = lax.axis_index("row")
    zh = (tm // 2) % 2
    core = tm % 2
    y = row // 2
    zl = row % 2
    hz = (zl + zh) % 2
    oz = 1 - zl
    partner_row = y * 2 + oz
    outer_tm = tm + 2 - 4 * zh
    other_core = tm + 1 - 2 * core
    ym, yp, yq = (y + 3) % 4, (y + 1) % 4, (y + 2) % 4
    up, down = (tm, yp * 2 + zl), (tm, ym * 2 + zl)
    y_of = (y, y, ym, yp, ym, yp, yq, yq)
    half_of = (0, 1, 0, 0, 1, 1, 0, 1)

    def rcopy(src, dst, send, recv, dev):
        return pltpu.make_async_remote_copy(
            src_ref=src, dst_ref=dst, send_sem=send, recv_sem=recv,
            device_id=dev, device_id_type=MESH,
        )

    def await_bytes(ref, sem):
        pltpu.make_async_copy(ref, ref, sem).wait()

    x = tm // 4
    xs = [((x + d) % 4) for d in range(4)]
    zs = [zh, 1 - zh]
    cs = [core, 1 - core]
    rows_of = [y * 2 + (hz + zh) % 2, y * 2 + (hz + 1 - zh) % 2]
    offsets = [(dx, dz, dc) for dx in (1, 3, 2, 0) for dz in range(2) for dc in range(2)][:-4]
    offsets = offsets + [(0, 1, 0), (0, 1, 1), (0, 0, 1)]
    me_at = core * 8 + x * 2 + zh

    def peer(dx, dz, dc):
        t = xs[dx] * 4 + zs[dz] * 2 + cs[dc]
        return (t, rows_of[dz]), cs[dc] * 8 + xs[dx] * 2 + zs[dz]

    load_stream = [
        pltpu.make_async_copy(stream_hbm.at[:, pl.ds(32 * u, 32)], stream_v.at[:, pl.ds(32 * u, 32)],
                              load_sem.at[u])
        for u in range(2)
    ]
    load_w = pltpu.make_async_copy(w_hbm, wbuf.at[zl], load_sem.at[2])
    load_wo = pltpu.make_async_copy(wo_hbm, wo, load_sem.at[3])
    for c in load_stream:
        c.start()

    barrier = pltpu.get_barrier_semaphore()
    for o in offsets:
        pl.semaphore_signal(barrier, inc=1, device_id=peer(*o)[0], device_id_type=MESH)
    row_peers = [(tm, r * 2 + (zl if i == 0 else oz)) for r in (y, ym, yp, yq) for i in range(2)][1:]
    for dev in row_peers:
        pl.semaphore_signal(barrier, inc=1, device_id=dev, device_id_type=MESH)

    x_par = x % 2
    x_up, x_down = (tm + 4) % 16, (tm + 12) % 16
    e_own = core * 4 + x_par * 2
    e_x = core * 4 + (1 - x_par) * 2
    e_cores = ((1 - core) * 4 + x_par * 2, (1 - core) * 4 + (1 - x_par) * 2)

    def wz_copy(p, i, side):
        dev = ((tm, partner_row), (outer_tm, partner_row))[i]
        return rcopy(w_hbm.at[p, e_own + i], wbuf.at[side, p, e_own + i],
                     wz_send.at[p, i], wz_recv.at[p, i], dev)

    def wx_copy(p, i, e):
        dev = ((x_up, row), (x_down, row))[i]
        return rcopy(wbuf.at[oz, p, e + i], wbuf.at[oz, p, e + i],
                     wx_send.at[p, i], wx_recv.at[p, i], dev)

    def wc_copy(p, j, e):
        pair = wbuf.at[oz, p, pl.ds(e, 2)]
        return rcopy(pair, pair, wc_send.at[p, j], wc_recv.at[p, j], (other_core, row))


    def norm(unit):
        @pl.loop(0, 4)
        def _(f):
            clip = clip_ref[tm * 4 + f]
            shift = mod_ref[0, pl.ds(clip, 1), :]
            scale = 1.0 + mod_ref[1, pl.ds(clip, 1), :]
            v = stream_v[f, pl.ds(unit * 32, 32), :]
            centred = v - jnp.mean(v, axis=-1, keepdims=True)
            var = jnp.mean(centred * centred, axis=-1, keepdims=True)
            n = centred * lax.rsqrt(var + 1e-06) * scale + shift
            xg[unit, pl.ds(f * 32, 32), :] = n.astype(BF)

    def ycopy(i, src, dst, half, dev):
        if half is None:
            return rcopy(xg.at[src], xg.at[dst], y_send.at[i], y_recv.at[i], dev)
        rows = pl.ds(half * 64, 64)
        return rcopy(xg.at[src, rows], xg.at[dst, rows], y_send.at[i], y_recv.at[i], dev)

    y_copies = [
        ycopy(0, 0, 2, None, up), ycopy(1, 0, 3, None, down),
        ycopy(2, 1, 4, None, up), ycopy(3, 1, 5, None, down),
        ycopy(4, 2, 6, 0, up), ycopy(5, 3, 6, 1, down),
        ycopy(6, 4, 7, 0, up), ycopy(7, 5, 7, 1, down),
    ]
    for unit in range(2):
        load_stream[unit].wait()
        norm(unit)
        if unit == 0:
            pl.semaphore_wait(barrier, 22)
            load_w.start()
            for p in range(3):
                for i in range(2):
                    wz_copy(p, i, zl).start()
        if unit == 0:
            y_copies[0].start()
            y_copies[1].start()

    def unit_row(j):
        return (j & 128) + ((j >> 2) & 3) * 32 + ((j >> 4) & 7) * 4 + (j & 3)

    r_i = lax.broadcasted_iota(jnp.int32, (256, 256), 0)
    c_i = lax.broadcasted_iota(jnp.int32, (256, 256), 1)
    perm[...] = (unit_row(r_i) == c_i).astype(BF)
    perm_t[...] = (unit_row(c_i) == r_i).astype(BF)
    lane = lax.broadcasted_iota(jnp.int32, (1, 256), 1)

    def clip_of(f, found):
        return jnp.where((lane >> 2) == f, clip_ref[f], found)

    key = lax.fori_loop(0, 64, clip_of, jnp.zeros((1, 256), jnp.int32)) * 4 + (lane & 3)
    key = jnp.broadcast_to(key.astype(F32), (256, 256))
    mask[...] = jnp.where(key == key.T, 0.0, -1e30).astype(F32)

    def project_part(b, pz, part):
        k, n = batches[b]
        kk = (pz + hz) % 2
        slot = kk * 2 + (1 - kk) * zl
        x = xg[k:k + n].reshape(n * 128, 3072)
        out = dot(x, wbuf[pz, part].reshape(3072, 256)).astype(BF)
        qkv[slot, part, k:k + n] = out.reshape(n, 128, 256)

    def zcopy(b, part, slot):
        k, n = batches[b]
        units = pl.ds(k, n)
        return rcopy(qkv.at[2, part, units], qkv.at[slot, part, units], z_send.at[b, part],
                     z_recv.at[b, part], (tm, partner_row))

    def project(b):
        @pl.loop(0, 3)
        def _(part):
            project_part(b, 1 - hz, part)
            zcopy(b, part, zl).start()

        @pl.loop(0, 3)
        def _(part):
            project_part(b, hz, part)

    def stage_part(b, zz, part):
        k, n = batches[b]
        rows = qkv[zz, part, k:k + n].reshape(n * 128, 256)
        moved = dot(perm[:n * 128, :n * 128], rows).astype(BF).reshape(n, 8, 16, 256)
        tsend[k:k + n, part, pl.ds(zz * 8, 8)] = moved

    def send_time(b, zz):
        k, n = batches[b]
        units = pl.ds(k, n)
        for dx in (1, 3, 2, 0):
            for dz in (1, 0):
                t = xs[dx] * 4 + zs[dz] * 2 + zz
                at = zz * 8 + xs[dx] * 2 + zs[dz]

                def send(t=t, at=at, dz=dz):
                    rcopy(tsend.at[units, :, at], trecv.at[units, :, tm], t_send.at[b], t_recv.at[b],
                          (t, rows_of[dz])).start()

                def keep(at=at):
                    trecv[k:k + n, :, tm] = tsend[k:k + n, :, at]

                if (dx, dz) == (0, 0):
                    pl.when(zz != core)(send)
                    pl.when(zz == core)(keep)
                else:
                    send()

    def stage_own(b):
        @pl.loop(0, 3)
        def _(part):
            stage_part(b, zl, part)

        send_time(b, zl)

    def stage_partner(b):
        @pl.loop(0, 3)
        def _(part):
            zcopy(b, part, oz).wait_recv()
            stage_part(b, oz, part)

        send_time(b, oz)

    factor = LOG2E / math.sqrt(HD)

    def soften(s):
        p = jnp.exp2((s - jnp.max(s, axis=-1, keepdims=True)) * factor)
        return p, jnp.sum(p, axis=-1, keepdims=True)

    def temporal(b):
        k, n = batches[b]
        units = pl.ds(k, n)
        await_bytes(trecv.at[units, :, pl.ds(0, 15)], t_recv.at[b])
        for u in range(k, k + n):
            for h in range(2):
                cols = slice(h * HD, (h + 1) * HD)
                q, kk, v = (trecv[u, part, :, :, cols].reshape(256, HD) for part in range(3))
                p, total = soften(dot_nt(q, kk) + mask[...])
                o = dot(p.astype(BF), v) / total
                osend[u, :, :, cols] = o.astype(BF).reshape(16, 16, HD)
        orecv[k:k + n, me_at] = osend[k:k + n, tm]
        for o in offsets:
            dev, _ = peer(*o)
            rcopy(osend.at[units, dev[0]], orecv.at[units, me_at], o_send.at[b], o_recv.at[b], dev).start()

    def wait_back(b):
        k, n = batches[b]
        await_bytes(orecv.at[pl.ds(k, n), pl.ds(0, 15)], o_recv.at[b])

    def spatial(ka, kb):
        @pl.loop(0, 2)
        def _(pair):
            for f in range(2):
                rows = pl.ds(pl.multiple_of(pair * 64 + f * 32, 32), 32)
                for h in range(2):
                    cols = slice(h * HD, (h + 1) * HD)
                    q = jnp.concatenate(
                        [qkv[0:2, 0, k:k + 2, rows, cols].reshape(128, HD) for k in (ka, kb)], axis=0)
                    kk, v = (qkv[0:2, part, :, rows, cols].reshape(512, HD) for part in (1, 2))
                    p, total = soften(dot_nt(q, kk))
                    o = (dot(p.astype(BF), v) / total).reshape(2, 2, 2, 32, HD)
                    sp[:, ka:ka + 2, rows, cols] = o[0]
                    sp[:, kb:kb + 2, rows, cols] = o[1]

    def ccopy(u, r, at, kept):
        half = half_of[u]
        return rcopy(csend.at[u, r % 2], comb.at[kept, half], c_send.at[u, r % 2], c_recv.at[at, half],
                     (tm, r))

    def combine(u):
        for zz in range(2):
            back = dot(perm_t[:128, :128], orecv[u, zz * 8:(zz + 1) * 8].reshape(128, 256))
            csend[u, zz] = (sp[zz, u] + back).astype(BF)
        if u < 2:
            ccopy(u, partner_row, row, y * 2 + hz).start()
            comb[y * 2 + hz, u] = csend[u, zl]
        else:
            for zz in range(2):
                ccopy(u, y_of[u] * 2 + zz, row, y * 2 + hz).start()

    def project_out(pair, first, last=True):
        for ys in pair:
            for i in range(2):
                r = ys * 2 + i
                for half in range(2):
                    def wait(r=r, half=half, ys=ys):
                        dst = comb.at[ys * 2 + (r + zh) % 2, half]
                        rcopy(csend.at[0, 0], dst, c_send.at[0, 0], c_recv.at[r, half], (tm, r)).wait_recv()
                    if ys is y:
                        pl.when(i != zl)(wait)
                    else:
                        wait()

        @pl.loop(0, 6)
        def _(n):
            cols = pl.ds(pl.multiple_of(n * 512, 512), 512)
            heads = [2 * ys + i for ys in pair for i in range(2)]
            left = jnp.concatenate([comb[h].reshape(256, 256) for h in heads], axis=1)
            right = jnp.concatenate([wo[h, :, cols] for h in heads], axis=0)
            acc = dot(left, right)
            for half in range(2):
                for f in range(4):
                    at = (half * 4 + f) * 32
                    rows = slice(half * 32, (half + 1) * 32)
                    piece = acc[at:at + 32]
                    if not first:
                        piece = piece + out_ref[f, rows, cols]
                    if not first and last:
                        clip = clip_ref[tm * 4 + f]
                        piece = piece * mod_ref[2, pl.ds(clip, 1), cols]
                    out_ref[f, rows, cols] = piece

    load_w.wait()
    for p in range(3):
        for i in range(2):
            wz_copy(p, i, oz).wait_recv()
            wx_copy(p, i, e_own).start()
        wc_copy(p, 0, e_own).start()
        project_part(0, zl, p)
    y_copies[2].start()
    y_copies[3].start()

    def pass_x(p):
        for i in range(2):
            wx_copy(p, i, e_x).wait_recv()
        wc_copy(p, 1, e_x).start()

    pass_x(0)
    pass_x(1)
    for p in range(3):
        for j in range(2):
            wc_copy(p, j, e_cores[j]).wait_recv()
        project_part(0, oz, p)
        zcopy(0, p, zl).start()
        if p == 0:
            pass_x(2)
    load_wo.start()
    for i in range(2):
        y_copies[i].wait_recv()
        y_copies[4 + i].start()
    stage_own(0)
    project(1)
    stage_own(1)
    stage_partner(0)

    for i in range(2):
        y_copies[2 + i].wait_recv()
        y_copies[6 + i].start()
    project(2)
    stage_own(2)
    stage_partner(1)

    y_copies[4].wait_recv()
    y_copies[5].wait_recv()
    project(3)
    stage_own(3)
    stage_partner(2)
    temporal(0)

    y_copies[6].wait_recv()
    y_copies[7].wait_recv()
    project(4)
    stage_own(4)
    stage_partner(3)
    temporal(1)
    stage_partner(4)

    spatial(2, 4)
    temporal(2)
    temporal(3)
    wait_back(1)
    combine(2)
    combine(3)
    temporal(4)
    spatial(6, 0)
    wait_back(2)
    combine(4)
    combine(5)
    wait_back(3)
    combine(6)
    wait_back(0)
    combine(0)
    combine(1)
    wait_back(4)
    combine(7)
    load_wo.wait()
    project_out((yp, ym), first=True)
    project_out((y,), first=False, last=False)
    project_out((yq,), first=False)

    for p in range(3):
        for i in range(2):
            wz_copy(p, i, zl).wait_send()
            wx_copy(p, i, e_own).wait_send()
            wc_copy(p, i, e_own).wait_send()
    for c in y_copies:
        c.wait_send()
    for b, (k, n) in enumerate(batches):
        for part in range(3):
            zcopy(b, part, zl).wait_send()
        await_bytes(tsend.at[pl.ds(k, n), :, pl.ds(0, 15)], t_send.at[b])
        await_bytes(osend.at[pl.ds(k, n), pl.ds(0, 15)], o_send.at[b])
    for u in range(8):
        if u < 2:
            ccopy(u, partner_row, row, y * 2 + hz).wait_send()
        else:
            for zz in range(2):
                ccopy(u, y_of[u] * 2 + zz, row, y * 2 + hz).wait_send()


def attention(clip_ids, stream, mod, weight, out_weight):
    vmem = pl.BlockSpec(memory_space=pltpu.VMEM)
    hbm = pl.BlockSpec(memory_space=pl.ANY)
    dma = pltpu.SemaphoreType.DMA
    return pl.pallas_call(
        attention_kernel,
        out_shape=pltpu.VMEM((4, 64, 3072), F32),
        in_specs=[pl.BlockSpec(memory_space=pltpu.SMEM), hbm, vmem, hbm, hbm],
        out_specs=vmem,
        scratch_shapes=[
            pltpu.VMEM((4, 64, 3072), F32),
            pltpu.VMEM((8, 128, 3072), BF),
            pltpu.VMEM((2, 3, 8, 384, 256), BF),
            pltpu.VMEM((8, 256, 3072), BF),
            pltpu.VMEM((3, 3, 8, 128, 256), BF),
            pltpu.VMEM((8, 3, 16, 16, 256), BF),
            pltpu.VMEM((8, 3, 16, 16, 256), BF),
            pltpu.VMEM((8, 16, 16, 256), BF),
            pltpu.VMEM((8, 16, 16, 256), BF),
            pltpu.VMEM((8, 2, 128, 256), BF),
            pltpu.VMEM((8, 2, 128, 256), BF),
            pltpu.VMEM((2, 8, 128, 256), F32),
            pltpu.VMEM((256, 256), BF),
            pltpu.VMEM((256, 256), BF),
            pltpu.VMEM((256, 256), F32),
            dma((4,)),
            dma((8,)), dma((8,)),
            dma((3, 2)), dma((3, 2)),
            dma((3, 2)), dma((3, 2)),
            dma((3, 2)), dma((3, 2)),
            dma((5, 3)), dma((5, 3)),
            dma((5,)), dma((5,)),
            dma((5,)), dma((5,)),
            dma((8, 2)), dma((8, 2)),
        ],
        compiler_params=pltpu.CompilerParams(
            collective_id=0, has_side_effects=True, vmem_limit_bytes=60 * 1024 * 1024
        ),
        name="attention",
    )(clip_ids, stream, mod, weight, out_weight)


def per_device(stream, clip_ids, modulation, qkv_weight, out_weight):
    mod = jnp.transpose(modulation, (1, 0, 2))
    weight = jnp.transpose(qkv_weight, (1, 0, 2)).reshape(3, 8, 384, 256)
    return attention(clip_ids, stream, mod, weight, out_weight.reshape(8, 256, 3072))


def solution(mesh):
    placed = (P("tm", "row", None), P(), P(), P(None, None, "row"), P())
    return jax.shard_map(
        per_device, mesh=mesh, in_specs=placed, out_specs=P("tm", "row", None), check_vma=False
    )
```

```python
import math

import jax
import jax.numpy as jnp
from jax import lax
from jax.experimental import pallas as pl
from jax.experimental.pallas import tpu as pltpu
from jax.sharding import PartitionSpec as P

HD = 128
MESH = pl.DeviceIdType.MESH
BF = jnp.bfloat16
F32 = jnp.float32
LOG2E = 1.4426950408889634


def dot(a, b):
    return jnp.dot(a, b, preferred_element_type=F32)


def dot_nt(a, b):
    return lax.dot_general(a, b, (((1,), (1,)), ((), ())), preferred_element_type=F32)


def attention_kernel(
    clip_ref, stream_hbm, mod_ref, w_hbm, wo_hbm, out_ref,
    stream_v, xg, wbuf, wo, qkv, tsend, trecv, osend, orecv, csend, comb, sp, perm, perm_t, mask,
    load_sem, y_send, y_recv, wz_send, wz_recv, wx_send, wx_recv, wc_send, wc_recv, z_send, z_recv,
    t_send, t_recv, o_send, o_recv, c_send, c_recv,
):
    batches = ((0, 2), (2, 2), (4, 2), (6, 1), (7, 1))
    sets = ((0, 2), (2, 2), (4, 3), (7, 1))
    tm = lax.axis_index("tm")
    row = lax.axis_index("row")
    zh = (tm // 2) % 2
    core = tm % 2
    y = row // 2
    zl = row % 2
    hz = (zl + zh) % 2
    oz = 1 - zl
    partner_row = y * 2 + oz
    outer_tm = tm + 2 - 4 * zh
    other_core = tm + 1 - 2 * core
    ym, yp, yq = (y + 3) % 4, (y + 1) % 4, (y + 2) % 4
    up, down = (tm, yp * 2 + zl), (tm, ym * 2 + zl)
    y_of = (y, y, ym, yp, ym, yp, yq, yq)
    half_of = (0, 1, 0, 0, 1, 1, 0, 1)

    def rcopy(src, dst, send, recv, dev):
        return pltpu.make_async_remote_copy(
            src_ref=src, dst_ref=dst, send_sem=send, recv_sem=recv,
            device_id=dev, device_id_type=MESH,
        )

    def await_bytes(ref, sem):
        pltpu.make_async_copy(ref, ref, sem).wait()

    x = tm // 4
    xs = [((x + d) % 4) for d in range(4)]
    zs = [zh, 1 - zh]
    cs = [core, 1 - core]
    rows_of = [y * 2 + (hz + zh) % 2, y * 2 + (hz + 1 - zh) % 2]
    offsets = [(dx, dz, dc) for dx in (1, 3, 2, 0) for dz in range(2) for dc in range(2)][:-4]
    offsets = offsets + [(0, 1, 0), (0, 1, 1), (0, 0, 1)]
    me_at = core * 8 + x * 2 + zh

    def peer(dx, dz, dc):
        t = xs[dx] * 4 + zs[dz] * 2 + cs[dc]
        return (t, rows_of[dz]), cs[dc] * 8 + xs[dx] * 2 + zs[dz]

    load_stream = [
        pltpu.make_async_copy(stream_hbm.at[:, pl.ds(32 * u, 32)], stream_v.at[:, pl.ds(32 * u, 32)],
                              load_sem.at[u])
        for u in range(2)
    ]
    load_w = pltpu.make_async_copy(w_hbm, wbuf.at[zl], load_sem.at[2])
    load_wo = pltpu.make_async_copy(wo_hbm, wo, load_sem.at[3])
    for c in load_stream:
        c.start()

    barrier = pltpu.get_barrier_semaphore()
    for o in offsets:
        pl.semaphore_signal(barrier, inc=1, device_id=peer(*o)[0], device_id_type=MESH)
    row_peers = [(tm, r * 2 + (zl if i == 0 else oz)) for r in (y, ym, yp, yq) for i in range(2)][1:]
    for dev in row_peers:
        pl.semaphore_signal(barrier, inc=1, device_id=dev, device_id_type=MESH)

    x_par = x % 2
    x_up, x_down = (tm + 4) % 16, (tm + 12) % 16
    e_own = core * 4 + x_par * 2
    e_x = core * 4 + (1 - x_par) * 2
    e_cores = ((1 - core) * 4 + x_par * 2, (1 - core) * 4 + (1 - x_par) * 2)

    def wz_copy(p, i, side):
        dev = ((tm, partner_row), (outer_tm, partner_row))[i]
        return rcopy(w_hbm.at[p, e_own + i], wbuf.at[side, p, e_own + i],
                     wz_send.at[p, i], wz_recv.at[p, i], dev)

    def wx_copy(p, i, e):
        dev = ((x_up, row), (x_down, row))[i]
        return rcopy(wbuf.at[oz, p, e + i], wbuf.at[oz, p, e + i],
                     wx_send.at[p, i], wx_recv.at[p, i], dev)

    def wc_copy(p, j, e):
        pair = wbuf.at[oz, p, pl.ds(e, 2)]
        return rcopy(pair, pair, wc_send.at[p, j], wc_recv.at[p, j], (other_core, row))


    def norm(unit):
        @pl.loop(0, 4)
        def _(f):
            clip = clip_ref[tm * 4 + f]
            shift = mod_ref[0, pl.ds(clip, 1), :]
            scale = 1.0 + mod_ref[1, pl.ds(clip, 1), :]
            v = stream_v[f, pl.ds(unit * 32, 32), :]
            centred = v - jnp.mean(v, axis=-1, keepdims=True)
            var = jnp.mean(centred * centred, axis=-1, keepdims=True)
            n = centred * lax.rsqrt(var + 1e-06) * scale + shift
            xg[unit, pl.ds(f * 32, 32), :] = n.astype(BF)

    def ycopy(i, src, dst, half, dev):
        if half is None:
            return rcopy(xg.at[src], xg.at[dst], y_send.at[i], y_recv.at[i], dev)
        rows = pl.ds(half * 64, 64)
        return rcopy(xg.at[src, rows], xg.at[dst, rows], y_send.at[i], y_recv.at[i], dev)

    y_copies = [
        ycopy(0, 0, 2, None, up), ycopy(1, 0, 3, None, down),
        ycopy(2, 1, 4, None, up), ycopy(3, 1, 5, None, down),
        ycopy(4, 2, 6, 0, up), ycopy(5, 3, 6, 1, down),
        ycopy(6, 4, 7, 0, up), ycopy(7, 5, 7, 1, down),
    ]
    for unit in range(2):
        load_stream[unit].wait()
        norm(unit)
        if unit == 0:
            pl.semaphore_wait(barrier, 22)
            load_w.start()
            for p in range(3):
                for i in range(2):
                    wz_copy(p, i, zl).start()
        y_copies[2 * unit].start()
        y_copies[2 * unit + 1].start()

    def unit_row(j):
        return (j & 128) + ((j >> 2) & 3) * 32 + ((j >> 4) & 7) * 4 + (j & 3)

    r_i = lax.broadcasted_iota(jnp.int32, (256, 256), 0)
    c_i = lax.broadcasted_iota(jnp.int32, (256, 256), 1)
    perm[...] = (unit_row(r_i) == c_i).astype(BF)
    perm_t[...] = (unit_row(c_i) == r_i).astype(BF)
    lane = lax.broadcasted_iota(jnp.int32, (1, 256), 1)

    def clip_of(f, found):
        return jnp.where((lane >> 2) == f, clip_ref[f], found)

    key = lax.fori_loop(0, 64, clip_of, jnp.zeros((1, 256), jnp.int32)) * 4 + (lane & 3)
    key = jnp.broadcast_to(key.astype(F32), (256, 256))
    mask[...] = jnp.where(key == key.T, 0.0, -1e30).astype(F32)

    def project_part(b, pz, part):
        k, n = batches[b]
        kk = (pz + hz) % 2
        slot = kk * 2 + (1 - kk) * zl
        x = xg[k:k + n].reshape(n * 128, 3072)
        out = dot(x, wbuf[pz, part].reshape(3072, 256)).astype(BF)
        qkv[slot, part, k:k + n] = out.reshape(n, 128, 256)

    def zcopy(b, part, slot):
        k, n = batches[b]
        units = pl.ds(k, n)
        return rcopy(qkv.at[2, part, units], qkv.at[slot, part, units], z_send.at[b, part],
                     z_recv.at[b, part], (tm, partner_row))

    def project_sent(b):
        @pl.loop(0, 3)
        def _(part):
            project_part(b, 1 - hz, part)
            zcopy(b, part, zl).start()

    def project(b):
        project_sent(b)

        @pl.loop(0, 3)
        def _(part):
            project_part(b, hz, part)

    def stage_part(b, zz, part):
        k, n = batches[b]
        rows = qkv[zz, part, k:k + n].reshape(n * 128, 256)
        moved = dot(perm[:n * 128, :n * 128], rows).astype(BF).reshape(n, 8, 16, 256)
        tsend[k:k + n, part, pl.ds(zz * 8, 8)] = moved

    def send_time(b, zz):
        k, n = batches[b]
        units = pl.ds(k, n)
        for dx in (1, 3, 2, 0):
            for dz in (1, 0):
                t = xs[dx] * 4 + zs[dz] * 2 + zz
                at = zz * 8 + xs[dx] * 2 + zs[dz]

                def send(t=t, at=at, dz=dz):
                    rcopy(tsend.at[units, :, at], trecv.at[units, :, tm], t_send.at[b], t_recv.at[b],
                          (t, rows_of[dz])).start()

                def keep(at=at):
                    trecv[k:k + n, :, tm] = tsend[k:k + n, :, at]

                if (dx, dz) == (0, 0):
                    pl.when(zz != core)(send)
                    pl.when(zz == core)(keep)
                else:
                    send()

    def stage_own(b):
        @pl.loop(0, 3)
        def _(part):
            stage_part(b, zl, part)

        send_time(b, zl)

    def stage_partner(b):
        @pl.loop(0, 3)
        def _(part):
            zcopy(b, part, oz).wait_recv()
            stage_part(b, oz, part)

        send_time(b, oz)

    factor = LOG2E / math.sqrt(HD)

    def soften(s):
        p = jnp.exp2((s - jnp.max(s, axis=-1, keepdims=True)) * factor)
        return p, jnp.sum(p, axis=-1, keepdims=True)

    def wait_time(b):
        k, n = batches[b]
        await_bytes(trecv.at[pl.ds(k, n), :, pl.ds(0, 15)], t_recv.at[b])

    def temporal_head(u, h):
        cols = slice(h * HD, (h + 1) * HD)
        q, kk, v = (trecv[u, part, :, :, cols].reshape(256, HD) for part in range(3))
        p, total = soften(dot_nt(q, kk) + mask[...])
        o = dot(p.astype(BF), v) / total
        osend[u, :, :, cols] = o.astype(BF).reshape(16, 16, HD)

    def temporal(b):
        k, n = batches[b]
        wait_time(b)
        for u in range(k, k + n):
            for h in range(2):
                temporal_head(u, h)

    def send_back(s):
        k, n = sets[s]
        units = pl.ds(k, n)
        orecv[k:k + n, me_at] = osend[k:k + n, tm]
        for o in offsets:
            dev, _ = peer(*o)
            rcopy(osend.at[units, dev[0]], orecv.at[units, me_at], o_send.at[s], o_recv.at[s], dev).start()

    def wait_back(s):
        k, n = sets[s]
        await_bytes(orecv.at[pl.ds(k, n), pl.ds(0, 15)], o_recv.at[s])

    def spatial(ka, kb):
        @pl.loop(0, 2)
        def _(pair):
            for f in range(2):
                rows = pl.ds(pl.multiple_of(pair * 64 + f * 32, 32), 32)
                for h in range(2):
                    cols = slice(h * HD, (h + 1) * HD)
                    q = jnp.concatenate(
                        [qkv[0:2, 0, k:k + 2, rows, cols].reshape(128, HD) for k in (ka, kb)], axis=0)
                    kk, v = (qkv[0:2, part, :, rows, cols].reshape(512, HD) for part in (1, 2))
                    p, total = soften(dot_nt(q, kk))
                    o = (dot(p.astype(BF), v) / total).reshape(2, 2, 2, 32, HD)
                    sp[:, ka:ka + 2, rows, cols] = o[0]
                    sp[:, kb:kb + 2, rows, cols] = o[1]

    def ccopy(u, r, at, kept):
        half = half_of[u]
        return rcopy(csend.at[u, r % 2], comb.at[kept, half], c_send.at[u, r % 2], c_recv.at[at, half],
                     (tm, r))

    def combine(*units):
        for u in units:
            for zz in range(2):
                back = dot(perm_t[:128, :128], orecv[u, zz * 8:(zz + 1) * 8].reshape(128, 256))
                csend[u, zz] = (sp[zz, u] + back).astype(BF)
        for u in units:
            if u < 2:
                ccopy(u, partner_row, row, y * 2 + hz).start()
                comb[y * 2 + hz, u] = csend[u, zl]
            else:
                for zz in range(2):
                    ccopy(u, y_of[u] * 2 + zz, row, y * 2 + hz).start()

    def project_out(pair, first, last=True):
        for ys in pair:
            for i in range(2):
                r = ys * 2 + i
                for half in range(2):
                    def wait(r=r, half=half, ys=ys):
                        dst = comb.at[ys * 2 + (r + zh) % 2, half]
                        rcopy(csend.at[0, 0], dst, c_send.at[0, 0], c_recv.at[r, half], (tm, r)).wait_recv()
                    if ys is y:
                        pl.when(i != zl)(wait)
                    else:
                        wait()

        @pl.loop(0, 3)
        def _(n):
            cols = pl.ds(pl.multiple_of(n * 1024, 1024), 1024)
            heads = [2 * ys + i for ys in pair for i in range(2)]
            left = jnp.concatenate([comb[h].reshape(256, 256) for h in heads], axis=1)
            right = jnp.concatenate([wo[h, :, cols] for h in heads], axis=0)
            acc = dot(left, right)
            for half in range(2):
                for f in range(4):
                    at = (half * 4 + f) * 32
                    rows = slice(half * 32, (half + 1) * 32)
                    piece = acc[at:at + 32]
                    if not first:
                        piece = piece + out_ref[f, rows, cols]
                    if not first and last:
                        clip = clip_ref[tm * 4 + f]
                        piece = piece * mod_ref[2, pl.ds(clip, 1), cols]
                    out_ref[f, rows, cols] = piece

    load_w.wait()
    for p in range(3):
        for i in range(2):
            wz_copy(p, i, oz).wait_recv()
            wx_copy(p, i, e_own).start()
        wc_copy(p, 0, e_own).start()
        project_part(0, zl, p)
    def pass_x(p):
        for i in range(2):
            wx_copy(p, i, e_x).wait_recv()
        wc_copy(p, 1, e_x).start()

    pass_x(0)
    pass_x(1)
    for p in range(3):
        for j in range(2):
            wc_copy(p, j, e_cores[j]).wait_recv()
        project_part(0, oz, p)
        zcopy(0, p, zl).start()
        if p == 0:
            pass_x(2)
    load_wo.start()
    for i in range(2):
        y_copies[i].wait_recv()
        y_copies[4 + i].start()
    stage_own(0)
    project(1)
    stage_own(1)
    stage_partner(0)

    for i in range(2):
        y_copies[2 + i].wait_recv()
        y_copies[6 + i].start()
    project(2)
    stage_own(2)
    stage_partner(1)
    temporal(0)
    send_back(0)

    y_copies[4].wait_recv()
    y_copies[5].wait_recv()
    project(3)
    stage_own(3)
    stage_partner(2)
    temporal(1)
    send_back(1)
    stage_partner(3)

    y_copies[6].wait_recv()
    y_copies[7].wait_recv()
    project_sent(4)
    wait_time(2)
    temporal_head(4, 0)
    project_part(4, hz, 0)
    temporal_head(4, 1)
    project_part(4, hz, 1)
    temporal_head(5, 0)
    project_part(4, hz, 2)
    temporal_head(5, 1)
    stage_own(4)
    temporal(3)
    send_back(2)
    stage_partner(4)

    spatial(2, 4)
    wait_back(1)
    combine(2, 3)
    temporal(4)
    send_back(3)
    wait_back(2)
    combine(4, 5)
    spatial(6, 0)
    wait_back(0)
    combine(6, 0, 1)
    wait_back(3)
    combine(7)
    load_wo.wait()
    project_out((yp, ym), first=True)
    project_out((y,), first=False, last=False)
    project_out((yq,), first=False)

    for p in range(3):
        for i in range(2):
            wz_copy(p, i, zl).wait_send()
            wx_copy(p, i, e_own).wait_send()
            wc_copy(p, i, e_own).wait_send()
    for c in y_copies:
        c.wait_send()
    for b, (k, n) in enumerate(batches):
        for part in range(3):
            zcopy(b, part, zl).wait_send()
        await_bytes(tsend.at[pl.ds(k, n), :, pl.ds(0, 15)], t_send.at[b])
    for s, (k, n) in enumerate(sets):
        await_bytes(osend.at[pl.ds(k, n), pl.ds(0, 15)], o_send.at[s])
    for u in range(8):
        if u < 2:
            ccopy(u, partner_row, row, y * 2 + hz).wait_send()
        else:
            for zz in range(2):
                ccopy(u, y_of[u] * 2 + zz, row, y * 2 + hz).wait_send()


def attention(clip_ids, stream, mod, weight, out_weight):
    vmem = pl.BlockSpec(memory_space=pltpu.VMEM)
    hbm = pl.BlockSpec(memory_space=pl.ANY)
    dma = pltpu.SemaphoreType.DMA
    return pl.pallas_call(
        attention_kernel,
        out_shape=pltpu.VMEM((4, 64, 3072), F32),
        in_specs=[pl.BlockSpec(memory_space=pltpu.SMEM), hbm, vmem, hbm, hbm],
        out_specs=vmem,
        scratch_shapes=[
            pltpu.VMEM((4, 64, 3072), F32),
            pltpu.VMEM((8, 128, 3072), BF),
            pltpu.VMEM((2, 3, 8, 384, 256), BF),
            pltpu.VMEM((8, 256, 3072), BF),
            pltpu.VMEM((3, 3, 8, 128, 256), BF),
            pltpu.VMEM((8, 3, 16, 16, 256), BF),
            pltpu.VMEM((8, 3, 16, 16, 256), BF),
            pltpu.VMEM((8, 16, 16, 256), BF),
            pltpu.VMEM((8, 16, 16, 256), BF),
            pltpu.VMEM((8, 2, 128, 256), BF),
            pltpu.VMEM((8, 2, 128, 256), BF),
            pltpu.VMEM((2, 8, 128, 256), F32),
            pltpu.VMEM((256, 256), BF),
            pltpu.VMEM((256, 256), BF),
            pltpu.VMEM((256, 256), F32),
            dma((4,)),
            dma((8,)), dma((8,)),
            dma((3, 2)), dma((3, 2)),
            dma((3, 2)), dma((3, 2)),
            dma((3, 2)), dma((3, 2)),
            dma((5, 3)), dma((5, 3)),
            dma((5,)), dma((5,)),
            dma((4,)), dma((4,)),
            dma((8, 2)), dma((8, 2)),
        ],
        compiler_params=pltpu.CompilerParams(
            collective_id=0, has_side_effects=True, vmem_limit_bytes=60 * 1024 * 1024
        ),
        name="attention",
    )(clip_ids, stream, mod, weight, out_weight)


def per_device(stream, clip_ids, modulation, qkv_weight, out_weight):
    mod = jnp.transpose(modulation, (1, 0, 2))
    weight = jnp.transpose(qkv_weight, (1, 0, 2)).reshape(3, 8, 384, 256)
    return attention(clip_ids, stream, mod, weight, out_weight.reshape(8, 256, 3072))


def solution(mesh):
    placed = (P("tm", "row", None), P(), P(), P(None, None, "row"), P())
    return jax.shard_map(
        per_device, mesh=mesh, in_specs=placed, out_specs=P("tm", "row", None), check_vma=False
    )
```

```python
import math

import jax
import jax.numpy as jnp
from jax import lax
from jax.experimental import pallas as pl
from jax.experimental.pallas import tpu as pltpu
from jax.sharding import PartitionSpec as P

HD = 128
MESH = pl.DeviceIdType.MESH
BF = jnp.bfloat16
F32 = jnp.float32
LOG2E = 1.4426950408889634


def dot(a, b):
    return jnp.dot(a, b, preferred_element_type=F32)


def dot_nt(a, b):
    return lax.dot_general(a, b, (((1,), (1,)), ((), ())), preferred_element_type=F32)


def attention_kernel(
    clip_ref, stream_hbm, mod_ref, w_hbm, wo_hbm, out_ref,
    stream_v, xg, wbuf, wo, qkv, tsend, trecv, osend, orecv, csend, comb, sp, perm, perm_t, mask,
    load_sem, y_send, y_recv, wz_send, wz_recv, wx_send, wx_recv, wc_send, wc_recv, z_send, z_recv,
    t_send, t_recv, o_send, o_recv, c_send, c_recv,
):
    batches = ((0, 2), (2, 2), (4, 2), (6, 2))
    tm = lax.axis_index("tm")
    row = lax.axis_index("row")
    zh = (tm // 2) % 2
    core = tm % 2
    y = row // 2
    zl = row % 2
    hz = (zl + zh) % 2
    oz = 1 - zl
    partner_row = y * 2 + oz
    outer_tm = tm + 2 - 4 * zh
    other_core = tm + 1 - 2 * core
    ym, yp, yq = (y + 3) % 4, (y + 1) % 4, (y + 2) % 4
    up, down = (tm, yp * 2 + zl), (tm, ym * 2 + zl)
    y_of = (y, y, ym, yp, ym, yp, yq, yq)
    half_of = (0, 1, 0, 0, 1, 1, 0, 1)

    def rcopy(src, dst, send, recv, dev):
        return pltpu.make_async_remote_copy(
            src_ref=src, dst_ref=dst, send_sem=send, recv_sem=recv,
            device_id=dev, device_id_type=MESH,
        )

    def await_bytes(ref, sem):
        pltpu.make_async_copy(ref, ref, sem).wait()

    x = tm // 4
    xs = [((x + d) % 4) for d in range(4)]
    zs = [zh, 1 - zh]
    cs = [core, 1 - core]
    rows_of = [y * 2 + (hz + zh) % 2, y * 2 + (hz + 1 - zh) % 2]
    offsets = [(dx, dz, dc) for dx in (1, 3, 2, 0) for dz in range(2) for dc in range(2)][:-4]
    offsets = offsets + [(0, 1, 0), (0, 1, 1), (0, 0, 1)]
    me_at = core * 8 + x * 2 + zh

    def peer(dx, dz, dc):
        t = xs[dx] * 4 + zs[dz] * 2 + cs[dc]
        return (t, rows_of[dz]), cs[dc] * 8 + xs[dx] * 2 + zs[dz]

    load_stream = [
        pltpu.make_async_copy(stream_hbm.at[:, pl.ds(32 * u, 32)], stream_v.at[:, pl.ds(32 * u, 32)],
                              load_sem.at[u])
        for u in range(2)
    ]
    load_w = pltpu.make_async_copy(w_hbm, wbuf.at[zl], load_sem.at[2])
    load_wo = pltpu.make_async_copy(wo_hbm, wo, load_sem.at[3])
    for c in load_stream:
        c.start()

    barrier = pltpu.get_barrier_semaphore()
    for o in offsets:
        pl.semaphore_signal(barrier, inc=1, device_id=peer(*o)[0], device_id_type=MESH)
    row_peers = [(tm, r * 2 + (zl if i == 0 else oz)) for r in (y, ym, yp, yq) for i in range(2)][1:]
    for dev in row_peers:
        pl.semaphore_signal(barrier, inc=1, device_id=dev, device_id_type=MESH)

    x_par = x % 2
    x_up, x_down = (tm + 4) % 16, (tm + 12) % 16
    e_own = core * 4 + x_par * 2
    e_x = core * 4 + (1 - x_par) * 2
    e_cores = ((1 - core) * 4 + x_par * 2, (1 - core) * 4 + (1 - x_par) * 2)

    def wz_copy(p, i, side):
        dev = ((tm, partner_row), (outer_tm, partner_row))[i]
        return rcopy(w_hbm.at[p, e_own + i], wbuf.at[side, p, e_own + i],
                     wz_send.at[p, i], wz_recv.at[p, i], dev)

    def wx_copy(p, i, e):
        dev = ((x_up, row), (x_down, row))[i]
        return rcopy(wbuf.at[oz, p, e + i], wbuf.at[oz, p, e + i],
                     wx_send.at[p, i], wx_recv.at[p, i], dev)

    def wc_copy(p, j, e):
        pair = wbuf.at[oz, p, pl.ds(e, 2)]
        return rcopy(pair, pair, wc_send.at[p, j], wc_recv.at[p, j], (other_core, row))


    def norm(unit):
        @pl.loop(0, 4)
        def _(f):
            clip = clip_ref[tm * 4 + f]
            shift = mod_ref[0, pl.ds(clip, 1), :]
            scale = 1.0 + mod_ref[1, pl.ds(clip, 1), :]
            v = stream_v[f, pl.ds(unit * 32, 32), :]
            centred = v - jnp.mean(v, axis=-1, keepdims=True)
            var = jnp.mean(centred * centred, axis=-1, keepdims=True)
            n = centred * lax.rsqrt(var + 1e-06) * scale + shift
            xg[unit, pl.ds(f * 32, 32), :] = n.astype(BF)

    def ycopy(i, src, dst, half, dev):
        if half is None:
            return rcopy(xg.at[src], xg.at[dst], y_send.at[i], y_recv.at[i], dev)
        rows = pl.ds(half * 64, 64)
        return rcopy(xg.at[src, rows], xg.at[dst, rows], y_send.at[i], y_recv.at[i], dev)

    y_copies = [
        ycopy(0, 0, 2, None, up), ycopy(1, 0, 3, None, down),
        ycopy(2, 1, 4, None, up), ycopy(3, 1, 5, None, down),
        ycopy(4, 2, 6, 0, up), ycopy(5, 3, 6, 1, down),
        ycopy(6, 4, 7, 0, up), ycopy(7, 5, 7, 1, down),
    ]
    for unit in range(2):
        load_stream[unit].wait()
        norm(unit)
        if unit == 0:
            pl.semaphore_wait(barrier, 22)
            load_w.start()
            for p in range(3):
                for i in range(2):
                    wz_copy(p, i, zl).start()
        y_copies[2 * unit].start()
        y_copies[2 * unit + 1].start()

    def unit_row(j):
        return (j & 128) + ((j >> 2) & 3) * 32 + ((j >> 4) & 7) * 4 + (j & 3)

    r_i = lax.broadcasted_iota(jnp.int32, (256, 256), 0)
    c_i = lax.broadcasted_iota(jnp.int32, (256, 256), 1)
    perm[...] = (unit_row(r_i) == c_i).astype(BF)
    perm_t[...] = (unit_row(c_i) == r_i).astype(BF)
    lane = lax.broadcasted_iota(jnp.int32, (1, 256), 1)

    def clip_of(f, found):
        return jnp.where((lane >> 2) == f, clip_ref[f], found)

    key = lax.fori_loop(0, 64, clip_of, jnp.zeros((1, 256), jnp.int32)) * 4 + (lane & 3)
    key = jnp.broadcast_to(key.astype(F32), (256, 256))
    mask[...] = jnp.where(key == key.T, 0.0, -1e30).astype(F32)

    def project_part(b, pz, part):
        k, n = batches[b]
        kk = (pz + hz) % 2
        slot = kk * 2 + (1 - kk) * zl
        x = xg[k:k + n].reshape(n * 128, 3072)
        out = dot(x, wbuf[pz, part].reshape(3072, 256)).astype(BF)
        qkv[slot, part, k:k + n] = out.reshape(n, 128, 256)

    def zcopy(b, part, slot):
        k, n = batches[b]
        units = pl.ds(k, n)
        return rcopy(qkv.at[2, part, units], qkv.at[slot, part, units], z_send.at[b, part],
                     z_recv.at[b, part], (tm, partner_row))

    def project(b):
        @pl.loop(0, 3)
        def _(part):
            project_part(b, 1 - hz, part)
            zcopy(b, part, zl).start()

        @pl.loop(0, 3)
        def _(part):
            project_part(b, hz, part)

    def stage_part(b, zz, part):
        k, n = batches[b]
        rows = qkv[zz, part, k:k + n].reshape(n * 128, 256)
        moved = dot(perm[:n * 128, :n * 128], rows).astype(BF).reshape(n, 8, 16, 256)
        tsend[k:k + n, part, pl.ds(zz * 8, 8)] = moved

    def send_time(b, zz):
        k, n = batches[b]
        units = pl.ds(k, n)
        for dx in (1, 3, 2, 0):
            for dz in (1, 0):
                t = xs[dx] * 4 + zs[dz] * 2 + zz
                at = zz * 8 + xs[dx] * 2 + zs[dz]

                def send(t=t, at=at, dz=dz):
                    rcopy(tsend.at[units, :, at], trecv.at[units, :, tm], t_send.at[b], t_recv.at[b],
                          (t, rows_of[dz])).start()

                def keep(at=at):
                    trecv[k:k + n, :, tm] = tsend[k:k + n, :, at]

                if (dx, dz) == (0, 0):
                    pl.when(zz != core)(send)
                    pl.when(zz == core)(keep)
                else:
                    send()

    def stage_own(b):
        @pl.loop(0, 3)
        def _(part):
            stage_part(b, zl, part)

        send_time(b, zl)

    def stage_partner(b):
        @pl.loop(0, 3)
        def _(part):
            zcopy(b, part, oz).wait_recv()
            stage_part(b, oz, part)

        send_time(b, oz)

    factor = LOG2E / math.sqrt(HD)

    def soften(s):
        p = jnp.exp2((s - jnp.max(s, axis=-1, keepdims=True)) * factor)
        return p, jnp.sum(p, axis=-1, keepdims=True)

    def temporal(b):
        k, n = batches[b]
        units = pl.ds(k, n)
        await_bytes(trecv.at[units, :, pl.ds(0, 15)], t_recv.at[b])
        for u in range(k, k + n):
            for h in range(2):
                cols = slice(h * HD, (h + 1) * HD)
                q, kk, v = (trecv[u, part, :, :, cols].reshape(256, HD) for part in range(3))
                p, total = soften(dot_nt(q, kk) + mask[...])
                o = dot(p.astype(BF), v) / total
                osend[u, :, :, cols] = o.astype(BF).reshape(16, 16, HD)
        orecv[k:k + n, me_at] = osend[k:k + n, tm]
        for o in offsets:
            dev, _ = peer(*o)
            rcopy(osend.at[units, dev[0]], orecv.at[units, me_at], o_send.at[b], o_recv.at[b], dev).start()

    def wait_back(b):
        k, n = batches[b]
        await_bytes(orecv.at[pl.ds(k, n), pl.ds(0, 15)], o_recv.at[b])

    def spatial(ka, kb):
        @pl.loop(0, 2)
        def _(pair):
            for f in range(2):
                rows = pl.ds(pl.multiple_of(pair * 64 + f * 32, 32), 32)
                for h in range(2):
                    cols = slice(h * HD, (h + 1) * HD)
                    q = jnp.concatenate(
                        [qkv[0:2, 0, k:k + 2, rows, cols].reshape(128, HD) for k in (ka, kb)], axis=0)
                    kk, v = (qkv[0:2, part, :, rows, cols].reshape(512, HD) for part in (1, 2))
                    p, total = soften(dot_nt(q, kk))
                    o = (dot(p.astype(BF), v) / total).reshape(2, 2, 2, 32, HD)
                    sp[:, ka:ka + 2, rows, cols] = o[0]
                    sp[:, kb:kb + 2, rows, cols] = o[1]

    def ccopy(u, r, at, kept):
        half = half_of[u]
        return rcopy(csend.at[u, r % 2], comb.at[kept, half], c_send.at[u, r % 2], c_recv.at[at, half],
                     (tm, r))

    def combine(u):
        back = dot(perm_t[...], orecv[u].reshape(256, 256)).reshape(2, 128, 256)
        csend[u] = (sp[:, u] + back).astype(BF)
        if u < 2:
            ccopy(u, partner_row, row, y * 2 + hz).start()
            comb[y * 2 + hz, u] = csend[u, zl]
        else:
            for zz in range(2):
                ccopy(u, y_of[u] * 2 + zz, row, y * 2 + hz).start()

    def project_out(pair, first, last=True):
        for ys in pair:
            for i in range(2):
                r = ys * 2 + i
                for half in range(2):
                    def wait(r=r, half=half, ys=ys):
                        dst = comb.at[ys * 2 + (r + zh) % 2, half]
                        rcopy(csend.at[0, 0], dst, c_send.at[0, 0], c_recv.at[r, half], (tm, r)).wait_recv()
                    if ys is y:
                        pl.when(i != zl)(wait)
                    else:
                        wait()

        @pl.loop(0, 6)
        def _(n):
            cols = pl.ds(pl.multiple_of(n * 512, 512), 512)
            heads = [2 * ys + i for ys in pair for i in range(2)]
            left = jnp.concatenate([comb[h].reshape(256, 256) for h in heads], axis=1)
            right = jnp.concatenate([wo[h, :, cols] for h in heads], axis=0)
            acc = dot(left, right)
            for half in range(2):
                for f in range(4):
                    at = (half * 4 + f) * 32
                    rows = slice(half * 32, (half + 1) * 32)
                    piece = acc[at:at + 32]
                    if not first:
                        piece = piece + out_ref[f, rows, cols]
                    if not first and last:
                        clip = clip_ref[tm * 4 + f]
                        piece = piece * mod_ref[2, pl.ds(clip, 1), cols]
                    out_ref[f, rows, cols] = piece

    load_w.wait()
    for p in range(3):
        for i in range(2):
            wz_copy(p, i, oz).wait_recv()
            wx_copy(p, i, e_own).start()
        wc_copy(p, 0, e_own).start()
        project_part(0, zl, p)
    def pass_x(p):
        for i in range(2):
            wx_copy(p, i, e_x).wait_recv()
        wc_copy(p, 1, e_x).start()

    pass_x(0)
    pass_x(1)
    for p in range(3):
        for j in range(2):
            wc_copy(p, j, e_cores[j]).wait_recv()
        project_part(0, oz, p)
        zcopy(0, p, zl).start()
        if p == 0:
            pass_x(2)
    load_wo.start()
    for i in range(2):
        y_copies[i].wait_recv()
        y_copies[4 + i].start()
    stage_own(0)
    project(1)
    stage_own(1)
    stage_partner(0)

    for i in range(2):
        y_copies[2 + i].wait_recv()
        y_copies[6 + i].start()
    project(2)
    stage_own(2)
    stage_partner(1)
    temporal(0)
    stage_partner(2)
    temporal(1)

    for i in range(4):
        y_copies[4 + i].wait_recv()
    project(3)
    stage_own(3)
    temporal(2)
    stage_partner(3)

    spatial(2, 4)
    wait_back(1)
    combine(2)
    combine(3)
    wait_back(2)
    combine(4)
    combine(5)
    temporal(3)
    spatial(6, 0)
    wait_back(0)
    combine(0)
    combine(1)
    wait_back(3)
    combine(6)
    combine(7)
    load_wo.wait()
    project_out((yp, ym), first=True)
    project_out((y,), first=False, last=False)
    project_out((yq,), first=False)

    for p in range(3):
        for i in range(2):
            wz_copy(p, i, zl).wait_send()
            wx_copy(p, i, e_own).wait_send()
            wc_copy(p, i, e_own).wait_send()
    for c in y_copies:
        c.wait_send()
    for b, (k, n) in enumerate(batches):
        for part in range(3):
            zcopy(b, part, zl).wait_send()
        await_bytes(tsend.at[pl.ds(k, n), :, pl.ds(0, 15)], t_send.at[b])
        await_bytes(osend.at[pl.ds(k, n), pl.ds(0, 15)], o_send.at[b])
    for u in range(8):
        if u < 2:
            ccopy(u, partner_row, row, y * 2 + hz).wait_send()
        else:
            for zz in range(2):
                ccopy(u, y_of[u] * 2 + zz, row, y * 2 + hz).wait_send()


def attention(clip_ids, stream, mod, weight, out_weight):
    vmem = pl.BlockSpec(memory_space=pltpu.VMEM)
    hbm = pl.BlockSpec(memory_space=pl.ANY)
    dma = pltpu.SemaphoreType.DMA
    return pl.pallas_call(
        attention_kernel,
        out_shape=pltpu.VMEM((4, 64, 3072), F32),
        in_specs=[pl.BlockSpec(memory_space=pltpu.SMEM), hbm, vmem, hbm, hbm],
        out_specs=vmem,
        scratch_shapes=[
            pltpu.VMEM((4, 64, 3072), F32),
            pltpu.VMEM((8, 128, 3072), BF),
            pltpu.VMEM((2, 3, 8, 384, 256), BF),
            pltpu.VMEM((8, 256, 3072), BF),
            pltpu.VMEM((3, 3, 8, 128, 256), BF),
            pltpu.VMEM((8, 3, 16, 16, 256), BF),
            pltpu.VMEM((8, 3, 16, 16, 256), BF),
            pltpu.VMEM((8, 16, 16, 256), BF),
            pltpu.VMEM((8, 16, 16, 256), BF),
            pltpu.VMEM((8, 2, 128, 256), BF),
            pltpu.VMEM((8, 2, 128, 256), BF),
            pltpu.VMEM((2, 8, 128, 256), F32),
            pltpu.VMEM((256, 256), BF),
            pltpu.VMEM((256, 256), BF),
            pltpu.VMEM((256, 256), F32),
            dma((4,)),
            dma((8,)), dma((8,)),
            dma((3, 2)), dma((3, 2)),
            dma((3, 2)), dma((3, 2)),
            dma((3, 2)), dma((3, 2)),
            dma((4, 3)), dma((4, 3)),
            dma((4,)), dma((4,)),
            dma((4,)), dma((4,)),
            dma((8, 2)), dma((8, 2)),
        ],
        compiler_params=pltpu.CompilerParams(
            collective_id=0, has_side_effects=True, vmem_limit_bytes=60 * 1024 * 1024
        ),
        name="attention",
    )(clip_ids, stream, mod, weight, out_weight)


def per_device(stream, clip_ids, modulation, qkv_weight, out_weight):
    mod = jnp.transpose(modulation, (1, 0, 2))
    weight = jnp.transpose(qkv_weight, (1, 0, 2)).reshape(3, 8, 384, 256)
    return attention(clip_ids, stream, mod, weight, out_weight.reshape(8, 256, 3072))


def solution(mesh):
    placed = (P("tm", "row", None), P(), P(), P(None, None, "row"), P())
    return jax.shard_map(
        per_device, mesh=mesh, in_specs=placed, out_specs=P("tm", "row", None), check_vma=False
    )
```

```python
import math

import jax
import jax.numpy as jnp
from jax import lax
from jax.experimental import pallas as pl
from jax.experimental.pallas import tpu as pltpu
from jax.sharding import PartitionSpec as P

HD = 128
MESH = pl.DeviceIdType.MESH
BF = jnp.bfloat16
F32 = jnp.float32
LOG2E = 1.4426950408889634


def dot(a, b):
    return jnp.dot(a, b, preferred_element_type=F32)


def dot_nt(a, b):
    return lax.dot_general(a, b, (((1,), (1,)), ((), ())), preferred_element_type=F32)


def attention_kernel(
    clip_ref, stream_hbm, mod_ref, w_hbm, wo_hbm, out_ref,
    stream_v, xg, wbuf, wo, qkv, tsend, trecv, osend, orecv, csend, comb, sp, perm, perm_t, mask,
    load_sem, y_send, y_recv, wz_send, wz_recv, wx_send, wx_recv, wc_send, wc_recv, z_send, z_recv,
    t_send, t_recv, o_send, o_recv, c_send, c_recv,
):
    batches = ((0, 2), (2, 2), (4, 2), (6, 1), (7, 1))
    tm = lax.axis_index("tm")
    row = lax.axis_index("row")
    zh = (tm // 2) % 2
    core = tm % 2
    y = row // 2
    zl = row % 2
    hz = (zl + zh) % 2
    oz = 1 - zl
    partner_row = y * 2 + oz
    outer_tm = tm + 2 - 4 * zh
    other_core = tm + 1 - 2 * core
    ym, yp, yq = (y + 3) % 4, (y + 1) % 4, (y + 2) % 4
    up, down = (tm, yp * 2 + zl), (tm, ym * 2 + zl)
    y_of = (y, y, ym, yp, ym, yp, yq, yq)
    half_of = (0, 1, 0, 0, 1, 1, 0, 1)

    def rcopy(src, dst, send, recv, dev):
        return pltpu.make_async_remote_copy(
            src_ref=src, dst_ref=dst, send_sem=send, recv_sem=recv,
            device_id=dev, device_id_type=MESH,
        )

    def await_bytes(ref, sem):
        pltpu.make_async_copy(ref, ref, sem).wait()

    x = tm // 4
    xs = [((x + d) % 4) for d in range(4)]
    zs = [zh, 1 - zh]
    cs = [core, 1 - core]
    rows_of = [y * 2 + (hz + zh) % 2, y * 2 + (hz + 1 - zh) % 2]
    offsets = [(dx, dz, dc) for dx in (1, 3, 2, 0) for dz in range(2) for dc in range(2)][:-4]
    offsets = offsets + [(0, 1, 0), (0, 1, 1), (0, 0, 1)]
    me_at = core * 8 + x * 2 + zh

    def peer(dx, dz, dc):
        t = xs[dx] * 4 + zs[dz] * 2 + cs[dc]
        return (t, rows_of[dz]), cs[dc] * 8 + xs[dx] * 2 + zs[dz]

    load_stream = [
        pltpu.make_async_copy(stream_hbm.at[:, pl.ds(32 * u, 32)], stream_v.at[:, pl.ds(32 * u, 32)],
                              load_sem.at[u])
        for u in range(2)
    ]
    load_w = pltpu.make_async_copy(w_hbm, wbuf.at[zl], load_sem.at[2])
    load_wo = pltpu.make_async_copy(wo_hbm, wo, load_sem.at[3])
    for c in load_stream:
        c.start()

    barrier = pltpu.get_barrier_semaphore()
    for o in offsets:
        pl.semaphore_signal(barrier, inc=1, device_id=peer(*o)[0], device_id_type=MESH)
    row_peers = [(tm, r * 2 + (zl if i == 0 else oz)) for r in (y, ym, yp, yq) for i in range(2)][1:]
    for dev in row_peers:
        pl.semaphore_signal(barrier, inc=1, device_id=dev, device_id_type=MESH)

    x_par = x % 2
    x_up, x_down = (tm + 4) % 16, (tm + 12) % 16
    e_own = core * 4 + x_par * 2
    e_x = core * 4 + (1 - x_par) * 2
    e_cores = ((1 - core) * 4 + x_par * 2, (1 - core) * 4 + (1 - x_par) * 2)

    def wz_copy(p, i, side):
        dev = ((tm, partner_row), (outer_tm, partner_row))[i]
        return rcopy(w_hbm.at[p, e_own + i], wbuf.at[side, p, e_own + i],
                     wz_send.at[p, i], wz_recv.at[p, i], dev)

    def wx_copy(p, i, e):
        dev = ((x_up, row), (x_down, row))[i]
        return rcopy(wbuf.at[oz, p, e + i], wbuf.at[oz, p, e + i],
                     wx_send.at[p, i], wx_recv.at[p, i], dev)

    def wc_copy(p, j, e):
        pair = wbuf.at[oz, p, pl.ds(e, 2)]
        return rcopy(pair, pair, wc_send.at[p, j], wc_recv.at[p, j], (other_core, row))


    def norm(unit):
        @pl.loop(0, 4)
        def _(f):
            clip = clip_ref[tm * 4 + f]
            shift = mod_ref[0, pl.ds(clip, 1), :]
            scale = 1.0 + mod_ref[1, pl.ds(clip, 1), :]
            v = stream_v[f, pl.ds(unit * 32, 32), :]
            centred = v - jnp.mean(v, axis=-1, keepdims=True)
            var = jnp.mean(centred * centred, axis=-1, keepdims=True)
            n = centred * lax.rsqrt(var + 1e-06) * scale + shift
            xg[unit, pl.ds(f * 32, 32), :] = n.astype(BF)

    def ycopy(i, src, dst, half, dev):
        if half is None:
            return rcopy(xg.at[src], xg.at[dst], y_send.at[i], y_recv.at[i], dev)
        rows = pl.ds(half * 64, 64)
        return rcopy(xg.at[src, rows], xg.at[dst, rows], y_send.at[i], y_recv.at[i], dev)

    y_copies = [
        ycopy(0, 0, 2, None, up), ycopy(1, 0, 3, None, down),
        ycopy(2, 1, 4, None, up), ycopy(3, 1, 5, None, down),
        ycopy(4, 2, 6, 0, up), ycopy(5, 3, 6, 1, down),
        ycopy(6, 4, 7, 0, up), ycopy(7, 5, 7, 1, down),
    ]
    for unit in range(2):
        load_stream[unit].wait()
        norm(unit)
        if unit == 0:
            pl.semaphore_wait(barrier, 22)
            load_w.start()
            for p in range(3):
                for i in range(2):
                    wz_copy(p, i, zl).start()
        y_copies[2 * unit].start()
        y_copies[2 * unit + 1].start()

    def unit_row(j):
        return (j & 128) + ((j >> 2) & 3) * 32 + ((j >> 4) & 7) * 4 + (j & 3)

    r_i = lax.broadcasted_iota(jnp.int32, (256, 256), 0)
    c_i = lax.broadcasted_iota(jnp.int32, (256, 256), 1)
    perm[...] = (unit_row(r_i) == c_i).astype(BF)
    perm_t[...] = (unit_row(c_i) == r_i).astype(BF)
    lane = lax.broadcasted_iota(jnp.int32, (1, 256), 1)

    def clip_of(f, found):
        return jnp.where((lane >> 2) == f, clip_ref[f], found)

    key = lax.fori_loop(0, 64, clip_of, jnp.zeros((1, 256), jnp.int32)) * 4 + (lane & 3)
    key = jnp.broadcast_to(key.astype(F32), (256, 256))
    mask[...] = jnp.where(key == key.T, 0.0, -1e30).astype(F32)

    def project_part(b, pz, part):
        k, n = batches[b]
        kk = (pz + hz) % 2
        slot = kk * 2 + (1 - kk) * zl
        x = xg[k:k + n].reshape(n * 128, 3072)
        out = dot(x, wbuf[pz, part].reshape(3072, 256)).astype(BF)
        qkv[slot, part, k:k + n] = out.reshape(n, 128, 256)

    def zcopy(b, part, slot):
        k, n = batches[b]
        units = pl.ds(k, n)
        return rcopy(qkv.at[2, part, units], qkv.at[slot, part, units], z_send.at[b, part],
                     z_recv.at[b, part], (tm, partner_row))

    def project(b):
        @pl.loop(0, 3)
        def _(part):
            project_part(b, 1 - hz, part)
            zcopy(b, part, zl).start()

        @pl.loop(0, 3)
        def _(part):
            project_part(b, hz, part)

    def stage_part(b, zz, part):
        k, n = batches[b]
        rows = qkv[zz, part, k:k + n].reshape(n * 128, 256)
        moved = dot(perm[:n * 128, :n * 128], rows).astype(BF).reshape(n, 8, 16, 256)
        for i in range(n):
            tsend[pl.ds(zz * 8, 8), k + i, part] = moved[i]

    def send_time(b, zz):
        k, n = batches[b]
        units = pl.ds(k, n)
        for dx in (1, 3, 2, 0):
            for dz in (1, 0):
                t = xs[dx] * 4 + zs[dz] * 2 + zz
                at = zz * 8 + xs[dx] * 2 + zs[dz]

                def send(t=t, at=at, dz=dz):
                    rcopy(tsend.at[at, units], trecv.at[tm, units], t_send.at[b], t_recv.at[b],
                          (t, rows_of[dz])).start()

                def keep(at=at):
                    trecv[tm, k:k + n] = tsend[at, k:k + n]

                if (dx, dz) == (0, 0):
                    pl.when(zz != core)(send)
                    pl.when(zz == core)(keep)
                else:
                    send()

    def stage_own(b):
        @pl.loop(0, 3)
        def _(part):
            stage_part(b, zl, part)

        send_time(b, zl)

    def stage_partner(b):
        @pl.loop(0, 3)
        def _(part):
            zcopy(b, part, oz).wait_recv()
            stage_part(b, oz, part)

        send_time(b, oz)

    factor = LOG2E / math.sqrt(HD)

    def soften(s):
        p = jnp.exp2((s - jnp.max(s, axis=-1, keepdims=True)) * factor)
        return p, jnp.sum(p, axis=-1, keepdims=True)

    def temporal(b):
        k, n = batches[b]
        units = pl.ds(k, n)
        await_bytes(trecv.at[pl.ds(0, 15), units], t_recv.at[b])
        for u in range(k, k + n):
            for h in range(2):
                cols = slice(h * HD, (h + 1) * HD)
                q, kk, v = (trecv[:, u, part, :, cols].reshape(256, HD) for part in range(3))
                p, total = soften(dot_nt(q, kk) + mask[...])
                o = dot(p.astype(BF), v) / total
                osend[:, u, :, cols] = o.astype(BF).reshape(16, 16, HD)
        orecv[me_at, k:k + n] = osend[tm, k:k + n]
        for o in offsets:
            dev, _ = peer(*o)
            rcopy(osend.at[dev[0], units], orecv.at[me_at, units], o_send.at[b], o_recv.at[b], dev).start()

    def wait_back(b):
        k, n = batches[b]
        await_bytes(orecv.at[pl.ds(0, 15), pl.ds(k, n)], o_recv.at[b])

    def spatial(ka, kb):
        @pl.loop(0, 2)
        def _(pair):
            for f in range(2):
                rows = pl.ds(pl.multiple_of(pair * 64 + f * 32, 32), 32)
                for h in range(2):
                    cols = slice(h * HD, (h + 1) * HD)
                    q = jnp.concatenate(
                        [qkv[0:2, 0, k:k + 2, rows, cols].reshape(128, HD) for k in (ka, kb)], axis=0)
                    kk, v = (qkv[0:2, part, :, rows, cols].reshape(512, HD) for part in (1, 2))
                    p, total = soften(dot_nt(q, kk))
                    o = (dot(p.astype(BF), v) / total).reshape(2, 2, 2, 32, HD)
                    sp[:, ka:ka + 2, rows, cols] = o[0]
                    sp[:, kb:kb + 2, rows, cols] = o[1]

    def ccopy(u, r, at, kept):
        half = half_of[u]
        return rcopy(csend.at[u, r % 2], comb.at[kept, half], c_send.at[u, r % 2], c_recv.at[at, half],
                     (tm, r))

    def combine(u):
        for zz in range(2):
            back = dot(perm_t[:128, :128], orecv[zz * 8:(zz + 1) * 8, u].reshape(128, 256))
            csend[u, zz] = (sp[zz, u] + back).astype(BF)
        if u < 2:
            ccopy(u, partner_row, row, y * 2 + hz).start()
            comb[y * 2 + hz, u] = csend[u, zl]
        else:
            for zz in range(2):
                ccopy(u, y_of[u] * 2 + zz, row, y * 2 + hz).start()

    def project_out(pair, first, last=True):
        for ys in pair:
            for i in range(2):
                r = ys * 2 + i
                for half in range(2):
                    def wait(r=r, half=half, ys=ys):
                        dst = comb.at[ys * 2 + (r + zh) % 2, half]
                        rcopy(csend.at[0, 0], dst, c_send.at[0, 0], c_recv.at[r, half], (tm, r)).wait_recv()
                    if ys is y:
                        pl.when(i != zl)(wait)
                    else:
                        wait()

        @pl.loop(0, 6)
        def _(n):
            cols = pl.ds(pl.multiple_of(n * 512, 512), 512)
            heads = [2 * ys + i for ys in pair for i in range(2)]
            left = jnp.concatenate([comb[h].reshape(256, 256) for h in heads], axis=1)
            right = jnp.concatenate([wo[h, :, cols] for h in heads], axis=0)
            acc = dot(left, right)
            for half in range(2):
                for f in range(4):
                    at = (half * 4 + f) * 32
                    rows = slice(half * 32, (half + 1) * 32)
                    piece = acc[at:at + 32]
                    if not first:
                        piece = piece + out_ref[f, rows, cols]
                    if not first and last:
                        clip = clip_ref[tm * 4 + f]
                        piece = piece * mod_ref[2, pl.ds(clip, 1), cols]
                    out_ref[f, rows, cols] = piece

    load_w.wait()
    for p in range(3):
        for i in range(2):
            wz_copy(p, i, oz).wait_recv()
            wx_copy(p, i, e_own).start()
        wc_copy(p, 0, e_own).start()
        project_part(0, zl, p)
    def pass_x(p):
        for i in range(2):
            wx_copy(p, i, e_x).wait_recv()
        wc_copy(p, 1, e_x).start()

    pass_x(0)
    pass_x(1)
    for p in range(3):
        for j in range(2):
            wc_copy(p, j, e_cores[j]).wait_recv()
        project_part(0, oz, p)
        zcopy(0, p, zl).start()
        if p == 0:
            pass_x(2)
    load_wo.start()
    for i in range(2):
        y_copies[i].wait_recv()
        y_copies[4 + i].start()
    stage_own(0)
    project(1)
    stage_own(1)
    stage_partner(0)

    for i in range(2):
        y_copies[2 + i].wait_recv()
        y_copies[6 + i].start()
    project(2)
    stage_own(2)
    stage_partner(1)
    temporal(0)

    y_copies[4].wait_recv()
    y_copies[5].wait_recv()
    project(3)
    stage_own(3)
    stage_partner(2)
    temporal(1)
    stage_partner(3)

    y_copies[6].wait_recv()
    y_copies[7].wait_recv()
    project(4)
    stage_own(4)
    temporal(2)
    stage_partner(4)
    temporal(3)

    spatial(2, 4)
    wait_back(1)
    combine(2)
    combine(3)
    wait_back(2)
    combine(4)
    combine(5)
    temporal(4)
    spatial(6, 0)
    wait_back(3)
    combine(6)
    wait_back(0)
    combine(0)
    combine(1)
    wait_back(4)
    combine(7)
    load_wo.wait()
    project_out((yp, ym), first=True)
    project_out((y,), first=False, last=False)
    project_out((yq,), first=False)

    for p in range(3):
        for i in range(2):
            wz_copy(p, i, zl).wait_send()
            wx_copy(p, i, e_own).wait_send()
            wc_copy(p, i, e_own).wait_send()
    for c in y_copies:
        c.wait_send()
    for b, (k, n) in enumerate(batches):
        for part in range(3):
            zcopy(b, part, zl).wait_send()
        await_bytes(tsend.at[pl.ds(0, 15), pl.ds(k, n)], t_send.at[b])
        await_bytes(osend.at[pl.ds(0, 15), pl.ds(k, n)], o_send.at[b])
    for u in range(8):
        if u < 2:
            ccopy(u, partner_row, row, y * 2 + hz).wait_send()
        else:
            for zz in range(2):
                ccopy(u, y_of[u] * 2 + zz, row, y * 2 + hz).wait_send()


def attention(clip_ids, stream, mod, weight, out_weight):
    vmem = pl.BlockSpec(memory_space=pltpu.VMEM)
    hbm = pl.BlockSpec(memory_space=pl.ANY)
    dma = pltpu.SemaphoreType.DMA
    return pl.pallas_call(
        attention_kernel,
        out_shape=pltpu.VMEM((4, 64, 3072), F32),
        in_specs=[pl.BlockSpec(memory_space=pltpu.SMEM), hbm, vmem, hbm, hbm],
        out_specs=vmem,
        scratch_shapes=[
            pltpu.VMEM((4, 64, 3072), F32),
            pltpu.VMEM((8, 128, 3072), BF),
            pltpu.VMEM((2, 3, 8, 384, 256), BF),
            pltpu.VMEM((8, 256, 3072), BF),
            pltpu.VMEM((3, 3, 8, 128, 256), BF),
            pltpu.VMEM((16, 8, 3, 16, 256), BF),
            pltpu.VMEM((16, 8, 3, 16, 256), BF),
            pltpu.VMEM((16, 8, 16, 256), BF),
            pltpu.VMEM((16, 8, 16, 256), BF),
            pltpu.VMEM((8, 2, 128, 256), BF),
            pltpu.VMEM((8, 2, 128, 256), BF),
            pltpu.VMEM((2, 8, 128, 256), F32),
            pltpu.VMEM((256, 256), BF),
            pltpu.VMEM((256, 256), BF),
            pltpu.VMEM((256, 256), F32),
            dma((4,)),
            dma((8,)), dma((8,)),
            dma((3, 2)), dma((3, 2)),
            dma((3, 2)), dma((3, 2)),
            dma((3, 2)), dma((3, 2)),
            dma((5, 3)), dma((5, 3)),
            dma((5,)), dma((5,)),
            dma((5,)), dma((5,)),
            dma((8, 2)), dma((8, 2)),
        ],
        compiler_params=pltpu.CompilerParams(
            collective_id=0, has_side_effects=True, vmem_limit_bytes=60 * 1024 * 1024
        ),
        name="attention",
    )(clip_ids, stream, mod, weight, out_weight)


def per_device(stream, clip_ids, modulation, qkv_weight, out_weight):
    mod = jnp.transpose(modulation, (1, 0, 2))
    weight = jnp.transpose(qkv_weight, (1, 0, 2)).reshape(3, 8, 384, 256)
    return attention(clip_ids, stream, mod, weight, out_weight.reshape(8, 256, 3072))


def solution(mesh):
    placed = (P("tm", "row", None), P(), P(), P(None, None, "row"), P())
    return jax.shard_map(
        per_device, mesh=mesh, in_specs=placed, out_specs=P("tm", "row", None), check_vma=False
    )
```

```python
import math

import jax
import jax.numpy as jnp
from jax import lax
from jax.experimental import pallas as pl
from jax.experimental.pallas import tpu as pltpu
from jax.sharding import PartitionSpec as P

HD = 128
MESH = pl.DeviceIdType.MESH
BF = jnp.bfloat16
F32 = jnp.float32
LOG2E = 1.4426950408889634


def dot(a, b):
    return jnp.dot(a, b, preferred_element_type=F32)


def dot_nt(a, b):
    return lax.dot_general(a, b, (((1,), (1,)), ((), ())), preferred_element_type=F32)


def attention_kernel(
    clip_ref, stream_hbm, mod_ref, w_hbm, wo_hbm, out_ref,
    stream_v, xg, wbuf, wo, qkv, tsend, trecv, osend, orecv, csend, comb, sp, perm, perm_t, mask,
    load_sem, y_send, y_recv, wz_send, wz_recv, wx_send, wx_recv, wc_send, wc_recv, z_send, z_recv,
    t_send, t_recv, o_send, o_recv, c_send, c_recv,
):
    batches = ((0, 2), (2, 2), (4, 2), (6, 2))
    tm = lax.axis_index("tm")
    row = lax.axis_index("row")
    zh = (tm // 2) % 2
    core = tm % 2
    y = row // 2
    zl = row % 2
    hz = (zl + zh) % 2
    oz = 1 - zl
    partner_row = y * 2 + oz
    outer_tm = tm + 2 - 4 * zh
    other_core = tm + 1 - 2 * core
    ym, yp, yq = (y + 3) % 4, (y + 1) % 4, (y + 2) % 4
    up, down = (tm, yp * 2 + zl), (tm, ym * 2 + zl)
    y_of = (y, y, ym, yp, ym, yp, yq, yq)
    half_of = (0, 1, 0, 1, 1, 0, 0, 1)

    def rcopy(src, dst, send, recv, dev):
        return pltpu.make_async_remote_copy(
            src_ref=src, dst_ref=dst, send_sem=send, recv_sem=recv,
            device_id=dev, device_id_type=MESH,
        )

    def await_bytes(ref, sem):
        pltpu.make_async_copy(ref, ref, sem).wait()

    x = tm // 4
    xs = [((x + d) % 4) for d in range(4)]
    zs = [zh, 1 - zh]
    cs = [core, 1 - core]
    rows_of = [y * 2 + (hz + zh) % 2, y * 2 + (hz + 1 - zh) % 2]
    offsets = [(dx, dz, dc) for dx in (1, 3, 2, 0) for dz in range(2) for dc in range(2)][:-4]
    offsets = offsets + [(0, 1, 0), (0, 1, 1), (0, 0, 1)]
    me_at = core * 8 + x * 2 + zh

    def peer(dx, dz, dc):
        t = xs[dx] * 4 + zs[dz] * 2 + cs[dc]
        return (t, rows_of[dz]), cs[dc] * 8 + xs[dx] * 2 + zs[dz]

    load_stream = [
        pltpu.make_async_copy(stream_hbm.at[:, pl.ds(32 * u, 32)], stream_v.at[:, pl.ds(32 * u, 32)],
                              load_sem.at[u])
        for u in range(2)
    ]
    load_w = pltpu.make_async_copy(w_hbm, wbuf.at[zl], load_sem.at[2])
    load_wo = pltpu.make_async_copy(wo_hbm, wo, load_sem.at[3])
    for c in load_stream:
        c.start()

    barrier = pltpu.get_barrier_semaphore()
    for o in offsets:
        pl.semaphore_signal(barrier, inc=1, device_id=peer(*o)[0], device_id_type=MESH)
    row_peers = [(tm, r * 2 + (zl if i == 0 else oz)) for r in (y, ym, yp, yq) for i in range(2)][1:]
    for dev in row_peers:
        pl.semaphore_signal(barrier, inc=1, device_id=dev, device_id_type=MESH)

    x_par = x % 2
    x_up, x_down = (tm + 4) % 16, (tm + 12) % 16
    e_own = core * 4 + x_par * 2
    e_x = core * 4 + (1 - x_par) * 2
    e_cores = ((1 - core) * 4 + x_par * 2, (1 - core) * 4 + (1 - x_par) * 2)

    def wz_copy(p, i, side):
        dev = ((tm, partner_row), (outer_tm, partner_row))[i]
        return rcopy(w_hbm.at[p, e_own + i], wbuf.at[side, p, e_own + i],
                     wz_send.at[p, i], wz_recv.at[p, i], dev)

    def wx_copy(p, i, e):
        dev = ((x_up, row), (x_down, row))[i]
        return rcopy(wbuf.at[oz, p, e + i], wbuf.at[oz, p, e + i],
                     wx_send.at[p, i], wx_recv.at[p, i], dev)

    def wc_copy(p, j, e):
        pair = wbuf.at[oz, p, pl.ds(e, 2)]
        return rcopy(pair, pair, wc_send.at[p, j], wc_recv.at[p, j], (other_core, row))


    def norm(unit):
        @pl.loop(0, 4)
        def _(f):
            clip = clip_ref[tm * 4 + f]
            shift = mod_ref[0, pl.ds(clip, 1), :]
            scale = 1.0 + mod_ref[1, pl.ds(clip, 1), :]
            v = stream_v[f, pl.ds(unit * 32, 32), :]
            centred = v - jnp.mean(v, axis=-1, keepdims=True)
            var = jnp.mean(centred * centred, axis=-1, keepdims=True)
            n = centred * lax.rsqrt(var + 1e-06) * scale + shift
            xg[unit, pl.ds(f * 32, 32), :] = n.astype(BF)

    def ycopy(i, src, dst, dev):
        return rcopy(xg.at[src], xg.at[dst], y_send.at[i], y_recv.at[i], dev)

    y_copies = [
        ycopy(0, 0, 2, up), ycopy(1, 1, 3, down),
        ycopy(2, 1, 4, up), ycopy(3, 0, 5, down),
        ycopy(4, 2, 6, up), ycopy(5, 3, 7, down),
    ]
    for unit in range(2):
        load_stream[unit].wait()
        norm(unit)
        if unit == 0:
            pl.semaphore_wait(barrier, 22)
            load_w.start()
            for p in range(3):
                for i in range(2):
                    wz_copy(p, i, zl).start()
        y_copies[unit].start()
    y_copies[2].start()
    y_copies[3].start()

    def unit_row(j):
        return (j & 128) + ((j >> 2) & 3) * 32 + ((j >> 4) & 7) * 4 + (j & 3)

    r_i = lax.broadcasted_iota(jnp.int32, (256, 256), 0)
    c_i = lax.broadcasted_iota(jnp.int32, (256, 256), 1)
    perm[...] = (unit_row(r_i) == c_i).astype(BF)
    perm_t[...] = (unit_row(c_i) == r_i).astype(BF)
    lane = lax.broadcasted_iota(jnp.int32, (1, 256), 1)

    def clip_of(f, found):
        return jnp.where((lane >> 2) == f, clip_ref[f], found)

    key = lax.fori_loop(0, 64, clip_of, jnp.zeros((1, 256), jnp.int32)) * 4 + (lane & 3)
    key = jnp.broadcast_to(key.astype(F32), (256, 256))
    mask[...] = jnp.where(key == key.T, 0.0, -1e30).astype(F32)

    def project_part(b, pz, part):
        k, n = batches[b]
        kk = (pz + hz) % 2
        slot = kk * 2 + (1 - kk) * zl
        x = xg[k:k + n].reshape(n * 128, 3072)
        out = dot(x, wbuf[pz, part].reshape(3072, 256)).astype(BF)
        qkv[slot, part, k:k + n] = out.reshape(n, 128, 256)

    def zcopy(b, part, slot):
        k, n = batches[b]
        units = pl.ds(k, n)
        return rcopy(qkv.at[2, part, units], qkv.at[slot, part, units], z_send.at[b, part],
                     z_recv.at[b, part], (tm, partner_row))

    def project(b):
        @pl.loop(0, 3)
        def _(part):
            project_part(b, 1 - hz, part)
            zcopy(b, part, zl).start()

        @pl.loop(0, 3)
        def _(part):
            project_part(b, hz, part)

    def stage_part(b, zz, part):
        k, n = batches[b]
        rows = qkv[zz, part, k:k + n].reshape(n * 128, 256)
        moved = dot(perm[:n * 128, :n * 128], rows).astype(BF).reshape(n, 8, 16, 256)
        for i in range(n):
            tsend[pl.ds(zz * 8, 8), k + i, part] = moved[i]

    def send_time(b, zz):
        k, n = batches[b]
        units = pl.ds(k, n)
        for dx in (1, 3, 2, 0):
            for dz in (1, 0):
                t = xs[dx] * 4 + zs[dz] * 2 + zz
                at = zz * 8 + xs[dx] * 2 + zs[dz]

                def send(t=t, at=at, dz=dz):
                    rcopy(tsend.at[at, units], trecv.at[tm, units], t_send.at[b], t_recv.at[b],
                          (t, rows_of[dz])).start()

                def keep(at=at):
                    trecv[tm, k:k + n] = tsend[at, k:k + n]

                if (dx, dz) == (0, 0):
                    pl.when(zz != core)(send)
                    pl.when(zz == core)(keep)
                else:
                    send()

    def stage_own(b):
        @pl.loop(0, 3)
        def _(part):
            stage_part(b, zl, part)

        send_time(b, zl)

    def stage_partner(b):
        @pl.loop(0, 3)
        def _(part):
            zcopy(b, part, oz).wait_recv()
            stage_part(b, oz, part)

        send_time(b, oz)

    factor = LOG2E / math.sqrt(HD)

    def soften(s):
        p = jnp.exp2((s - jnp.max(s, axis=-1, keepdims=True)) * factor)
        return p, jnp.sum(p, axis=-1, keepdims=True)

    def temporal(b):
        k, n = batches[b]
        units = pl.ds(k, n)
        await_bytes(trecv.at[pl.ds(0, 15), units], t_recv.at[b])
        for u in range(k, k + n):
            for h in range(2):
                cols = slice(h * HD, (h + 1) * HD)
                q, kk, v = (trecv[:, u, part, :, cols].reshape(256, HD) for part in range(3))
                p, total = soften(dot_nt(q, kk) + mask[...])
                o = dot(p.astype(BF), v) / total
                osend[:, u, :, cols] = o.astype(BF).reshape(16, 16, HD)
        orecv[me_at, k:k + n] = osend[tm, k:k + n]
        for o in offsets:
            dev, _ = peer(*o)
            rcopy(osend.at[dev[0], units], orecv.at[me_at, units], o_send.at[b], o_recv.at[b], dev).start()

    def wait_back(b):
        k, n = batches[b]
        await_bytes(orecv.at[pl.ds(0, 15), pl.ds(k, n)], o_recv.at[b])

    def spatial(ka, kb):
        @pl.loop(0, 2)
        def _(pair):
            for f in range(2):
                rows = pl.ds(pl.multiple_of(pair * 64 + f * 32, 32), 32)
                for h in range(2):
                    cols = slice(h * HD, (h + 1) * HD)
                    q = jnp.concatenate(
                        [qkv[0:2, 0, k:k + 2, rows, cols].reshape(128, HD) for k in (ka, kb)], axis=0)
                    kk, v = (qkv[0:2, part, :, rows, cols].reshape(512, HD) for part in (1, 2))
                    p, total = soften(dot_nt(q, kk))
                    o = (dot(p.astype(BF), v) / total).reshape(2, 2, 2, 32, HD)
                    sp[:, ka:ka + 2, rows, cols] = o[0]
                    sp[:, kb:kb + 2, rows, cols] = o[1]

    def ccopy(u, r, at, kept):
        half = half_of[u]
        return rcopy(csend.at[u, r % 2], comb.at[kept, half], c_send.at[u, r % 2], c_recv.at[at, half],
                     (tm, r))

    def combine(u):
        back = dot(perm_t[...], orecv[:, u].reshape(256, 256)).reshape(2, 128, 256)
        csend[u] = (sp[:, u] + back).astype(BF)
        if u < 2:
            ccopy(u, partner_row, row, y * 2 + hz).start()
            comb[y * 2 + hz, u] = csend[u, zl]
        else:
            for zz in range(2):
                ccopy(u, y_of[u] * 2 + zz, row, y * 2 + hz).start()

    def project_out(pair, first, last=True):
        for ys in pair:
            for i in range(2):
                r = ys * 2 + i
                for half in range(2):
                    def wait(r=r, half=half, ys=ys):
                        dst = comb.at[ys * 2 + (r + zh) % 2, half]
                        rcopy(csend.at[0, 0], dst, c_send.at[0, 0], c_recv.at[r, half], (tm, r)).wait_recv()
                    if ys is y:
                        pl.when(i != zl)(wait)
                    else:
                        wait()

        @pl.loop(0, 6)
        def _(n):
            cols = pl.ds(pl.multiple_of(n * 512, 512), 512)
            heads = [2 * ys + i for ys in pair for i in range(2)]
            left = jnp.concatenate([comb[h].reshape(256, 256) for h in heads], axis=1)
            right = jnp.concatenate([wo[h, :, cols] for h in heads], axis=0)
            acc = dot(left, right)
            for half in range(2):
                for f in range(4):
                    at = (half * 4 + f) * 32
                    rows = slice(half * 32, (half + 1) * 32)
                    piece = acc[at:at + 32]
                    if not first:
                        piece = piece + out_ref[f, rows, cols]
                    if not first and last:
                        clip = clip_ref[tm * 4 + f]
                        piece = piece * mod_ref[2, pl.ds(clip, 1), cols]
                    out_ref[f, rows, cols] = piece

    load_w.wait()
    for p in range(3):
        for i in range(2):
            wz_copy(p, i, oz).wait_recv()
            wx_copy(p, i, e_own).start()
        wc_copy(p, 0, e_own).start()
        project_part(0, zl, p)
    def pass_x(p):
        for i in range(2):
            wx_copy(p, i, e_x).wait_recv()
        wc_copy(p, 1, e_x).start()

    pass_x(0)
    pass_x(1)
    for p in range(3):
        for j in range(2):
            wc_copy(p, j, e_cores[j]).wait_recv()
        project_part(0, oz, p)
        zcopy(0, p, zl).start()
        if p == 0:
            pass_x(2)
    load_wo.start()
    for i in range(2):
        y_copies[i].wait_recv()
        y_copies[4 + i].start()
    stage_own(0)
    project(1)
    stage_own(1)
    stage_partner(0)

    y_copies[2].wait_recv()
    y_copies[3].wait_recv()
    project(2)
    stage_own(2)
    stage_partner(1)
    temporal(0)
    stage_partner(2)
    temporal(1)

    y_copies[4].wait_recv()
    y_copies[5].wait_recv()
    project(3)
    stage_own(3)
    temporal(2)
    stage_partner(3)

    spatial(2, 4)
    wait_back(1)
    combine(2)
    combine(3)
    wait_back(2)
    combine(4)
    combine(5)
    temporal(3)
    spatial(6, 0)
    wait_back(0)
    combine(0)
    combine(1)
    wait_back(3)
    combine(6)
    combine(7)
    load_wo.wait()
    project_out((yp, ym), first=True)
    project_out((y,), first=False, last=False)
    project_out((yq,), first=False)

    for p in range(3):
        for i in range(2):
            wz_copy(p, i, zl).wait_send()
            wx_copy(p, i, e_own).wait_send()
            wc_copy(p, i, e_own).wait_send()
    for c in y_copies:
        c.wait_send()
    for b, (k, n) in enumerate(batches):
        for part in range(3):
            zcopy(b, part, zl).wait_send()
        await_bytes(tsend.at[pl.ds(0, 15), pl.ds(k, n)], t_send.at[b])
        await_bytes(osend.at[pl.ds(0, 15), pl.ds(k, n)], o_send.at[b])
    for u in range(8):
        if u < 2:
            ccopy(u, partner_row, row, y * 2 + hz).wait_send()
        else:
            for zz in range(2):
                ccopy(u, y_of[u] * 2 + zz, row, y * 2 + hz).wait_send()


def attention(clip_ids, stream, mod, weight, out_weight):
    vmem = pl.BlockSpec(memory_space=pltpu.VMEM)
    hbm = pl.BlockSpec(memory_space=pl.ANY)
    dma = pltpu.SemaphoreType.DMA
    return pl.pallas_call(
        attention_kernel,
        out_shape=pltpu.VMEM((4, 64, 3072), F32),
        in_specs=[pl.BlockSpec(memory_space=pltpu.SMEM), hbm, vmem, hbm, hbm],
        out_specs=vmem,
        scratch_shapes=[
            pltpu.VMEM((4, 64, 3072), F32),
            pltpu.VMEM((8, 128, 3072), BF),
            pltpu.VMEM((2, 3, 8, 384, 256), BF),
            pltpu.VMEM((8, 256, 3072), BF),
            pltpu.VMEM((3, 3, 8, 128, 256), BF),
            pltpu.VMEM((16, 8, 3, 16, 256), BF),
            pltpu.VMEM((16, 8, 3, 16, 256), BF),
            pltpu.VMEM((16, 8, 16, 256), BF),
            pltpu.VMEM((16, 8, 16, 256), BF),
            pltpu.VMEM((8, 2, 128, 256), BF),
            pltpu.VMEM((8, 2, 128, 256), BF),
            pltpu.VMEM((2, 8, 128, 256), F32),
            pltpu.VMEM((256, 256), BF),
            pltpu.VMEM((256, 256), BF),
            pltpu.VMEM((256, 256), F32),
            dma((4,)),
            dma((6,)), dma((6,)),
            dma((3, 2)), dma((3, 2)),
            dma((3, 2)), dma((3, 2)),
            dma((3, 2)), dma((3, 2)),
            dma((4, 3)), dma((4, 3)),
            dma((4,)), dma((4,)),
            dma((4,)), dma((4,)),
            dma((8, 2)), dma((8, 2)),
        ],
        compiler_params=pltpu.CompilerParams(
            collective_id=0, has_side_effects=True, vmem_limit_bytes=60 * 1024 * 1024
        ),
        name="attention",
    )(clip_ids, stream, mod, weight, out_weight)


def per_device(stream, clip_ids, modulation, qkv_weight, out_weight):
    mod = jnp.transpose(modulation, (1, 0, 2))
    weight = jnp.transpose(qkv_weight, (1, 0, 2)).reshape(3, 8, 384, 256)
    return attention(clip_ids, stream, mod, weight, out_weight.reshape(8, 256, 3072))


def solution(mesh):
    placed = (P("tm", "row", None), P(), P(), P(None, None, "row"), P())
    return jax.shard_map(
        per_device, mesh=mesh, in_specs=placed, out_specs=P("tm", "row", None), check_vma=False
    )
```

```python
import math

import jax
import jax.numpy as jnp
from jax import lax
from jax.experimental import pallas as pl
from jax.experimental.pallas import tpu as pltpu
from jax.sharding import PartitionSpec as P

HD = 128
MESH = pl.DeviceIdType.MESH
BF = jnp.bfloat16
F32 = jnp.float32
LOG2E = 1.4426950408889634


def dot(a, b):
    return jnp.dot(a, b, preferred_element_type=F32)


def dot_nt(a, b):
    return lax.dot_general(a, b, (((1,), (1,)), ((), ())), preferred_element_type=F32)


def attention_kernel(
    clip_ref, stream_hbm, mod_ref, w_hbm, wo_hbm, out_ref,
    stream_v, xg, wbuf, wo, qkv, tsend, trecv, osend, orecv, csend, comb, sp, total, perm, perm_t, mask,
    load_sem, y_send, y_recv, wz_send, wz_recv, wx_send, wx_recv, wc_send, wc_recv, z_send, z_recv,
    t_send, t_recv, o_send, o_recv, c_send, c_recv,
):
    batches = ((0, 2), (2, 2), (4, 2), (6, 2))
    tm = lax.axis_index("tm")
    row = lax.axis_index("row")
    zh = (tm // 2) % 2
    core = tm % 2
    y = row // 2
    zl = row % 2
    hz = (zl + zh) % 2
    oz = 1 - zl
    partner_row = y * 2 + oz
    outer_tm = tm + 2 - 4 * zh
    other_core = tm + 1 - 2 * core
    ym, yp, yq = (y + 3) % 4, (y + 1) % 4, (y + 2) % 4
    up, down = (tm, yp * 2 + zl), (tm, ym * 2 + zl)
    y_of = (y, y, ym, yp, ym, yp, yq, yq)
    half_of = (0, 1, 0, 1, 1, 0, 0, 1)

    def rcopy(src, dst, send, recv, dev):
        return pltpu.make_async_remote_copy(
            src_ref=src, dst_ref=dst, send_sem=send, recv_sem=recv,
            device_id=dev, device_id_type=MESH,
        )

    def await_bytes(ref, sem):
        pltpu.make_async_copy(ref, ref, sem).wait()

    x = tm // 4
    xs = [((x + d) % 4) for d in range(4)]
    zs = [zh, 1 - zh]
    cs = [core, 1 - core]
    rows_of = [y * 2 + (hz + zh) % 2, y * 2 + (hz + 1 - zh) % 2]
    offsets = [(dx, dz, dc) for dx in (1, 3, 2, 0) for dz in range(2) for dc in range(2)][:-4]
    offsets = offsets + [(0, 1, 0), (0, 1, 1), (0, 0, 1)]
    me_at = core * 8 + x * 2 + zh

    def peer(dx, dz, dc):
        t = xs[dx] * 4 + zs[dz] * 2 + cs[dc]
        return (t, rows_of[dz]), cs[dc] * 8 + xs[dx] * 2 + zs[dz]

    load_stream = [
        pltpu.make_async_copy(stream_hbm.at[:, pl.ds(32 * u, 32)], stream_v.at[:, pl.ds(32 * u, 32)],
                              load_sem.at[u])
        for u in range(2)
    ]
    load_w = pltpu.make_async_copy(w_hbm, wbuf.at[zl], load_sem.at[2])
    load_wo = pltpu.make_async_copy(wo_hbm, wo, load_sem.at[3])
    for c in load_stream:
        c.start()

    barrier = pltpu.get_barrier_semaphore()
    for o in offsets:
        pl.semaphore_signal(barrier, inc=1, device_id=peer(*o)[0], device_id_type=MESH)
    row_peers = [(tm, r * 2 + (zl if i == 0 else oz)) for r in (y, ym, yp, yq) for i in range(2)][1:]
    for dev in row_peers:
        pl.semaphore_signal(barrier, inc=1, device_id=dev, device_id_type=MESH)

    x_par = x % 2
    x_up, x_down = (tm + 4) % 16, (tm + 12) % 16
    e_own = core * 4 + x_par * 2
    e_x = core * 4 + (1 - x_par) * 2
    e_cores = ((1 - core) * 4 + x_par * 2, (1 - core) * 4 + (1 - x_par) * 2)

    def wz_copy(p, i, side):
        dev = ((tm, partner_row), (outer_tm, partner_row))[i]
        return rcopy(w_hbm.at[p, e_own + i], wbuf.at[side, p, e_own + i],
                     wz_send.at[p, i], wz_recv.at[p, i], dev)

    def wx_copy(p, i, e):
        dev = ((x_up, row), (x_down, row))[i]
        return rcopy(wbuf.at[oz, p, e + i], wbuf.at[oz, p, e + i],
                     wx_send.at[p, i], wx_recv.at[p, i], dev)

    def wc_copy(p, j, e):
        pair = wbuf.at[oz, p, pl.ds(e, 2)]
        return rcopy(pair, pair, wc_send.at[p, j], wc_recv.at[p, j], (other_core, row))


    def norm(unit):
        @pl.loop(0, 4)
        def _(f):
            clip = clip_ref[tm * 4 + f]
            shift = mod_ref[0, pl.ds(clip, 1), :]
            scale = 1.0 + mod_ref[1, pl.ds(clip, 1), :]
            v = stream_v[f, pl.ds(unit * 32, 32), :]
            centred = v - jnp.mean(v, axis=-1, keepdims=True)
            var = jnp.mean(centred * centred, axis=-1, keepdims=True)
            n = centred * lax.rsqrt(var + 1e-06) * scale + shift
            xg[unit, pl.ds(f * 32, 32), :] = n.astype(BF)

    def ycopy(i, src, dst, dev, half=None):
        if half is None:
            return rcopy(xg.at[src], xg.at[dst], y_send.at[i], y_recv.at[i], dev)
        cols = pl.ds(half * 1536, 1536)
        return rcopy(xg.at[src, :, cols], xg.at[dst, :, cols], y_send.at[i], y_recv.at[i], dev)

    y_copies = [
        ycopy(0, 0, 2, up), ycopy(1, 1, 3, down),
        ycopy(2, 1, 4, up), ycopy(3, 0, 5, down),
        ycopy(4, 2, 6, up, 0), ycopy(5, 3, 7, down, 0),
        ycopy(6, 2, 6, up, 1), ycopy(7, 3, 7, down, 1),
    ]
    for unit in range(2):
        load_stream[unit].wait()
        norm(unit)
        if unit == 0:
            pl.semaphore_wait(barrier, 22)
            load_w.start()
            for p in range(3):
                for i in range(2):
                    wz_copy(p, i, zl).start()
        y_copies[unit].start()
    y_copies[2].start()
    y_copies[3].start()

    def unit_row(j):
        return (j & 128) + ((j >> 2) & 3) * 32 + ((j >> 4) & 7) * 4 + (j & 3)

    r_i = lax.broadcasted_iota(jnp.int32, (256, 256), 0)
    c_i = lax.broadcasted_iota(jnp.int32, (256, 256), 1)
    perm[...] = (unit_row(r_i) == c_i).astype(BF)
    perm_t[...] = (unit_row(c_i) == r_i).astype(BF)
    lane = lax.broadcasted_iota(jnp.int32, (1, 256), 1)

    def clip_of(f, found):
        return jnp.where((lane >> 2) == f, clip_ref[f], found)

    key = lax.fori_loop(0, 64, clip_of, jnp.zeros((1, 256), jnp.int32)) * 4 + (lane & 3)
    key = jnp.broadcast_to(key.astype(F32), (256, 256))
    mask[...] = jnp.where(key == key.T, 0.0, -1e30).astype(F32)

    def slot_of(pz):
        kk = (pz + hz) % 2
        return kk * 2 + (1 - kk) * zl

    def project_part(b, pz, part):
        k, n = batches[b]
        x = xg[k:k + n].reshape(n * 128, 3072)
        out = dot(x, wbuf[pz, part].reshape(3072, 256)).astype(BF)
        qkv[slot_of(pz), part, k:k + n] = out.reshape(n, 128, 256)

    def far_first():
        @pl.loop(0, 6)
        def _(i):
            w = wbuf[i // 3, i % 3, 0:4].reshape(1536, 256)
            total[i // 3, i % 3] = dot(xg[6:8, :, 0:1536].reshape(256, 1536), w)

    def far_part(pz, part):
        w = wbuf[pz, part, 4:8].reshape(1536, 256)
        out = total[pz, part] + dot(xg[6:8, :, 1536:3072].reshape(256, 1536), w)
        qkv[slot_of(pz), part, 6:8] = out.astype(BF).reshape(2, 128, 256)

    def zcopy(b, part, slot):
        k, n = batches[b]
        units = pl.ds(k, n)
        return rcopy(qkv.at[2, part, units], qkv.at[slot, part, units], z_send.at[b, part],
                     z_recv.at[b, part], (tm, partner_row))

    def project(b):
        @pl.loop(0, 3)
        def _(part):
            far_part(1 - hz, part) if b == 3 else project_part(b, 1 - hz, part)
            zcopy(b, part, zl).start()

        @pl.loop(0, 3)
        def _(part):
            far_part(hz, part) if b == 3 else project_part(b, hz, part)

    def stage_part(b, zz, part):
        k, n = batches[b]
        rows = qkv[zz, part, k:k + n].reshape(n * 128, 256)
        moved = dot(perm[:n * 128, :n * 128], rows).astype(BF).reshape(n, 8, 16, 256)
        for i in range(n):
            tsend[pl.ds(zz * 8, 8), k + i, part] = moved[i]

    def send_time(b, zz):
        k, n = batches[b]
        units = pl.ds(k, n)
        for dx in (1, 3, 2, 0):
            for dz in (1, 0):
                t = xs[dx] * 4 + zs[dz] * 2 + zz
                at = zz * 8 + xs[dx] * 2 + zs[dz]

                def send(t=t, at=at, dz=dz):
                    rcopy(tsend.at[at, units], trecv.at[tm, units], t_send.at[b], t_recv.at[b],
                          (t, rows_of[dz])).start()

                def keep(at=at):
                    trecv[tm, k:k + n] = tsend[at, k:k + n]

                if (dx, dz) == (0, 0):
                    pl.when(zz != core)(send)
                    pl.when(zz == core)(keep)
                else:
                    send()

    def stage_own(b):
        @pl.loop(0, 3)
        def _(part):
            stage_part(b, zl, part)

        send_time(b, zl)

    def stage_partner(b):
        @pl.loop(0, 3)
        def _(part):
            zcopy(b, part, oz).wait_recv()
            stage_part(b, oz, part)

        send_time(b, oz)

    factor = LOG2E / math.sqrt(HD)

    def attend(s, v):
        p = jnp.exp2((s - jnp.max(s, axis=-1, keepdims=True)) * factor).astype(BF)
        out = dot(p, jnp.concatenate([v, jnp.ones(v.shape, BF)], axis=1))
        return out[:, :HD] / out[:, HD:]

    def temporal(b):
        k, n = batches[b]
        units = pl.ds(k, n)
        await_bytes(trecv.at[pl.ds(0, 15), units], t_recv.at[b])
        for u in range(k, k + n):
            for h in range(2):
                cols = slice(h * HD, (h + 1) * HD)
                q, kk, v = (trecv[:, u, part, :, cols].reshape(256, HD) for part in range(3))
                o = attend(dot_nt(q, kk) + mask[...], v)
                osend[:, u, :, cols] = o.astype(BF).reshape(16, 16, HD)
        orecv[me_at, k:k + n] = osend[tm, k:k + n]
        for o in offsets:
            dev, _ = peer(*o)
            rcopy(osend.at[dev[0], units], orecv.at[me_at, units], o_send.at[b], o_recv.at[b], dev).start()

    def wait_back(b):
        k, n = batches[b]
        await_bytes(orecv.at[pl.ds(0, 15), pl.ds(k, n)], o_recv.at[b])

    def spatial(ka, kb):
        @pl.loop(0, 2)
        def _(pair):
            for f in range(2):
                rows = pl.ds(pl.multiple_of(pair * 64 + f * 32, 32), 32)
                for h in range(2):
                    cols = slice(h * HD, (h + 1) * HD)
                    q = jnp.concatenate(
                        [qkv[0:2, 0, k:k + 2, rows, cols].reshape(128, HD) for k in (ka, kb)], axis=0)
                    kk, v = (qkv[0:2, part, :, rows, cols].reshape(512, HD) for part in (1, 2))
                    o = attend(dot_nt(q, kk), v).reshape(2, 2, 2, 32, HD)
                    sp[:, ka:ka + 2, rows, cols] = o[0]
                    sp[:, kb:kb + 2, rows, cols] = o[1]

    def ccopy(u, r, at, kept):
        half = half_of[u]
        return rcopy(csend.at[u, r % 2], comb.at[kept, half], c_send.at[u, r % 2], c_recv.at[at, half],
                     (tm, r))

    def combine(u):
        back = dot(perm_t[...], orecv[:, u].reshape(256, 256)).reshape(2, 128, 256)
        csend[u] = (sp[:, u] + back).astype(BF)
        if u < 2:
            ccopy(u, partner_row, row, y * 2 + hz).start()
            comb[y * 2 + hz, u] = csend[u, zl]
        else:
            for zz in range(2):
                ccopy(u, y_of[u] * 2 + zz, row, y * 2 + hz).start()

    def project_out(pair, first, last=True):
        for ys in pair:
            for i in range(2):
                r = ys * 2 + i
                for half in range(2):
                    def wait(r=r, half=half, ys=ys):
                        dst = comb.at[ys * 2 + (r + zh) % 2, half]
                        rcopy(csend.at[0, 0], dst, c_send.at[0, 0], c_recv.at[r, half], (tm, r)).wait_recv()
                    if ys is y:
                        pl.when(i != zl)(wait)
                    else:
                        wait()

        @pl.loop(0, 6)
        def _(n):
            cols = pl.ds(pl.multiple_of(n * 512, 512), 512)
            heads = [2 * ys + i for ys in pair for i in range(2)]
            left = jnp.concatenate([comb[h].reshape(256, 256) for h in heads], axis=1)
            right = jnp.concatenate([wo[h, :, cols] for h in heads], axis=0)
            acc = dot(left, right)
            for half in range(2):
                for f in range(4):
                    at = (half * 4 + f) * 32
                    rows = slice(half * 32, (half + 1) * 32)
                    piece = acc[at:at + 32]
                    if not first:
                        piece = piece + out_ref[f, rows, cols]
                    if not first and last:
                        clip = clip_ref[tm * 4 + f]
                        piece = piece * mod_ref[2, pl.ds(clip, 1), cols]
                    out_ref[f, rows, cols] = piece

    load_w.wait()
    for p in range(3):
        for i in range(2):
            wz_copy(p, i, oz).wait_recv()
            wx_copy(p, i, e_own).start()
        wc_copy(p, 0, e_own).start()
        project_part(0, zl, p)
    def pass_x(p):
        for i in range(2):
            wx_copy(p, i, e_x).wait_recv()
        wc_copy(p, 1, e_x).start()

    pass_x(0)
    pass_x(1)
    for p in range(3):
        for j in range(2):
            wc_copy(p, j, e_cores[j]).wait_recv()
        project_part(0, oz, p)
        zcopy(0, p, zl).start()
        if p == 0:
            pass_x(2)
    load_wo.start()
    for i in range(2):
        y_copies[i].wait_recv()
        y_copies[4 + i].start()
    stage_own(0)
    project(1)
    y_copies[6].start()
    y_copies[7].start()
    stage_own(1)
    stage_partner(0)

    y_copies[2].wait_recv()
    y_copies[3].wait_recv()
    project(2)
    stage_own(2)
    stage_partner(1)
    temporal(0)
    stage_partner(2)
    y_copies[4].wait_recv()
    y_copies[5].wait_recv()
    far_first()
    temporal(1)

    y_copies[6].wait_recv()
    y_copies[7].wait_recv()
    project(3)
    stage_own(3)
    temporal(2)
    stage_partner(3)

    spatial(2, 4)
    wait_back(1)
    combine(2)
    combine(3)
    wait_back(2)
    combine(4)
    combine(5)
    temporal(3)
    spatial(6, 0)
    wait_back(0)
    combine(0)
    combine(1)
    wait_back(3)
    combine(6)
    combine(7)
    load_wo.wait()
    project_out((yp, ym), first=True)
    project_out((y,), first=False, last=False)
    project_out((yq,), first=False)

    for p in range(3):
        for i in range(2):
            wz_copy(p, i, zl).wait_send()
            wx_copy(p, i, e_own).wait_send()
            wc_copy(p, i, e_own).wait_send()
    for c in y_copies:
        c.wait_send()
    for b, (k, n) in enumerate(batches):
        for part in range(3):
            zcopy(b, part, zl).wait_send()
        await_bytes(tsend.at[pl.ds(0, 15), pl.ds(k, n)], t_send.at[b])
        await_bytes(osend.at[pl.ds(0, 15), pl.ds(k, n)], o_send.at[b])
    for u in range(8):
        if u < 2:
            ccopy(u, partner_row, row, y * 2 + hz).wait_send()
        else:
            for zz in range(2):
                ccopy(u, y_of[u] * 2 + zz, row, y * 2 + hz).wait_send()


def attention(clip_ids, stream, mod, weight, out_weight):
    vmem = pl.BlockSpec(memory_space=pltpu.VMEM)
    hbm = pl.BlockSpec(memory_space=pl.ANY)
    dma = pltpu.SemaphoreType.DMA
    return pl.pallas_call(
        attention_kernel,
        out_shape=pltpu.VMEM((4, 64, 3072), F32),
        in_specs=[pl.BlockSpec(memory_space=pltpu.SMEM), hbm, vmem, hbm, hbm],
        out_specs=vmem,
        scratch_shapes=[
            pltpu.VMEM((4, 64, 3072), F32),
            pltpu.VMEM((8, 128, 3072), BF),
            pltpu.VMEM((2, 3, 8, 384, 256), BF),
            pltpu.VMEM((8, 256, 3072), BF),
            pltpu.VMEM((3, 3, 8, 128, 256), BF),
            pltpu.VMEM((16, 8, 3, 16, 256), BF),
            pltpu.VMEM((16, 8, 3, 16, 256), BF),
            pltpu.VMEM((16, 8, 16, 256), BF),
            pltpu.VMEM((16, 8, 16, 256), BF),
            pltpu.VMEM((8, 2, 128, 256), BF),
            pltpu.VMEM((8, 2, 128, 256), BF),
            pltpu.VMEM((2, 8, 128, 256), F32),
            pltpu.VMEM((2, 3, 256, 256), F32),
            pltpu.VMEM((256, 256), BF),
            pltpu.VMEM((256, 256), BF),
            pltpu.VMEM((256, 256), F32),
            dma((4,)),
            dma((8,)), dma((8,)),
            dma((3, 2)), dma((3, 2)),
            dma((3, 2)), dma((3, 2)),
            dma((3, 2)), dma((3, 2)),
            dma((4, 3)), dma((4, 3)),
            dma((4,)), dma((4,)),
            dma((4,)), dma((4,)),
            dma((8, 2)), dma((8, 2)),
        ],
        compiler_params=pltpu.CompilerParams(
            collective_id=0, has_side_effects=True, vmem_limit_bytes=60 * 1024 * 1024
        ),
        name="attention",
    )(clip_ids, stream, mod, weight, out_weight)


def per_device(stream, clip_ids, modulation, qkv_weight, out_weight):
    mod = jnp.transpose(modulation, (1, 0, 2))
    weight = jnp.transpose(qkv_weight, (1, 0, 2)).reshape(3, 8, 384, 256)
    return attention(clip_ids, stream, mod, weight, out_weight.reshape(8, 256, 3072))


def solution(mesh):
    placed = (P("tm", "row", None), P(), P(), P(None, None, "row"), P())
    return jax.shard_map(
        per_device, mesh=mesh, in_specs=placed, out_specs=P("tm", "row", None), check_vma=False
    )
```

```python
import math

import jax
import jax.numpy as jnp
from jax import lax
from jax.experimental import pallas as pl
from jax.experimental.pallas import tpu as pltpu
from jax.sharding import PartitionSpec as P

HD = 128
MESH = pl.DeviceIdType.MESH
BF = jnp.bfloat16
F32 = jnp.float32
LOG2E = 1.4426950408889634


def dot(a, b):
    return jnp.dot(a, b, preferred_element_type=F32)


def dot_nt(a, b):
    return lax.dot_general(a, b, (((1,), (1,)), ((), ())), preferred_element_type=F32)


def attention_kernel(
    clip_ref, stream_hbm, mod_ref, w_hbm, wo_hbm, out_ref,
    stream_v, xg, wbuf, wo, qkv, tsend, trecv, osend, orecv, csend, comb, sp, perm, perm_t, mask,
    load_sem, y_send, y_recv, wz_send, wz_recv, wx_send, wx_recv, wc_send, wc_recv, z_send, z_recv,
    t_send, t_recv, o_send, o_recv, c_send, c_recv,
):
    batches = ((0, 2), (2, 2), (4, 2), (6, 1), (7, 1))
    tm = lax.axis_index("tm")
    row = lax.axis_index("row")
    zh = (tm // 2) % 2
    core = tm % 2
    y = row // 2
    zl = row % 2
    hz = (zl + zh) % 2
    oz = 1 - zl
    partner_row = y * 2 + oz
    outer_tm = tm + 2 - 4 * zh
    other_core = tm + 1 - 2 * core
    ym, yp, yq = (y + 3) % 4, (y + 1) % 4, (y + 2) % 4
    up, down = (tm, yp * 2 + zl), (tm, ym * 2 + zl)
    y_of = (y, y, ym, yp, ym, yp, yq, yq)
    half_of = (0, 1, 0, 0, 1, 1, 0, 1)

    def rcopy(src, dst, send, recv, dev):
        return pltpu.make_async_remote_copy(
            src_ref=src, dst_ref=dst, send_sem=send, recv_sem=recv,
            device_id=dev, device_id_type=MESH,
        )

    def await_bytes(ref, sem):
        pltpu.make_async_copy(ref, ref, sem).wait()

    x = tm // 4
    xs = [((x + d) % 4) for d in range(4)]
    zs = [zh, 1 - zh]
    cs = [core, 1 - core]
    rows_of = [y * 2 + (hz + zh) % 2, y * 2 + (hz + 1 - zh) % 2]
    offsets = [(dx, dz, dc) for dx in (1, 3, 2, 0) for dz in range(2) for dc in range(2)][:-4]
    offsets = offsets + [(0, 1, 0), (0, 1, 1), (0, 0, 1)]
    me_at = core * 8 + x * 2 + zh

    def peer(dx, dz, dc):
        t = xs[dx] * 4 + zs[dz] * 2 + cs[dc]
        return (t, rows_of[dz]), cs[dc] * 8 + xs[dx] * 2 + zs[dz]

    load_stream = [
        pltpu.make_async_copy(stream_hbm.at[:, pl.ds(32 * u, 32)], stream_v.at[:, pl.ds(32 * u, 32)],
                              load_sem.at[u])
        for u in range(2)
    ]
    load_w = pltpu.make_async_copy(w_hbm, wbuf.at[zl], load_sem.at[2])
    load_wo = pltpu.make_async_copy(wo_hbm, wo, load_sem.at[3])
    for c in load_stream:
        c.start()

    barrier = pltpu.get_barrier_semaphore()
    for o in offsets:
        pl.semaphore_signal(barrier, inc=1, device_id=peer(*o)[0], device_id_type=MESH)
    row_peers = [(tm, r * 2 + (zl if i == 0 else oz)) for r in (y, ym, yp, yq) for i in range(2)][1:]
    for dev in row_peers:
        pl.semaphore_signal(barrier, inc=1, device_id=dev, device_id_type=MESH)

    x_par = x % 2
    x_up, x_down = (tm + 4) % 16, (tm + 12) % 16
    e_own = core * 4 + x_par * 2
    e_x = core * 4 + (1 - x_par) * 2
    e_cores = ((1 - core) * 4 + x_par * 2, (1 - core) * 4 + (1 - x_par) * 2)

    def wz_copy(p, i, side):
        dev = ((tm, partner_row), (outer_tm, partner_row))[i]
        return rcopy(w_hbm.at[p, e_own + i], wbuf.at[side, p, e_own + i],
                     wz_send.at[p, i], wz_recv.at[p, i], dev)

    def wx_copy(p, i, e):
        dev = ((x_up, row), (x_down, row))[i]
        return rcopy(wbuf.at[oz, p, e + i], wbuf.at[oz, p, e + i],
                     wx_send.at[p, i], wx_recv.at[p, i], dev)

    def wc_copy(p, j, e):
        pair = wbuf.at[oz, p, pl.ds(e, 2)]
        return rcopy(pair, pair, wc_send.at[p, j], wc_recv.at[p, j], (other_core, row))


    def norm(unit):
        @pl.loop(0, 4)
        def _(f):
            clip = clip_ref[tm * 4 + f]
            shift = mod_ref[0, pl.ds(clip, 1), :]
            scale = 1.0 + mod_ref[1, pl.ds(clip, 1), :]
            v = stream_v[f, pl.ds(unit * 32, 32), :]
            centred = v - jnp.mean(v, axis=-1, keepdims=True)
            var = jnp.mean(centred * centred, axis=-1, keepdims=True)
            n = centred * lax.rsqrt(var + 1e-06) * scale + shift
            xg[unit, pl.ds(f * 32, 32), :] = n.astype(BF)

    def ycopy(i, src, dst, half, dev):
        if half is None:
            return rcopy(xg.at[src], xg.at[dst], y_send.at[i], y_recv.at[i], dev)
        rows = pl.ds(half * 64, 64)
        return rcopy(xg.at[src, rows], xg.at[dst, rows], y_send.at[i], y_recv.at[i], dev)

    y_copies = [
        ycopy(0, 0, 2, None, up), ycopy(1, 0, 3, None, down),
        ycopy(2, 1, 4, None, up), ycopy(3, 1, 5, None, down),
        ycopy(4, 2, 6, 0, up), ycopy(5, 3, 6, 1, down),
        ycopy(6, 4, 7, 0, up), ycopy(7, 5, 7, 1, down),
    ]
    for unit in range(2):
        load_stream[unit].wait()
        norm(unit)
        if unit == 0:
            pl.semaphore_wait(barrier, 22)
            load_w.start()
            for p in range(3):
                for i in range(2):
                    wz_copy(p, i, zl).start()
        y_copies[2 * unit].start()
        y_copies[2 * unit + 1].start()

    def unit_row(j):
        return (j & 128) + ((j >> 2) & 3) * 32 + ((j >> 4) & 7) * 4 + (j & 3)

    r_i = lax.broadcasted_iota(jnp.int32, (256, 256), 0)
    c_i = lax.broadcasted_iota(jnp.int32, (256, 256), 1)
    perm[...] = (unit_row(r_i) == c_i).astype(BF)
    perm_t[...] = (unit_row(c_i) == r_i).astype(BF)
    lane = lax.broadcasted_iota(jnp.int32, (1, 256), 1)

    def clip_of(f, found):
        return jnp.where((lane >> 2) == f, clip_ref[f], found)

    key = lax.fori_loop(0, 64, clip_of, jnp.zeros((1, 256), jnp.int32)) * 4 + (lane & 3)
    key = jnp.broadcast_to(key.astype(F32), (256, 256))
    mask[...] = jnp.where(key == key.T, 0.0, -1e30).astype(F32)

    def project_part(b, pz, part):
        k, n = batches[b]
        kk = (pz + hz) % 2
        slot = kk * 2 + (1 - kk) * zl
        x = xg[k:k + n].reshape(n * 128, 3072)
        out = dot(x, wbuf[pz, part].reshape(3072, 256)).astype(BF)
        qkv[slot, part, k:k + n] = out.reshape(n, 128, 256)

    def zcopy(b, part, slot):
        k, n = batches[b]
        units = pl.ds(k, n)
        return rcopy(qkv.at[2, part, units], qkv.at[slot, part, units], z_send.at[b, part],
                     z_recv.at[b, part], (tm, partner_row))

    def project(b):
        @pl.loop(0, 3)
        def _(part):
            project_part(b, 1 - hz, part)
            zcopy(b, part, zl).start()

        @pl.loop(0, 3)
        def _(part):
            project_part(b, hz, part)

    def stage_part(b, zz, part):
        k, n = batches[b]
        rows = qkv[zz, part, k:k + n].reshape(n * 128, 256)
        moved = dot(perm[:n * 128, :n * 128], rows).astype(BF).reshape(n, 8, 16, 256)
        for i in range(n):
            tsend[pl.ds(zz * 8, 8), k + i, part] = moved[i]

    def send_time(b, zz):
        k, n = batches[b]
        units = pl.ds(k, n)
        for dx in (1, 3, 2, 0):
            for dz in (1, 0):
                t = xs[dx] * 4 + zs[dz] * 2 + zz
                at = zz * 8 + xs[dx] * 2 + zs[dz]

                def send(t=t, at=at, dz=dz):
                    rcopy(tsend.at[at, units], trecv.at[tm, units], t_send.at[b], t_recv.at[b],
                          (t, rows_of[dz])).start()

                def keep(at=at):
                    trecv[tm, k:k + n] = tsend[at, k:k + n]

                if (dx, dz) == (0, 0):
                    pl.when(zz != core)(send)
                    pl.when(zz == core)(keep)
                else:
                    send()

    def stage_own(b):
        @pl.loop(0, 3)
        def _(part):
            stage_part(b, zl, part)

        send_time(b, zl)

    def stage_partner(b):
        @pl.loop(0, 3)
        def _(part):
            zcopy(b, part, oz).wait_recv()
            stage_part(b, oz, part)

        send_time(b, oz)

    factor = LOG2E / math.sqrt(HD)

    def attend(s, v):
        p = jnp.exp2((s - jnp.max(s, axis=-1, keepdims=True)) * factor).astype(BF)
        out = dot(p, jnp.concatenate([v, jnp.ones(v.shape, BF)], axis=1))
        return out[:, :HD] / out[:, HD:]

    def temporal(b):
        k, n = batches[b]
        units = pl.ds(k, n)
        await_bytes(trecv.at[pl.ds(0, 15), units], t_recv.at[b])
        for u in range(k, k + n):
            for h in range(2):
                cols = slice(h * HD, (h + 1) * HD)
                q, kk, v = (trecv[:, u, part, :, cols].reshape(256, HD) for part in range(3))
                o = attend(dot_nt(q, kk) + mask[...], v)
                osend[:, u, :, cols] = o.astype(BF).reshape(16, 16, HD)
        orecv[me_at, k:k + n] = osend[tm, k:k + n]
        for o in offsets:
            dev, _ = peer(*o)
            rcopy(osend.at[dev[0], units], orecv.at[me_at, units], o_send.at[b], o_recv.at[b], dev).start()

    def wait_back(b):
        k, n = batches[b]
        await_bytes(orecv.at[pl.ds(0, 15), pl.ds(k, n)], o_recv.at[b])

    def spatial(k):
        @pl.loop(0, 2)
        def _(pair):
            for f in range(2):
                rows = pl.ds(pl.multiple_of(pair * 64 + f * 32, 32), 32)
                for h in range(2):
                    cols = slice(h * HD, (h + 1) * HD)
                    q = qkv[0:2, 0, k:k + 2, rows, cols].reshape(128, HD)
                    kk, v = (qkv[0:2, part, :, rows, cols].reshape(512, HD) for part in (1, 2))
                    sp[:, k:k + 2, rows, cols] = attend(dot_nt(q, kk), v).reshape(2, 2, 32, HD)

    def ccopy(u, r, at, kept):
        half = half_of[u]
        return rcopy(csend.at[u, r % 2], comb.at[kept, half], c_send.at[u, r % 2], c_recv.at[at, half],
                     (tm, r))

    def combine(*units):
        for u in units:
            back = dot(perm_t[...], orecv[:, u].reshape(256, 256)).reshape(2, 128, 256)
            csend[u] = (sp[:, u] + back).astype(BF)
        for u in units:
            if u < 2:
                ccopy(u, partner_row, row, y * 2 + hz).start()
                comb[y * 2 + hz, u] = csend[u, zl]
            else:
                for zz in range(2):
                    ccopy(u, y_of[u] * 2 + zz, row, y * 2 + hz).start()

    def project_out(pair, first, last=True):
        for ys in pair:
            for i in range(2):
                r = ys * 2 + i
                for half in range(2):
                    def wait(r=r, half=half, ys=ys):
                        dst = comb.at[ys * 2 + (r + zh) % 2, half]
                        rcopy(csend.at[0, 0], dst, c_send.at[0, 0], c_recv.at[r, half], (tm, r)).wait_recv()
                    if ys is y:
                        pl.when(i != zl)(wait)
                    else:
                        wait()

        @pl.loop(0, 6)
        def _(n):
            cols = pl.ds(pl.multiple_of(n * 512, 512), 512)
            heads = [2 * ys + i for ys in pair for i in range(2)]
            left = jnp.concatenate([comb[h].reshape(256, 256) for h in heads], axis=1)
            right = jnp.concatenate([wo[h, :, cols] for h in heads], axis=0)
            acc = dot(left, right)
            for half in range(2):
                for f in range(4):
                    at = (half * 4 + f) * 32
                    rows = slice(half * 32, (half + 1) * 32)
                    piece = acc[at:at + 32]
                    if not first:
                        piece = piece + out_ref[f, rows, cols]
                    if not first and last:
                        clip = clip_ref[tm * 4 + f]
                        piece = piece * mod_ref[2, pl.ds(clip, 1), cols]
                    out_ref[f, rows, cols] = piece

    load_w.wait()
    for p in range(3):
        for i in range(2):
            wz_copy(p, i, oz).wait_recv()
            wx_copy(p, i, e_own).start()
        wc_copy(p, 0, e_own).start()
        project_part(0, zl, p)
    def pass_x(p):
        for i in range(2):
            wx_copy(p, i, e_x).wait_recv()
        wc_copy(p, 1, e_x).start()

    pass_x(0)
    pass_x(1)
    for p in range(3):
        for j in range(2):
            wc_copy(p, j, e_cores[j]).wait_recv()
        project_part(0, oz, p)
        zcopy(0, p, zl).start()
        if p == 0:
            pass_x(2)
    load_wo.start()
    for i in range(2):
        y_copies[i].wait_recv()
        y_copies[4 + i].start()
    stage_own(0)
    project(1)
    stage_own(1)
    stage_partner(0)

    for i in range(2):
        y_copies[2 + i].wait_recv()
        y_copies[6 + i].start()
    project(2)
    stage_own(2)
    stage_partner(1)
    temporal(0)

    y_copies[4].wait_recv()
    y_copies[5].wait_recv()
    project(3)
    stage_own(3)
    stage_partner(2)
    temporal(1)
    stage_partner(3)

    y_copies[6].wait_recv()
    y_copies[7].wait_recv()
    project(4)
    stage_own(4)
    temporal(2)
    temporal(3)
    stage_partner(4)

    spatial(2)
    wait_back(1)
    combine(2, 3)
    spatial(4)
    wait_back(2)
    combine(4, 5)
    temporal(4)
    spatial(6)
    wait_back(3)
    combine(6)
    spatial(0)
    wait_back(0)
    combine(0, 1)
    wait_back(4)
    combine(7)
    load_wo.wait()
    project_out((yp, ym), first=True)
    project_out((y,), first=False, last=False)
    project_out((yq,), first=False)

    for p in range(3):
        for i in range(2):
            wz_copy(p, i, zl).wait_send()
            wx_copy(p, i, e_own).wait_send()
            wc_copy(p, i, e_own).wait_send()
    for c in y_copies:
        c.wait_send()
    for b, (k, n) in enumerate(batches):
        for part in range(3):
            zcopy(b, part, zl).wait_send()
        await_bytes(tsend.at[pl.ds(0, 15), pl.ds(k, n)], t_send.at[b])
        await_bytes(osend.at[pl.ds(0, 15), pl.ds(k, n)], o_send.at[b])
    for u in range(8):
        if u < 2:
            ccopy(u, partner_row, row, y * 2 + hz).wait_send()
        else:
            for zz in range(2):
                ccopy(u, y_of[u] * 2 + zz, row, y * 2 + hz).wait_send()


def attention(clip_ids, stream, mod, weight, out_weight):
    vmem = pl.BlockSpec(memory_space=pltpu.VMEM)
    hbm = pl.BlockSpec(memory_space=pl.ANY)
    dma = pltpu.SemaphoreType.DMA
    return pl.pallas_call(
        attention_kernel,
        out_shape=pltpu.VMEM((4, 64, 3072), F32),
        in_specs=[pl.BlockSpec(memory_space=pltpu.SMEM), hbm, vmem, hbm, hbm],
        out_specs=vmem,
        scratch_shapes=[
            pltpu.VMEM((4, 64, 3072), F32),
            pltpu.VMEM((8, 128, 3072), BF),
            pltpu.VMEM((2, 3, 8, 384, 256), BF),
            pltpu.VMEM((8, 256, 3072), BF),
            pltpu.VMEM((3, 3, 8, 128, 256), BF),
            pltpu.VMEM((16, 8, 3, 16, 256), BF),
            pltpu.VMEM((16, 8, 3, 16, 256), BF),
            pltpu.VMEM((16, 8, 16, 256), BF),
            pltpu.VMEM((16, 8, 16, 256), BF),
            pltpu.VMEM((8, 2, 128, 256), BF),
            pltpu.VMEM((8, 2, 128, 256), BF),
            pltpu.VMEM((2, 8, 128, 256), F32),
            pltpu.VMEM((256, 256), BF),
            pltpu.VMEM((256, 256), BF),
            pltpu.VMEM((256, 256), F32),
            dma((4,)),
            dma((8,)), dma((8,)),
            dma((3, 2)), dma((3, 2)),
            dma((3, 2)), dma((3, 2)),
            dma((3, 2)), dma((3, 2)),
            dma((5, 3)), dma((5, 3)),
            dma((5,)), dma((5,)),
            dma((5,)), dma((5,)),
            dma((8, 2)), dma((8, 2)),
        ],
        compiler_params=pltpu.CompilerParams(
            collective_id=0, has_side_effects=True, vmem_limit_bytes=60 * 1024 * 1024
        ),
        name="attention",
    )(clip_ids, stream, mod, weight, out_weight)


def per_device(stream, clip_ids, modulation, qkv_weight, out_weight):
    mod = jnp.transpose(modulation, (1, 0, 2))
    weight = jnp.transpose(qkv_weight, (1, 0, 2)).reshape(3, 8, 384, 256)
    return attention(clip_ids, stream, mod, weight, out_weight.reshape(8, 256, 3072))


def solution(mesh):
    placed = (P("tm", "row", None), P(), P(), P(None, None, "row"), P())
    return jax.shard_map(
        per_device, mesh=mesh, in_specs=placed, out_specs=P("tm", "row", None), check_vma=False
    )
```

```python
import math

import jax
import jax.numpy as jnp
from jax import lax
from jax.experimental import pallas as pl
from jax.experimental.pallas import tpu as pltpu
from jax.sharding import PartitionSpec as P

HD = 128
MESH = pl.DeviceIdType.MESH
BF = jnp.bfloat16
F32 = jnp.float32
LOG2E = 1.4426950408889634


def dot(a, b):
    return jnp.dot(a, b, preferred_element_type=F32)


def dot_nt(a, b):
    return lax.dot_general(a, b, (((1,), (1,)), ((), ())), preferred_element_type=F32)


def attention_kernel(
    clip_ref, stream_hbm, mod_ref, w_hbm, wo_hbm, out_ref,
    stream_v, xg, wbuf, wo, qkv, tsend, trecv, osend, orecv, csend, comb, sp, perm, perm_t, mask,
    load_sem, y_send, y_recv, wz_send, wz_recv, wx_send, wx_recv, wc_send, wc_recv, z_send, z_recv,
    t_send, t_recv, o_send, o_recv, c_send, c_recv,
):
    batches = ((0, 2), (2, 2), (4, 2), (6, 1), (7, 1))
    tm = lax.axis_index("tm")
    row = lax.axis_index("row")
    zh = (tm // 2) % 2
    core = tm % 2
    y = row // 2
    zl = row % 2
    hz = (zl + zh) % 2
    oz = 1 - zl
    partner_row = y * 2 + oz
    outer_tm = tm + 2 - 4 * zh
    other_core = tm + 1 - 2 * core
    ym, yp, yq = (y + 3) % 4, (y + 1) % 4, (y + 2) % 4
    up, down = (tm, yp * 2 + zl), (tm, ym * 2 + zl)
    y_of = (y, y, ym, yp, ym, yp, yq, yq)
    half_of = (0, 1, 0, 0, 1, 1, 0, 1)

    def rcopy(src, dst, send, recv, dev):
        return pltpu.make_async_remote_copy(
            src_ref=src, dst_ref=dst, send_sem=send, recv_sem=recv,
            device_id=dev, device_id_type=MESH,
        )

    def await_bytes(ref, sem):
        pltpu.make_async_copy(ref, ref, sem).wait()

    x = tm // 4
    xs = [((x + d) % 4) for d in range(4)]
    zs = [zh, 1 - zh]
    cs = [core, 1 - core]
    rows_of = [y * 2 + (hz + zh) % 2, y * 2 + (hz + 1 - zh) % 2]
    offsets = [(dx, dz, dc) for dx in (1, 3, 2, 0) for dz in range(2) for dc in range(2)][:-4]
    offsets = offsets + [(0, 1, 0), (0, 1, 1), (0, 0, 1)]
    me_at = core * 8 + x * 2 + zh

    def peer(dx, dz, dc):
        t = xs[dx] * 4 + zs[dz] * 2 + cs[dc]
        return (t, rows_of[dz]), cs[dc] * 8 + xs[dx] * 2 + zs[dz]

    load_stream = [
        pltpu.make_async_copy(stream_hbm.at[:, pl.ds(32 * u, 32)], stream_v.at[:, pl.ds(32 * u, 32)],
                              load_sem.at[u])
        for u in range(2)
    ]
    load_w = pltpu.make_async_copy(w_hbm, wbuf.at[zl], load_sem.at[2])
    load_wo = pltpu.make_async_copy(wo_hbm, wo, load_sem.at[3])
    for c in load_stream:
        c.start()

    barrier = pltpu.get_barrier_semaphore()
    for o in offsets:
        pl.semaphore_signal(barrier, inc=1, device_id=peer(*o)[0], device_id_type=MESH)
    row_peers = [(tm, r * 2 + (zl if i == 0 else oz)) for r in (y, ym, yp, yq) for i in range(2)][1:]
    for dev in row_peers:
        pl.semaphore_signal(barrier, inc=1, device_id=dev, device_id_type=MESH)

    x_par = x % 2
    x_up, x_down = (tm + 4) % 16, (tm + 12) % 16
    e_own = core * 4 + x_par * 2
    e_x = core * 4 + (1 - x_par) * 2
    e_cores = ((1 - core) * 4 + x_par * 2, (1 - core) * 4 + (1 - x_par) * 2)

    def wz_copy(p, i, side):
        dev = ((tm, partner_row), (outer_tm, partner_row))[i]
        return rcopy(w_hbm.at[p, e_own + i], wbuf.at[side, p, e_own + i],
                     wz_send.at[p, i], wz_recv.at[p, i], dev)

    def wx_copy(p, i, e):
        dev = ((x_up, row), (x_down, row))[i]
        return rcopy(wbuf.at[oz, p, e + i], wbuf.at[oz, p, e + i],
                     wx_send.at[p, i], wx_recv.at[p, i], dev)

    def wc_copy(p, j, e):
        pair = wbuf.at[oz, p, pl.ds(e, 2)]
        return rcopy(pair, pair, wc_send.at[p, j], wc_recv.at[p, j], (other_core, row))


    def norm(unit):
        @pl.loop(0, 4)
        def _(f):
            clip = clip_ref[tm * 4 + f]
            shift = mod_ref[0, pl.ds(clip, 1), :]
            scale = 1.0 + mod_ref[1, pl.ds(clip, 1), :]
            v = stream_v[f, pl.ds(unit * 32, 32), :]
            centred = v - jnp.mean(v, axis=-1, keepdims=True)
            var = jnp.mean(centred * centred, axis=-1, keepdims=True)
            n = centred * lax.rsqrt(var + 1e-06) * scale + shift
            xg[unit, pl.ds(f * 32, 32), :] = n.astype(BF)

    def ycopy(i, src, dst, half, dev):
        if half is None:
            return rcopy(xg.at[src], xg.at[dst], y_send.at[i], y_recv.at[i], dev)
        rows = pl.ds(half * 64, 64)
        return rcopy(xg.at[src, rows], xg.at[dst, rows], y_send.at[i], y_recv.at[i], dev)

    y_copies = [
        ycopy(0, 0, 2, None, up), ycopy(1, 0, 3, None, down),
        ycopy(2, 1, 4, None, up), ycopy(3, 1, 5, None, down),
        ycopy(4, 2, 6, 0, up), ycopy(5, 3, 6, 1, down),
        ycopy(6, 4, 7, 0, up), ycopy(7, 5, 7, 1, down),
    ]
    for unit in range(2):
        load_stream[unit].wait()
        norm(unit)
        if unit == 0:
            pl.semaphore_wait(barrier, 22)
            load_w.start()
            for p in range(3):
                for i in range(2):
                    wz_copy(p, i, zl).start()
        y_copies[2 * unit].start()
        y_copies[2 * unit + 1].start()

    def unit_row(j):
        return (j & 128) + ((j >> 2) & 3) * 32 + ((j >> 4) & 7) * 4 + (j & 3)

    r_i = lax.broadcasted_iota(jnp.int32, (256, 256), 0)
    c_i = lax.broadcasted_iota(jnp.int32, (256, 256), 1)
    perm[...] = (unit_row(r_i) == c_i).astype(BF)
    perm_t[...] = (unit_row(c_i) == r_i).astype(BF)
    lane = lax.broadcasted_iota(jnp.int32, (1, 256), 1)

    def clip_of(f, found):
        return jnp.where((lane >> 2) == f, clip_ref[f], found)

    key = lax.fori_loop(0, 64, clip_of, jnp.zeros((1, 256), jnp.int32)) * 4 + (lane & 3)
    key = jnp.broadcast_to(key.astype(F32), (256, 256))
    mask[...] = jnp.where(key == key.T, 0.0, -1e30).astype(F32)

    def project_part(b, pz, part):
        k, n = batches[b]
        kk = (pz + hz) % 2
        slot = kk * 2 + (1 - kk) * zl
        x = xg[k:k + n].reshape(n * 128, 3072)
        out = dot(x, wbuf[pz, part].reshape(3072, 256)).astype(BF)
        qkv[slot, part, k:k + n] = out.reshape(n, 128, 256)

    def zcopy(b, part, slot):
        k, n = batches[b]
        units = pl.ds(k, n)
        return rcopy(qkv.at[2, part, units], qkv.at[slot, part, units], z_send.at[b, part],
                     z_recv.at[b, part], (tm, partner_row))

    def project(b):
        @pl.loop(0, 3)
        def _(part):
            project_part(b, 1 - hz, part)
            zcopy(b, part, zl).start()

        @pl.loop(0, 3)
        def _(part):
            project_part(b, hz, part)

    def stage_part(b, zz, part):
        k, n = batches[b]
        rows = qkv[zz, part, k:k + n].reshape(n * 128, 256)
        moved = dot(perm[:n * 128, :n * 128], rows).astype(BF).reshape(n, 8, 16, 256)
        for i in range(n):
            tsend[pl.ds(zz * 8, 8), k + i, part] = moved[i]

    def send_time(b, zz):
        k, n = batches[b]
        units = pl.ds(k, n)
        for dx in (1, 3, 2, 0):
            for dz in (1, 0):
                t = xs[dx] * 4 + zs[dz] * 2 + zz
                at = zz * 8 + xs[dx] * 2 + zs[dz]

                def send(t=t, at=at, dz=dz):
                    rcopy(tsend.at[at, units], trecv.at[tm, units], t_send.at[b], t_recv.at[b],
                          (t, rows_of[dz])).start()

                def keep(at=at):
                    trecv[tm, k:k + n] = tsend[at, k:k + n]

                if (dx, dz) == (0, 0):
                    pl.when(zz != core)(send)
                    pl.when(zz == core)(keep)
                else:
                    send()

    def stage_own(b):
        @pl.loop(0, 3)
        def _(part):
            stage_part(b, zl, part)

        send_time(b, zl)

    def stage_partner(b):
        @pl.loop(0, 3)
        def _(part):
            zcopy(b, part, oz).wait_recv()
            stage_part(b, oz, part)

        send_time(b, oz)

    factor = LOG2E / math.sqrt(HD)

    def attend(s, v):
        p = jnp.exp2((s - jnp.max(s, axis=-1, keepdims=True)) * factor).astype(BF)
        out = dot(p, jnp.concatenate([v, jnp.ones(v.shape, BF)], axis=1))
        return out[:, :HD] / out[:, HD:]

    def temporal(b):
        k, n = batches[b]
        units = pl.ds(k, n)
        await_bytes(trecv.at[pl.ds(0, 15), units], t_recv.at[b])
        for u in range(k, k + n):
            for h in range(2):
                cols = slice(h * HD, (h + 1) * HD)
                q, kk, v = (trecv[:, u, part, :, cols].reshape(256, HD) for part in range(3))
                o = attend(dot_nt(q, kk) + mask[...], v)
                osend[:, u, :, cols] = o.astype(BF).reshape(16, 16, HD)
        orecv[me_at, k:k + n] = osend[tm, k:k + n]
        for o in offsets:
            dev, _ = peer(*o)
            rcopy(osend.at[dev[0], units], orecv.at[me_at, units], o_send.at[b], o_recv.at[b], dev).start()

    def wait_back(b):
        k, n = batches[b]
        await_bytes(orecv.at[pl.ds(0, 15), pl.ds(k, n)], o_recv.at[b])

    def spatial(k):
        @pl.loop(0, 2)
        def _(pair):
            for f in range(2):
                rows = pl.ds(pl.multiple_of(pair * 64 + f * 32, 32), 32)
                for h in range(2):
                    cols = slice(h * HD, (h + 1) * HD)
                    q = qkv[0:2, 0, k:k + 2, rows, cols].reshape(128, HD)
                    kk, v = (qkv[0:2, part, :, rows, cols].reshape(512, HD) for part in (1, 2))
                    sp[:, k:k + 2, rows, cols] = attend(dot_nt(q, kk), v).reshape(2, 2, 32, HD)

    def ccopy(u, r, at, kept):
        half = half_of[u]
        return rcopy(csend.at[u, r % 2], comb.at[kept, half], c_send.at[u, r % 2], c_recv.at[at, half],
                     (tm, r))

    def combine(*units):
        for u in units:
            back = dot(perm_t[...], orecv[:, u].reshape(256, 256)).reshape(2, 128, 256)
            csend[u] = (sp[:, u] + back).astype(BF)
        for u in units:
            if u < 2:
                ccopy(u, partner_row, row, y * 2 + hz).start()
                comb[y * 2 + hz, u] = csend[u, zl]
            else:
                for zz in range(2):
                    ccopy(u, y_of[u] * 2 + zz, row, y * 2 + hz).start()

    def project_out(pair, first, last=True):
        for ys in pair:
            for i in range(2):
                r = ys * 2 + i
                for half in range(2):
                    def wait(r=r, half=half, ys=ys):
                        dst = comb.at[ys * 2 + (r + zh) % 2, half]
                        rcopy(csend.at[0, 0], dst, c_send.at[0, 0], c_recv.at[r, half], (tm, r)).wait_recv()
                    if ys is y:
                        pl.when(i != zl)(wait)
                    else:
                        wait()

        @pl.loop(0, 6)
        def _(n):
            cols = pl.ds(pl.multiple_of(n * 512, 512), 512)
            heads = [2 * ys + i for ys in pair for i in range(2)]
            left = jnp.concatenate([comb[h].reshape(256, 256) for h in heads], axis=1)
            right = jnp.concatenate([wo[h, :, cols] for h in heads], axis=0)
            acc = dot(left, right)
            for half in range(2):
                for f in range(4):
                    at = (half * 4 + f) * 32
                    rows = slice(half * 32, (half + 1) * 32)
                    piece = acc[at:at + 32]
                    if not first:
                        piece = piece + out_ref[f, rows, cols]
                    if not first and last:
                        clip = clip_ref[tm * 4 + f]
                        piece = piece * mod_ref[2, pl.ds(clip, 1), cols]
                    out_ref[f, rows, cols] = piece

    load_w.wait()
    for p in range(3):
        for i in range(2):
            wz_copy(p, i, oz).wait_recv()
            wx_copy(p, i, e_own).start()
        wc_copy(p, 0, e_own).start()
        project_part(0, zl, p)
    def hand_over(p):
        zcopy(0, p, zl).start()

    pl.when(zh == 0)(lambda: stage_own(0))
    for p in range(3):
        pl.when(zh == 1)(lambda p=p: hand_over(p))

    def pass_x(p):
        for i in range(2):
            wx_copy(p, i, e_x).wait_recv()
        wc_copy(p, 1, e_x).start()

    pass_x(0)
    pass_x(1)
    for p in range(3):
        for j in range(2):
            wc_copy(p, j, e_cores[j]).wait_recv()
        project_part(0, oz, p)
        pl.when(zh == 0)(lambda p=p: hand_over(p))
        if p == 0:
            pass_x(2)
    load_wo.start()
    for i in range(2):
        y_copies[i].wait_recv()
        y_copies[4 + i].start()
    pl.when(zh == 1)(lambda: stage_own(0))
    project(1)
    stage_own(1)
    stage_partner(0)

    for i in range(2):
        y_copies[2 + i].wait_recv()
        y_copies[6 + i].start()
    project(2)
    stage_own(2)
    stage_partner(1)
    temporal(0)

    y_copies[4].wait_recv()
    y_copies[5].wait_recv()
    project(3)
    stage_own(3)
    stage_partner(2)
    temporal(1)
    stage_partner(3)

    y_copies[6].wait_recv()
    y_copies[7].wait_recv()
    project(4)
    stage_own(4)
    temporal(2)
    temporal(3)
    stage_partner(4)

    spatial(2)
    wait_back(1)
    combine(2, 3)
    spatial(4)
    wait_back(2)
    combine(4, 5)
    temporal(4)
    spatial(6)
    wait_back(3)
    combine(6)
    spatial(0)
    wait_back(0)
    combine(0, 1)
    wait_back(4)
    combine(7)
    load_wo.wait()
    project_out((yp, ym), first=True)
    project_out((y,), first=False, last=False)
    project_out((yq,), first=False)

    for p in range(3):
        for i in range(2):
            wz_copy(p, i, zl).wait_send()
            wx_copy(p, i, e_own).wait_send()
            wc_copy(p, i, e_own).wait_send()
    for c in y_copies:
        c.wait_send()
    for b, (k, n) in enumerate(batches):
        for part in range(3):
            zcopy(b, part, zl).wait_send()
        await_bytes(tsend.at[pl.ds(0, 15), pl.ds(k, n)], t_send.at[b])
        await_bytes(osend.at[pl.ds(0, 15), pl.ds(k, n)], o_send.at[b])
    for u in range(8):
        if u < 2:
            ccopy(u, partner_row, row, y * 2 + hz).wait_send()
        else:
            for zz in range(2):
                ccopy(u, y_of[u] * 2 + zz, row, y * 2 + hz).wait_send()


def attention(clip_ids, stream, mod, weight, out_weight):
    vmem = pl.BlockSpec(memory_space=pltpu.VMEM)
    hbm = pl.BlockSpec(memory_space=pl.ANY)
    dma = pltpu.SemaphoreType.DMA
    return pl.pallas_call(
        attention_kernel,
        out_shape=pltpu.VMEM((4, 64, 3072), F32),
        in_specs=[pl.BlockSpec(memory_space=pltpu.SMEM), hbm, vmem, hbm, hbm],
        out_specs=vmem,
        scratch_shapes=[
            pltpu.VMEM((4, 64, 3072), F32),
            pltpu.VMEM((8, 128, 3072), BF),
            pltpu.VMEM((2, 3, 8, 384, 256), BF),
            pltpu.VMEM((8, 256, 3072), BF),
            pltpu.VMEM((3, 3, 8, 128, 256), BF),
            pltpu.VMEM((16, 8, 3, 16, 256), BF),
            pltpu.VMEM((16, 8, 3, 16, 256), BF),
            pltpu.VMEM((16, 8, 16, 256), BF),
            pltpu.VMEM((16, 8, 16, 256), BF),
            pltpu.VMEM((8, 2, 128, 256), BF),
            pltpu.VMEM((8, 2, 128, 256), BF),
            pltpu.VMEM((2, 8, 128, 256), F32),
            pltpu.VMEM((256, 256), BF),
            pltpu.VMEM((256, 256), BF),
            pltpu.VMEM((256, 256), F32),
            dma((4,)),
            dma((8,)), dma((8,)),
            dma((3, 2)), dma((3, 2)),
            dma((3, 2)), dma((3, 2)),
            dma((3, 2)), dma((3, 2)),
            dma((5, 3)), dma((5, 3)),
            dma((5,)), dma((5,)),
            dma((5,)), dma((5,)),
            dma((8, 2)), dma((8, 2)),
        ],
        compiler_params=pltpu.CompilerParams(
            collective_id=0, has_side_effects=True, vmem_limit_bytes=60 * 1024 * 1024
        ),
        name="attention",
    )(clip_ids, stream, mod, weight, out_weight)


def per_device(stream, clip_ids, modulation, qkv_weight, out_weight):
    mod = jnp.transpose(modulation, (1, 0, 2))
    weight = jnp.transpose(qkv_weight, (1, 0, 2)).reshape(3, 8, 384, 256)
    return attention(clip_ids, stream, mod, weight, out_weight.reshape(8, 256, 3072))


def solution(mesh):
    placed = (P("tm", "row", None), P(), P(), P(None, None, "row"), P())
    return jax.shard_map(
        per_device, mesh=mesh, in_specs=placed, out_specs=P("tm", "row", None), check_vma=False
    )
```

```python
import math

import jax
import jax.numpy as jnp
from jax import lax
from jax.experimental import pallas as pl
from jax.experimental.pallas import tpu as pltpu
from jax.sharding import PartitionSpec as P

HD = 128
MESH = pl.DeviceIdType.MESH
BF = jnp.bfloat16
F32 = jnp.float32
LOG2E = 1.4426950408889634


def dot(a, b):
    return jnp.dot(a, b, preferred_element_type=F32)


def dot_nt(a, b):
    return lax.dot_general(a, b, (((1,), (1,)), ((), ())), preferred_element_type=F32)


def attention_kernel(
    clip_ref, stream_hbm, mod_ref, w_hbm, wo_hbm, out_ref,
    stream_v, xg, wbuf, wo, qkv, tsend, trecv, osend, orecv, csend, comb, sp, perm, perm_t, mask,
    load_sem, y_send, y_recv, wz_send, wz_recv, wx_send, wx_recv, wc_send, wc_recv, z_send, z_recv,
    t_send, t_recv, o_send, o_recv, c_send, c_recv,
):
    batches = ((0, 2), (2, 2), (4, 2), (6, 1), (7, 1))
    tm = lax.axis_index("tm")
    row = lax.axis_index("row")
    zh = (tm // 2) % 2
    core = tm % 2
    y = row // 2
    zl = row % 2
    hz = (zl + zh) % 2
    oz = 1 - zl
    partner_row = y * 2 + oz
    outer_tm = tm + 2 - 4 * zh
    other_core = tm + 1 - 2 * core
    ym, yp, yq = (y + 3) % 4, (y + 1) % 4, (y + 2) % 4
    up, down = (tm, yp * 2 + zl), (tm, ym * 2 + zl)
    y_of = (y, y, ym, yp, ym, yp, yq, yq)
    half_of = (0, 1, 0, 0, 1, 1, 0, 1)

    def rcopy(src, dst, send, recv, dev):
        return pltpu.make_async_remote_copy(
            src_ref=src, dst_ref=dst, send_sem=send, recv_sem=recv,
            device_id=dev, device_id_type=MESH,
        )

    def await_bytes(ref, sem):
        pltpu.make_async_copy(ref, ref, sem).wait()

    x = tm // 4
    xs = [((x + d) % 4) for d in range(4)]
    zs = [zh, 1 - zh]
    cs = [core, 1 - core]
    rows_of = [y * 2 + (hz + zh) % 2, y * 2 + (hz + 1 - zh) % 2]
    offsets = [(dx, dz, dc) for dx in (1, 3, 2, 0) for dz in range(2) for dc in range(2)][:-4]
    offsets = offsets + [(0, 1, 0), (0, 1, 1), (0, 0, 1)]
    me_at = core * 8 + x * 2 + zh

    def peer(dx, dz, dc):
        t = xs[dx] * 4 + zs[dz] * 2 + cs[dc]
        return (t, rows_of[dz]), cs[dc] * 8 + xs[dx] * 2 + zs[dz]

    load_stream = [
        pltpu.make_async_copy(stream_hbm.at[:, pl.ds(32 * u, 32)], stream_v.at[:, pl.ds(32 * u, 32)],
                              load_sem.at[u])
        for u in range(2)
    ]
    load_w = pltpu.make_async_copy(w_hbm, wbuf.at[zl], load_sem.at[2])
    load_wo = pltpu.make_async_copy(wo_hbm, wo, load_sem.at[3])
    for c in load_stream:
        c.start()

    barrier = pltpu.get_barrier_semaphore()
    for o in offsets:
        pl.semaphore_signal(barrier, inc=1, device_id=peer(*o)[0], device_id_type=MESH)
    row_peers = [(tm, r * 2 + (zl if i == 0 else oz)) for r in (y, ym, yp, yq) for i in range(2)][1:]
    for dev in row_peers:
        pl.semaphore_signal(barrier, inc=1, device_id=dev, device_id_type=MESH)

    x_par = x % 2
    x_up, x_down = (tm + 4) % 16, (tm + 12) % 16
    e_own = core * 4 + x_par * 2
    e_x = core * 4 + (1 - x_par) * 2
    e_cores = ((1 - core) * 4 + x_par * 2, (1 - core) * 4 + (1 - x_par) * 2)

    def wz_copy(p, i, side):
        dev = ((tm, partner_row), (outer_tm, partner_row))[i]
        return rcopy(w_hbm.at[p, e_own + i], wbuf.at[side, p, e_own + i],
                     wz_send.at[p, i], wz_recv.at[p, i], dev)

    def wx_copy(p, i, e):
        dev = ((x_up, row), (x_down, row))[i]
        return rcopy(wbuf.at[oz, p, e + i], wbuf.at[oz, p, e + i],
                     wx_send.at[p, i], wx_recv.at[p, i], dev)

    def wc_copy(p, j, e):
        pair = wbuf.at[oz, p, pl.ds(e, 2)]
        return rcopy(pair, pair, wc_send.at[p, j], wc_recv.at[p, j], (other_core, row))


    def norm(unit):
        @pl.loop(0, 4)
        def _(f):
            clip = clip_ref[tm * 4 + f]
            shift = mod_ref[0, pl.ds(clip, 1), :]
            scale = 1.0 + mod_ref[1, pl.ds(clip, 1), :]
            v = stream_v[f, pl.ds(unit * 32, 32), :]
            centred = v - jnp.mean(v, axis=-1, keepdims=True)
            var = jnp.mean(centred * centred, axis=-1, keepdims=True)
            n = centred * lax.rsqrt(var + 1e-06) * scale + shift
            xg[unit, pl.ds(f * 32, 32), :] = n.astype(BF)

    def ycopy(i, src, dst, half, dev):
        if half is None:
            return rcopy(xg.at[src], xg.at[dst], y_send.at[i], y_recv.at[i], dev)
        rows = pl.ds(half * 64, 64)
        return rcopy(xg.at[src, rows], xg.at[dst, rows], y_send.at[i], y_recv.at[i], dev)

    y_copies = [
        ycopy(0, 0, 2, None, up), ycopy(1, 0, 3, None, down),
        ycopy(2, 1, 4, None, up), ycopy(3, 1, 5, None, down),
        ycopy(4, 2, 6, 0, up), ycopy(5, 3, 6, 1, down),
        ycopy(6, 4, 7, 0, up), ycopy(7, 5, 7, 1, down),
    ]
    for unit in range(2):
        load_stream[unit].wait()
        norm(unit)
        if unit == 0:
            pl.semaphore_wait(barrier, 22)
            load_w.start()
            for p in range(3):
                for i in range(2):
                    wz_copy(p, i, zl).start()
        y_copies[2 * unit].start()
        y_copies[2 * unit + 1].start()

    def unit_row(j):
        return (j & 128) + ((j >> 2) & 3) * 32 + ((j >> 4) & 7) * 4 + (j & 3)

    r_i = lax.broadcasted_iota(jnp.int32, (256, 256), 0)
    c_i = lax.broadcasted_iota(jnp.int32, (256, 256), 1)
    perm[...] = (unit_row(r_i) == c_i).astype(BF)
    perm_t[...] = (unit_row(c_i) == r_i).astype(BF)
    lane = lax.broadcasted_iota(jnp.int32, (1, 256), 1)

    def clip_of(f, found):
        return jnp.where((lane >> 2) == f, clip_ref[f], found)

    key = lax.fori_loop(0, 64, clip_of, jnp.zeros((1, 256), jnp.int32)) * 4 + (lane & 3)
    key = jnp.broadcast_to(key.astype(F32), (256, 256))
    mask[...] = jnp.where(key == key.T, 0.0, -1e30).astype(F32)

    def project_part(b, pz, part):
        k, n = batches[b]
        kk = (pz + hz) % 2
        slot = kk * 2 + (1 - kk) * zl
        x = xg[k:k + n].reshape(n * 128, 3072)
        out = dot(x, wbuf[pz, part].reshape(3072, 256)).astype(BF)
        qkv[slot, part, k:k + n] = out.reshape(n, 128, 256)

    def zcopy(b, part, slot):
        k, n = batches[b]
        units = pl.ds(k, n)
        return rcopy(qkv.at[2, part, units], qkv.at[slot, part, units], z_send.at[b, part],
                     z_recv.at[b, part], (tm, partner_row))

    def project(b):
        def sent(part):
            project_part(b, 1 - hz, part)
            zcopy(b, part, zl).start()

        def kept(part):
            project_part(b, hz, part)

        for step in (sent, kept):
            if b == 4:
                for part in range(3):
                    step(part)
            else:
                pl.loop(0, 3)(step)

    def stage_part(b, zz, part):
        k, n = batches[b]
        rows = qkv[zz, part, k:k + n].reshape(n * 128, 256)
        moved = dot(perm[:n * 128, :n * 128], rows).astype(BF).reshape(n, 8, 16, 256)
        for i in range(n):
            tsend[pl.ds(zz * 8, 8), k + i, part] = moved[i]

    def send_time(b, zz):
        k, n = batches[b]
        units = pl.ds(k, n)
        for dx in (1, 3, 2, 0):
            for dz in (1, 0):
                t = xs[dx] * 4 + zs[dz] * 2 + zz
                at = zz * 8 + xs[dx] * 2 + zs[dz]

                def send(t=t, at=at, dz=dz):
                    rcopy(tsend.at[at, units], trecv.at[tm, units], t_send.at[b], t_recv.at[b],
                          (t, rows_of[dz])).start()

                def keep(at=at):
                    trecv[tm, k:k + n] = tsend[at, k:k + n]

                if (dx, dz) == (0, 0):
                    pl.when(zz != core)(send)
                    pl.when(zz == core)(keep)
                else:
                    send()

    def stage_own(b):
        @pl.loop(0, 3)
        def _(part):
            stage_part(b, zl, part)

        send_time(b, zl)

    def stage_partner(b):
        @pl.loop(0, 3)
        def _(part):
            zcopy(b, part, oz).wait_recv()
            stage_part(b, oz, part)

        send_time(b, oz)

    factor = LOG2E / math.sqrt(HD)

    def attend(s, v):
        p = jnp.exp2((s - jnp.max(s, axis=-1, keepdims=True)) * factor).astype(BF)
        out = dot(p, jnp.concatenate([v, jnp.ones(v.shape, BF)], axis=1))
        return out[:, :HD] / out[:, HD:]

    def temporal(b):
        k, n = batches[b]
        units = pl.ds(k, n)
        await_bytes(trecv.at[pl.ds(0, 15), units], t_recv.at[b])
        for u in range(k, k + n):
            for h in range(2):
                cols = slice(h * HD, (h + 1) * HD)
                q, kk, v = (trecv[:, u, part, :, cols].reshape(256, HD) for part in range(3))
                o = attend(dot_nt(q, kk) + mask[...], v)
                osend[:, u, :, cols] = o.astype(BF).reshape(16, 16, HD)
        orecv[me_at, k:k + n] = osend[tm, k:k + n]
        for o in offsets:
            dev, _ = peer(*o)
            rcopy(osend.at[dev[0], units], orecv.at[me_at, units], o_send.at[b], o_recv.at[b], dev).start()

    def wait_back(b):
        k, n = batches[b]
        await_bytes(orecv.at[pl.ds(0, 15), pl.ds(k, n)], o_recv.at[b])

    def spatial(ka, kb):
        @pl.loop(0, 2)
        def _(pair):
            for f in range(2):
                rows = pl.ds(pl.multiple_of(pair * 64 + f * 32, 32), 32)
                for h in range(2):
                    cols = slice(h * HD, (h + 1) * HD)
                    q = jnp.concatenate(
                        [qkv[0:2, 0, k:k + 2, rows, cols].reshape(128, HD) for k in (ka, kb)], axis=0)
                    kk, v = (qkv[0:2, part, :, rows, cols].reshape(512, HD) for part in (1, 2))
                    o = attend(dot_nt(q, kk), v).reshape(2, 2, 2, 32, HD)
                    sp[:, ka:ka + 2, rows, cols] = o[0]
                    sp[:, kb:kb + 2, rows, cols] = o[1]

    def ccopy(u, r, at, kept):
        half = half_of[u]
        return rcopy(csend.at[u, r % 2], comb.at[kept, half], c_send.at[u, r % 2], c_recv.at[at, half],
                     (tm, r))

    def combine(*units):
        for u in units:
            back = dot(perm_t[...], orecv[:, u].reshape(256, 256)).reshape(2, 128, 256)
            csend[u] = (sp[:, u] + back).astype(BF)
        for u in units:
            if u < 2:
                ccopy(u, partner_row, row, y * 2 + hz).start()
                comb[y * 2 + hz, u] = csend[u, zl]
            else:
                for zz in range(2):
                    ccopy(u, y_of[u] * 2 + zz, row, y * 2 + hz).start()

    def project_out(pair, first):
        for ys in pair:
            for i in range(2):
                r = ys * 2 + i
                for half in range(2):
                    def wait(r=r, half=half, ys=ys):
                        dst = comb.at[ys * 2 + (r + zh) % 2, half]
                        rcopy(csend.at[0, 0], dst, c_send.at[0, 0], c_recv.at[r, half], (tm, r)).wait_recv()
                    if ys is y:
                        pl.when(i != zl)(wait)
                    else:
                        wait()

        heads = [2 * ys + i for ys in pair for i in range(2)]

        def tile(cols):
            left = jnp.concatenate([comb[h].reshape(256, 256) for h in heads], axis=1)
            right = jnp.concatenate([wo[h, :, cols] for h in heads], axis=0)
            acc = dot(left, right)
            for half in range(2):
                for f in range(4):
                    at = (half * 4 + f) * 32
                    rows = slice(half * 32, (half + 1) * 32)
                    piece = acc[at:at + 32]
                    if not first:
                        clip = clip_ref[tm * 4 + f]
                        piece = (piece + out_ref[f, rows, cols]) * mod_ref[2, pl.ds(clip, 1), cols]
                    out_ref[f, rows, cols] = piece

        @pl.loop(0, 3)
        def _(n):
            for i in range(2):
                tile(pl.ds(pl.multiple_of(n * 1024 + i * 512, 512), 512))

    load_w.wait()
    for p in range(3):
        for i in range(2):
            wz_copy(p, i, oz).wait_recv()
            wx_copy(p, i, e_own).start()
        wc_copy(p, 0, e_own).start()
        project_part(0, zl, p)
    def pass_x(p):
        for i in range(2):
            wx_copy(p, i, e_x).wait_recv()
        wc_copy(p, 1, e_x).start()

    pass_x(0)
    pass_x(1)
    for p in range(3):
        for j in range(2):
            wc_copy(p, j, e_cores[j]).wait_recv()
        project_part(0, oz, p)
        zcopy(0, p, zl).start()
        if p == 0:
            pass_x(2)
    load_wo.start()
    for i in range(2):
        y_copies[i].wait_recv()
        y_copies[4 + i].start()
    stage_own(0)
    project(1)
    stage_own(1)
    stage_partner(0)

    for i in range(2):
        y_copies[2 + i].wait_recv()
        y_copies[6 + i].start()
    project(2)
    stage_own(2)
    stage_partner(1)
    temporal(0)

    y_copies[4].wait_recv()
    y_copies[5].wait_recv()
    project(3)
    stage_own(3)
    stage_partner(2)
    temporal(1)
    stage_partner(3)

    y_copies[6].wait_recv()
    y_copies[7].wait_recv()
    project(4)
    stage_own(4)
    temporal(2)
    temporal(3)
    stage_partner(4)

    spatial(2, 4)
    wait_back(1)
    combine(2, 3)
    wait_back(2)
    combine(4, 5)
    temporal(4)
    spatial(6, 0)
    wait_back(3)
    wait_back(0)
    combine(6, 0, 1)
    wait_back(4)
    combine(7)
    load_wo.wait()
    project_out((yp, ym), first=True)
    project_out((y, yq), first=False)

    for p in range(3):
        for i in range(2):
            wz_copy(p, i, zl).wait_send()
            wx_copy(p, i, e_own).wait_send()
            wc_copy(p, i, e_own).wait_send()
    for c in y_copies:
        c.wait_send()
    for b, (k, n) in enumerate(batches):
        for part in range(3):
            zcopy(b, part, zl).wait_send()
        await_bytes(tsend.at[pl.ds(0, 15), pl.ds(k, n)], t_send.at[b])
        await_bytes(osend.at[pl.ds(0, 15), pl.ds(k, n)], o_send.at[b])
    for u in range(8):
        if u < 2:
            ccopy(u, partner_row, row, y * 2 + hz).wait_send()
        else:
            for zz in range(2):
                ccopy(u, y_of[u] * 2 + zz, row, y * 2 + hz).wait_send()


def attention(clip_ids, stream, mod, weight, out_weight):
    vmem = pl.BlockSpec(memory_space=pltpu.VMEM)
    hbm = pl.BlockSpec(memory_space=pl.ANY)
    dma = pltpu.SemaphoreType.DMA
    return pl.pallas_call(
        attention_kernel,
        out_shape=pltpu.VMEM((4, 64, 3072), F32),
        in_specs=[pl.BlockSpec(memory_space=pltpu.SMEM), hbm, vmem, hbm, hbm],
        out_specs=vmem,
        scratch_shapes=[
            pltpu.VMEM((4, 64, 3072), F32),
            pltpu.VMEM((8, 128, 3072), BF),
            pltpu.VMEM((2, 3, 8, 384, 256), BF),
            pltpu.VMEM((8, 256, 3072), BF),
            pltpu.VMEM((3, 3, 8, 128, 256), BF),
            pltpu.VMEM((16, 8, 3, 16, 256), BF),
            pltpu.VMEM((16, 8, 3, 16, 256), BF),
            pltpu.VMEM((16, 8, 16, 256), BF),
            pltpu.VMEM((16, 8, 16, 256), BF),
            pltpu.VMEM((8, 2, 128, 256), BF),
            pltpu.VMEM((8, 2, 128, 256), BF),
            pltpu.VMEM((2, 8, 128, 256), F32),
            pltpu.VMEM((256, 256), BF),
            pltpu.VMEM((256, 256), BF),
            pltpu.VMEM((256, 256), F32),
            dma((4,)),
            dma((8,)), dma((8,)),
            dma((3, 2)), dma((3, 2)),
            dma((3, 2)), dma((3, 2)),
            dma((3, 2)), dma((3, 2)),
            dma((5, 3)), dma((5, 3)),
            dma((5,)), dma((5,)),
            dma((5,)), dma((5,)),
            dma((8, 2)), dma((8, 2)),
        ],
        compiler_params=pltpu.CompilerParams(
            collective_id=0, has_side_effects=True, vmem_limit_bytes=60 * 1024 * 1024
        ),
        name="attention",
    )(clip_ids, stream, mod, weight, out_weight)


def per_device(stream, clip_ids, modulation, qkv_weight, out_weight):
    mod = jnp.transpose(modulation, (1, 0, 2))
    weight = jnp.transpose(qkv_weight, (1, 0, 2)).reshape(3, 8, 384, 256)
    return attention(clip_ids, stream, mod, weight, out_weight.reshape(8, 256, 3072))


def solution(mesh):
    placed = (P("tm", "row", None), P(), P(), P(None, None, "row"), P())
    return jax.shard_map(
        per_device, mesh=mesh, in_specs=placed, out_specs=P("tm", "row", None), check_vma=False
    )
```

```python
import math

import jax
import jax.numpy as jnp
from jax import lax
from jax.experimental import pallas as pl
from jax.experimental.pallas import tpu as pltpu
from jax.sharding import PartitionSpec as P

HD = 128
MESH = pl.DeviceIdType.MESH
BF = jnp.bfloat16
F32 = jnp.float32
LOG2E = 1.4426950408889634


def dot(a, b):
    return jnp.dot(a, b, preferred_element_type=F32)


def dot_nt(a, b):
    return lax.dot_general(a, b, (((1,), (1,)), ((), ())), preferred_element_type=F32)


def attention_kernel(
    clip_ref, stream_hbm, mod_ref, w_hbm, wo_hbm, out_ref,
    stream_v, xg, wbuf, wo, qkv, tsend, trecv, osend, orecv, csend, comb, sp, perm, perm_t, mask,
    load_sem, y_send, y_recv, wz_send, wz_recv, wx_send, wx_recv, wc_send, wc_recv, z_send, z_recv,
    t_send, t_recv, o_send, o_recv, c_send, c_recv,
):
    batches = ((0, 2), (2, 2), (4, 2), (6, 1), (7, 1))
    tm = lax.axis_index("tm")
    row = lax.axis_index("row")
    zh = (tm // 2) % 2
    core = tm % 2
    y = row // 2
    zl = row % 2
    hz = (zl + zh) % 2
    oz = 1 - zl
    partner_row = y * 2 + oz
    outer_tm = tm + 2 - 4 * zh
    other_core = tm + 1 - 2 * core
    ym, yp, yq = (y + 3) % 4, (y + 1) % 4, (y + 2) % 4
    up, down = (tm, yp * 2 + zl), (tm, ym * 2 + zl)
    y_of = (y, y, ym, yp, ym, yp, yq, yq)
    half_of = (0, 1, 0, 0, 1, 1, 0, 1)

    def rcopy(src, dst, send, recv, dev):
        return pltpu.make_async_remote_copy(
            src_ref=src, dst_ref=dst, send_sem=send, recv_sem=recv,
            device_id=dev, device_id_type=MESH,
        )

    def await_bytes(ref, sem):
        pltpu.make_async_copy(ref, ref, sem).wait()

    x = tm // 4
    xs = [((x + d) % 4) for d in range(4)]
    zs = [zh, 1 - zh]
    cs = [core, 1 - core]
    rows_of = [y * 2 + (hz + zh) % 2, y * 2 + (hz + 1 - zh) % 2]
    offsets = [(dx, dz, dc) for dx in (1, 3, 2, 0) for dz in range(2) for dc in range(2)][:-4]
    offsets = offsets + [(0, 1, 0), (0, 1, 1), (0, 0, 1)]
    me_at = core * 8 + x * 2 + zh

    def peer(dx, dz, dc):
        t = xs[dx] * 4 + zs[dz] * 2 + cs[dc]
        return (t, rows_of[dz]), cs[dc] * 8 + xs[dx] * 2 + zs[dz]

    load_stream = [
        pltpu.make_async_copy(stream_hbm.at[:, pl.ds(32 * u, 32)], stream_v.at[:, pl.ds(32 * u, 32)],
                              load_sem.at[u])
        for u in range(2)
    ]
    load_w = pltpu.make_async_copy(w_hbm, wbuf.at[zl], load_sem.at[2])
    load_wo = pltpu.make_async_copy(wo_hbm, wo, load_sem.at[3])
    for c in load_stream:
        c.start()

    barrier = pltpu.get_barrier_semaphore()
    for o in offsets:
        pl.semaphore_signal(barrier, inc=1, device_id=peer(*o)[0], device_id_type=MESH)
    row_peers = [(tm, r * 2 + (zl if i == 0 else oz)) for r in (y, ym, yp, yq) for i in range(2)][1:]
    for dev in row_peers:
        pl.semaphore_signal(barrier, inc=1, device_id=dev, device_id_type=MESH)

    x_par = x % 2
    x_up, x_down = (tm + 4) % 16, (tm + 12) % 16
    e_own = core * 4 + x_par * 2
    e_x = core * 4 + (1 - x_par) * 2
    e_cores = ((1 - core) * 4 + x_par * 2, (1 - core) * 4 + (1 - x_par) * 2)

    def wz_copy(p, i, side):
        dev = ((tm, partner_row), (outer_tm, partner_row))[i]
        return rcopy(w_hbm.at[p, e_own + i], wbuf.at[side, p, e_own + i],
                     wz_send.at[p, i], wz_recv.at[p, i], dev)

    def wx_copy(p, i, e):
        dev = ((x_up, row), (x_down, row))[i]
        return rcopy(wbuf.at[oz, p, e + i], wbuf.at[oz, p, e + i],
                     wx_send.at[p, i], wx_recv.at[p, i], dev)

    def wc_copy(p, j, e):
        pair = wbuf.at[oz, p, pl.ds(e, 2)]
        return rcopy(pair, pair, wc_send.at[p, j], wc_recv.at[p, j], (other_core, row))


    def norm(unit):
        @pl.loop(0, 4)
        def _(f):
            clip = clip_ref[tm * 4 + f]
            shift = mod_ref[0, pl.ds(clip, 1), :]
            scale = 1.0 + mod_ref[1, pl.ds(clip, 1), :]
            v = stream_v[f, pl.ds(unit * 32, 32), :]
            centred = v - jnp.mean(v, axis=-1, keepdims=True)
            var = jnp.mean(centred * centred, axis=-1, keepdims=True)
            n = centred * lax.rsqrt(var + 1e-06) * scale + shift
            xg[unit, pl.ds(f * 32, 32), :] = n.astype(BF)

    def ycopy(i, src, dst, half, dev):
        if half is None:
            return rcopy(xg.at[src], xg.at[dst], y_send.at[i], y_recv.at[i], dev)
        rows = pl.ds(half * 64, 64)
        return rcopy(xg.at[src, rows], xg.at[dst, rows], y_send.at[i], y_recv.at[i], dev)

    y_copies = [
        ycopy(0, 0, 2, None, up), ycopy(1, 0, 3, None, down),
        ycopy(2, 1, 4, None, up), ycopy(3, 1, 5, None, down),
        ycopy(4, 2, 6, 0, up), ycopy(5, 3, 6, 1, down),
        ycopy(6, 4, 7, 0, up), ycopy(7, 5, 7, 1, down),
    ]
    for unit in range(2):
        load_stream[unit].wait()
        norm(unit)
        if unit == 0:
            pl.semaphore_wait(barrier, 22)
            load_w.start()
            for p in range(3):
                for i in range(2):
                    wz_copy(p, i, zl).start()
        if unit == 0:
            y_copies[0].start()
            y_copies[1].start()

    def unit_row(j):
        return (j & 128) + ((j >> 2) & 3) * 32 + ((j >> 4) & 7) * 4 + (j & 3)

    r_i = lax.broadcasted_iota(jnp.int32, (256, 256), 0)
    c_i = lax.broadcasted_iota(jnp.int32, (256, 256), 1)
    perm[...] = (unit_row(r_i) == c_i).astype(BF)
    perm_t[...] = (unit_row(c_i) == r_i).astype(BF)
    lane = lax.broadcasted_iota(jnp.int32, (1, 256), 1)

    def clip_of(f, found):
        return jnp.where((lane >> 2) == f, clip_ref[f], found)

    key = lax.fori_loop(0, 64, clip_of, jnp.zeros((1, 256), jnp.int32)) * 4 + (lane & 3)
    key = jnp.broadcast_to(key.astype(F32), (256, 256))
    mask[...] = jnp.where(key == key.T, 0.0, -1e30).astype(F32)

    def project_part(b, pz, part):
        k, n = batches[b]
        kk = (pz + hz) % 2
        slot = kk * 2 + (1 - kk) * zl
        x = xg[k:k + n].reshape(n * 128, 3072)
        out = dot(x, wbuf[pz, part].reshape(3072, 256)).astype(BF)
        qkv[slot, part, k:k + n] = out.reshape(n, 128, 256)

    def zcopy(b, part, slot):
        k, n = batches[b]
        units = pl.ds(k, n)
        return rcopy(qkv.at[2, part, units], qkv.at[slot, part, units], z_send.at[b, part],
                     z_recv.at[b, part], (tm, partner_row))

    def project(b):
        def sent(part):
            project_part(b, 1 - hz, part)
            zcopy(b, part, zl).start()

        def kept(part):
            project_part(b, hz, part)

        for step in (sent, kept):
            if b == 4:
                for part in range(3):
                    step(part)
            else:
                pl.loop(0, 3)(step)

    def stage_part(b, zz, part):
        k, n = batches[b]
        rows = qkv[zz, part, k:k + n].reshape(n * 128, 256)
        moved = dot(perm[:n * 128, :n * 128], rows).astype(BF).reshape(n, 8, 16, 256)
        for i in range(n):
            tsend[pl.ds(zz * 8, 8), k + i, part] = moved[i]

    def send_time(b, zz):
        k, n = batches[b]
        units = pl.ds(k, n)
        for dx in (1, 3, 2, 0):
            for dz in (1, 0):
                t = xs[dx] * 4 + zs[dz] * 2 + zz
                at = zz * 8 + xs[dx] * 2 + zs[dz]

                def send(t=t, at=at, dz=dz):
                    rcopy(tsend.at[at, units], trecv.at[tm, units], t_send.at[b], t_recv.at[b],
                          (t, rows_of[dz])).start()

                def keep(at=at):
                    trecv[tm, k:k + n] = tsend[at, k:k + n]

                if (dx, dz) == (0, 0):
                    pl.when(zz != core)(send)
                    pl.when(zz == core)(keep)
                else:
                    send()

    def stage_own(b):
        @pl.loop(0, 3)
        def _(part):
            stage_part(b, zl, part)

        send_time(b, zl)

    def stage_partner(b):
        @pl.loop(0, 3)
        def _(part):
            zcopy(b, part, oz).wait_recv()
            stage_part(b, oz, part)

        send_time(b, oz)

    factor = LOG2E / math.sqrt(HD)

    def attend(s, v):
        p = jnp.exp2((s - jnp.max(s, axis=-1, keepdims=True)) * factor).astype(BF)
        out = dot(p, jnp.concatenate([v, jnp.ones(v.shape, BF)], axis=1))
        return out[:, :HD] / out[:, HD:]

    def temporal(b):
        k, n = batches[b]
        units = pl.ds(k, n)
        await_bytes(trecv.at[pl.ds(0, 15), units], t_recv.at[b])
        for u in range(k, k + n):
            for h in range(2):
                cols = slice(h * HD, (h + 1) * HD)
                q, kk, v = (trecv[:, u, part, :, cols].reshape(256, HD) for part in range(3))
                o = attend(dot_nt(q, kk) + mask[...], v)
                osend[:, u, :, cols] = o.astype(BF).reshape(16, 16, HD)
        orecv[me_at, k:k + n] = osend[tm, k:k + n]
        for o in offsets:
            dev, _ = peer(*o)
            rcopy(osend.at[dev[0], units], orecv.at[me_at, units], o_send.at[b], o_recv.at[b], dev).start()

    def wait_back(b):
        k, n = batches[b]
        await_bytes(orecv.at[pl.ds(0, 15), pl.ds(k, n)], o_recv.at[b])

    def spatial(ka, kb):
        @pl.loop(0, 2)
        def _(pair):
            for f in range(2):
                rows = pl.ds(pl.multiple_of(pair * 64 + f * 32, 32), 32)
                for h in range(2):
                    cols = slice(h * HD, (h + 1) * HD)
                    q = jnp.concatenate(
                        [qkv[0:2, 0, k:k + 2, rows, cols].reshape(128, HD) for k in (ka, kb)], axis=0)
                    kk, v = (qkv[0:2, part, :, rows, cols].reshape(512, HD) for part in (1, 2))
                    o = attend(dot_nt(q, kk), v).reshape(2, 2, 2, 32, HD)
                    sp[:, ka:ka + 2, rows, cols] = o[0]
                    sp[:, kb:kb + 2, rows, cols] = o[1]

    def ccopy(u, r, at, kept):
        half = half_of[u]
        return rcopy(csend.at[u, r % 2], comb.at[kept, half], c_send.at[u, r % 2], c_recv.at[at, half],
                     (tm, r))

    def combine(*units):
        for u in units:
            back = dot(perm_t[...], orecv[:, u].reshape(256, 256)).reshape(2, 128, 256)
            csend[u] = (sp[:, u] + back).astype(BF)
        for u in units:
            if u < 2:
                ccopy(u, partner_row, row, y * 2 + hz).start()
                comb[y * 2 + hz, u] = csend[u, zl]
            else:
                for zz in range(2):
                    ccopy(u, y_of[u] * 2 + zz, row, y * 2 + hz).start()

    def project_out(pair, first):
        for ys in pair:
            for i in range(2):
                r = ys * 2 + i
                for half in range(2):
                    def wait(r=r, half=half, ys=ys):
                        dst = comb.at[ys * 2 + (r + zh) % 2, half]
                        rcopy(csend.at[0, 0], dst, c_send.at[0, 0], c_recv.at[r, half], (tm, r)).wait_recv()
                    if ys is y:
                        pl.when(i != zl)(wait)
                    else:
                        wait()

        heads = [2 * ys + i for ys in pair for i in range(2)]

        def tile(cols):
            left = jnp.concatenate([comb[h].reshape(256, 256) for h in heads], axis=1)
            right = jnp.concatenate([wo[h, :, cols] for h in heads], axis=0)
            acc = dot(left, right)
            for half in range(2):
                for f in range(4):
                    at = (half * 4 + f) * 32
                    rows = slice(half * 32, (half + 1) * 32)
                    piece = acc[at:at + 32]
                    if not first:
                        clip = clip_ref[tm * 4 + f]
                        piece = (piece + out_ref[f, rows, cols]) * mod_ref[2, pl.ds(clip, 1), cols]
                    out_ref[f, rows, cols] = piece

        @pl.loop(0, 3)
        def _(n):
            for i in range(2):
                tile(pl.ds(pl.multiple_of(n * 1024 + i * 512, 512), 512))

    load_w.wait()
    for p in range(3):
        for i in range(2):
            wz_copy(p, i, oz).wait_recv()
            wx_copy(p, i, e_own).start()
        wc_copy(p, 0, e_own).start()
        project_part(0, zl, p)
    y_copies[2].start()
    y_copies[3].start()

    def pass_x(p):
        for i in range(2):
            wx_copy(p, i, e_x).wait_recv()
        wc_copy(p, 1, e_x).start()

    pass_x(0)
    pass_x(1)
    for p in range(3):
        for j in range(2):
            wc_copy(p, j, e_cores[j]).wait_recv()
        project_part(0, oz, p)
        zcopy(0, p, zl).start()
        if p == 0:
            pass_x(2)
    load_wo.start()
    for i in range(2):
        y_copies[i].wait_recv()
    stage_own(0)
    project(1)
    stage_own(1)
    stage_partner(0)

    for i in range(2):
        y_copies[2 + i].wait_recv()
        y_copies[4 + i].start()
    project(2)
    for i in range(2):
        y_copies[6 + i].start()
    stage_own(2)
    stage_partner(1)
    temporal(0)

    y_copies[4].wait_recv()
    y_copies[5].wait_recv()
    project(3)
    stage_own(3)
    stage_partner(2)
    temporal(1)
    stage_partner(3)

    y_copies[6].wait_recv()
    y_copies[7].wait_recv()
    project(4)
    stage_own(4)
    temporal(2)
    temporal(3)
    stage_partner(4)

    spatial(2, 4)
    wait_back(1)
    combine(2, 3)
    wait_back(2)
    combine(4, 5)
    temporal(4)
    spatial(6, 0)
    wait_back(3)
    wait_back(0)
    combine(6, 0, 1)
    wait_back(4)
    combine(7)
    load_wo.wait()
    project_out((yp, ym), first=True)
    project_out((y, yq), first=False)

    for p in range(3):
        for i in range(2):
            wz_copy(p, i, zl).wait_send()
            wx_copy(p, i, e_own).wait_send()
            wc_copy(p, i, e_own).wait_send()
    for c in y_copies:
        c.wait_send()
    for b, (k, n) in enumerate(batches):
        for part in range(3):
            zcopy(b, part, zl).wait_send()
        await_bytes(tsend.at[pl.ds(0, 15), pl.ds(k, n)], t_send.at[b])
        await_bytes(osend.at[pl.ds(0, 15), pl.ds(k, n)], o_send.at[b])
    for u in range(8):
        if u < 2:
            ccopy(u, partner_row, row, y * 2 + hz).wait_send()
        else:
            for zz in range(2):
                ccopy(u, y_of[u] * 2 + zz, row, y * 2 + hz).wait_send()


def attention(clip_ids, stream, mod, weight, out_weight):
    vmem = pl.BlockSpec(memory_space=pltpu.VMEM)
    hbm = pl.BlockSpec(memory_space=pl.ANY)
    dma = pltpu.SemaphoreType.DMA
    return pl.pallas_call(
        attention_kernel,
        out_shape=pltpu.VMEM((4, 64, 3072), F32),
        in_specs=[pl.BlockSpec(memory_space=pltpu.SMEM), hbm, vmem, hbm, hbm],
        out_specs=vmem,
        scratch_shapes=[
            pltpu.VMEM((4, 64, 3072), F32),
            pltpu.VMEM((8, 128, 3072), BF),
            pltpu.VMEM((2, 3, 8, 384, 256), BF),
            pltpu.VMEM((8, 256, 3072), BF),
            pltpu.VMEM((3, 3, 8, 128, 256), BF),
            pltpu.VMEM((16, 8, 3, 16, 256), BF),
            pltpu.VMEM((16, 8, 3, 16, 256), BF),
            pltpu.VMEM((16, 8, 16, 256), BF),
            pltpu.VMEM((16, 8, 16, 256), BF),
            pltpu.VMEM((8, 2, 128, 256), BF),
            pltpu.VMEM((8, 2, 128, 256), BF),
            pltpu.VMEM((2, 8, 128, 256), F32),
            pltpu.VMEM((256, 256), BF),
            pltpu.VMEM((256, 256), BF),
            pltpu.VMEM((256, 256), F32),
            dma((4,)),
            dma((8,)), dma((8,)),
            dma((3, 2)), dma((3, 2)),
            dma((3, 2)), dma((3, 2)),
            dma((3, 2)), dma((3, 2)),
            dma((5, 3)), dma((5, 3)),
            dma((5,)), dma((5,)),
            dma((5,)), dma((5,)),
            dma((8, 2)), dma((8, 2)),
        ],
        compiler_params=pltpu.CompilerParams(
            collective_id=0, has_side_effects=True, vmem_limit_bytes=60 * 1024 * 1024
        ),
        name="attention",
    )(clip_ids, stream, mod, weight, out_weight)


def per_device(stream, clip_ids, modulation, qkv_weight, out_weight):
    mod = jnp.transpose(modulation, (1, 0, 2))
    weight = jnp.transpose(qkv_weight, (1, 0, 2)).reshape(3, 8, 384, 256)
    return attention(clip_ids, stream, mod, weight, out_weight.reshape(8, 256, 3072))


def solution(mesh):
    placed = (P("tm", "row", None), P(), P(), P(None, None, "row"), P())
    return jax.shard_map(
        per_device, mesh=mesh, in_specs=placed, out_specs=P("tm", "row", None), check_vma=False
    )
```

```python
import math

import jax
import jax.numpy as jnp
from jax import lax
from jax.experimental import pallas as pl
from jax.experimental.pallas import tpu as pltpu
from jax.sharding import PartitionSpec as P

HD = 128
MESH = pl.DeviceIdType.MESH
BF = jnp.bfloat16
F32 = jnp.float32
LOG2E = 1.4426950408889634


def dot(a, b):
    return jnp.dot(a, b, preferred_element_type=F32)


def dot_nt(a, b):
    return lax.dot_general(a, b, (((1,), (1,)), ((), ())), preferred_element_type=F32)


def attention_kernel(
    clip_ref, stream_hbm, mod_ref, w_hbm, wo_hbm, out_ref,
    stream_v, xg, wbuf, wo, qkv, tsend, trecv, osend, orecv, csend, comb, sp, perm, perm_t, mask,
    load_sem, y_send, y_recv, wz_send, wz_recv, wx_send, wx_recv, wc_send, wc_recv, z_send, z_recv,
    t_send, t_recv, o_send, o_recv, c_send, c_recv,
):
    batches = ((0, 2), (2, 2), (4, 2), (6, 1), (7, 1))
    tm = lax.axis_index("tm")
    row = lax.axis_index("row")
    zh = (tm // 2) % 2
    core = tm % 2
    y = row // 2
    zl = row % 2
    hz = (zl + zh) % 2
    oz = 1 - zl
    partner_row = y * 2 + oz
    outer_tm = tm + 2 - 4 * zh
    other_core = tm + 1 - 2 * core
    ym, yp, yq = (y + 3) % 4, (y + 1) % 4, (y + 2) % 4
    up, down = (tm, yp * 2 + zl), (tm, ym * 2 + zl)
    y_of = (y, y, ym, yp, ym, yp, yq, yq)
    half_of = (0, 1, 0, 0, 1, 1, 0, 1)

    def rcopy(src, dst, send, recv, dev):
        return pltpu.make_async_remote_copy(
            src_ref=src, dst_ref=dst, send_sem=send, recv_sem=recv,
            device_id=dev, device_id_type=MESH,
        )

    def await_bytes(ref, sem):
        pltpu.make_async_copy(ref, ref, sem).wait()

    x = tm // 4
    xs = [((x + d) % 4) for d in range(4)]
    zs = [zh, 1 - zh]
    cs = [core, 1 - core]
    rows_of = [y * 2 + (hz + zh) % 2, y * 2 + (hz + 1 - zh) % 2]
    offsets = [(dx, dz, dc) for dx in (1, 3, 2, 0) for dz in range(2) for dc in range(2)][:-4]
    offsets = offsets + [(0, 1, 0), (0, 1, 1), (0, 0, 1)]
    me_at = core * 8 + x * 2 + zh

    def peer(dx, dz, dc):
        t = xs[dx] * 4 + zs[dz] * 2 + cs[dc]
        return (t, rows_of[dz]), cs[dc] * 8 + xs[dx] * 2 + zs[dz]

    load_stream = [
        pltpu.make_async_copy(stream_hbm.at[:, pl.ds(32 * u, 32)], stream_v.at[:, pl.ds(32 * u, 32)],
                              load_sem.at[u])
        for u in range(2)
    ]
    load_w = pltpu.make_async_copy(w_hbm, wbuf.at[zl], load_sem.at[2])
    load_wo = pltpu.make_async_copy(wo_hbm, wo, load_sem.at[3])
    for c in load_stream:
        c.start()

    barrier = pltpu.get_barrier_semaphore()
    for o in offsets:
        pl.semaphore_signal(barrier, inc=1, device_id=peer(*o)[0], device_id_type=MESH)
    row_peers = [(tm, r * 2 + (zl if i == 0 else oz)) for r in (y, ym, yp, yq) for i in range(2)][1:]
    for dev in row_peers:
        pl.semaphore_signal(barrier, inc=1, device_id=dev, device_id_type=MESH)

    x_par = x % 2
    x_up, x_down = (tm + 4) % 16, (tm + 12) % 16
    e_own = core * 4 + x_par * 2
    e_x = core * 4 + (1 - x_par) * 2
    e_cores = ((1 - core) * 4 + x_par * 2, (1 - core) * 4 + (1 - x_par) * 2)

    def wz_copy(p, i, side):
        dev = ((tm, partner_row), (outer_tm, partner_row))[i]
        return rcopy(w_hbm.at[p, e_own + i], wbuf.at[side, p, e_own + i],
                     wz_send.at[p, i], wz_recv.at[p, i], dev)

    def wx_copy(p, i, e):
        dev = ((x_up, row), (x_down, row))[i]
        return rcopy(wbuf.at[oz, p, e + i], wbuf.at[oz, p, e + i],
                     wx_send.at[p, i], wx_recv.at[p, i], dev)

    def wc_copy(p, j, e):
        pair = wbuf.at[oz, p, pl.ds(e, 2)]
        return rcopy(pair, pair, wc_send.at[p, j], wc_recv.at[p, j], (other_core, row))


    def norm(unit):
        @pl.loop(0, 4)
        def _(f):
            clip = clip_ref[tm * 4 + f]
            shift = mod_ref[0, pl.ds(clip, 1), :]
            scale = 1.0 + mod_ref[1, pl.ds(clip, 1), :]
            v = stream_v[f, pl.ds(unit * 32, 32), :]
            centred = v - jnp.mean(v, axis=-1, keepdims=True)
            var = jnp.mean(centred * centred, axis=-1, keepdims=True)
            n = centred * lax.rsqrt(var + 1e-06) * scale + shift
            xg[unit, pl.ds(f * 32, 32), :] = n.astype(BF)

    def ycopy(i, src, dst, half, dev):
        if half is None:
            return rcopy(xg.at[src], xg.at[dst], y_send.at[i], y_recv.at[i], dev)
        rows = pl.ds(half * 64, 64)
        return rcopy(xg.at[src, rows], xg.at[dst, rows], y_send.at[i], y_recv.at[i], dev)

    y_copies = [
        ycopy(0, 0, 2, None, up), ycopy(1, 0, 3, None, down),
        ycopy(2, 1, 4, None, up), ycopy(3, 1, 5, None, down),
        ycopy(4, 2, 6, 0, up), ycopy(5, 3, 6, 1, down),
        ycopy(6, 4, 7, 0, up), ycopy(7, 5, 7, 1, down),
    ]
    for unit in range(2):
        load_stream[unit].wait()
        norm(unit)
        if unit == 0:
            pl.semaphore_wait(barrier, 22)
            load_w.start()
            for p in range(3):
                for i in range(2):
                    wz_copy(p, i, zl).start()
        if unit == 0:
            y_copies[0].start()
            y_copies[1].start()

    def unit_row(j):
        return (j & 128) + ((j >> 2) & 3) * 32 + ((j >> 4) & 7) * 4 + (j & 3)

    r_i = lax.broadcasted_iota(jnp.int32, (256, 256), 0)
    c_i = lax.broadcasted_iota(jnp.int32, (256, 256), 1)
    perm[...] = (unit_row(r_i) == c_i).astype(BF)
    perm_t[...] = (unit_row(c_i) == r_i).astype(BF)
    lane = lax.broadcasted_iota(jnp.int32, (1, 256), 1)

    def clip_of(f, found):
        return jnp.where((lane >> 2) == f, clip_ref[f], found)

    key = lax.fori_loop(0, 64, clip_of, jnp.zeros((1, 256), jnp.int32)) * 4 + (lane & 3)
    key = jnp.broadcast_to(key.astype(F32), (256, 256))
    mask[...] = jnp.where(key == key.T, 0.0, -1e30).astype(F32)

    def project_part(b, pz, part):
        k, n = batches[b]
        kk = (pz + hz) % 2
        slot = kk * 2 + (1 - kk) * zl
        x = xg[k:k + n].reshape(n * 128, 3072)
        out = dot(x, wbuf[pz, part].reshape(3072, 256)).astype(BF)
        qkv[slot, part, k:k + n] = out.reshape(n, 128, 256)

    def zcopy(b, part, slot):
        k, n = batches[b]
        units = pl.ds(k, n)
        return rcopy(qkv.at[2, part, units], qkv.at[slot, part, units], z_send.at[b, part],
                     z_recv.at[b, part], (tm, partner_row))

    def project(b):
        for part in range(3):
            project_part(b, 1 - hz, part)
            if b == 4:
                zcopy(b, part, zl).start()
        if b < 4:
            for part in range(3):
                zcopy(b, part, zl).start()
        for part in range(3):
            project_part(b, hz, part)

    def stage_part(b, zz, part):
        k, n = batches[b]
        rows = qkv[zz, part, k:k + n].reshape(n * 128, 256)
        moved = dot(perm[:n * 128, :n * 128], rows).astype(BF).reshape(n, 8, 16, 256)
        for i in range(n):
            tsend[pl.ds(zz * 8, 8), k + i, part] = moved[i]

    def send_time(b, zz):
        k, n = batches[b]
        units = pl.ds(k, n)
        for dx in (1, 3, 2, 0):
            for dz in (1, 0):
                t = xs[dx] * 4 + zs[dz] * 2 + zz
                at = zz * 8 + xs[dx] * 2 + zs[dz]

                def send(t=t, at=at, dz=dz):
                    rcopy(tsend.at[at, units], trecv.at[tm, units], t_send.at[b], t_recv.at[b],
                          (t, rows_of[dz])).start()

                def keep(at=at):
                    trecv[tm, k:k + n] = tsend[at, k:k + n]

                if (dx, dz) == (0, 0):
                    pl.when(zz != core)(send)
                    pl.when(zz == core)(keep)
                else:
                    send()

    def stage_own(b):
        for part in range(3):
            stage_part(b, zl, part)
        send_time(b, zl)

    def stage_partner(b):
        for part in range(3):
            zcopy(b, part, oz).wait_recv()
        for part in range(3):
            stage_part(b, oz, part)
        send_time(b, oz)

    factor = LOG2E / math.sqrt(HD)

    def attend(s, v):
        p = jnp.exp2((s - jnp.max(s, axis=-1, keepdims=True)) * factor).astype(BF)
        out = dot(p, jnp.concatenate([v, jnp.ones(v.shape, BF)], axis=1))
        return out[:, :HD] / out[:, HD:]

    def temporal(b):
        k, n = batches[b]
        units = pl.ds(k, n)
        await_bytes(trecv.at[pl.ds(0, 15), units], t_recv.at[b])
        for u in range(k, k + n):
            for h in range(2):
                cols = slice(h * HD, (h + 1) * HD)
                q, kk, v = (trecv[:, u, part, :, cols].reshape(256, HD) for part in range(3))
                o = attend(dot_nt(q, kk) + mask[...], v)
                osend[:, u, :, cols] = o.astype(BF).reshape(16, 16, HD)
        orecv[me_at, k:k + n] = osend[tm, k:k + n]
        for o in offsets:
            dev, _ = peer(*o)
            rcopy(osend.at[dev[0], units], orecv.at[me_at, units], o_send.at[b], o_recv.at[b], dev).start()

    def wait_back(b):
        k, n = batches[b]
        await_bytes(orecv.at[pl.ds(0, 15), pl.ds(k, n)], o_recv.at[b])

    def spatial(ka, kb):
        @pl.loop(0, 2)
        def _(pair):
            for f in range(2):
                rows = pl.ds(pl.multiple_of(pair * 64 + f * 32, 32), 32)
                for h in range(2):
                    cols = slice(h * HD, (h + 1) * HD)
                    q = jnp.concatenate(
                        [qkv[0:2, 0, k:k + 2, rows, cols].reshape(128, HD) for k in (ka, kb)], axis=0)
                    kk, v = (qkv[0:2, part, :, rows, cols].reshape(512, HD) for part in (1, 2))
                    o = attend(dot_nt(q, kk), v).reshape(2, 2, 2, 32, HD)
                    sp[:, ka:ka + 2, rows, cols] = o[0]
                    sp[:, kb:kb + 2, rows, cols] = o[1]

    def ccopy(u, r, at, kept):
        half = half_of[u]
        return rcopy(csend.at[u, r % 2], comb.at[kept, half], c_send.at[u, r % 2], c_recv.at[at, half],
                     (tm, r))

    def combine(*units):
        for u in units:
            back = dot(perm_t[...], orecv[:, u].reshape(256, 256)).reshape(2, 128, 256)
            csend[u] = (sp[:, u] + back).astype(BF)
        for u in units:
            if u < 2:
                ccopy(u, partner_row, row, y * 2 + hz).start()
                comb[y * 2 + hz, u] = csend[u, zl]
            else:
                for zz in range(2):
                    ccopy(u, y_of[u] * 2 + zz, row, y * 2 + hz).start()

    def project_out(pair, first):
        for ys in pair:
            for i in range(2):
                r = ys * 2 + i
                for half in range(2):
                    def wait(r=r, half=half, ys=ys):
                        dst = comb.at[ys * 2 + (r + zh) % 2, half]
                        rcopy(csend.at[0, 0], dst, c_send.at[0, 0], c_recv.at[r, half], (tm, r)).wait_recv()
                    if ys is y:
                        pl.when(i != zl)(wait)
                    else:
                        wait()

        heads = [2 * ys + i for ys in pair for i in range(2)]

        def tile(cols):
            left = jnp.concatenate([comb[h].reshape(256, 256) for h in heads], axis=1)
            right = jnp.concatenate([wo[h, :, cols] for h in heads], axis=0)
            acc = dot(left, right)
            for half in range(2):
                for f in range(4):
                    at = (half * 4 + f) * 32
                    rows = slice(half * 32, (half + 1) * 32)
                    piece = acc[at:at + 32]
                    if not first:
                        clip = clip_ref[tm * 4 + f]
                        piece = (piece + out_ref[f, rows, cols]) * mod_ref[2, pl.ds(clip, 1), cols]
                    out_ref[f, rows, cols] = piece

        @pl.loop(0, 3)
        def _(n):
            for i in range(2):
                tile(pl.ds(pl.multiple_of(n * 1024 + i * 512, 512), 512))

    load_w.wait()
    for p in range(3):
        for i in range(2):
            wz_copy(p, i, oz).wait_recv()
            wx_copy(p, i, e_own).start()
        wc_copy(p, 0, e_own).start()
        project_part(0, zl, p)
    y_copies[2].start()
    y_copies[3].start()

    def pass_x(p):
        for i in range(2):
            wx_copy(p, i, e_x).wait_recv()
        wc_copy(p, 1, e_x).start()

    pass_x(0)
    pass_x(1)
    for p in range(3):
        for j in range(2):
            wc_copy(p, j, e_cores[j]).wait_recv()
        project_part(0, oz, p)
        zcopy(0, p, zl).start()
        if p == 0:
            pass_x(2)
    load_wo.start()
    for i in range(2):
        y_copies[i].wait_recv()
    stage_own(0)
    project(1)
    stage_own(1)
    stage_partner(0)

    for i in range(2):
        y_copies[2 + i].wait_recv()
        y_copies[4 + i].start()
    project(2)
    for i in range(2):
        y_copies[6 + i].start()
    stage_own(2)
    stage_partner(1)
    temporal(0)

    y_copies[4].wait_recv()
    y_copies[5].wait_recv()
    project(3)
    stage_own(3)
    stage_partner(2)
    temporal(1)
    stage_partner(3)

    y_copies[6].wait_recv()
    y_copies[7].wait_recv()
    project(4)
    stage_own(4)
    temporal(2)
    temporal(3)
    stage_partner(4)

    spatial(2, 4)
    wait_back(1)
    combine(2, 3)
    wait_back(2)
    combine(4, 5)
    temporal(4)
    spatial(6, 0)
    wait_back(3)
    wait_back(0)
    combine(6, 0, 1)
    wait_back(4)
    combine(7)
    load_wo.wait()
    project_out((yp, ym), first=True)
    project_out((y, yq), first=False)

    for p in range(3):
        for i in range(2):
            wz_copy(p, i, zl).wait_send()
            wx_copy(p, i, e_own).wait_send()
            wc_copy(p, i, e_own).wait_send()
    for c in y_copies:
        c.wait_send()
    for b, (k, n) in enumerate(batches):
        for part in range(3):
            zcopy(b, part, zl).wait_send()
        await_bytes(tsend.at[pl.ds(0, 15), pl.ds(k, n)], t_send.at[b])
        await_bytes(osend.at[pl.ds(0, 15), pl.ds(k, n)], o_send.at[b])
    for u in range(8):
        if u < 2:
            ccopy(u, partner_row, row, y * 2 + hz).wait_send()
        else:
            for zz in range(2):
                ccopy(u, y_of[u] * 2 + zz, row, y * 2 + hz).wait_send()


def attention(clip_ids, stream, mod, weight, out_weight):
    vmem = pl.BlockSpec(memory_space=pltpu.VMEM)
    hbm = pl.BlockSpec(memory_space=pl.ANY)
    dma = pltpu.SemaphoreType.DMA
    return pl.pallas_call(
        attention_kernel,
        out_shape=pltpu.VMEM((4, 64, 3072), F32),
        in_specs=[pl.BlockSpec(memory_space=pltpu.SMEM), hbm, vmem, hbm, hbm],
        out_specs=vmem,
        scratch_shapes=[
            pltpu.VMEM((4, 64, 3072), F32),
            pltpu.VMEM((8, 128, 3072), BF),
            pltpu.VMEM((2, 3, 8, 384, 256), BF),
            pltpu.VMEM((8, 256, 3072), BF),
            pltpu.VMEM((3, 3, 8, 128, 256), BF),
            pltpu.VMEM((16, 8, 3, 16, 256), BF),
            pltpu.VMEM((16, 8, 3, 16, 256), BF),
            pltpu.VMEM((16, 8, 16, 256), BF),
            pltpu.VMEM((16, 8, 16, 256), BF),
            pltpu.VMEM((8, 2, 128, 256), BF),
            pltpu.VMEM((8, 2, 128, 256), BF),
            pltpu.VMEM((2, 8, 128, 256), F32),
            pltpu.VMEM((256, 256), BF),
            pltpu.VMEM((256, 256), BF),
            pltpu.VMEM((256, 256), F32),
            dma((4,)),
            dma((8,)), dma((8,)),
            dma((3, 2)), dma((3, 2)),
            dma((3, 2)), dma((3, 2)),
            dma((3, 2)), dma((3, 2)),
            dma((5, 3)), dma((5, 3)),
            dma((5,)), dma((5,)),
            dma((5,)), dma((5,)),
            dma((8, 2)), dma((8, 2)),
        ],
        compiler_params=pltpu.CompilerParams(
            collective_id=0, has_side_effects=True, vmem_limit_bytes=60 * 1024 * 1024
        ),
        name="attention",
    )(clip_ids, stream, mod, weight, out_weight)


def per_device(stream, clip_ids, modulation, qkv_weight, out_weight):
    mod = jnp.transpose(modulation, (1, 0, 2))
    weight = jnp.transpose(qkv_weight, (1, 0, 2)).reshape(3, 8, 384, 256)
    return attention(clip_ids, stream, mod, weight, out_weight.reshape(8, 256, 3072))


def solution(mesh):
    placed = (P("tm", "row", None), P(), P(), P(None, None, "row"), P())
    return jax.shard_map(
        per_device, mesh=mesh, in_specs=placed, out_specs=P("tm", "row", None), check_vma=False
    )
```

```python
import math

import jax
import jax.numpy as jnp
from jax import lax
from jax.experimental import pallas as pl
from jax.experimental.pallas import tpu as pltpu
from jax.sharding import PartitionSpec as P

HD = 128
MESH = pl.DeviceIdType.MESH
BF = jnp.bfloat16
F32 = jnp.float32
LOG2E = 1.4426950408889634


def dot(a, b):
    return jnp.dot(a, b, preferred_element_type=F32)


def dot_nt(a, b):
    return lax.dot_general(a, b, (((1,), (1,)), ((), ())), preferred_element_type=F32)


def attention_kernel(
    clip_ref, stream_hbm, mod_ref, w_hbm, wo_hbm, out_ref,
    stream_v, xg, wbuf, wo, qkv, tsend, trecv, osend, orecv, csend, comb, sp, perm, perm_t, mask,
    load_sem, y_send, y_recv, wz_send, wz_recv, wx_send, wx_recv, wc_send, wc_recv, z_send, z_recv,
    t_send, t_recv, o_send, o_recv, c_send, c_recv,
):
    batches = ((0, 2), (2, 2), (4, 2), (6, 1), (7, 1))
    tm = lax.axis_index("tm")
    row = lax.axis_index("row")
    zh = (tm // 2) % 2
    core = tm % 2
    y = row // 2
    zl = row % 2
    hz = (zl + zh) % 2
    oz = 1 - zl
    partner_row = y * 2 + oz
    outer_tm = tm + 2 - 4 * zh
    other_core = tm + 1 - 2 * core
    ym, yp, yq = (y + 3) % 4, (y + 1) % 4, (y + 2) % 4
    up, down = (tm, yp * 2 + zl), (tm, ym * 2 + zl)
    y_of = (y, y, ym, yp, ym, yp, yq, yq)
    half_of = (0, 1, 0, 0, 1, 1, 0, 1)

    def rcopy(src, dst, send, recv, dev):
        return pltpu.make_async_remote_copy(
            src_ref=src, dst_ref=dst, send_sem=send, recv_sem=recv,
            device_id=dev, device_id_type=MESH,
        )

    def await_bytes(ref, sem):
        pltpu.make_async_copy(ref, ref, sem).wait()

    x = tm // 4
    xs = [((x + d) % 4) for d in range(4)]
    zs = [zh, 1 - zh]
    cs = [core, 1 - core]
    rows_of = [y * 2 + (hz + zh) % 2, y * 2 + (hz + 1 - zh) % 2]
    offsets = [(dx, dz, dc) for dx in (1, 3, 2, 0) for dz in range(2) for dc in range(2)][:-4]
    offsets = offsets + [(0, 1, 0), (0, 1, 1), (0, 0, 1)]
    me_at = core * 8 + x * 2 + zh

    def peer(dx, dz, dc):
        t = xs[dx] * 4 + zs[dz] * 2 + cs[dc]
        return (t, rows_of[dz]), cs[dc] * 8 + xs[dx] * 2 + zs[dz]

    load_stream = [
        pltpu.make_async_copy(stream_hbm.at[:, pl.ds(32 * u, 32)], stream_v.at[:, pl.ds(32 * u, 32)],
                              load_sem.at[u])
        for u in range(2)
    ]
    load_w = pltpu.make_async_copy(w_hbm, wbuf.at[zl], load_sem.at[2])
    load_wo = pltpu.make_async_copy(wo_hbm, wo, load_sem.at[3])
    for c in load_stream:
        c.start()

    barrier = pltpu.get_barrier_semaphore()
    for o in offsets:
        pl.semaphore_signal(barrier, inc=1, device_id=peer(*o)[0], device_id_type=MESH)
    row_peers = [(tm, r * 2 + (zl if i == 0 else oz)) for r in (y, ym, yp, yq) for i in range(2)][1:]
    for dev in row_peers:
        pl.semaphore_signal(barrier, inc=1, device_id=dev, device_id_type=MESH)

    x_par = x % 2
    x_up, x_down = (tm + 4) % 16, (tm + 12) % 16
    e_own = core * 4 + x_par * 2
    e_x = core * 4 + (1 - x_par) * 2
    e_cores = ((1 - core) * 4 + x_par * 2, (1 - core) * 4 + (1 - x_par) * 2)

    def wz_copy(p, i, side):
        dev = ((tm, partner_row), (outer_tm, partner_row))[i]
        return rcopy(w_hbm.at[p, e_own + i], wbuf.at[side, p, e_own + i],
                     wz_send.at[p, i], wz_recv.at[p, i], dev)

    def wx_copy(p, i, e):
        dev = ((x_up, row), (x_down, row))[i]
        return rcopy(wbuf.at[oz, p, e + i], wbuf.at[oz, p, e + i],
                     wx_send.at[p, i], wx_recv.at[p, i], dev)

    def wc_copy(p, j, e):
        pair = wbuf.at[oz, p, pl.ds(e, 2)]
        return rcopy(pair, pair, wc_send.at[p, j], wc_recv.at[p, j], (other_core, row))


    def norm(unit):
        @pl.loop(0, 4)
        def _(f):
            clip = clip_ref[tm * 4 + f]
            shift = mod_ref[0, pl.ds(clip, 1), :]
            scale = 1.0 + mod_ref[1, pl.ds(clip, 1), :]
            v = stream_v[f, pl.ds(unit * 32, 32), :]
            centred = v - jnp.mean(v, axis=-1, keepdims=True)
            var = jnp.mean(centred * centred, axis=-1, keepdims=True)
            n = centred * lax.rsqrt(var + 1e-06) * scale + shift
            xg[unit, pl.ds(f * 32, 32), :] = n.astype(BF)

    def ycopy(i, src, dst, half, dev):
        if half is None:
            return rcopy(xg.at[src], xg.at[dst], y_send.at[i], y_recv.at[i], dev)
        rows = pl.ds(half * 64, 64)
        return rcopy(xg.at[src, rows], xg.at[dst, rows], y_send.at[i], y_recv.at[i], dev)

    y_copies = [
        ycopy(0, 0, 2, None, up), ycopy(1, 0, 3, None, down),
        ycopy(2, 1, 4, None, up), ycopy(3, 1, 5, None, down),
        ycopy(4, 2, 6, 0, up), ycopy(5, 3, 6, 1, down),
        ycopy(6, 4, 7, 0, up), ycopy(7, 5, 7, 1, down),
    ]
    for unit in range(2):
        load_stream[unit].wait()
        norm(unit)
        if unit == 0:
            load_w.start()
            load_wo.start()
            pl.semaphore_wait(barrier, 22)
            y_copies[0].start()
            y_copies[1].start()
            for p in range(3):
                for i in range(2):
                    wz_copy(p, i, zl).start()

    def unit_row(j):
        return (j & 128) + ((j >> 2) & 3) * 32 + ((j >> 4) & 7) * 4 + (j & 3)

    r_i = lax.broadcasted_iota(jnp.int32, (256, 256), 0)
    c_i = lax.broadcasted_iota(jnp.int32, (256, 256), 1)
    perm[...] = (unit_row(r_i) == c_i).astype(BF)
    perm_t[...] = (unit_row(c_i) == r_i).astype(BF)
    lane = lax.broadcasted_iota(jnp.int32, (1, 256), 1)

    def clip_of(f, found):
        return jnp.where((lane >> 2) == f, clip_ref[f], found)

    key = lax.fori_loop(0, 64, clip_of, jnp.zeros((1, 256), jnp.int32)) * 4 + (lane & 3)
    key = jnp.broadcast_to(key.astype(F32), (256, 256))
    mask[...] = jnp.where(key == key.T, 0.0, -1e30).astype(F32)

    def project_part(b, pz, part):
        k, n = batches[b]
        kk = (pz + hz) % 2
        slot = kk * 2 + (1 - kk) * zl
        x = xg[k:k + n].reshape(n * 128, 3072)
        out = dot(x, wbuf[pz, part].reshape(3072, 256)).astype(BF)
        qkv[slot, part, k:k + n] = out.reshape(n, 128, 256)

    def zcopy(b, part, slot):
        k, n = batches[b]
        units = pl.ds(k, n)
        return rcopy(qkv.at[2, part, units], qkv.at[slot, part, units], z_send.at[b, part],
                     z_recv.at[b, part], (tm, partner_row))

    def project(b):
        def sent(part):
            project_part(b, 1 - hz, part)
            zcopy(b, part, zl).start()

        def kept(part):
            project_part(b, hz, part)

        for step in (sent, kept):
            if b == 4:
                for part in range(3):
                    step(part)
            else:
                pl.loop(0, 3)(step)

    def stage_part(b, zz, part):
        k, n = batches[b]
        rows = qkv[zz, part, k:k + n].reshape(n * 128, 256)
        moved = dot(perm[:n * 128, :n * 128], rows).astype(BF).reshape(n, 8, 16, 256)
        for i in range(n):
            tsend[pl.ds(zz * 8, 8), k + i, part] = moved[i]

    def send_time(b, zz):
        k, n = batches[b]
        units = pl.ds(k, n)
        for dx in (1, 3, 2, 0):
            for dz in (1, 0):
                t = xs[dx] * 4 + zs[dz] * 2 + zz
                at = zz * 8 + xs[dx] * 2 + zs[dz]

                def send(t=t, at=at, dz=dz):
                    rcopy(tsend.at[at, units], trecv.at[tm, units], t_send.at[b], t_recv.at[b],
                          (t, rows_of[dz])).start()

                def keep(at=at):
                    trecv[tm, k:k + n] = tsend[at, k:k + n]

                if (dx, dz) == (0, 0):
                    pl.when(zz != core)(send)
                    pl.when(zz == core)(keep)
                else:
                    send()

    def stage_own(b):
        @pl.loop(0, 3)
        def _(part):
            stage_part(b, zl, part)

        send_time(b, zl)

    def stage_partner(b):
        @pl.loop(0, 3)
        def _(part):
            zcopy(b, part, oz).wait_recv()
            stage_part(b, oz, part)

        send_time(b, oz)

    factor = LOG2E / math.sqrt(HD)

    def attend(s, v):
        p = jnp.exp2((s - jnp.max(s, axis=-1, keepdims=True)) * factor).astype(BF)
        out = dot(p, jnp.concatenate([v, jnp.ones(v.shape, BF)], axis=1))
        return out[:, :HD] / out[:, HD:]

    def temporal(b):
        k, n = batches[b]
        units = pl.ds(k, n)
        await_bytes(trecv.at[pl.ds(0, 15), units], t_recv.at[b])
        for u in range(k, k + n):
            for h in range(2):
                cols = slice(h * HD, (h + 1) * HD)
                q, kk, v = (trecv[:, u, part, :, cols].reshape(256, HD) for part in range(3))
                o = attend(dot_nt(q, kk) + mask[...], v)
                osend[:, u, :, cols] = o.astype(BF).reshape(16, 16, HD)
        orecv[me_at, k:k + n] = osend[tm, k:k + n]
        for o in offsets:
            dev, _ = peer(*o)
            rcopy(osend.at[dev[0], units], orecv.at[me_at, units], o_send.at[b], o_recv.at[b], dev).start()

    def wait_back(b):
        k, n = batches[b]
        await_bytes(orecv.at[pl.ds(0, 15), pl.ds(k, n)], o_recv.at[b])

    def spatial(ka, kb):
        @pl.loop(0, 2)
        def _(pair):
            for f in range(2):
                rows = pl.ds(pl.multiple_of(pair * 64 + f * 32, 32), 32)
                for h in range(2):
                    cols = slice(h * HD, (h + 1) * HD)
                    q = jnp.concatenate(
                        [qkv[0:2, 0, k:k + 2, rows, cols].reshape(128, HD) for k in (ka, kb)], axis=0)
                    kk, v = (qkv[0:2, part, :, rows, cols].reshape(512, HD) for part in (1, 2))
                    o = attend(dot_nt(q, kk), v).reshape(2, 2, 2, 32, HD)
                    sp[:, ka:ka + 2, rows, cols] = o[0]
                    sp[:, kb:kb + 2, rows, cols] = o[1]

    def ccopy(u, r, at, kept):
        half = half_of[u]
        return rcopy(csend.at[u, r % 2], comb.at[kept, half], c_send.at[u, r % 2], c_recv.at[at, half],
                     (tm, r))

    def combine(*units):
        for u in units:
            back = dot(perm_t[...], orecv[:, u].reshape(256, 256)).reshape(2, 128, 256)
            csend[u] = (sp[:, u] + back).astype(BF)
        for u in units:
            if u < 2:
                ccopy(u, partner_row, row, y * 2 + hz).start()
                comb[y * 2 + hz, u] = csend[u, zl]
            else:
                for zz in range(2):
                    ccopy(u, y_of[u] * 2 + zz, row, y * 2 + hz).start()

    def project_out(pair, first):
        for ys in pair:
            for i in range(2):
                r = ys * 2 + i
                for half in range(2):
                    def wait(r=r, half=half, ys=ys):
                        dst = comb.at[ys * 2 + (r + zh) % 2, half]
                        rcopy(csend.at[0, 0], dst, c_send.at[0, 0], c_recv.at[r, half], (tm, r)).wait_recv()
                    if ys is y:
                        pl.when(i != zl)(wait)
                    else:
                        wait()

        heads = [2 * ys + i for ys in pair for i in range(2)]

        def tile(cols):
            left = jnp.concatenate([comb[h].reshape(256, 256) for h in heads], axis=1)
            right = jnp.concatenate([wo[h, :, cols] for h in heads], axis=0)
            acc = dot(left, right)
            for half in range(2):
                for f in range(4):
                    at = (half * 4 + f) * 32
                    rows = slice(half * 32, (half + 1) * 32)
                    piece = acc[at:at + 32]
                    if not first:
                        clip = clip_ref[tm * 4 + f]
                        piece = (piece + out_ref[f, rows, cols]) * mod_ref[2, pl.ds(clip, 1), cols]
                    out_ref[f, rows, cols] = piece

        @pl.loop(0, 3)
        def _(n):
            for i in range(2):
                tile(pl.ds(pl.multiple_of(n * 1024 + i * 512, 512), 512))

    load_w.wait()
    for p in range(3):
        for i in range(2):
            wz_copy(p, i, oz).wait_recv()
            wx_copy(p, i, e_own).start()
        wc_copy(p, 0, e_own).start()
        project_part(0, zl, p)
    y_copies[2].start()
    y_copies[3].start()

    def pass_x(p):
        for i in range(2):
            wx_copy(p, i, e_x).wait_recv()
        wc_copy(p, 1, e_x).start()

    pass_x(0)
    pass_x(1)
    for p in range(3):
        for j in range(2):
            wc_copy(p, j, e_cores[j]).wait_recv()
        project_part(0, oz, p)
        zcopy(0, p, zl).start()
        if p == 0:
            pass_x(2)
    for i in range(2):
        y_copies[i].wait_recv()
    stage_own(0)
    project(1)
    stage_own(1)
    stage_partner(0)

    for i in range(2):
        y_copies[2 + i].wait_recv()
        y_copies[4 + i].start()
    project(2)
    for i in range(2):
        y_copies[6 + i].start()
    stage_own(2)
    stage_partner(1)
    temporal(0)

    y_copies[4].wait_recv()
    y_copies[5].wait_recv()
    project(3)
    stage_own(3)
    stage_partner(2)
    temporal(1)
    stage_partner(3)

    y_copies[6].wait_recv()
    y_copies[7].wait_recv()
    project(4)
    stage_own(4)
    temporal(2)
    temporal(3)
    stage_partner(4)

    spatial(2, 4)
    wait_back(1)
    combine(2, 3)
    wait_back(2)
    combine(4, 5)
    temporal(4)
    spatial(6, 0)
    wait_back(3)
    wait_back(0)
    combine(6, 0, 1)
    wait_back(4)
    combine(7)
    load_wo.wait()
    project_out((yp, ym), first=True)
    project_out((y, yq), first=False)

    for p in range(3):
        for i in range(2):
            wz_copy(p, i, zl).wait_send()
            wx_copy(p, i, e_own).wait_send()
            wc_copy(p, i, e_own).wait_send()
    for c in y_copies:
        c.wait_send()
    for b, (k, n) in enumerate(batches):
        for part in range(3):
            zcopy(b, part, zl).wait_send()
        await_bytes(tsend.at[pl.ds(0, 15), pl.ds(k, n)], t_send.at[b])
        await_bytes(osend.at[pl.ds(0, 15), pl.ds(k, n)], o_send.at[b])
    for u in range(8):
        if u < 2:
            ccopy(u, partner_row, row, y * 2 + hz).wait_send()
        else:
            for zz in range(2):
                ccopy(u, y_of[u] * 2 + zz, row, y * 2 + hz).wait_send()


def attention(clip_ids, stream, mod, weight, out_weight):
    vmem = pl.BlockSpec(memory_space=pltpu.VMEM)
    hbm = pl.BlockSpec(memory_space=pl.ANY)
    dma = pltpu.SemaphoreType.DMA
    return pl.pallas_call(
        attention_kernel,
        out_shape=pltpu.VMEM((4, 64, 3072), F32),
        in_specs=[pl.BlockSpec(memory_space=pltpu.SMEM), hbm, vmem, hbm, hbm],
        out_specs=vmem,
        scratch_shapes=[
            pltpu.VMEM((4, 64, 3072), F32),
            pltpu.VMEM((8, 128, 3072), BF),
            pltpu.VMEM((2, 3, 8, 384, 256), BF),
            pltpu.VMEM((8, 256, 3072), BF),
            pltpu.VMEM((3, 3, 8, 128, 256), BF),
            pltpu.VMEM((16, 8, 3, 16, 256), BF),
            pltpu.VMEM((16, 8, 3, 16, 256), BF),
            pltpu.VMEM((16, 8, 16, 256), BF),
            pltpu.VMEM((16, 8, 16, 256), BF),
            pltpu.VMEM((8, 2, 128, 256), BF),
            pltpu.VMEM((8, 2, 128, 256), BF),
            pltpu.VMEM((2, 8, 128, 256), F32),
            pltpu.VMEM((256, 256), BF),
            pltpu.VMEM((256, 256), BF),
            pltpu.VMEM((256, 256), F32),
            dma((4,)),
            dma((8,)), dma((8,)),
            dma((3, 2)), dma((3, 2)),
            dma((3, 2)), dma((3, 2)),
            dma((3, 2)), dma((3, 2)),
            dma((5, 3)), dma((5, 3)),
            dma((5,)), dma((5,)),
            dma((5,)), dma((5,)),
            dma((8, 2)), dma((8, 2)),
        ],
        compiler_params=pltpu.CompilerParams(
            collective_id=0, has_side_effects=True, vmem_limit_bytes=60 * 1024 * 1024
        ),
        name="attention",
    )(clip_ids, stream, mod, weight, out_weight)


def per_device(stream, clip_ids, modulation, qkv_weight, out_weight):
    mod = jnp.transpose(modulation, (1, 0, 2))
    weight = jnp.transpose(qkv_weight, (1, 0, 2)).reshape(3, 8, 384, 256)
    return attention(clip_ids, stream, mod, weight, out_weight.reshape(8, 256, 3072))


def solution(mesh):
    placed = (P("tm", "row", None), P(), P(), P(None, None, "row"), P())
    return jax.shard_map(
        per_device, mesh=mesh, in_specs=placed, out_specs=P("tm", "row", None), check_vma=False
    )
```

```python
import math

import jax
import jax.numpy as jnp
from jax import lax
from jax.experimental import pallas as pl
from jax.experimental.pallas import tpu as pltpu
from jax.sharding import PartitionSpec as P

HD = 128
MESH = pl.DeviceIdType.MESH
BF = jnp.bfloat16
F32 = jnp.float32
LOG2E = 1.4426950408889634


def dot(a, b):
    return jnp.dot(a, b, preferred_element_type=F32)


def dot_nt(a, b):
    return lax.dot_general(a, b, (((1,), (1,)), ((), ())), preferred_element_type=F32)


def attention_kernel(
    clip_ref, stream_hbm, mod_ref, w_hbm, wo_hbm, out_ref,
    stream_v, xg, wbuf, wo, qkv, tsend, trecv, osend, orecv, csend, comb, sp, perm, perm_t, mask,
    load_sem, y_send, y_recv, wz_send, wz_recv, wx_send, wx_recv, wc_send, wc_recv, z_send, z_recv,
    t_send, t_recv, o_send, o_recv, c_send, c_recv,
):
    batches = ((0, 2), (2, 2), (4, 2), (6, 1), (7, 1))
    tm = lax.axis_index("tm")
    row = lax.axis_index("row")
    zh = (tm // 2) % 2
    core = tm % 2
    y = row // 2
    zl = row % 2
    hz = (zl + zh) % 2
    oz = 1 - zl
    partner_row = y * 2 + oz
    outer_tm = tm + 2 - 4 * zh
    other_core = tm + 1 - 2 * core
    ym, yp, yq = (y + 3) % 4, (y + 1) % 4, (y + 2) % 4
    up, down = (tm, yp * 2 + zl), (tm, ym * 2 + zl)
    y_of = (y, y, ym, yp, ym, yp, yq, yq)
    half_of = (0, 1, 0, 0, 1, 1, 0, 1)

    def rcopy(src, dst, send, recv, dev):
        return pltpu.make_async_remote_copy(
            src_ref=src, dst_ref=dst, send_sem=send, recv_sem=recv,
            device_id=dev, device_id_type=MESH,
        )

    def await_bytes(ref, sem):
        pltpu.make_async_copy(ref, ref, sem).wait()

    x = tm // 4
    xs = [((x + d) % 4) for d in range(4)]
    zs = [zh, 1 - zh]
    cs = [core, 1 - core]
    rows_of = [y * 2 + (hz + zh) % 2, y * 2 + (hz + 1 - zh) % 2]
    offsets = [(dx, dz, dc) for dx in (2, 1, 3, 0) for dz in range(2) for dc in range(2)][:-4]
    offsets = offsets + [(0, 1, 0), (0, 1, 1), (0, 0, 1)]
    me_at = core * 8 + x * 2 + zh

    def peer(dx, dz, dc):
        t = xs[dx] * 4 + zs[dz] * 2 + cs[dc]
        return (t, rows_of[dz]), cs[dc] * 8 + xs[dx] * 2 + zs[dz]

    load_stream = [
        pltpu.make_async_copy(stream_hbm.at[:, pl.ds(32 * u, 32)], stream_v.at[:, pl.ds(32 * u, 32)],
                              load_sem.at[u])
        for u in range(2)
    ]
    load_w = pltpu.make_async_copy(w_hbm, wbuf.at[zl], load_sem.at[2])
    load_wo = pltpu.make_async_copy(wo_hbm, wo, load_sem.at[3])
    for c in load_stream:
        c.start()

    barrier = pltpu.get_barrier_semaphore()
    for o in offsets:
        pl.semaphore_signal(barrier, inc=1, device_id=peer(*o)[0], device_id_type=MESH)
    row_peers = [(tm, r * 2 + (zl if i == 0 else oz)) for r in (y, ym, yp, yq) for i in range(2)][1:]
    for dev in row_peers:
        pl.semaphore_signal(barrier, inc=1, device_id=dev, device_id_type=MESH)

    x_par = x % 2
    x_up, x_down = (tm + 4) % 16, (tm + 12) % 16
    e_own = core * 4 + x_par * 2
    e_x = core * 4 + (1 - x_par) * 2
    e_cores = ((1 - core) * 4 + x_par * 2, (1 - core) * 4 + (1 - x_par) * 2)

    def wz_copy(p, i, side):
        dev = ((tm, partner_row), (outer_tm, partner_row))[i]
        return rcopy(w_hbm.at[p, e_own + i], wbuf.at[side, p, e_own + i],
                     wz_send.at[p, i], wz_recv.at[p, i], dev)

    def wx_copy(p, i, e):
        dev = ((x_up, row), (x_down, row))[i]
        return rcopy(wbuf.at[oz, p, e + i], wbuf.at[oz, p, e + i],
                     wx_send.at[p, i], wx_recv.at[p, i], dev)

    def wc_copy(p, j, e):
        pair = wbuf.at[oz, p, pl.ds(e, 2)]
        return rcopy(pair, pair, wc_send.at[p, j], wc_recv.at[p, j], (other_core, row))


    def norm(unit):
        @pl.loop(0, 4)
        def _(f):
            clip = clip_ref[tm * 4 + f]
            shift = mod_ref[0, pl.ds(clip, 1), :]
            scale = 1.0 + mod_ref[1, pl.ds(clip, 1), :]
            v = stream_v[f, pl.ds(unit * 32, 32), :]
            centred = v - jnp.mean(v, axis=-1, keepdims=True)
            var = jnp.mean(centred * centred, axis=-1, keepdims=True)
            n = centred * lax.rsqrt(var + 1e-06) * scale + shift
            xg[unit, pl.ds(f * 32, 32), :] = n.astype(BF)

    def ycopy(i, src, dst, half, dev):
        if half is None:
            return rcopy(xg.at[src], xg.at[dst], y_send.at[i], y_recv.at[i], dev)
        rows = pl.ds(half * 64, 64)
        return rcopy(xg.at[src, rows], xg.at[dst, rows], y_send.at[i], y_recv.at[i], dev)

    y_copies = [
        ycopy(0, 0, 2, None, up), ycopy(1, 0, 3, None, down),
        ycopy(2, 1, 4, None, up), ycopy(3, 1, 5, None, down),
        ycopy(4, 2, 6, 0, up), ycopy(5, 3, 6, 1, down),
        ycopy(6, 4, 7, 0, up), ycopy(7, 5, 7, 1, down),
    ]
    for unit in range(2):
        load_stream[unit].wait()
        norm(unit)
        if unit == 0:
            pl.semaphore_wait(barrier, 22)
            load_w.start()
            for p in range(3):
                for i in range(2):
                    wz_copy(p, i, zl).start()
        if unit == 0:
            y_copies[0].start()
            y_copies[1].start()

    def unit_row(j):
        return (j & 128) + ((j >> 2) & 3) * 32 + ((j >> 4) & 7) * 4 + (j & 3)

    r_i = lax.broadcasted_iota(jnp.int32, (256, 256), 0)
    c_i = lax.broadcasted_iota(jnp.int32, (256, 256), 1)
    perm[...] = (unit_row(r_i) == c_i).astype(BF)
    perm_t[...] = (unit_row(c_i) == r_i).astype(BF)
    lane = lax.broadcasted_iota(jnp.int32, (1, 256), 1)

    def clip_of(f, found):
        return jnp.where((lane >> 2) == f, clip_ref[f], found)

    key = lax.fori_loop(0, 64, clip_of, jnp.zeros((1, 256), jnp.int32)) * 4 + (lane & 3)
    key = jnp.broadcast_to(key.astype(F32), (256, 256))
    mask[...] = jnp.where(key == key.T, 0.0, -1e30).astype(F32)

    def project_part(b, pz, part):
        k, n = batches[b]
        kk = (pz + hz) % 2
        slot = kk * 2 + (1 - kk) * zl
        x = xg[k:k + n].reshape(n * 128, 3072)
        out = dot(x, wbuf[pz, part].reshape(3072, 256)).astype(BF)
        qkv[slot, part, k:k + n] = out.reshape(n, 128, 256)

    def zcopy(b, part, slot):
        k, n = batches[b]
        units = pl.ds(k, n)
        return rcopy(qkv.at[2, part, units], qkv.at[slot, part, units], z_send.at[b, part],
                     z_recv.at[b, part], (tm, partner_row))

    def project(b):
        def sent(part):
            project_part(b, 1 - hz, part)
            zcopy(b, part, zl).start()

        def kept(part):
            project_part(b, hz, part)

        for step in (sent, kept):
            if b == 4:
                for part in range(3):
                    step(part)
            else:
                pl.loop(0, 3)(step)

    def stage_part(b, zz, part):
        k, n = batches[b]
        rows = qkv[zz, part, k:k + n].reshape(n * 128, 256)
        moved = dot(perm[:n * 128, :n * 128], rows).astype(BF).reshape(n, 8, 16, 256)
        for i in range(n):
            tsend[pl.ds(zz * 8, 8), k + i, part] = moved[i]

    def send_time(b, zz):
        k, n = batches[b]
        units = pl.ds(k, n)
        for dx in (2, 1, 3, 0):
            for dz in (1, 0):
                t = xs[dx] * 4 + zs[dz] * 2 + zz
                at = zz * 8 + xs[dx] * 2 + zs[dz]

                def send(t=t, at=at, dz=dz):
                    rcopy(tsend.at[at, units], trecv.at[tm, units], t_send.at[b], t_recv.at[b],
                          (t, rows_of[dz])).start()

                def keep(at=at):
                    trecv[tm, k:k + n] = tsend[at, k:k + n]

                if (dx, dz) == (0, 0):
                    pl.when(zz != core)(send)
                    pl.when(zz == core)(keep)
                else:
                    send()

    def stage_own(b):
        @pl.loop(0, 3)
        def _(part):
            stage_part(b, zl, part)

        send_time(b, zl)

    def stage_partner(b):
        @pl.loop(0, 3)
        def _(part):
            zcopy(b, part, oz).wait_recv()
            stage_part(b, oz, part)

        send_time(b, oz)

    factor = LOG2E / math.sqrt(HD)

    def attend(s, v):
        p = jnp.exp2((s - jnp.max(s, axis=-1, keepdims=True)) * factor).astype(BF)
        out = dot(p, jnp.concatenate([v, jnp.ones(v.shape, BF)], axis=1))
        return out[:, :HD] / out[:, HD:]

    def temporal(b):
        k, n = batches[b]
        units = pl.ds(k, n)
        await_bytes(trecv.at[pl.ds(0, 15), units], t_recv.at[b])
        for u in range(k, k + n):
            for h in range(2):
                cols = slice(h * HD, (h + 1) * HD)
                q, kk, v = (trecv[:, u, part, :, cols].reshape(256, HD) for part in range(3))
                o = attend(dot_nt(q, kk) + mask[...], v)
                osend[:, u, :, cols] = o.astype(BF).reshape(16, 16, HD)
        orecv[me_at, k:k + n] = osend[tm, k:k + n]
        for o in offsets:
            dev, _ = peer(*o)
            rcopy(osend.at[dev[0], units], orecv.at[me_at, units], o_send.at[b], o_recv.at[b], dev).start()

    def wait_back(b):
        k, n = batches[b]
        await_bytes(orecv.at[pl.ds(0, 15), pl.ds(k, n)], o_recv.at[b])

    def spatial(ka, kb):
        @pl.loop(0, 2)
        def _(pair):
            for f in range(2):
                rows = pl.ds(pl.multiple_of(pair * 64 + f * 32, 32), 32)
                for h in range(2):
                    cols = slice(h * HD, (h + 1) * HD)
                    q = jnp.concatenate(
                        [qkv[0:2, 0, k:k + 2, rows, cols].reshape(128, HD) for k in (ka, kb)], axis=0)
                    kk, v = (qkv[0:2, part, :, rows, cols].reshape(512, HD) for part in (1, 2))
                    o = attend(dot_nt(q, kk), v).reshape(2, 2, 2, 32, HD)
                    sp[:, ka:ka + 2, rows, cols] = o[0]
                    sp[:, kb:kb + 2, rows, cols] = o[1]

    def ccopy(u, r, at, kept):
        half = half_of[u]
        return rcopy(csend.at[u, r % 2], comb.at[kept, half], c_send.at[u, r % 2], c_recv.at[at, half],
                     (tm, r))

    def combine(*units):
        for u in units:
            back = dot(perm_t[...], orecv[:, u].reshape(256, 256)).reshape(2, 128, 256)
            csend[u] = (sp[:, u] + back).astype(BF)
        for u in units:
            if u < 2:
                ccopy(u, partner_row, row, y * 2 + hz).start()
                comb[y * 2 + hz, u] = csend[u, zl]
            else:
                for zz in range(2):
                    ccopy(u, y_of[u] * 2 + zz, row, y * 2 + hz).start()

    def project_out(pair, first):
        for ys in pair:
            for i in range(2):
                r = ys * 2 + i
                for half in range(2):
                    def wait(r=r, half=half, ys=ys):
                        dst = comb.at[ys * 2 + (r + zh) % 2, half]
                        rcopy(csend.at[0, 0], dst, c_send.at[0, 0], c_recv.at[r, half], (tm, r)).wait_recv()
                    if ys is y:
                        pl.when(i != zl)(wait)
                    else:
                        wait()

        heads = [2 * ys + i for ys in pair for i in range(2)]

        def tile(cols):
            left = jnp.concatenate([comb[h].reshape(256, 256) for h in heads], axis=1)
            right = jnp.concatenate([wo[h, :, cols] for h in heads], axis=0)
            acc = dot(left, right)
            for half in range(2):
                for f in range(4):
                    at = (half * 4 + f) * 32
                    rows = slice(half * 32, (half + 1) * 32)
                    piece = acc[at:at + 32]
                    if not first:
                        clip = clip_ref[tm * 4 + f]
                        piece = (piece + out_ref[f, rows, cols]) * mod_ref[2, pl.ds(clip, 1), cols]
                    out_ref[f, rows, cols] = piece

        @pl.loop(0, 3)
        def _(n):
            for i in range(2):
                tile(pl.ds(pl.multiple_of(n * 1024 + i * 512, 512), 512))

    load_w.wait()
    for p in range(3):
        for i in range(2):
            wz_copy(p, i, oz).wait_recv()
            wx_copy(p, i, e_own).start()
        wc_copy(p, 0, e_own).start()
        project_part(0, zl, p)
    y_copies[2].start()
    y_copies[3].start()

    def pass_x(p):
        for i in range(2):
            wx_copy(p, i, e_x).wait_recv()
        wc_copy(p, 1, e_x).start()

    pass_x(0)
    pass_x(1)
    for p in range(3):
        for j in range(2):
            wc_copy(p, j, e_cores[j]).wait_recv()
        project_part(0, oz, p)
        zcopy(0, p, zl).start()
        if p == 0:
            pass_x(2)
    load_wo.start()
    for i in range(2):
        y_copies[i].wait_recv()
    stage_own(0)
    project(1)
    stage_own(1)
    stage_partner(0)

    for i in range(2):
        y_copies[2 + i].wait_recv()
        y_copies[4 + i].start()
    project(2)
    for i in range(2):
        y_copies[6 + i].start()
    stage_own(2)
    stage_partner(1)
    temporal(0)

    y_copies[4].wait_recv()
    y_copies[5].wait_recv()
    project(3)
    stage_own(3)
    stage_partner(2)
    temporal(1)
    stage_partner(3)

    y_copies[6].wait_recv()
    y_copies[7].wait_recv()
    project(4)
    stage_own(4)
    temporal(2)
    temporal(3)
    stage_partner(4)

    spatial(2, 4)
    wait_back(1)
    combine(2, 3)
    wait_back(2)
    combine(4, 5)
    temporal(4)
    spatial(6, 0)
    wait_back(3)
    wait_back(0)
    combine(6, 0, 1)
    wait_back(4)
    combine(7)
    load_wo.wait()
    project_out((yp, ym), first=True)
    project_out((y, yq), first=False)

    for p in range(3):
        for i in range(2):
            wz_copy(p, i, zl).wait_send()
            wx_copy(p, i, e_own).wait_send()
            wc_copy(p, i, e_own).wait_send()
    for c in y_copies:
        c.wait_send()
    for b, (k, n) in enumerate(batches):
        for part in range(3):
            zcopy(b, part, zl).wait_send()
        await_bytes(tsend.at[pl.ds(0, 15), pl.ds(k, n)], t_send.at[b])
        await_bytes(osend.at[pl.ds(0, 15), pl.ds(k, n)], o_send.at[b])
    for u in range(8):
        if u < 2:
            ccopy(u, partner_row, row, y * 2 + hz).wait_send()
        else:
            for zz in range(2):
                ccopy(u, y_of[u] * 2 + zz, row, y * 2 + hz).wait_send()


def attention(clip_ids, stream, mod, weight, out_weight):
    vmem = pl.BlockSpec(memory_space=pltpu.VMEM)
    hbm = pl.BlockSpec(memory_space=pl.ANY)
    dma = pltpu.SemaphoreType.DMA
    return pl.pallas_call(
        attention_kernel,
        out_shape=pltpu.VMEM((4, 64, 3072), F32),
        in_specs=[pl.BlockSpec(memory_space=pltpu.SMEM), hbm, vmem, hbm, hbm],
        out_specs=vmem,
        scratch_shapes=[
            pltpu.VMEM((4, 64, 3072), F32),
            pltpu.VMEM((8, 128, 3072), BF),
            pltpu.VMEM((2, 3, 8, 384, 256), BF),
            pltpu.VMEM((8, 256, 3072), BF),
            pltpu.VMEM((3, 3, 8, 128, 256), BF),
            pltpu.VMEM((16, 8, 3, 16, 256), BF),
            pltpu.VMEM((16, 8, 3, 16, 256), BF),
            pltpu.VMEM((16, 8, 16, 256), BF),
            pltpu.VMEM((16, 8, 16, 256), BF),
            pltpu.VMEM((8, 2, 128, 256), BF),
            pltpu.VMEM((8, 2, 128, 256), BF),
            pltpu.VMEM((2, 8, 128, 256), F32),
            pltpu.VMEM((256, 256), BF),
            pltpu.VMEM((256, 256), BF),
            pltpu.VMEM((256, 256), F32),
            dma((4,)),
            dma((8,)), dma((8,)),
            dma((3, 2)), dma((3, 2)),
            dma((3, 2)), dma((3, 2)),
            dma((3, 2)), dma((3, 2)),
            dma((5, 3)), dma((5, 3)),
            dma((5,)), dma((5,)),
            dma((5,)), dma((5,)),
            dma((8, 2)), dma((8, 2)),
        ],
        compiler_params=pltpu.CompilerParams(
            collective_id=0, has_side_effects=True, vmem_limit_bytes=60 * 1024 * 1024
        ),
        name="attention",
    )(clip_ids, stream, mod, weight, out_weight)


def per_device(stream, clip_ids, modulation, qkv_weight, out_weight):
    mod = jnp.transpose(modulation, (1, 0, 2))
    weight = jnp.transpose(qkv_weight, (1, 0, 2)).reshape(3, 8, 384, 256)
    return attention(clip_ids, stream, mod, weight, out_weight.reshape(8, 256, 3072))


def solution(mesh):
    placed = (P("tm", "row", None), P(), P(), P(None, None, "row"), P())
    return jax.shard_map(
        per_device, mesh=mesh, in_specs=placed, out_specs=P("tm", "row", None), check_vma=False
    )
```

```python
import math

import jax
import jax.numpy as jnp
from jax import lax
from jax.experimental import pallas as pl
from jax.experimental.pallas import tpu as pltpu
from jax.sharding import PartitionSpec as P

HD = 128
MESH = pl.DeviceIdType.MESH
BF = jnp.bfloat16
F32 = jnp.float32
LOG2E = 1.4426950408889634


def dot(a, b):
    return jnp.dot(a, b, preferred_element_type=F32)


def dot_nt(a, b):
    return lax.dot_general(a, b, (((1,), (1,)), ((), ())), preferred_element_type=F32)


def attention_kernel(
    clip_ref, stream_hbm, mod_ref, w_hbm, wo_hbm, out_ref,
    stream_v, xg, wbuf, wo, qkv, tsend, trecv, osend, orecv, csend, comb, sp, perm, perm_t, mask,
    load_sem, y_send, y_recv, wz_send, wz_recv, wx_send, wx_recv, wc_send, wc_recv, z_send, z_recv,
    t_send, t_recv, o_send, o_recv, c_send, c_recv,
):
    batches = ((0, 2), (2, 2), (4, 2), (6, 1), (7, 1))
    tm = lax.axis_index("tm")
    row = lax.axis_index("row")
    zh = (tm // 2) % 2
    core = tm % 2
    y = row // 2
    zl = row % 2
    hz = (zl + zh) % 2
    oz = 1 - zl
    partner_row = y * 2 + oz
    outer_tm = tm + 2 - 4 * zh
    other_core = tm + 1 - 2 * core
    ym, yp, yq = (y + 3) % 4, (y + 1) % 4, (y + 2) % 4
    up, down = (tm, yp * 2 + zl), (tm, ym * 2 + zl)
    y_of = (y, y, ym, yp, ym, yp, yq, yq)
    half_of = (0, 1, 0, 0, 1, 1, 0, 1)

    def rcopy(src, dst, send, recv, dev):
        return pltpu.make_async_remote_copy(
            src_ref=src, dst_ref=dst, send_sem=send, recv_sem=recv,
            device_id=dev, device_id_type=MESH,
        )

    def await_bytes(ref, sem):
        pltpu.make_async_copy(ref, ref, sem).wait()

    x = tm // 4
    xs = [((x + d) % 4) for d in range(4)]
    zs = [zh, 1 - zh]
    cs = [core, 1 - core]
    rows_of = [y * 2 + (hz + zh) % 2, y * 2 + (hz + 1 - zh) % 2]
    offsets = [(dx, dz, dc) for dx in (2, 1, 3, 0) for dz in range(2) for dc in range(2)][:-4]
    offsets = offsets + [(0, 1, 0), (0, 1, 1), (0, 0, 1)]
    me_at = core * 8 + x * 2 + zh

    def peer(dx, dz, dc):
        t = xs[dx] * 4 + zs[dz] * 2 + cs[dc]
        return (t, rows_of[dz]), cs[dc] * 8 + xs[dx] * 2 + zs[dz]

    load_stream = [
        pltpu.make_async_copy(stream_hbm.at[:, pl.ds(32 * u, 32)], stream_v.at[:, pl.ds(32 * u, 32)],
                              load_sem.at[u])
        for u in range(2)
    ]
    load_w = pltpu.make_async_copy(w_hbm, wbuf.at[zl], load_sem.at[2])
    load_wo = pltpu.make_async_copy(wo_hbm, wo, load_sem.at[3])
    for c in load_stream:
        c.start()

    barrier = pltpu.get_barrier_semaphore()
    for o in offsets:
        pl.semaphore_signal(barrier, inc=1, device_id=peer(*o)[0], device_id_type=MESH)
    row_peers = [(tm, r * 2 + (zl if i == 0 else oz)) for r in (y, ym, yp, yq) for i in range(2)][1:]
    for dev in row_peers:
        pl.semaphore_signal(barrier, inc=1, device_id=dev, device_id_type=MESH)

    x_par = x % 2
    x_up, x_down = (tm + 4) % 16, (tm + 12) % 16
    e_own = core * 4 + x_par * 2
    e_x = core * 4 + (1 - x_par) * 2
    e_cores = ((1 - core) * 4 + x_par * 2, (1 - core) * 4 + (1 - x_par) * 2)

    def wz_copy(p, i, side):
        dev = ((tm, partner_row), (outer_tm, partner_row))[i]
        return rcopy(w_hbm.at[p, e_own + i], wbuf.at[side, p, e_own + i],
                     wz_send.at[p, i], wz_recv.at[p, i], dev)

    def wx_copy(p, i, e):
        dev = ((x_up, row), (x_down, row))[i]
        return rcopy(wbuf.at[oz, p, e + i], wbuf.at[oz, p, e + i],
                     wx_send.at[p, i], wx_recv.at[p, i], dev)

    def wc_copy(p, j, e):
        pair = wbuf.at[oz, p, pl.ds(e, 2)]
        return rcopy(pair, pair, wc_send.at[p, j], wc_recv.at[p, j], (other_core, row))


    def norm(unit):
        @pl.loop(0, 4)
        def _(f):
            clip = clip_ref[tm * 4 + f]
            shift = mod_ref[0, pl.ds(clip, 1), :]
            scale = 1.0 + mod_ref[1, pl.ds(clip, 1), :]
            v = stream_v[f, pl.ds(unit * 32, 32), :]
            centred = v - jnp.mean(v, axis=-1, keepdims=True)
            var = jnp.mean(centred * centred, axis=-1, keepdims=True)
            n = centred * lax.rsqrt(var + 1e-06) * scale + shift
            xg[unit, pl.ds(f * 32, 32), :] = n.astype(BF)

    def ycopy(i, src, dst, half, dev):
        if half is None:
            return rcopy(xg.at[src], xg.at[dst], y_send.at[i], y_recv.at[i], dev)
        rows = pl.ds(half * 64, 64)
        return rcopy(xg.at[src, rows], xg.at[dst, rows], y_send.at[i], y_recv.at[i], dev)

    y_copies = [
        ycopy(0, 0, 2, None, up), ycopy(1, 0, 3, None, down),
        ycopy(2, 1, 4, None, up), ycopy(3, 1, 5, None, down),
        ycopy(4, 2, 6, 0, up), ycopy(5, 3, 6, 1, down),
        ycopy(6, 4, 7, 0, up), ycopy(7, 5, 7, 1, down),
    ]
    for unit in range(2):
        load_stream[unit].wait()
        norm(unit)
        if unit == 0:
            pl.semaphore_wait(barrier, 22)
            load_w.start()
            for p in range(3):
                for i in range(2):
                    wz_copy(p, i, zl).start()
        if unit == 0:
            y_copies[0].start()
            y_copies[1].start()

    def unit_row(j):
        return (j & 128) + ((j >> 2) & 3) * 32 + ((j >> 4) & 7) * 4 + (j & 3)

    r_i = lax.broadcasted_iota(jnp.int32, (256, 256), 0)
    c_i = lax.broadcasted_iota(jnp.int32, (256, 256), 1)
    perm[...] = (unit_row(r_i) == c_i).astype(BF)
    perm_t[...] = (unit_row(c_i) == r_i).astype(BF)
    lane = lax.broadcasted_iota(jnp.int32, (1, 256), 1)

    def clip_of(f, found):
        return jnp.where((lane >> 2) == f, clip_ref[f], found)

    key = lax.fori_loop(0, 64, clip_of, jnp.zeros((1, 256), jnp.int32)) * 4 + (lane & 3)
    key = jnp.broadcast_to(key.astype(F32), (256, 256))
    mask[...] = jnp.where(key == key.T, 0.0, -1e30).astype(F32)

    def project_part(b, pz, part):
        k, n = batches[b]
        kk = (pz + hz) % 2
        slot = kk * 2 + (1 - kk) * zl
        x = xg[k:k + n].reshape(n * 128, 3072)
        out = dot(x, wbuf[pz, part].reshape(3072, 256)).astype(BF)
        qkv[slot, part, k:k + n] = out.reshape(n, 128, 256)

    def zcopy(b, part, slot):
        k, n = batches[b]
        units = pl.ds(k, n)
        return rcopy(qkv.at[2, part, units], qkv.at[slot, part, units], z_send.at[b, part],
                     z_recv.at[b, part], (tm, partner_row))

    def project(b):
        def sent(part):
            project_part(b, 1 - hz, part)
            zcopy(b, part, zl).start()

        def kept(part):
            project_part(b, hz, part)

        for step in (sent, kept):
            if b == 4:
                for part in range(3):
                    step(part)
            else:
                pl.loop(0, 3)(step)

    def stage_part(b, zz, part):
        k, n = batches[b]
        rows = qkv[zz, part, k:k + n].reshape(n * 128, 256)
        moved = dot(perm[:n * 128, :n * 128], rows).astype(BF).reshape(n, 8, 16, 256)
        for i in range(n):
            tsend[pl.ds(zz * 8, 8), k + i, part] = moved[i]

    def send_time(b, zz):
        k, n = batches[b]
        units = pl.ds(k, n)
        for dx in (2, 1, 3, 0):
            for dz in (1, 0):
                t = xs[dx] * 4 + zs[dz] * 2 + zz
                at = zz * 8 + xs[dx] * 2 + zs[dz]

                def send(t=t, at=at, dz=dz):
                    rcopy(tsend.at[at, units], trecv.at[tm, units], t_send.at[b], t_recv.at[b],
                          (t, rows_of[dz])).start()

                def keep(at=at):
                    trecv[tm, k:k + n] = tsend[at, k:k + n]

                if (dx, dz) == (0, 0):
                    pl.when(zz != core)(send)
                    pl.when(zz == core)(keep)
                else:
                    send()

    def stage_own(b):
        @pl.loop(0, 3)
        def _(part):
            stage_part(b, zl, part)

        send_time(b, zl)

    def stage_partner(b):
        @pl.loop(0, 3)
        def _(part):
            zcopy(b, part, oz).wait_recv()
            stage_part(b, oz, part)

        send_time(b, oz)

    factor = LOG2E / math.sqrt(HD)

    def attend(s, v):
        p = jnp.exp2((s - jnp.max(s, axis=-1, keepdims=True)) * factor).astype(BF)
        out = dot(p, jnp.concatenate([v, jnp.ones(v.shape, BF)], axis=1))
        return out[:, :HD] / out[:, HD:]

    def temporal(b):
        k, n = batches[b]
        units = pl.ds(k, n)
        await_bytes(trecv.at[pl.ds(0, 15), units], t_recv.at[b])
        for u in range(k, k + n):
            for h in range(2):
                cols = slice(h * HD, (h + 1) * HD)
                q, kk, v = (trecv[:, u, part, :, cols].reshape(256, HD) for part in range(3))
                o = attend(dot_nt(q, kk) + mask[...], v)
                osend[:, u, :, cols] = o.astype(BF).reshape(16, 16, HD)
        orecv[me_at, k:k + n] = osend[tm, k:k + n]
        for o in offsets:
            dev, _ = peer(*o)
            rcopy(osend.at[dev[0], units], orecv.at[me_at, units], o_send.at[b], o_recv.at[b], dev).start()

    def wait_back(b):
        k, n = batches[b]
        await_bytes(orecv.at[pl.ds(0, 15), pl.ds(k, n)], o_recv.at[b])

    def spatial(ka, kb):
        @pl.loop(0, 2)
        def _(pair):
            for f in range(2):
                rows = pl.ds(pl.multiple_of(pair * 64 + f * 32, 32), 32)
                for h in range(2):
                    cols = slice(h * HD, (h + 1) * HD)
                    q = jnp.concatenate(
                        [qkv[0:2, 0, k:k + 2, rows, cols].reshape(128, HD) for k in (ka, kb)], axis=0)
                    kk, v = (qkv[0:2, part, :, rows, cols].reshape(512, HD) for part in (1, 2))
                    o = attend(dot_nt(q, kk), v).reshape(2, 2, 2, 32, HD)
                    sp[:, ka:ka + 2, rows, cols] = o[0]
                    sp[:, kb:kb + 2, rows, cols] = o[1]

    def ccopy(u, r, at, kept):
        half = half_of[u]
        return rcopy(csend.at[u, r % 2], comb.at[kept, half], c_send.at[u, r % 2], c_recv.at[at, half],
                     (tm, r))

    def combine(*units):
        for u in units:
            back = dot(perm_t[...], orecv[:, u].reshape(256, 256)).reshape(2, 128, 256)
            csend[u] = (sp[:, u] + back).astype(BF)
        for u in units:
            if u < 2:
                ccopy(u, partner_row, row, y * 2 + hz).start()
                comb[y * 2 + hz, u] = csend[u, zl]
            else:
                for zz in range(2):
                    ccopy(u, y_of[u] * 2 + zz, row, y * 2 + hz).start()

    def project_out(pair, first):
        for ys in pair:
            for i in range(2):
                r = ys * 2 + i
                for half in range(2):
                    def wait(r=r, half=half, ys=ys):
                        dst = comb.at[ys * 2 + (r + zh) % 2, half]
                        rcopy(csend.at[0, 0], dst, c_send.at[0, 0], c_recv.at[r, half], (tm, r)).wait_recv()
                    if ys is y:
                        pl.when(i != zl)(wait)
                    else:
                        wait()

        heads = [2 * ys + i for ys in pair for i in range(2)]

        def tile(cols):
            left = jnp.concatenate([comb[h].reshape(256, 256) for h in heads], axis=1)
            right = jnp.concatenate([wo[h, :, cols] for h in heads], axis=0)
            acc = dot(left, right)
            for half in range(2):
                for f in range(4):
                    at = (half * 4 + f) * 32
                    rows = slice(half * 32, (half + 1) * 32)
                    piece = acc[at:at + 32]
                    if not first:
                        clip = clip_ref[tm * 4 + f]
                        piece = (piece + out_ref[f, rows, cols]) * mod_ref[2, pl.ds(clip, 1), cols]
                    out_ref[f, rows, cols] = piece

        @pl.loop(0, 3)
        def _(n):
            for i in range(2):
                tile(pl.ds(pl.multiple_of(n * 1024 + i * 512, 512), 512))

    load_w.wait()
    for p in range(3):
        for i in range(2):
            wz_copy(p, i, oz).wait_recv()
            wx_copy(p, i, e_own).start()
        wc_copy(p, 0, e_own).start()
        project_part(0, zl, p)
    y_copies[2].start()
    y_copies[3].start()

    def pass_x(p):
        for i in range(2):
            wx_copy(p, i, e_x).wait_recv()
        wc_copy(p, 1, e_x).start()

    pass_x(0)
    pass_x(1)
    for p in range(3):
        for j in range(2):
            wc_copy(p, j, e_cores[j]).wait_recv()
        project_part(0, oz, p)
        zcopy(0, p, zl).start()
        if p == 0:
            pass_x(2)
    load_wo.start()
    for i in range(2):
        y_copies[i].wait_recv()
    stage_own(0)
    project(1)
    stage_own(1)
    stage_partner(0)

    for i in range(2):
        y_copies[2 + i].wait_recv()
        y_copies[4 + i].start()
    project(2)
    for i in range(2):
        y_copies[6 + i].start()
    stage_own(2)
    stage_partner(1)
    temporal(0)

    y_copies[4].wait_recv()
    y_copies[5].wait_recv()
    project(3)
    stage_own(3)
    stage_partner(2)
    temporal(1)
    stage_partner(3)

    y_copies[6].wait_recv()
    y_copies[7].wait_recv()
    project(4)
    stage_own(4)
    temporal(2)
    stage_partner(4)
    temporal(3)

    spatial(2, 4)
    wait_back(1)
    combine(2, 3)
    wait_back(2)
    combine(4, 5)
    temporal(4)
    spatial(6, 0)
    wait_back(3)
    wait_back(0)
    combine(6, 0, 1)
    wait_back(4)
    combine(7)
    load_wo.wait()
    project_out((yp, ym), first=True)
    project_out((y, yq), first=False)

    for p in range(3):
        for i in range(2):
            wz_copy(p, i, zl).wait_send()
            wx_copy(p, i, e_own).wait_send()
            wc_copy(p, i, e_own).wait_send()
    for c in y_copies:
        c.wait_send()
    for b, (k, n) in enumerate(batches):
        for part in range(3):
            zcopy(b, part, zl).wait_send()
        await_bytes(tsend.at[pl.ds(0, 15), pl.ds(k, n)], t_send.at[b])
        await_bytes(osend.at[pl.ds(0, 15), pl.ds(k, n)], o_send.at[b])
    for u in range(8):
        if u < 2:
            ccopy(u, partner_row, row, y * 2 + hz).wait_send()
        else:
            for zz in range(2):
                ccopy(u, y_of[u] * 2 + zz, row, y * 2 + hz).wait_send()


def attention(clip_ids, stream, mod, weight, out_weight):
    vmem = pl.BlockSpec(memory_space=pltpu.VMEM)
    hbm = pl.BlockSpec(memory_space=pl.ANY)
    dma = pltpu.SemaphoreType.DMA
    return pl.pallas_call(
        attention_kernel,
        out_shape=pltpu.VMEM((4, 64, 3072), F32),
        in_specs=[pl.BlockSpec(memory_space=pltpu.SMEM), hbm, vmem, hbm, hbm],
        out_specs=vmem,
        scratch_shapes=[
            pltpu.VMEM((4, 64, 3072), F32),
            pltpu.VMEM((8, 128, 3072), BF),
            pltpu.VMEM((2, 3, 8, 384, 256), BF),
            pltpu.VMEM((8, 256, 3072), BF),
            pltpu.VMEM((3, 3, 8, 128, 256), BF),
            pltpu.VMEM((16, 8, 3, 16, 256), BF),
            pltpu.VMEM((16, 8, 3, 16, 256), BF),
            pltpu.VMEM((16, 8, 16, 256), BF),
            pltpu.VMEM((16, 8, 16, 256), BF),
            pltpu.VMEM((8, 2, 128, 256), BF),
            pltpu.VMEM((8, 2, 128, 256), BF),
            pltpu.VMEM((2, 8, 128, 256), F32),
            pltpu.VMEM((256, 256), BF),
            pltpu.VMEM((256, 256), BF),
            pltpu.VMEM((256, 256), F32),
            dma((4,)),
            dma((8,)), dma((8,)),
            dma((3, 2)), dma((3, 2)),
            dma((3, 2)), dma((3, 2)),
            dma((3, 2)), dma((3, 2)),
            dma((5, 3)), dma((5, 3)),
            dma((5,)), dma((5,)),
            dma((5,)), dma((5,)),
            dma((8, 2)), dma((8, 2)),
        ],
        compiler_params=pltpu.CompilerParams(
            collective_id=0, has_side_effects=True, vmem_limit_bytes=60 * 1024 * 1024
        ),
        name="attention",
    )(clip_ids, stream, mod, weight, out_weight)


def per_device(stream, clip_ids, modulation, qkv_weight, out_weight):
    mod = jnp.transpose(modulation, (1, 0, 2))
    weight = jnp.transpose(qkv_weight, (1, 0, 2)).reshape(3, 8, 384, 256)
    return attention(clip_ids, stream, mod, weight, out_weight.reshape(8, 256, 3072))


def solution(mesh):
    placed = (P("tm", "row", None), P(), P(), P(None, None, "row"), P())
    return jax.shard_map(
        per_device, mesh=mesh, in_specs=placed, out_specs=P("tm", "row", None), check_vma=False
    )
```
